32 devices in a mesh: section: 4 (over y, x), dp: 8 (over z, core).
Axes of the slice: x: 2, y: 2, z: 4, core: 2. Of those that a mesh axis runs over, the one named last changes fastest.
Arguments:
- tokens: bfloat16 [2, 2048, 512], P(None, 'dp'), may hold values from -40 to 40
- seq_lengths: int32 [2, 16], P(None, 'dp'), may hold values from 0 to 256, as said below
- out_grad: bfloat16 [2, 2048, 512], P(None, 'dp'), may hold values from -6 to 6
- norm_gain: float32 [2, 512], replicated, may hold values from 0.25 to 1.75
- norm_bias: float32 [2, 512], replicated, may hold values from -3 to 3
- decay_rate: float32 [2, 192], replicated, may hold values from 0.05 to 2
- frequency: float32 [2, 192], replicated, may hold values from -8 to 8
- log_step: float32 [2, 192], replicated, may hold values from -6.9 to -2.3
- input_matrix: bfloat16 [2, 512, 384], replicated, may hold values from -0.25 to 0.25
- output_matrix: bfloat16 [2, 384, 512], replicated, may hold values from -0.625 to 0.625
- skip_gain: float32 [2, 512], replicated, may hold values from -4 to 4
- gate_matrix: bfloat16 [2, 512, 512], replicated, may hold values from -0.25 to 0.25
- gate_bias: float32 [2, 512], replicated, may hold values from -3 to 3
Outputs:
- mixed_out: bfloat16 [2, 2048, 512], P(None, 'dp', 'section')
- token_grad: float32 [2, 2048, 512], P(None, 'dp', 'section')
- norm_gain_grad: float32 [2, 512], replicated
- norm_bias_grad: float32 [2, 512], replicated
- decay_rate_grad: float32 [2, 192], replicated
- frequency_grad: float32 [2, 192], replicated
- log_step_grad: float32 [2, 192], replicated
- input_matrix_grad: float32 [2, 512, 384], replicated
- output_matrix_grad: float32 [2, 384, 512], replicated
- skip_gain_grad: float32 [2, 512], replicated
- gate_matrix_grad: float32 [2, 512, 512], replicated
- gate_bias_grad: float32 [2, 512], replicated
The draws below stay inside these ranges and needn't reach their ends.
Inputs may be any that keep to these rules, and one draw needn't show every extreme that they name: `seq_lengths`: for each micro-batch and device the two entries are a first length of at least 32 and a second length that is either 0 or 256 minus the first; in every micro-batch some device's first length is 256.
All inputs are finite; a program needn't handle non-finite values.
Results may differ from the reference program's by a relative error of at most 0.012.
Values may be sent and summed in bfloat16 or wider, within the bound.
A program may use at most 320 MiB of HBM per device.

```python
import math
import jax
import jax.numpy as jnp
from jax import lax

H = 512
P_SIZE = 384
ROWS = 256
MICRO = 2
BATCH_ROWS = 2048


def draw_tokens(key, part):
    key = jax.random.fold_in(key, 11)
    noise_key, offset_key = jax.random.split(key)
    buckets = BATCH_ROWS // ROWS
    position_ratio = (jnp.arange(BATCH_ROWS, dtype=jnp.int32) // ROWS).astype(jnp.float32) / max(buckets - 1, 1)
    base_noise = jnp.clip(jax.random.normal(noise_key, (MICRO, BATCH_ROWS, H), jnp.float32), -5.0, 5.0)
    offset = jnp.clip(0.5 * jax.random.normal(offset_key, (H,), jnp.float32), -2.0, 2.0)
    spread = jnp.exp(position_ratio * math.log(3.0))
    return (spread[None, :, None] * (base_noise + offset[None, None, :])).astype(jnp.bfloat16)


def draw_seq_lengths(key, part):
    key = jax.random.fold_in(key, 23)
    first_key, full_key, coin_key = jax.random.split(key, 3)
    buckets = BATCH_ROWS // ROWS
    first_len = jax.random.randint(first_key, (MICRO, buckets), ROWS // 8, ROWS + 1)
    chosen = jax.random.randint(full_key, (MICRO, 1), 0, buckets)
    first_len = jnp.where(jnp.arange(buckets)[None, :] == chosen, ROWS, first_len)
    coin_flip = jax.random.randint(coin_key, (MICRO, buckets), 0, 2)
    second = (ROWS - first_len) * coin_flip
    return jnp.stack([first_len, second], axis=2).reshape(MICRO, 2 * buckets).astype(jnp.int32)


def block_scale(own_key, dims, pieces, smallest, high):
    factor_of, own = 1.0, jax.random.fold_in(own_key, 6)
    for position, parts in pieces:
        draws = jnp.exp(jax.random.uniform(jax.random.fold_in(own, position), (parts,), jnp.float32, smallest / len(pieces), high / len(pieces)))
        factor_of = factor_of * jnp.repeat(draws, dims[position] // parts).reshape([-1 if axis == position else 1 for axis in range(len(dims))])
    return factor_of


def bell_draw(key, extent, width, reach, cuts=(), kind=jnp.bfloat16):
    gain = block_scale(key, extent, cuts, -0.22, 0.18) if cuts else 1.0
    entries = jax.random.normal(key, extent, jnp.float32) * width * gain
    return jnp.minimum(jnp.maximum(entries, -reach), reach).astype(kind)


def setup_inputs(seed: int = 0) -> dict:
    streams_of = jax.random.split(jax.random.key(seed), 14)
    tokens = draw_tokens(jax.random.fold_in(streams_of[13], 71), 0)
    seq_lengths = draw_seq_lengths(jax.random.fold_in(streams_of[13], 71), 0)
    out_grad = bell_draw(streams_of[2], (MICRO, BATCH_ROWS, H), 1.0, 6.0, ((1, 8),))
    norm_gain = jnp.clip(1.0 + 0.15 * jax.random.normal(streams_of[3], (2, H), jnp.float32), 0.25, 1.75)
    norm_bias = bell_draw(streams_of[4], (2, H), 0.5, 3.0, (), jnp.float32)
    decay_rate = jnp.clip(jnp.exp(jax.random.uniform(streams_of[5], (2, P_SIZE // 2), jnp.float32, math.log(0.05), math.log(2.0))), 0.05, 2.0)
    frequency = jnp.clip(jax.random.uniform(streams_of[6], (2, P_SIZE // 2), jnp.float32, -8.0, 8.0), -8.0, 8.0)
    log_step = jnp.clip(jax.random.uniform(streams_of[7], (2, P_SIZE // 2), jnp.float32, -6.9, -2.3), -6.9, -2.3)
    input_matrix = bell_draw(streams_of[8], (2, H, P_SIZE), H ** -0.5, 0.25)
    output_matrix = bell_draw(streams_of[9], (2, P_SIZE, H), (P_SIZE // 4) ** -0.5, 0.625)
    skip_gain = bell_draw(streams_of[10], (2, H), 1.0, 4.0, (), jnp.float32)
    gate_matrix = bell_draw(streams_of[11], (2, H, H), H ** -0.5, 0.25)
    gate_bias = bell_draw(streams_of[12], (2, H), 0.5, 3.0, (), jnp.float32)
    return dict(tokens=tokens, seq_lengths=seq_lengths, out_grad=out_grad, norm_gain=norm_gain, norm_bias=norm_bias, decay_rate=decay_rate, frequency=frequency, log_step=log_step, input_matrix=input_matrix, output_matrix=output_matrix, skip_gain=skip_gain, gate_matrix=gate_matrix, gate_bias=gate_bias)


epsilon = 1e-05
highest = lax.Precision.HIGHEST

@jax.custom_vjp
def low(v):
    return lax.optimization_barrier(v.astype(jnp.bfloat16)).astype(jnp.float32)

@jax.custom_vjp
def low_back(v):
    return v

def low_keep(v):
    return (low(v), None)

def low_pass(kept, grad):
    return (grad,)

def back_keep(v):
    return (v, None)

def back_low(kept, grad):
    return (low(grad),)
low.defvjp(low_keep, low_pass)
low_back.defvjp(back_keep, back_low)

def row_masks(lengths, row_total):
    row_place = jnp.arange(row_total, dtype=jnp.int32)[None, :]
    first_len = lengths[:, 0:1].astype(jnp.int32)
    total_len = first_len + lengths[:, 1:2].astype(jnp.int32)
    valid_rows = (row_place < total_len).astype(jnp.float32)
    starts = (row_place == 0) | (row_place == first_len) | (row_place >= total_len)
    end_rows = (row_place == first_len - 1) | (row_place == total_len - 1) | (row_place >= total_len) | (row_place == row_total - 1)
    return (valid_rows, 1.0 - starts.astype(jnp.float32), 1.0 - end_rows.astype(jnp.float32))

def discretize(decay_row, spin_row, step_row):
    step_size = jnp.exp(step_row)
    damping = jnp.exp(-decay_row * step_size)
    bar_re = damping * jnp.cos(spin_row * step_size)
    bar_im = damping * jnp.sin(spin_row * step_size)
    modulus = decay_row * decay_row + spin_row * spin_row
    fac_re = ((bar_re - 1.0) * -decay_row + bar_im * spin_row) / modulus
    fac_im = (bar_im * -decay_row - (bar_re - 1.0) * spin_row) / modulus
    return (bar_re, bar_im, fac_re, fac_im)

def combine(earlier, later):
    first_re, first_im, carry_re, carry_im = earlier
    second_re, second_im, add_re, add_im = later
    return (second_re * first_re - second_im * first_im, second_re * first_im + second_im * first_re, second_re * carry_re - second_im * carry_im + add_re, second_re * carry_im + second_im * carry_re + add_im)

def mixer_bucket(operands, center, inv_scale, gain_row, bias_row, bars, in_matrix, out_matrix, skip_row, reverse):
    stream, valid_rows, keep_rows = operands
    normed = (stream - center) * inv_scale
    scaled = normed * gain_row + bias_row
    driven = low_back(jnp.dot(low(scaled), in_matrix, precision=highest))
    half_width = driven.shape[1] // 2
    bar_re, bar_im, fac_re, fac_im = bars
    valid_col = valid_rows[:, None]
    keep_col = keep_rows[:, None]
    drive_real = driven[:, :half_width]
    drive_imag = driven[:, half_width:]
    elements = (keep_col * bar_re, keep_col * bar_im, valid_col * (fac_re * drive_real - fac_im * drive_imag), valid_col * (fac_re * drive_imag + fac_im * drive_real))
    states = lax.associative_scan(combine, elements, reverse=reverse, axis=0)
    joined = jnp.concatenate([states[2], -states[3]], axis=1)
    return 2.0 * jnp.dot(low(joined), out_matrix, precision=highest) + skip_row * scaled

def mixer_layer(stream, valid_rows, keep_rows, params, layer_pos, reverse):
    norm_gain, norm_bias, decay_rate, frequency, log_step, input_matrix, output_matrix, skip_gain = params[:8]
    valid_flat = valid_rows.reshape(-1)[:, None]
    row_count = jnp.sum(valid_rows)
    center = lax.optimization_barrier(jnp.sum(stream * valid_flat, axis=0)) / row_count
    square_mean = lax.optimization_barrier(jnp.sum(stream * stream * valid_flat, axis=0)) / row_count
    inv_scale = lax.rsqrt(square_mean - center * center + epsilon)
    bars = discretize(decay_rate[layer_pos], frequency[layer_pos], log_step[layer_pos])
    buckets = stream.reshape(valid_rows.shape + (stream.shape[1],))

    def one_bucket(operands):
        return mixer_bucket(operands, center, inv_scale, norm_gain[layer_pos], norm_bias[layer_pos], bars, input_matrix[layer_pos], output_matrix[layer_pos], skip_gain[layer_pos], reverse)
    mixed_rows = lax.map(jax.checkpoint(one_bucket), (buckets, valid_rows, keep_rows))
    return mixed_rows.reshape(stream.shape)

def gate_bucket(operands, matrix_row, bias_row):
    branch, valid_rows = operands
    active = jax.nn.gelu(branch, approximate=False)
    logits = low_back(jnp.dot(low(active), matrix_row, precision=highest)) + bias_row
    return valid_rows[:, None] * active * jax.nn.sigmoid(logits)

def gate_layer(branch, valid_rows, params, layer_pos):
    buckets = branch.reshape(valid_rows.shape + (branch.shape[1],))

    def one_bucket(operands):
        return gate_bucket(operands, params[8][layer_pos], params[9][layer_pos])
    gated_rows = lax.map(jax.checkpoint(one_bucket), (buckets, valid_rows))
    return gated_rows.reshape(branch.shape)

def reference(tokens, seq_lengths, out_grad, norm_gain, norm_bias, decay_rate, frequency, log_step, input_matrix, output_matrix, skip_gain, gate_matrix, gate_bias):
    params = tuple((member.astype(jnp.float32) for member in (norm_gain, norm_bias, decay_rate, frequency, log_step, input_matrix, output_matrix, skip_gain, gate_matrix, gate_bias)))

    def forward(weights, streams):
        results = []
        for micro_index in range(MICRO):
            valid_rows, keep_fore, keep_back = row_masks(seq_lengths[micro_index].reshape(-1, 2), ROWS)
            first_in = streams[micro_index]
            first_mix = low_back(low(mixer_layer(first_in, valid_rows, keep_fore, weights, 0, False)))
            first_gate = low_back(low(gate_layer(first_mix, valid_rows, weights, 0)))
            second_in = low_back(first_in) + first_gate
            second_mix = low_back(low(mixer_layer(low_back(second_in), valid_rows, keep_back, weights, 1, True)))
            second_gate = gate_layer(second_mix, valid_rows, weights, 1)
            results.append(low_back(low(second_in)) + second_gate)
        return jnp.stack(results)
    mixed_out, pullback = jax.vjp(forward, params, tokens.astype(jnp.float32))
    weight_grads, token_grad = pullback(out_grad.astype(jnp.float32))
    return (mixed_out.astype(jnp.bfloat16), token_grad, weight_grads[0], weight_grads[1], weight_grads[2], weight_grads[3], weight_grads[4], weight_grads[5], weight_grads[6], weight_grads[7], weight_grads[8], weight_grads[9])
```

```python
from functools import partial
from types import SimpleNamespace

import jax
import jax.numpy as jnp
from jax import lax
from jax.experimental import pallas as pl
from jax.experimental.pallas import tpu as pltpu
from jax.sharding import PartitionSpec as P

epsilon = 1e-05
MESH = pl.DeviceIdType.MESH
F32 = jnp.float32
BF16 = jnp.bfloat16
SUB = 8
QUAD = 4
REDUCES = 9


STAGES = tuple(dict(mine=0, theirs=0, chip=0, quad=0, group=0, full=0))


def matmul(left, right):
    return jnp.dot(left, right, preferred_element_type=F32)


def matmul_nt(left, right):
    return lax.dot_general(left, right, (((1,), (1,)), ((), ())), preferred_element_type=F32)


def matmul_tn(left, right):
    return lax.dot_general(left, right, (((0,), (0,)), ((), ())), preferred_element_type=F32)


def cmul(ar, ai, br, bi):
    return ar * br - ai * bi, ar * bi + ai * br


def repeat_lanes(x, times):
    return jnp.concatenate([x] * times, axis=1)


def fold_rows(x):
    return jnp.sum(x.reshape(x.shape[0] // SUB, SUB, x.shape[1]), axis=0)


def unfold(total, first, count):
    return jnp.concatenate([total[first + k : first + k + 1, :] for k in range(count)], axis=1)


class SmallSum:
    def __init__(self, place, own, sibling, slots, send_sems, recv_sems, index):
        self.place, self.own, self.sibling, self.slots = place, own, sibling, slots
        self.send_sems, self.recv_sems, self.index = send_sems, recv_sems, index

    def start(self):
        at = self.place
        self.copy = pltpu.make_async_remote_copy(
            src_ref=self.own,
            dst_ref=self.sibling,
            send_sem=self.send_sems.at[self.index, 0],
            recv_sem=self.recv_sems.at[self.index, 0],
            device_id=(at.section, at.sibling),
            device_id_type=MESH,
        )
        self.copy.start()

    def turn(self):
        at = self.place
        self.copy.wait()
        chip = at.chip
        self.slots[chip] = self.own[...] + self.sibling[...]
        self.copies = []
        for step in range(1, at.chips):
            copy = pltpu.make_async_remote_copy(
                src_ref=self.slots.at[chip],
                dst_ref=self.slots.at[chip],
                send_sem=self.send_sems.at[self.index, step],
                recv_sem=self.recv_sems.at[self.index, step],
                device_id=(at.section, at.chip_peer(step)),
                device_id_type=MESH,
            )
            copy.start()
            self.copies.append(copy)

    def total(self):
        for copy in self.copies:
            copy.wait()
        result = self.slots[0]
        for chip in range(1, self.place.chips):
            result = result + self.slots[chip]
        return result


class GradSum:
    def __init__(self, place, refs, send_sems, recv_sems, index):
        self.place = place
        self.mine, self.theirs, self.chip_part, self.quad_in, self.group_in, self.full = refs
        self.send_sems, self.recv_sems, self.index = send_sems, recv_sems, index
        self.sem = 0

    def remote(self, src, dst, device):
        copy = pltpu.make_async_remote_copy(
            src_ref=src,
            dst_ref=dst,
            send_sem=self.send_sems.at[self.index, self.sem],
            recv_sem=self.recv_sems.at[self.index, self.sem],
            device_id=device,
            device_id_type=MESH,
        )
        self.sem += 1
        copy.start()
        return copy

    def to_core(self):
        at = self.place
        self.copy = self.remote(
            self.mine.at[1 - at.core], self.theirs, (at.section, at.sibling)
        )

    def to_quad(self):
        at = self.place
        self.copy.wait()
        for part in range(QUAD):
            both = self.mine[at.core, part].astype(F32) + self.theirs[part].astype(F32)
            self.chip_part[part] = both.astype(BF16)
        self.copies = []
        for step in range(1, QUAD):
            other = lax.rem(at.quad + step, QUAD)
            self.copies.append(
                self.remote(
                    self.chip_part.at[other],
                    self.quad_in.at[at.quad],
                    (at.section, at.quad_peer(step)),
                )
            )
        self.quad_in[at.quad] = self.chip_part[at.quad]

    def to_groups(self):
        at = self.place
        for copy in self.copies:
            copy.wait()
        total = self.quad_in[0].astype(F32)
        for part in range(1, QUAD):
            total = total + self.quad_in[part].astype(F32)
        if at.groups > 1:
            group = at.group
            self.group_in[group] = total.astype(BF16)
            copies = []
            for step in range(1, at.groups):
                copies.append(
                    self.remote(
                        self.group_in.at[group],
                        self.group_in.at[group],
                        (at.section, at.chip_peer(step * QUAD)),
                    )
                )
            for copy in copies:
                copy.wait()
            total = self.group_in[0].astype(F32)
            for other in range(1, at.groups):
                total = total + self.group_in[other].astype(F32)
        piece = self.full.at[at.core, at.section, at.quad]
        piece[...] = total.astype(BF16)
        self.copies = [
            self.remote(piece, piece, (at.section, at.quad_peer(step)))
            for step in range(1, QUAD)
        ]

    def to_sections(self):
        at = self.place
        for copy in self.copies:
            copy.wait()
        piece = self.full.at[at.core, at.section]
        self.copies = [
            self.remote(piece, piece, (lax.rem(at.section + step, at.sections), at.dp))
            for step in range(1, at.sections)
        ]

    def to_sibling(self):
        at = self.place
        for copy in self.copies:
            copy.wait()
        piece = self.full.at[at.core]
        self.copy = self.remote(piece, piece, (at.section, at.sibling))

    def to_result(self, result, sem):
        self.copy.wait()
        self.out = pltpu.make_async_copy(self.full, result, sem)
        self.out.start()

    def end(self):
        self.out.wait()


def main_kernel(cfg, names, *refs):
    r = SimpleNamespace(**dict(zip(names, refs)))
    rows, width, states, half, lanes = (
        cfg.rows,
        cfg.width,
        cfg.states,
        cfg.half,
        cfg.lanes,
    )
    steps = rows // SUB
    section = lax.axis_index("section")
    dp = lax.axis_index("dp")
    chips = cfg.dp // 2
    core, chip = lax.rem(dp, 2), lax.div(dp, 2)
    quad, group = lax.rem(chip, QUAD), lax.div(chip, QUAD)
    place = SimpleNamespace(
        section=section,
        sections=cfg.sections,
        dp=dp,
        core=core,
        chip=chip,
        chips=chips,
        quad=quad,
        group=group,
        groups=chips // QUAD,
        sibling=dp + 1 - 2 * core,
        chip_peer=lambda step: lax.rem(chip + step, chips) * 2 + core,
        quad_peer=lambda step: (group * QUAD + lax.rem(quad + step, QUAD)) * 2 + core,
    )

    peers = [(section, place.sibling)]
    peers += [(section, place.chip_peer(step)) for step in range(1, chips)]
    peers += [(lax.rem(section + step, cfg.sections), dp) for step in range(1, cfg.sections)]
    barrier = pltpu.get_barrier_semaphore()
    for peer in peers:
        pl.semaphore_signal(barrier, inc=1, device_id=peer, device_id_type=MESH)

    small = [
        SmallSum(
            place,
            r.sum_own.at[k],
            r.sum_sibling.at[k],
            r.sum_slots.at[k],
            r.sum_send,
            r.sum_recv,
            k,
        )
        for k in range(REDUCES)
    ]
    first_sum = small[0]
    mid_sum = [small[1], small[2]]
    upper_sum = [small[3], small[4]]
    lower_sum = [small[5], small[6]]
    layer_sum = [small[8], small[7]]
    batches = [
        GradSum(
            place,
            [getattr(r, f"{part}_{k}") for part in STAGES],
            r.grad_send,
            r.grad_recv,
            k,
        )
        for k in range(3)
    ]
    upper_batch, gate_batch, in_batch = batches

    first_len = [r.lengths[m, 0] for m in range(2)]
    total_len = [r.lengths[m, 0] + r.lengths[m, 1] for m in range(2)]

    def put(index, at, row):
        for k in range(row.shape[1] // 128):
            r.sum_own[index, at + k : at + k + 1, :] = row[:, k * 128 : (k + 1) * 128]

    chunk = 32
    for m in range(2):

        def token_sums(t, carry, m=m):
            at = pl.ds(pl.multiple_of(t * chunk, chunk), chunk)
            v = r.tokens[m, at, :].astype(F32)
            place_row = t * chunk + lax.broadcasted_iota(jnp.int32, (chunk, width), 0)
            kept = jnp.where(place_row < total_len[m], v, 0.0)
            return carry[0] + fold_rows(kept), carry[1] + fold_rows(kept * v)

        zero = jnp.zeros((SUB, width), F32)
        sums, squares = lax.fori_loop(0, rows // chunk, token_sums, (zero, zero))
        put(0, 8 * m, jnp.sum(sums, axis=0, keepdims=True))
        put(0, 8 * m + 4, jnp.sum(squares, axis=0, keepdims=True))
        count = jnp.minimum(total_len[m], rows).astype(F32)
        r.sum_own[0, 16 + m : 17 + m, :] = jnp.full((1, 128), count, F32)

    pl.semaphore_wait(barrier, len(peers))
    first_sum.start()

    at_i = lax.broadcasted_iota(jnp.int32, (rows, rows), 0)
    at_r = lax.broadcasted_iota(jnp.int32, (rows, rows), 1)
    r.spread[...] = jnp.where(
        at_r == (at_i % SUB) * steps + at_i // SUB, 1.0, 0.0
    ).astype(BF16)
    r.gather[...] = jnp.where(
        at_i == (at_r % SUB) * steps + at_r // SUB, 1.0, 0.0
    ).astype(BF16)
    for m in range(2):
        r.first_in[m] = matmul(r.spread[...], r.tokens[m]).astype(BF16)
    first_sum.turn()
    for m in range(2):
        r.out_grads[m] = matmul(r.spread[...], r.out_grad[m]).astype(BF16)
    held = lax.broadcasted_iota(jnp.int32, (rows, 128), 0)
    held = (held % SUB) * steps + held // SUB
    all_start, all_end = [], []
    for m in range(2):
        one, zero = jnp.float32(1.0), jnp.float32(0.0)
        past = held >= total_len[m]
        starts = (held == 0) | (held == first_len[m]) | past
        ends = (held == first_len[m] - 1) | (held == total_len[m] - 1) | past | (held == rows - 1)
        r.valid[m] = jnp.where(past, zero, one)
        r.keep_start[m] = jnp.where(starts, zero, one)
        r.keep_end[m] = jnp.where(ends, zero, one)
        for kept, mask in ((all_start, r.keep_start), (all_end, r.keep_end)):
            kept.append(jnp.min(mask[m].reshape(steps, SUB, 128), axis=0))

    r.par[...] = jnp.zeros((SUB, lanes), F32)
    r.par[0:2, :] = jnp.ones((2, lanes), F32)
    r.par[0:2, 0:half] = r.decay[...]
    r.par[2:4, 0:half] = r.freq[...]
    r.par[4:6, 0:half] = r.lstep[...]
    decay, spin = r.par[0:2, :], r.par[2:4, :]
    step_size = jnp.exp(r.par[4:6, :])
    damping = jnp.exp(-decay * step_size)
    bar_re = damping * jnp.cos(spin * step_size)
    bar_im = damping * jnp.sin(spin * step_size)
    modulus = decay * decay + spin * spin
    fac_re = ((bar_re - 1.0) * -decay + bar_im * spin) / modulus
    fac_im = (bar_im * -decay - (bar_re - 1.0) * spin) / modulus
    pow_re, pow_im = bar_re, bar_im
    power = 1
    while power < steps:
        pow_re, pow_im = cmul(pow_re, pow_im, pow_re, pow_im)
        power *= 2

    lane = lax.broadcasted_iota(jnp.int32, (1, 128), 1)
    low_lanes = lane < half - 128
    turn_by = half - 128

    for l in range(2):

        def pad_in(t, carry, l=l):
            at = pl.ds(pl.multiple_of(t * chunk, chunk), chunk)
            tile = [r.b_in[l, at, k * 128 : (k + 1) * 128].astype(F32) for k in range(3)]
            rolled = [pltpu.roll(x, 64, 1) for x in tile[1:]]
            padded = [
                tile[0],
                jnp.where(low_lanes, tile[1], 0.0),
                jnp.where(low_lanes, rolled[0], rolled[1]),
                jnp.where(low_lanes, rolled[1], 0.0),
            ]
            r.b_pad[l, at, :] = jnp.concatenate(padded, axis=1).astype(BF16)
            return carry

        lax.fori_loop(0, width // chunk, pad_in, 0)
        blank = jnp.zeros((lanes - half, width), BF16)
        r.c_pad[l, 0:half, :] = r.c_out[l, 0:half, :]
        r.c_pad[l, half:lanes, :] = blank
        r.c_pad[l, lanes : lanes + half, :] = r.c_out[l, half:states, :]
        r.c_pad[l, lanes + half : 2 * lanes, :] = blank

    def across(end, coef, reverse):
        end_re, end_im = end
        coef_re, coef_im = coef
        sub = lax.broadcasted_iota(jnp.int32, (SUB, lanes), 0)
        for by in (1, 2, 4):
            turn = SUB - by if reverse else by
            live = sub < SUB - by if reverse else sub >= by

            def moved(x):
                return jnp.where(live, pltpu.roll(x, turn, 0), 0.0)

            add_re, add_im = cmul(coef_re, coef_im, moved(end_re), moved(end_im))
            coef_re, coef_im = cmul(coef_re, coef_im, moved(coef_re), moved(coef_im))
            end_re, end_im = end_re + add_re, end_im + add_im
        turn = SUB - 1 if reverse else 1
        live = sub < SUB - 1 if reverse else sub >= 1
        return tuple(jnp.where(live, pltpu.roll(x, turn, 0), 0.0) for x in (end_re, end_im))

    def wide8(x, l):
        return jnp.broadcast_to(x[l : l + 1, :], (SUB, x.shape[1]))

    def group_rows(p):
        return pl.ds(pl.multiple_of(p * SUB, SUB), SUB)

    def scan_coefs(l, m, reverse):
        keep = r.keep_end if reverse else r.keep_start
        all_kept = repeat_lanes((all_end if reverse else all_start)[m], lanes // 128)
        product = (all_kept * wide8(pow_re, l), all_kept * wide8(pow_im, l))
        return keep, wide8(bar_re, l), wide8(bar_im, l), product

    def advance(keep, m, at, br, bi, re, im, src_re, src_im):
        k = repeat_lanes(keep[m, at, :], lanes // 128)
        kr, ki = k * br, k * bi
        return kr * re - ki * im + src_re, kr * im + ki * re + src_im

    def scan_states(l, m):
        reverse = l == 1
        lead = 0 if reverse else 1
        keep, br, bi, product = scan_coefs(l, m, reverse)
        fr, fi = wide8(fac_re, l), wide8(fac_im, l)
        zero = jnp.zeros((SUB, lanes), F32)

        def ends(t, carry):
            p = steps - 1 - t if reverse else t
            at = group_rows(p)
            v = repeat_lanes(r.valid[m, at, :], lanes // 128)
            drive_re = r.drive[l, m, at, 0:lanes]
            drive_im = r.drive[l, m, at, lanes : 2 * lanes]
            src_re, src_im = cmul(fr, fi, v * drive_re, v * drive_im)
            r.state[l, m, group_rows(p + lead), 0:lanes] = src_re
            r.state[l, m, group_rows(p + lead), lanes : 2 * lanes] = src_im
            return advance(keep, m, at, br, bi, *carry, src_re, src_im)

        end = lax.fori_loop(0, steps, ends, (zero, zero), unroll=4)
        enter = across(end, product, reverse)
        first = steps if reverse else 0
        r.state[l, m, first * SUB : (first + 1) * SUB, 0:lanes] = enter[0]
        r.state[l, m, first * SUB : (first + 1) * SUB, lanes : 2 * lanes] = enter[1]

        def fill(t, carry):
            done = []
            for k in range(2):
                p = steps - 1 - (2 * t + k) if reverse else 2 * t + k
                at, to = group_rows(p), group_rows(p + lead)
                src_re = r.state[l, m, to, 0:lanes]
                src_im = r.state[l, m, to, lanes : 2 * lanes]
                carry = advance(keep, m, at, br, bi, *carry, src_re, src_im)
                r.state[l, m, to, 0:lanes] = carry[0]
                r.state[l, m, to, lanes : 2 * lanes] = carry[1]
                done.append(jnp.concatenate([carry[0], -carry[1]], axis=1))
            pair = steps // 2 - 1 - t if reverse else t
            both = jnp.concatenate(done[::-1] if reverse else done, axis=0)
            to = pl.ds(pl.multiple_of(m * rows + pair * 16, 16), 16)
            r.joined[l, to, :] = both.astype(BF16)
            return carry

        lax.fori_loop(0, steps // 2, fill, enter, unroll=2)

    def scan_grads(l, m):
        reverse = l == 0
        back = 1 if l == 1 else 0
        keep, br, bi, product = scan_coefs(l, m, reverse)
        keep_state = r.keep_start if l == 0 else r.keep_end
        fr, fi = 2.0 * wide8(fac_re, l), 2.0 * wide8(fac_im, l)
        zero = jnp.zeros((SUB, lanes), F32)

        def ends(t, carry):
            p = steps - 1 - t if reverse else t
            at = group_rows(p)
            q_re = r.work[at, 0:lanes]
            q_im = r.work[at, lanes : 2 * lanes]
            return advance(keep, m, at, br, bi, *carry, q_re, q_im)

        end = lax.fori_loop(0, steps, ends, (zero, zero), unroll=4)
        enter = across(end, product, reverse)

        def fill(t, carry):
            w, bar_sum, fac_sum = carry
            done = []
            for k in range(2):
                p = steps - 1 - (2 * t + k) if reverse else 2 * t + k
                at, near = group_rows(p), group_rows(p + back)
                q_re = r.work[at, 0:lanes]
                q_im = r.work[at, lanes : 2 * lanes]
                w = advance(keep, m, at, br, bi, *w, q_re, q_im)
                kept = repeat_lanes(keep_state[m, at, :], lanes // 128)
                near_re = kept * r.state[l, m, near, 0:lanes]
                near_im = kept * r.state[l, m, near, lanes : 2 * lanes]
                term = cmul(*w, near_re, near_im)
                bar_sum = (bar_sum[0] + term[0], bar_sum[1] + term[1])
                v = repeat_lanes(r.valid[m, at, :], lanes // 128)
                vw = (v * w[0], v * w[1])
                drive_re = r.drive[l, m, at, 0:lanes]
                drive_im = r.drive[l, m, at, lanes : 2 * lanes]
                term = cmul(*vw, drive_re, drive_im)
                fac_sum = (fac_sum[0] + term[0], fac_sum[1] + term[1])
                gd_re, gd_im = cmul(fr, fi, *vw)
                im_low = pltpu.roll(-gd_im[:, 0:128], 64, 1)
                im_high = pltpu.roll(-gd_im[:, 128:256], 64, 1)
                done.append(
                    jnp.concatenate(
                        [
                            gd_re[:, 0:128],
                            jnp.where(low_lanes, gd_re[:, 128:256], im_low),
                            jnp.where(low_lanes, im_low, im_high),
                        ],
                        axis=1,
                    )
                )
            pair = steps // 2 - 1 - t if reverse else t
            both = jnp.concatenate(done[::-1] if reverse else done, axis=0)
            to = pl.ds(pl.multiple_of(m * rows + pair * 16, 16), 16)
            r.grad_drive[l, to, :] = both.astype(BF16)
            return w, bar_sum, fac_sum

        none = (zero, zero)
        _, bar_sum, fac_sum = lax.fori_loop(0, steps // 2, fill, (enter, none, none), unroll=2)
        for k, part in enumerate((*bar_sum, *fac_sum)):
            r.state_sums[l, m, k] = part

    def row_of(ref, l):
        return ref[l : l + 1, :]

    def micro_rows(m):
        return slice(m * rows, (m + 1) * rows)

    gelu_chunk = 16

    def mixer(l, m, center, inv, hook=None):
        gain, bias, skip = row_of(r.gain, l), row_of(r.bias, l), row_of(r.skip, l)

        def normalise(t, carry):
            at = pl.ds(pl.multiple_of(t * chunk, chunk), chunk)
            if l == 0:
                v = r.first_in[m, at, :].astype(F32)
            else:
                v = r.second_in[m, at, :]
            normed = (v - center) * inv
            r.normed[l, m, at, :] = normed
            to = pl.ds(pl.multiple_of(m * rows + t * chunk, chunk), chunk)
            r.scaled[l, to, :] = (normed * gain + bias).astype(BF16)
            return carry

        lax.fori_loop(0, rows // chunk, normalise, 0)
        r.drive[l, m] = matmul(r.scaled[l, micro_rows(m), :], r.b_pad[l])
        scan_states(l, m)
        r.work[...] = matmul(r.joined[l, micro_rows(m), :], r.c_pad[l])
        if hook is not None:
            hook()

        def activate(t, carry):
            at = pl.ds(pl.multiple_of(t * gelu_chunk, gelu_chunk), gelu_chunk)
            scaled = r.normed[l, m, at, :] * gain + bias
            y = (2.0 * r.work[at, :] + skip * scaled).astype(BF16).astype(F32)
            below = 0.5 + 0.5 * lax.erf(y * 0.7071067811865476)
            density = jnp.exp(-0.5 * y * y) * 0.3989422804014327
            active = y * below
            r.active[l, m, at, :] = active
            r.slope[l, m, at, :] = below + y * density
            to = pl.ds(pl.multiple_of(m * rows + t * gelu_chunk, gelu_chunk), gelu_chunk)
            r.active_low[l, to, :] = active.astype(BF16)
            return carry

        lax.fori_loop(0, rows // gelu_chunk, activate, 0)
        r.work[...] = matmul(r.active_low[l, micro_rows(m), :], r.gmat[l])

    def first_gate(m):
        gbias = row_of(r.gbias, 0)

        def gate(t, carry):
            at = pl.ds(pl.multiple_of(t * gelu_chunk, gelu_chunk), gelu_chunk)
            opened = jax.nn.sigmoid(r.work[at, :] + gbias)
            r.sig[0, m, at, :] = opened
            v = repeat_lanes(r.valid[m, at, :], width // 128)
            gated = v * r.active[0, m, at, :] * opened
            second = r.first_in[m, at, :].astype(F32) + gated.astype(BF16).astype(F32)
            r.second_in[m, at, :] = second
            kept = v * second
            return carry[0] + fold_rows(kept), carry[1] + fold_rows(kept * second)

        zero = jnp.zeros((SUB, width), F32)
        sums, squares = lax.fori_loop(0, rows // gelu_chunk, gate, (zero, zero))
        put(1 + m, 0, jnp.sum(sums, axis=0, keepdims=True))
        put(1 + m, 4, jnp.sum(squares, axis=0, keepdims=True))

    bias_sums = {}
    skip_sums = {}

    def gate_grad(l, m, grad_of):
        gbias = row_of(r.gbias, l)

        def gate(t, carry):
            at = pl.ds(pl.multiple_of(t * gelu_chunk, gelu_chunk), gelu_chunk)
            if l == 1:
                opened = jax.nn.sigmoid(r.work[at, :] + gbias)
                r.sig[1, m, at, :] = opened
            else:
                opened = r.sig[0, m, at, :]
            v = repeat_lanes(r.valid[m, at, :], width // 128)
            masked = v * grad_of(at, v)
            through = masked * opened
            r.through[at, :] = through
            grad_logits = through * r.active[l, m, at, :] * (1.0 - opened)
            to = pl.ds(pl.multiple_of(m * rows + t * gelu_chunk, gelu_chunk), gelu_chunk)
            r.grad_logits[l, to, :] = grad_logits.astype(BF16)
            return carry + fold_rows(grad_logits)

        zero = jnp.zeros((SUB, width), F32)
        bias_sums[l, m] = lax.fori_loop(0, rows // gelu_chunk, gate, zero)

    def branch_grad(l, m):
        gain, bias = row_of(r.gain, l), row_of(r.bias, l)
        r.work[...] = matmul_nt(r.grad_logits[l, micro_rows(m), :], r.gmat[l])

        def branch(t, carry):
            at = pl.ds(pl.multiple_of(t * chunk, chunk), chunk)
            grad_active = r.through[at, :] + r.work[at, :]
            g = (r.slope[l, m, at, :] * grad_active).astype(BF16)
            to = pl.ds(pl.multiple_of(m * rows + t * chunk, chunk), chunk)
            r.branch[l, to, :] = g
            scaled = r.normed[l, m, at, :] * gain + bias
            return carry + fold_rows(g.astype(F32) * scaled)

        zero = jnp.zeros((SUB, width), F32)
        skip_sums[l, m] = lax.fori_loop(0, rows // chunk, branch, zero)
        r.work[...] = matmul_nt(r.branch[l, micro_rows(m), :], r.c_pad[l])

    def mixer_grad(l, m, index):
        skip = row_of(r.skip, l)
        scan_grads(l, m)
        r.work[...] = matmul_nt(r.grad_drive[l, micro_rows(m), :], r.b_in[l])

        def scaled_grad(t, carry):
            at = pl.ds(pl.multiple_of(t * chunk, chunk), chunk)
            to = pl.ds(pl.multiple_of(m * rows + t * chunk, chunk), chunk)
            grad = r.work[at, :] + skip * r.branch[l, to, :].astype(F32)
            r.grad_scaled[l, m, at, :] = grad
            normed = r.normed[l, m, at, :]
            return carry[0] + fold_rows(grad), carry[1] + fold_rows(grad * normed)

        zero = jnp.zeros((SUB, width), F32)
        sums, products = lax.fori_loop(0, rows // chunk, scaled_grad, (zero, zero))
        put(index, 0, jnp.sum(sums, axis=0, keepdims=True))
        put(index, 4, jnp.sum(products, axis=0, keepdims=True))

    def moments(total, at, count):
        center = unfold(total, at, 4) / count
        return center, lax.rsqrt(unfold(total, at + 4, 4) / count - center * center + epsilon)

    own_columns = pl.ds(pl.multiple_of(section * 128, 128), 128)

    def gate_weights(l, ref):
        grad = matmul_tn(r.active_low[l, :, own_columns], r.grad_logits[l])
        ref[:, :, :, 0:width] = grad.astype(BF16).reshape(2, QUAD, 16, width)

    def out_weights(l, ref, at):
        grad = 2.0 * matmul_tn(r.joined[l], r.branch[l, :, own_columns])
        grad = jnp.concatenate([grad[0:half, :], grad[lanes : lanes + half, :]], axis=0)
        tall = states // (2 * QUAD)
        for k in range(tall // 16):
            for c in range(2):
                for z in range(QUAD):
                    first = (c * QUAD + z) * tall + 16 * k
                    ref[c, z, :, at + 128 * k : at + 128 * (k + 1)] = grad[
                        first : first + 16, :
                    ].astype(BF16)

    def in_weights(l, ref, at):
        grad = matmul_tn(r.scaled[l, :, own_columns], r.grad_drive[l])
        ref[:, :, :, at : at + states] = grad.astype(BF16).reshape(2, QUAD, 16, states)

    def layer_rows(l, index):
        def both(sums):
            return jnp.sum(sums[l, 0] + sums[l, 1], axis=0, keepdims=True)

        put(index, 0, both(skip_sums))
        put(index, 4, both(bias_sums))
        part = [
            jnp.sum(r.state_sums[l, 0, k] + r.state_sums[l, 1, k], axis=0, keepdims=True)
            for k in range(4)
        ]
        gb_re, gb_im = 2.0 * part[0], -2.0 * part[1]
        gf_re, gf_im = 2.0 * part[2], -2.0 * part[3]
        one = slice(l, l + 1)
        lam_re, lam_im, size = -decay[one], spin[one], step_size[one]
        b_re, b_im, f_re, f_im = bar_re[one], bar_im[one], fac_re[one], fac_im[one]
        top_re, top_im = size * b_re - f_re, size * b_im - f_im
        square = modulus[one]
        d_re = (top_re * lam_re + top_im * lam_im) / square
        d_im = (top_im * lam_re - top_re * lam_im) / square
        gl_re = size * (b_re * gb_re + b_im * gb_im) + (d_re * gf_re + d_im * gf_im)
        gl_im = size * (b_re * gb_im - b_im * gb_re) + (d_re * gf_im - d_im * gf_re)
        e_re, e_im = cmul(lam_re, lam_im, b_re, b_im)
        g_step = size * ((e_re * gb_re + e_im * gb_im) + (b_re * gf_re + b_im * gf_im))
        put(index, 8, -gl_re)
        put(index, 10, gl_im)
        put(index, 12, g_step)

    def mixed_rows(m):
        def mix(t, carry):
            at = pl.ds(pl.multiple_of(t * chunk, chunk), chunk)
            gated = (
                r.valid[m, at, :]
                * r.active[1, m, at, own_columns]
                * r.sig[1, m, at, own_columns]
            )
            stream = r.second_in[m, at, own_columns].astype(BF16).astype(F32)
            r.narrow[at, :] = (stream + gated).astype(BF16)
            return carry

        lax.fori_loop(0, rows // chunk, mix, 0)
        r.mixed[m] = matmul(r.gather[...], r.narrow[...]).astype(BF16)

    def stream_grad(l, m, total, count, inv):
        gain = row_of(r.gain, l)
        first = gain * unfold(total, 0, 4) / count
        second = gain * unfold(total, 4, 4) / count
        return gain, first, second, inv

    total0 = first_sum.total()
    counts = [repeat_lanes(total0[16 + m : 17 + m, :], width // 128) for m in range(2)]
    norm0 = [moments(total0, 8 * m, counts[m]) for m in range(2)]

    mixer(0, 0, *norm0[0])
    first_gate(0)
    mid_sum[0].start()
    mixer(0, 1, *norm0[1], hook=mid_sum[0].turn)
    first_gate(1)
    mid_sum[1].start()

    norm1 = [None, None]
    for m in range(2):
        norm1[m] = moments(mid_sum[m].total(), 0, counts[m])
        hook = mid_sum[1].turn if m == 0 else upper_sum[0].turn
        mixer(1, m, *norm1[m], hook=hook)
        gate_grad(1, m, lambda at, v, m=m: r.out_grads[m, at, :].astype(F32))
        branch_grad(1, m)
        mixer_grad(1, m, 3 + m)
        upper_sum[m].start()

    gate_weights(1, r.mine_0)
    out_weights(1, r.mine_0, width)
    in_weights(1, r.mine_0, width + states)
    upper_sum[1].turn()
    upper_batch.to_core()
    layer_rows(1, 7)
    layer_sum[1].start()

    upper_total = [None, None]
    for m in range(2):
        upper_total[m] = upper_sum[m].total()
        gain, first, second, inv = stream_grad(1, m, upper_total[m], counts[m], norm1[m][1])

        def second_grad(at, v, m=m, gain=gain, first=first, second=second, inv=inv):
            grad_normed = r.grad_scaled[1, m, at, :] * gain
            normed = r.normed[1, m, at, :]
            grad_stream = inv * (grad_normed - v * (first + normed * second))
            out_grad = r.out_grads[m, at, :].astype(F32)
            grad = (out_grad + grad_stream.astype(BF16).astype(F32)).astype(BF16)
            r.grad_second[m, at, :] = grad
            return grad.astype(F32)

        gate_grad(0, m, second_grad)
        if m == 0:
            upper_batch.to_quad()
            layer_sum[1].turn()
        else:
            lower_sum[0].turn()
            upper_batch.to_groups()
        branch_grad(0, m)
        if m == 1:
            gate_weights(0, r.mine_1)
            out_weights(0, r.mine_1, width)
            gate_batch.to_core()
        mixer_grad(0, m, 5 + m)
        lower_sum[m].start()

    in_weights(0, r.mine_2, 0)
    in_batch.to_core()
    layer_rows(0, 8)
    layer_sum[0].start()
    gate_batch.to_quad()
    lower_sum[1].turn()
    in_batch.to_quad()
    layer_sum[0].turn()
    upper_batch.to_sections()
    mixed_rows(0)
    gate_batch.to_groups()
    mixed_rows(1)
    in_batch.to_groups()
    upper_batch.to_sibling()

    lower_total = [None, None]
    for m in range(2):
        lower_total[m] = lower_sum[m].total()
        gain, first, second, inv = stream_grad(0, m, lower_total[m], counts[m], norm0[m][1])
        for k, row in enumerate((gain, first, second, inv)):
            r.rows[k : k + 1, :] = row
        gain, first, second, inv = [r.rows[k : k + 1, own_columns] for k in range(4)]

        def token_grad(t, carry, m=m, gain=gain, first=first, second=second, inv=inv):
            at = pl.ds(pl.multiple_of(t * chunk, chunk), chunk)
            grad_normed = r.grad_scaled[0, m, at, own_columns] * gain
            normed = r.normed[0, m, at, own_columns]
            grad_stream = inv * (grad_normed - r.valid[m, at, :] * (first + normed * second))
            grad = r.grad_second[m, at, own_columns].astype(F32) + grad_stream
            high = grad.astype(BF16)
            r.narrow[at, :] = high
            r.narrow_rest[at, :] = (grad - high.astype(F32)).astype(BF16)
            return carry

        lax.fori_loop(0, rows // chunk, token_grad, 0)
        r.token_grad[m] = matmul(r.gather[...], r.narrow[...]) + matmul(
            r.gather[...], r.narrow_rest[...]
        )
        if m == 0:
            gate_batch.to_sections()
            upper_batch.to_result(r.result_0, r.result_sem.at[0])

    in_batch.to_sections()
    gate_batch.to_sibling()
    for l, sums in ((0, lower_total), (1, upper_total)):
        r.small[l, 0:8, :] = (sums[0] + sums[1])[0:8, :]
        r.small[l, 8:24, :] = layer_sum[l].total()[0:16, :]
    gate_batch.to_result(r.result_1, r.result_sem.at[1])
    in_batch.to_sibling()
    in_batch.to_result(r.result_2, r.result_sem.at[2])
    for batch in batches:
        batch.end()


def lay_out_kernel(cfg, *refs):
    upper, gate_out, into, small, mixed, token_grad = refs[:6]
    (
        mixed_out,
        token_grad_out,
        gain_out,
        bias_out,
        decay_out,
        freq_out,
        step_out,
        in_out,
        out_out,
        skip_out,
        gate_out_out,
        gbias_out,
    ) = refs[6:]
    width, states, half = cfg.width, cfg.states, cfg.half
    mixed_out[...] = mixed[...]
    token_grad_out[...] = token_grad[...]
    for l in range(2):
        for out, first, count in (
            (bias_out, 0, 4),
            (gain_out, 4, 4),
            (skip_out, 8, 4),
            (gbias_out, 12, 4),
        ):
            out[l : l + 1, :] = unfold(small[l], first, count)
        for out, first in ((decay_out, 16), (freq_out, 18), (step_out, 20)):
            out[l : l + 1, :] = unfold(small[l], first, 2)[:, 0:half]
    tall = states // (2 * QUAD)
    for l in range(2):
        for s in range(cfg.sections):
            for c in range(2):
                for z in range(QUAD):
                    at = s * 128 + (c * QUAD + z) * 16
                    if l == 1:
                        piece = upper[c, s, z]
                        gate_part = piece[:, 0:width]
                        out_part = piece[:, width : width + states]
                        in_part = piece[:, width + states :]
                    else:
                        gate_part = gate_out[c, s, z, :, 0:width]
                        out_part = gate_out[c, s, z, :, width:]
                        in_part = into[c, s, z]
                    gate_out_out[l, at : at + 16, :] = gate_part.astype(F32)
                    in_out[l, at : at + 16, :] = in_part.astype(F32)
                    for k in range(tall // 16):
                        first = (c * QUAD + z) * tall + 16 * k
                        out_out[l, first : first + 16, s * 128 : (s + 1) * 128] = out_part[
                            :, k * 128 : (k + 1) * 128
                        ].astype(F32)


INPUTS = tuple(
    dict(tokens=0, lengths=0, out_grad=0, gain=0, bias=0, decay=0, freq=0, lstep=0, b_in=0, c_out=0, skip=0, gmat=0, gbias=0)
)


def per_device(cfg, *args):
    rows, width, states, lanes = cfg.rows, cfg.width, cfg.states, cfg.lanes
    sections, chips = cfg.sections, cfg.dp // 2
    groups = chips // QUAD
    steps = rows // SUB
    vmem, dma = pltpu.VMEM, pltpu.SemaphoreType.DMA
    widths = (width + 2 * states, width + states, states)
    outs = {f"result_{k}": ((2, sections, QUAD, 16, w), BF16) for k, w in enumerate(widths)}
    outs.update(
        small=((2, 24, 128), F32), mixed=((2, rows, 128), BF16), token_grad=((2, rows, 128), F32)
    )
    scratch = dict(
        sum_own=vmem((REDUCES, 24, 128), F32),
        sum_sibling=vmem((REDUCES, 24, 128), F32),
        sum_slots=vmem((REDUCES, chips, 24, 128), F32),
        sum_send=dma((REDUCES, chips)),
        sum_recv=dma((REDUCES, chips)),
        grad_send=dma((3, 2 * QUAD + sections + groups)),
        grad_recv=dma((3, 2 * QUAD + sections + groups)),
        result_sem=dma((3,)),
        spread=vmem((rows, rows), BF16),
        gather=vmem((rows, rows), BF16),
        first_in=vmem((2, rows, width), BF16),
        out_grads=vmem((2, rows, width), BF16),
        second_in=vmem((2, rows, width), F32),
        grad_second=vmem((2, rows, width), BF16),
        valid=vmem((2, rows, 128), F32),
        keep_start=vmem((2, rows, 128), F32),
        keep_end=vmem((2, rows, 128), F32),
        par=vmem((SUB, lanes), F32),
        b_pad=vmem((2, width, 2 * lanes), BF16),
        c_pad=vmem((2, 2 * lanes, width), BF16),
        normed=vmem((2, 2, rows, width), F32),
        scaled=vmem((2, 2 * rows, width), BF16),
        drive=vmem((2, 2, rows, 2 * lanes), F32),
        state=vmem((2, 2, (steps + 1) * SUB, 2 * lanes), F32),
        joined=vmem((2, 2 * rows, 2 * lanes), BF16),
        work=vmem((rows, width), F32),
        active=vmem((2, 2, rows, width), F32),
        active_low=vmem((2, 2 * rows, width), BF16),
        slope=vmem((2, 2, rows, width), F32),
        sig=vmem((2, 2, rows, width), F32),
        through=vmem((rows, width), F32),
        grad_logits=vmem((2, 2 * rows, width), BF16),
        branch=vmem((2, 2 * rows, width), BF16),
        grad_drive=vmem((2, 2 * rows, states), BF16),
        grad_scaled=vmem((2, 2, rows, width), F32),
        state_sums=vmem((2, 2, 4, SUB, lanes), F32),
        narrow=vmem((rows, 128), BF16),
        narrow_rest=vmem((rows, 128), BF16),
        rows=vmem((SUB, width), F32),
    )
    for k, w in enumerate(widths):
        blocks = (2, QUAD), (QUAD,), (QUAD,), (QUAD,), (groups,), (2, sections, QUAD)
        for part, block in zip(STAGES, blocks):
            scratch[f"{part}_{k}"] = vmem((*block, 16, w), BF16)
    in_vmem = pl.BlockSpec(memory_space=pltpu.VMEM)
    in_smem = pl.BlockSpec(memory_space=pltpu.SMEM)
    anywhere = pl.BlockSpec(memory_space=pl.ANY)
    names = INPUTS + tuple(outs) + tuple(scratch)
    made = pl.pallas_call(
        partial(main_kernel, cfg, names),
        name="layers",
        out_shape=[jax.ShapeDtypeStruct(*spec) for spec in outs.values()],
        in_specs=[in_smem if name == "lengths" else in_vmem for name in INPUTS],
        out_specs=[anywhere if name.startswith("result") else in_vmem for name in outs],
        scratch_shapes=list(scratch.values()),
        compiler_params=pltpu.CompilerParams(
            collective_id=0, has_side_effects=True, vmem_limit_bytes=56 * 2**20
        ),
    )(*args)
    shapes = [
        ((2, rows, 128), BF16),
        ((2, rows, 128), F32),
        ((2, width), F32),
        ((2, width), F32),
        ((2, states // 2), F32),
        ((2, states // 2), F32),
        ((2, states // 2), F32),
        ((2, width, states), F32),
        ((2, states, width), F32),
        ((2, width), F32),
        ((2, width, width), F32),
        ((2, width), F32),
    ]
    return pl.pallas_call(
        partial(lay_out_kernel, cfg),
        name="lay_out",
        out_shape=[jax.ShapeDtypeStruct(*spec) for spec in shapes],
        in_specs=[in_vmem] * 6,
        out_specs=[in_vmem] * 12,
        compiler_params=pltpu.CompilerParams(vmem_limit_bytes=40 * 2**20),
    )(*made)


def solution(mesh):
    sections, dp = mesh.shape["section"], mesh.shape["dp"]

    def run(*args):
        _, rows, width = args[0].shape
        states = args[8].shape[2]
        cfg = SimpleNamespace(
            rows=rows // dp,
            width=width,
            states=states,
            half=states // 2,
            lanes=-(-states // 256) * 128,
            sections=sections,
            dp=dp,
        )
        split = P(None, "dp", None)
        shared = P()
        placed = P(None, "dp", "section")
        return jax.shard_map(
            partial(per_device, cfg),
            mesh=mesh,
            in_specs=(split, P(None, "dp"), split) + (shared,) * 10,
            out_specs=(placed, placed) + (shared,) * 10,
            check_vma=False,
        )(*args)

    return run
```

```python
from functools import partial
from types import SimpleNamespace

import jax
import jax.numpy as jnp
from jax import lax
from jax.experimental import pallas as pl
from jax.experimental.pallas import tpu as pltpu
from jax.sharding import PartitionSpec as P

epsilon = 1e-05
MESH = pl.DeviceIdType.MESH
F32 = jnp.float32
BF16 = jnp.bfloat16
SUB = 8
QUAD = 4
REDUCES = 9


STAGES = tuple(dict(mine=0, theirs=0, chip=0, quad=0, group=0, full=0))


def matmul(left, right):
    return jnp.dot(left, right, preferred_element_type=F32)


def matmul_nt(left, right):
    return lax.dot_general(left, right, (((1,), (1,)), ((), ())), preferred_element_type=F32)


def matmul_tn(left, right):
    return lax.dot_general(left, right, (((0,), (0,)), ((), ())), preferred_element_type=F32)


def cmul(ar, ai, br, bi):
    return ar * br - ai * bi, ar * bi + ai * br


def repeat_lanes(x, times):
    return jnp.concatenate([x] * times, axis=1)


def fold_rows(x):
    return jnp.sum(x.reshape(x.shape[0] // SUB, SUB, x.shape[1]), axis=0)


def unfold(total, first, count):
    return jnp.concatenate([total[first + k : first + k + 1, :] for k in range(count)], axis=1)


class SmallSum:
    def __init__(self, place, own, sibling, slots, send_sems, recv_sems, index):
        self.place, self.own, self.sibling, self.slots = place, own, sibling, slots
        self.send_sems, self.recv_sems, self.index = send_sems, recv_sems, index

    def start(self):
        at = self.place
        self.copy = pltpu.make_async_remote_copy(
            src_ref=self.own,
            dst_ref=self.sibling,
            send_sem=self.send_sems.at[self.index, 0],
            recv_sem=self.recv_sems.at[self.index, 0],
            device_id=(at.section, at.sibling),
            device_id_type=MESH,
        )
        self.copy.start()

    def turn(self):
        at = self.place
        self.copy.wait()
        chip = at.chip
        self.slots[chip] = self.own[...] + self.sibling[...]
        self.copies = []
        for step in range(1, at.chips):
            copy = pltpu.make_async_remote_copy(
                src_ref=self.slots.at[chip],
                dst_ref=self.slots.at[chip],
                send_sem=self.send_sems.at[self.index, step],
                recv_sem=self.recv_sems.at[self.index, step],
                device_id=(at.section, at.chip_peer(step)),
                device_id_type=MESH,
            )
            copy.start()
            self.copies.append(copy)

    def total(self):
        for copy in self.copies:
            copy.wait()
        result = self.slots[0]
        for chip in range(1, self.place.chips):
            result = result + self.slots[chip]
        return result


class GradSum:
    def __init__(self, place, refs, send_sems, recv_sems, index):
        self.place = place
        self.mine, self.theirs, self.chip_part, self.quad_in, self.group_in, self.full = refs
        self.send_sems, self.recv_sems, self.index = send_sems, recv_sems, index
        self.sem = 0

    def remote(self, src, dst, device):
        copy = pltpu.make_async_remote_copy(
            src_ref=src,
            dst_ref=dst,
            send_sem=self.send_sems.at[self.index, self.sem],
            recv_sem=self.recv_sems.at[self.index, self.sem],
            device_id=device,
            device_id_type=MESH,
        )
        self.sem += 1
        copy.start()
        return copy

    def to_core(self):
        at = self.place
        self.copy = self.remote(
            self.mine.at[1 - at.core], self.theirs, (at.section, at.sibling)
        )

    def to_quad(self):
        at = self.place
        self.copy.wait()
        for part in range(QUAD):
            both = self.mine[at.core, part].astype(F32) + self.theirs[part].astype(F32)
            self.chip_part[part] = both.astype(BF16)
        self.copies = []
        for step in range(1, QUAD):
            other = lax.rem(at.quad + step, QUAD)
            self.copies.append(
                self.remote(
                    self.chip_part.at[other],
                    self.quad_in.at[at.quad],
                    (at.section, at.quad_peer(step)),
                )
            )
        self.quad_in[at.quad] = self.chip_part[at.quad]

    def to_groups(self):
        at = self.place
        for copy in self.copies:
            copy.wait()
        total = self.quad_in[0].astype(F32)
        for part in range(1, QUAD):
            total = total + self.quad_in[part].astype(F32)
        if at.groups > 1:
            group = at.group
            self.group_in[group] = total.astype(BF16)
            copies = []
            for step in range(1, at.groups):
                copies.append(
                    self.remote(
                        self.group_in.at[group],
                        self.group_in.at[group],
                        (at.section, at.chip_peer(step * QUAD)),
                    )
                )
            for copy in copies:
                copy.wait()
            total = self.group_in[0].astype(F32)
            for other in range(1, at.groups):
                total = total + self.group_in[other].astype(F32)
        piece = self.full.at[at.core, at.section, at.quad]
        piece[...] = total.astype(BF16)
        self.copies = [
            self.remote(piece, piece, (at.section, at.quad_peer(step))) for step in range(1, QUAD)
        ]
        self.spread = [self.over_sections(at.quad)]

    def over_sections(self, quad):
        at = self.place
        piece = self.full.at[at.core, at.section, quad]
        return [
            self.remote(piece, piece, (lax.rem(at.section + step, at.sections), at.dp))
            for step in range(1, at.sections)
        ]

    def to_sections(self):
        at = self.place
        for step in range(1, QUAD):
            self.copies[step - 1].wait()
            self.spread.append(self.over_sections(lax.rem(at.quad + QUAD - step, QUAD)))
        piece = self.full.at[at.core, at.section]
        self.last = [self.remote(piece, piece, (at.section, at.sibling))]

    def to_sibling(self):
        at = self.place
        for step in range(1, at.sections):
            for copies in self.spread:
                copies[step - 1].wait()
            other = lax.rem(at.section + at.sections - step, at.sections)
            piece = self.full.at[at.core, other]
            self.last.append(self.remote(piece, piece, (at.section, at.sibling)))

    def end(self):
        for copy in self.last:
            copy.wait()


def main_kernel(cfg, names, *refs):
    r = SimpleNamespace(**dict(zip(names, refs)))
    rows, width, states, half, lanes = (
        cfg.rows,
        cfg.width,
        cfg.states,
        cfg.half,
        cfg.lanes,
    )
    steps = rows // SUB
    section = lax.axis_index("section")
    dp = lax.axis_index("dp")
    chips = cfg.dp // 2
    core, chip = lax.rem(dp, 2), lax.div(dp, 2)
    quad, group = lax.rem(chip, QUAD), lax.div(chip, QUAD)
    place = SimpleNamespace(
        section=section,
        sections=cfg.sections,
        dp=dp,
        core=core,
        chip=chip,
        chips=chips,
        quad=quad,
        group=group,
        groups=chips // QUAD,
        sibling=dp + 1 - 2 * core,
        chip_peer=lambda step: lax.rem(chip + step, chips) * 2 + core,
        quad_peer=lambda step: (group * QUAD + lax.rem(quad + step, QUAD)) * 2 + core,
    )

    peers = [(section, place.sibling)]
    peers += [(section, place.chip_peer(step)) for step in range(1, chips)]
    peers += [(lax.rem(section + step, cfg.sections), dp) for step in range(1, cfg.sections)]
    barrier = pltpu.get_barrier_semaphore()
    for peer in peers:
        pl.semaphore_signal(barrier, inc=1, device_id=peer, device_id_type=MESH)

    small = [
        SmallSum(
            place,
            r.sum_own.at[k],
            r.sum_sibling.at[k],
            r.sum_slots.at[k],
            r.sum_send,
            r.sum_recv,
            k,
        )
        for k in range(REDUCES)
    ]
    first_sum = small[0]
    mid_sum = [small[1], small[2]]
    upper_sum = [small[3], small[4]]
    lower_sum = [small[5], small[6]]
    layer_sum = [small[8], small[7]]
    batches = [
        GradSum(
            place,
            [getattr(r, f"{part}_{k}") for part in STAGES],
            r.grad_send,
            r.grad_recv,
            k,
        )
        for k in range(4)
    ]
    upper_gate, upper_in, lower_gate, lower_in = batches

    fetched = []
    for k, (held, given) in enumerate(
        (
            (r.b_in, r.b_in_far),
            (r.out_grad, r.out_grad_far),
            (r.c_out, r.c_out_far),
            (r.gmat, r.gmat_far),
        )
    ):
        fetched.append(pltpu.make_async_copy(given, held, r.fetch_sem.at[k]))
        fetched[k].start()

    first_len = [r.lengths[m, 0] for m in range(2)]
    total_len = [r.lengths[m, 0] + r.lengths[m, 1] for m in range(2)]

    def put(index, at, row):
        for k in range(row.shape[1] // 128):
            r.sum_own[index, at + k : at + k + 1, :] = row[:, k * 128 : (k + 1) * 128]

    chunk = 32
    for m in range(2):

        def token_sums(t, carry, m=m):
            at = pl.ds(pl.multiple_of(t * chunk, chunk), chunk)
            v = r.tokens[m, at, :].astype(F32)
            place_row = t * chunk + lax.broadcasted_iota(jnp.int32, (chunk, width), 0)
            kept = jnp.where(place_row < total_len[m], v, 0.0)
            return carry[0] + fold_rows(kept), carry[1] + fold_rows(kept * v)

        zero = jnp.zeros((SUB, width), F32)
        sums, squares = lax.fori_loop(0, rows // chunk, token_sums, (zero, zero))
        put(0, 8 * m, jnp.sum(sums, axis=0, keepdims=True))
        put(0, 8 * m + 4, jnp.sum(squares, axis=0, keepdims=True))
        count = jnp.minimum(total_len[m], rows).astype(F32)
        r.sum_own[0, 16 + m : 17 + m, :] = jnp.full((1, 128), count, F32)

    pl.semaphore_wait(barrier, len(peers))
    first_sum.start()

    at_i = lax.broadcasted_iota(jnp.int32, (rows, rows), 0)
    at_r = lax.broadcasted_iota(jnp.int32, (rows, rows), 1)
    r.spread[...] = jnp.where(
        at_r == (at_i % SUB) * steps + at_i // SUB, 1.0, 0.0
    ).astype(BF16)
    r.gather[...] = jnp.where(
        at_i == (at_r % SUB) * steps + at_r // SUB, 1.0, 0.0
    ).astype(BF16)
    for m in range(2):
        r.first_in[m] = matmul(r.spread[...], r.tokens[m]).astype(BF16)
    first_sum.turn()
    fetched[1].wait()
    for m in range(2):
        r.out_grads[m] = matmul(r.spread[...], r.out_grad[m]).astype(BF16)
    held = lax.broadcasted_iota(jnp.int32, (rows, 128), 0)
    held = (held % SUB) * steps + held // SUB
    all_start, all_end = [], []
    for m in range(2):
        one, zero = jnp.float32(1.0), jnp.float32(0.0)
        past = held >= total_len[m]
        starts = (held == 0) | (held == first_len[m]) | past
        ends = (held == first_len[m] - 1) | (held == total_len[m] - 1) | past | (held == rows - 1)
        r.valid[m] = jnp.where(past, zero, one)
        r.keep_start[m] = jnp.where(starts, zero, one)
        r.keep_end[m] = jnp.where(ends, zero, one)
        for kept, mask in ((all_start, r.keep_start), (all_end, r.keep_end)):
            kept.append(jnp.min(mask[m].reshape(steps, SUB, 128), axis=0))

    r.par[...] = jnp.zeros((SUB, lanes), F32)
    r.par[0:2, :] = jnp.ones((2, lanes), F32)
    r.par[0:2, 0:half] = r.decay[...]
    r.par[2:4, 0:half] = r.freq[...]
    r.par[4:6, 0:half] = r.lstep[...]
    decay, spin = r.par[0:2, :], r.par[2:4, :]
    step_size = jnp.exp(r.par[4:6, :])
    damping = jnp.exp(-decay * step_size)
    bar_re = damping * jnp.cos(spin * step_size)
    bar_im = damping * jnp.sin(spin * step_size)
    modulus = decay * decay + spin * spin
    fac_re = ((bar_re - 1.0) * -decay + bar_im * spin) / modulus
    fac_im = (bar_im * -decay - (bar_re - 1.0) * spin) / modulus
    pow_re, pow_im = bar_re, bar_im
    power = 1
    while power < steps:
        pow_re, pow_im = cmul(pow_re, pow_im, pow_re, pow_im)
        power *= 2

    lane = lax.broadcasted_iota(jnp.int32, (1, 128), 1)
    low_lanes = lane < half - 128
    turn_by = half - 128

    from_column = lax.broadcasted_iota(jnp.int32, (states, 2 * lanes), 0)
    to_column = lax.broadcasted_iota(jnp.int32, (states, 2 * lanes), 1)
    moved_to = jnp.where(from_column < half, from_column, from_column + (lanes - half))
    r.widen[...] = jnp.where(to_column == moved_to, 1.0, 0.0).astype(BF16)
    for k in (0, 2, 3):
        fetched[k].wait()
    for l in range(2):
        r.b_pad[l] = matmul(r.b_in[l], r.widen[...]).astype(BF16)
        blank = jnp.zeros((lanes - half, width), BF16)
        r.c_pad[l, 0:half, :] = r.c_out[l, 0:half, :]
        r.c_pad[l, half:lanes, :] = blank
        r.c_pad[l, lanes : lanes + half, :] = r.c_out[l, half:states, :]
        r.c_pad[l, lanes + half : 2 * lanes, :] = blank

    def across(end, coef, reverse):
        end_re, end_im = end
        coef_re, coef_im = coef
        sub = lax.broadcasted_iota(jnp.int32, (SUB, lanes), 0)
        for by in (1, 2, 4):
            turn = SUB - by if reverse else by
            live = sub < SUB - by if reverse else sub >= by

            def moved(x):
                return jnp.where(live, pltpu.roll(x, turn, 0), 0.0)

            add_re, add_im = cmul(coef_re, coef_im, moved(end_re), moved(end_im))
            coef_re, coef_im = cmul(coef_re, coef_im, moved(coef_re), moved(coef_im))
            end_re, end_im = end_re + add_re, end_im + add_im
        turn = SUB - 1 if reverse else 1
        live = sub < SUB - 1 if reverse else sub >= 1
        return tuple(jnp.where(live, pltpu.roll(x, turn, 0), 0.0) for x in (end_re, end_im))

    def wide8(x, l):
        return jnp.broadcast_to(x[l : l + 1, :], (SUB, x.shape[1]))

    def group_rows(p):
        return pl.ds(pl.multiple_of(p * SUB, SUB), SUB)

    def scan_coefs(l, m, reverse):
        keep = r.keep_end if reverse else r.keep_start
        all_kept = repeat_lanes((all_end if reverse else all_start)[m], lanes // 128)
        product = (all_kept * wide8(pow_re, l), all_kept * wide8(pow_im, l))
        return keep, wide8(bar_re, l), wide8(bar_im, l), product

    def advance(keep, m, at, br, bi, re, im, src_re, src_im):
        k = repeat_lanes(keep[m, at, :], lanes // 128)
        kr, ki = k * br, k * bi
        return kr * re - ki * im + src_re, kr * im + ki * re + src_im

    def scan_states(l, m):
        reverse = l == 1
        lead = 0 if reverse else 1
        keep, br, bi, product = scan_coefs(l, m, reverse)
        fr, fi = wide8(fac_re, l), wide8(fac_im, l)
        zero = jnp.zeros((SUB, lanes), F32)

        def ends(t, carry):
            p = steps - 1 - t if reverse else t
            at = group_rows(p)
            v = repeat_lanes(r.valid[m, at, :], lanes // 128)
            drive_re = r.drive[l, m, at, 0:lanes]
            drive_im = r.drive[l, m, at, lanes : 2 * lanes]
            src_re, src_im = cmul(fr, fi, v * drive_re, v * drive_im)
            r.state[l, m, group_rows(p + lead), 0:lanes] = src_re
            r.state[l, m, group_rows(p + lead), lanes : 2 * lanes] = src_im
            return advance(keep, m, at, br, bi, *carry, src_re, src_im)

        end = lax.fori_loop(0, steps, ends, (zero, zero), unroll=4)
        enter = across(end, product, reverse)
        first = steps if reverse else 0
        r.state[l, m, first * SUB : (first + 1) * SUB, 0:lanes] = enter[0]
        r.state[l, m, first * SUB : (first + 1) * SUB, lanes : 2 * lanes] = enter[1]

        def fill(t, carry):
            done = []
            for k in range(2):
                p = steps - 1 - (2 * t + k) if reverse else 2 * t + k
                at, to = group_rows(p), group_rows(p + lead)
                src_re = r.state[l, m, to, 0:lanes]
                src_im = r.state[l, m, to, lanes : 2 * lanes]
                carry = advance(keep, m, at, br, bi, *carry, src_re, src_im)
                r.state[l, m, to, 0:lanes] = carry[0]
                r.state[l, m, to, lanes : 2 * lanes] = carry[1]
                done.append(jnp.concatenate([carry[0], -carry[1]], axis=1))
            pair = steps // 2 - 1 - t if reverse else t
            both = jnp.concatenate(done[::-1] if reverse else done, axis=0)
            to = pl.ds(pl.multiple_of(m * rows + pair * 16, 16), 16)
            r.joined[l, to, :] = both.astype(BF16)
            return carry

        lax.fori_loop(0, steps // 2, fill, enter, unroll=2)

    def scan_grads(l, m):
        reverse = l == 0
        back = 1 if l == 1 else 0
        keep, br, bi, product = scan_coefs(l, m, reverse)
        keep_state = r.keep_start if l == 0 else r.keep_end
        fr, fi = 2.0 * wide8(fac_re, l), 2.0 * wide8(fac_im, l)
        zero = jnp.zeros((SUB, lanes), F32)

        def ends(t, carry):
            p = steps - 1 - t if reverse else t
            at = group_rows(p)
            q_re = r.q[m, at, 0:lanes]
            q_im = r.q[m, at, lanes : 2 * lanes]
            return advance(keep, m, at, br, bi, *carry, q_re, q_im)

        end = lax.fori_loop(0, steps, ends, (zero, zero), unroll=4)
        enter = across(end, product, reverse)

        def fill(t, carry):
            w, bar_sum, fac_sum = carry
            done = []
            for k in range(2):
                p = steps - 1 - (2 * t + k) if reverse else 2 * t + k
                at, near = group_rows(p), group_rows(p + back)
                q_re = r.q[m, at, 0:lanes]
                q_im = r.q[m, at, lanes : 2 * lanes]
                w = advance(keep, m, at, br, bi, *w, q_re, q_im)
                kept = repeat_lanes(keep_state[m, at, :], lanes // 128)
                near_re = kept * r.state[l, m, near, 0:lanes]
                near_im = kept * r.state[l, m, near, lanes : 2 * lanes]
                term = cmul(*w, near_re, near_im)
                bar_sum = (bar_sum[0] + term[0], bar_sum[1] + term[1])
                v = repeat_lanes(r.valid[m, at, :], lanes // 128)
                vw = (v * w[0], v * w[1])
                drive_re = r.drive[l, m, at, 0:lanes]
                drive_im = r.drive[l, m, at, lanes : 2 * lanes]
                term = cmul(*vw, drive_re, drive_im)
                fac_sum = (fac_sum[0] + term[0], fac_sum[1] + term[1])
                gd_re, gd_im = cmul(fr, fi, *vw)
                im_low = pltpu.roll(-gd_im[:, 0:128], 64, 1)
                im_high = pltpu.roll(-gd_im[:, 128:256], 64, 1)
                done.append(
                    jnp.concatenate(
                        [
                            gd_re[:, 0:128],
                            jnp.where(low_lanes, gd_re[:, 128:256], im_low),
                            jnp.where(low_lanes, im_low, im_high),
                        ],
                        axis=1,
                    )
                )
            pair = steps // 2 - 1 - t if reverse else t
            both = jnp.concatenate(done[::-1] if reverse else done, axis=0)
            to = pl.ds(pl.multiple_of(m * rows + pair * 16, 16), 16)
            r.grad_drive[l, to, :] = both.astype(BF16)
            return w, bar_sum, fac_sum

        none = (zero, zero)
        _, bar_sum, fac_sum = lax.fori_loop(0, steps // 2, fill, (enter, none, none), unroll=2)
        for k, part in enumerate((*bar_sum, *fac_sum)):
            r.state_sums[l, m, k] = part

    def row_of(ref, l):
        return ref[l : l + 1, :]

    def micro_rows(m):
        return slice(m * rows, (m + 1) * rows)

    gelu_chunk = 16

    def mixer(l, m, center, inv, hook=None):
        gain, bias, skip = row_of(r.gain, l), row_of(r.bias, l), row_of(r.skip, l)

        def normalise(t, carry):
            at = pl.ds(pl.multiple_of(t * chunk, chunk), chunk)
            if l == 0:
                v = r.first_in[m, at, :].astype(F32)
            else:
                v = r.second_in[m, at, :]
            normed = (v - center) * inv
            r.normed[l, m, at, :] = normed
            to = pl.ds(pl.multiple_of(m * rows + t * chunk, chunk), chunk)
            r.scaled[l, to, :] = (normed * gain + bias).astype(BF16)
            return carry

        lax.fori_loop(0, rows // chunk, normalise, 0)
        r.drive[l, m] = matmul(r.scaled[l, micro_rows(m), :], r.b_pad[l])
        scan_states(l, m)
        if hook is not None:
            hook()
        r.work[...] = matmul(r.joined[l, micro_rows(m), :], r.c_pad[l])

        def activate(t, carry):
            at = pl.ds(pl.multiple_of(t * gelu_chunk, gelu_chunk), gelu_chunk)
            scaled = r.normed[l, m, at, :] * gain + bias
            y = (2.0 * r.work[at, :] + skip * scaled).astype(BF16).astype(F32)
            below = 0.5 + 0.5 * lax.erf(y * 0.7071067811865476)
            density = jnp.exp(-0.5 * y * y) * 0.3989422804014327
            active = y * below
            r.active[l, m, at, :] = active
            r.slope[l, m, at, :] = below + y * density
            to = pl.ds(pl.multiple_of(m * rows + t * gelu_chunk, gelu_chunk), gelu_chunk)
            r.active_low[l, to, :] = active.astype(BF16)
            return carry

        lax.fori_loop(0, rows // gelu_chunk, activate, 0)
        r.work[...] = matmul(r.active_low[l, micro_rows(m), :], r.gmat[l])

    def first_gate(m):
        gbias = row_of(r.gbias, 0)

        def gate(t, carry):
            at = pl.ds(pl.multiple_of(t * gelu_chunk, gelu_chunk), gelu_chunk)
            opened = jax.nn.sigmoid(r.work[at, :] + gbias)
            r.sig[0, m, at, :] = opened
            v = repeat_lanes(r.valid[m, at, :], width // 128)
            gated = v * r.active[0, m, at, :] * opened
            second = r.first_in[m, at, :].astype(F32) + gated.astype(BF16).astype(F32)
            r.second_in[m, at, :] = second
            kept = v * second
            return carry[0] + fold_rows(kept), carry[1] + fold_rows(kept * second)

        zero = jnp.zeros((SUB, width), F32)
        sums, squares = lax.fori_loop(0, rows // gelu_chunk, gate, (zero, zero))
        put(1 + m, 0, jnp.sum(sums, axis=0, keepdims=True))
        put(1 + m, 4, jnp.sum(squares, axis=0, keepdims=True))

    bias_sums = {}
    skip_sums = {}

    def gate_grad(l, m, grad_of):
        gbias = row_of(r.gbias, l)

        def gate(t, carry):
            at = pl.ds(pl.multiple_of(t * gelu_chunk, gelu_chunk), gelu_chunk)
            if l == 1:
                opened = jax.nn.sigmoid(r.work[at, :] + gbias)
                r.sig[1, m, at, :] = opened
            else:
                opened = r.sig[0, m, at, :]
            v = repeat_lanes(r.valid[m, at, :], width // 128)
            masked = v * grad_of(at, v)
            through = masked * opened
            r.through[at, :] = through
            grad_logits = through * r.active[l, m, at, :] * (1.0 - opened)
            to = pl.ds(pl.multiple_of(m * rows + t * gelu_chunk, gelu_chunk), gelu_chunk)
            r.grad_logits[l, to, :] = grad_logits.astype(BF16)
            return carry + fold_rows(grad_logits)

        zero = jnp.zeros((SUB, width), F32)
        bias_sums[l, m] = lax.fori_loop(0, rows // gelu_chunk, gate, zero)

    def branch_grad(l, m):
        gain, bias = row_of(r.gain, l), row_of(r.bias, l)
        r.work[...] = matmul_nt(r.grad_logits[l, micro_rows(m), :], r.gmat[l])

        def branch(t, carry):
            at = pl.ds(pl.multiple_of(t * chunk, chunk), chunk)
            grad_active = r.through[at, :] + r.work[at, :]
            g = (r.slope[l, m, at, :] * grad_active).astype(BF16)
            to = pl.ds(pl.multiple_of(m * rows + t * chunk, chunk), chunk)
            r.branch[l, to, :] = g
            scaled = r.normed[l, m, at, :] * gain + bias
            return carry + fold_rows(g.astype(F32) * scaled)

        zero = jnp.zeros((SUB, width), F32)
        skip_sums[l, m] = lax.fori_loop(0, rows // chunk, branch, zero)
        r.q[m] = matmul_nt(r.branch[l, micro_rows(m), :], r.c_pad[l])

    def mixer_grad(l, m, index, hook=None):
        skip = row_of(r.skip, l)
        scan_grads(l, m)
        if hook is not None:
            hook()
        r.work[...] = matmul_nt(r.grad_drive[l, micro_rows(m), :], r.b_in[l])

        def scaled_grad(t, carry):
            at = pl.ds(pl.multiple_of(t * chunk, chunk), chunk)
            to = pl.ds(pl.multiple_of(m * rows + t * chunk, chunk), chunk)
            grad = r.work[at, :] + skip * r.branch[l, to, :].astype(F32)
            r.grad_scaled[l, m, at, :] = grad
            normed = r.normed[l, m, at, :]
            return carry[0] + fold_rows(grad), carry[1] + fold_rows(grad * normed)

        zero = jnp.zeros((SUB, width), F32)
        sums, products = lax.fori_loop(0, rows // chunk, scaled_grad, (zero, zero))
        put(index, 0, jnp.sum(sums, axis=0, keepdims=True))
        put(index, 4, jnp.sum(products, axis=0, keepdims=True))

    def moments(total, at, count):
        center = unfold(total, at, 4) / count
        return center, lax.rsqrt(unfold(total, at + 4, 4) / count - center * center + epsilon)

    own_columns = pl.ds(pl.multiple_of(section * 128, 128), 128)

    def gate_weights(l, ref):
        grad = matmul_tn(r.active_low[l, :, own_columns], r.grad_logits[l])
        ref[:, :, :, 0:width] = grad.astype(BF16).reshape(2, QUAD, 16, width)

    def out_weights(l, ref, at):
        grad = 2.0 * matmul_tn(r.joined[l], r.branch[l, :, own_columns])
        grad = jnp.concatenate([grad[0:half, :], grad[lanes : lanes + half, :]], axis=0)
        tall = states // (2 * QUAD)
        for k in range(tall // 16):
            for c in range(2):
                for z in range(QUAD):
                    first = (c * QUAD + z) * tall + 16 * k
                    ref[c, z, :, at + 128 * k : at + 128 * (k + 1)] = grad[
                        first : first + 16, :
                    ].astype(BF16)

    def in_weights(l, ref, at):
        grad = matmul_tn(r.scaled[l, :, own_columns], r.grad_drive[l])
        ref[:, :, :, at : at + states] = grad.astype(BF16).reshape(2, QUAD, 16, states)

    def layer_rows(l, index):
        def both(sums):
            return jnp.sum(sums[l, 0] + sums[l, 1], axis=0, keepdims=True)

        put(index, 0, both(skip_sums))
        put(index, 4, both(bias_sums))
        part = [
            jnp.sum(r.state_sums[l, 0, k] + r.state_sums[l, 1, k], axis=0, keepdims=True)
            for k in range(4)
        ]
        gb_re, gb_im = 2.0 * part[0], -2.0 * part[1]
        gf_re, gf_im = 2.0 * part[2], -2.0 * part[3]
        one = slice(l, l + 1)
        lam_re, lam_im, size = -decay[one], spin[one], step_size[one]
        b_re, b_im, f_re, f_im = bar_re[one], bar_im[one], fac_re[one], fac_im[one]
        top_re, top_im = size * b_re - f_re, size * b_im - f_im
        square = modulus[one]
        d_re = (top_re * lam_re + top_im * lam_im) / square
        d_im = (top_im * lam_re - top_re * lam_im) / square
        gl_re = size * (b_re * gb_re + b_im * gb_im) + (d_re * gf_re + d_im * gf_im)
        gl_im = size * (b_re * gb_im - b_im * gb_re) + (d_re * gf_im - d_im * gf_re)
        e_re, e_im = cmul(lam_re, lam_im, b_re, b_im)
        g_step = size * ((e_re * gb_re + e_im * gb_im) + (b_re * gf_re + b_im * gf_im))
        put(index, 8, -gl_re)
        put(index, 10, gl_im)
        put(index, 12, g_step)

    def mixed_rows(m):
        def mix(t, carry):
            at = pl.ds(pl.multiple_of(t * chunk, chunk), chunk)
            gated = (
                r.valid[m, at, :]
                * r.active[1, m, at, own_columns]
                * r.sig[1, m, at, own_columns]
            )
            stream = r.second_in[m, at, own_columns].astype(BF16).astype(F32)
            r.narrow[at, :] = (stream + gated).astype(BF16)
            return carry

        lax.fori_loop(0, rows // chunk, mix, 0)
        r.mixed[m] = matmul(r.gather[...], r.narrow[...]).astype(BF16)

    def stream_grad(l, m, total, count, inv):
        gain = row_of(r.gain, l)
        first = gain * unfold(total, 0, 4) / count
        second = gain * unfold(total, 4, 4) / count
        return gain, first, second, inv

    total0 = first_sum.total()
    counts = [repeat_lanes(total0[16 + m : 17 + m, :], width // 128) for m in range(2)]
    norm0 = [moments(total0, 8 * m, counts[m]) for m in range(2)]

    mixer(0, 0, *norm0[0])
    first_gate(0)
    mid_sum[0].start()
    mixer(0, 1, *norm0[1], hook=mid_sum[0].turn)
    first_gate(1)
    mid_sum[1].start()

    norm1 = [None, None]
    for m in range(2):
        norm1[m] = moments(mid_sum[m].total(), 0, counts[m])
        hook = mid_sum[1].turn if m == 0 else upper_sum[0].turn
        mixer(1, m, *norm1[m], hook=hook)
        gate_grad(1, m, lambda at, v, m=m: r.out_grads[m, at, :].astype(F32))
        branch_grad(1, m)
        if m == 1:
            gate_weights(1, r.mine_0)
            out_weights(1, r.mine_0, width)
            upper_gate.to_core()
        mixer_grad(1, m, 3 + m, hook=upper_gate.to_quad if m == 1 else None)
        upper_sum[m].start()

    in_weights(1, r.mine_1, 0)
    upper_in.to_core()
    layer_rows(1, 7)

    def second_grad(m, total):
        gain, first, second, inv = stream_grad(1, m, total, counts[m], norm1[m][1])

        def grad_of(at, v):
            grad_normed = r.grad_scaled[1, m, at, :] * gain
            normed = r.normed[1, m, at, :]
            grad_stream = inv * (grad_normed - v * (first + normed * second))
            out_grad = r.out_grads[m, at, :].astype(F32)
            grad = (out_grad + grad_stream.astype(BF16).astype(F32)).astype(BF16)
            r.grad_second[m, at, :] = grad
            return grad.astype(F32)

        return grad_of

    upper_total = [upper_sum[0].total()]
    gate_grad(0, 0, second_grad(0, upper_total[0]))
    upper_sum[1].turn()
    upper_in.to_quad()
    layer_sum[1].start()
    branch_grad(0, 0)
    upper_gate.to_groups()
    mixer_grad(0, 0, 5, hook=layer_sum[1].turn)
    lower_sum[0].start()
    upper_in.to_groups()
    upper_total.append(upper_sum[1].total())
    gate_grad(0, 1, second_grad(1, upper_total[1]))
    lower_sum[0].turn()
    branch_grad(0, 1)
    gate_weights(0, r.mine_2)
    out_weights(0, r.mine_2, width)
    lower_gate.to_core()
    upper_gate.to_sections()
    mixer_grad(0, 1, 6, hook=lower_gate.to_quad)
    lower_sum[1].start()
    in_weights(0, r.mine_3, 0)
    lower_in.to_core()
    upper_in.to_sections()
    layer_rows(0, 8)
    layer_sum[0].start()
    lower_sum[1].turn()
    lower_in.to_quad()
    layer_sum[0].turn()
    mixed_rows(0)
    lower_gate.to_groups()
    mixed_rows(1)
    upper_gate.to_sibling()
    lower_in.to_groups()
    upper_in.to_sibling()
    lower_gate.to_sections()

    lower_total = [None, None]
    for m in range(2):
        lower_total[m] = lower_sum[m].total()
        gain, first, second, inv = stream_grad(0, m, lower_total[m], counts[m], norm0[m][1])
        for k, row in enumerate((gain, first, second, inv)):
            r.rows[k : k + 1, :] = row
        gain, first, second, inv = [r.rows[k : k + 1, own_columns] for k in range(4)]

        def token_grad(t, carry, m=m, gain=gain, first=first, second=second, inv=inv):
            at = pl.ds(pl.multiple_of(t * chunk, chunk), chunk)
            grad_normed = r.grad_scaled[0, m, at, own_columns] * gain
            normed = r.normed[0, m, at, own_columns]
            grad_stream = inv * (grad_normed - r.valid[m, at, :] * (first + normed * second))
            grad = r.grad_second[m, at, own_columns].astype(F32) + grad_stream
            high = grad.astype(BF16)
            r.narrow[at, :] = high
            r.narrow_rest[at, :] = (grad - high.astype(F32)).astype(BF16)
            return carry

        lax.fori_loop(0, rows // chunk, token_grad, 0)
        r.token_grad[m] = matmul(r.gather[...], r.narrow[...]) + matmul(
            r.gather[...], r.narrow_rest[...]
        )
        if m == 0:
            lower_in.to_sections()

    for l, sums in ((0, lower_total), (1, upper_total)):
        r.small[l, 0:8, :] = (sums[0] + sums[1])[0:8, :]
        r.small[l, 8:24, :] = layer_sum[l].total()[0:16, :]
    lower_gate.to_sibling()
    lower_in.to_sibling()
    for batch in batches:
        batch.end()


def lay_out_kernel(cfg, *refs):
    full = refs[0:4]
    small, mixed, token_grad = refs[4:7]
    (
        mixed_out,
        token_grad_out,
        gain_out,
        bias_out,
        decay_out,
        freq_out,
        step_out,
        in_out,
        out_out,
        skip_out,
        gate_out,
        gbias_out,
    ) = refs[7:19]
    in_held, out_held, gate_held = refs[19:22]
    rows_held, sems = refs[22:29], refs[29]
    width, states, half = cfg.width, cfg.states, cfg.half
    tall = states // (2 * QUAD)
    copies = []

    def send(held, out):
        copies.append(pltpu.make_async_copy(held, out, sems.at[len(copies)]))
        copies[-1].start()

    send(mixed, mixed_out)
    send(token_grad, token_grad_out)
    row_outs = (bias_out, gain_out, skip_out, gbias_out, decay_out, freq_out, step_out)
    for k, (held, out) in enumerate(zip(rows_held, row_outs)):
        for l in range(2):
            if k < 4:
                held[l : l + 1, :] = unfold(small[l], 4 * k, 4)
            else:
                held[l : l + 1, :] = unfold(small[l], 8 + 2 * k, 2)[:, 0:half]
        send(held, out)

    places = [(s, c, z) for s in range(cfg.sections) for c in range(2) for z in range(QUAD)]
    for l in (1, 0):
        gates, ins = full[2 - 2 * l], full[3 - 2 * l]
        for s, c, z in places:
            at = s * 128 + (c * QUAD + z) * 16
            gate_held[l, at : at + 16, :] = gates[c, s, z, :, 0:width].astype(F32)
        send(gate_held.at[l], gate_out.at[l])
        for s, c, z in places:
            for k in range(tall // 16):
                first = (c * QUAD + z) * tall + 16 * k
                out_held[l, first : first + 16, s * 128 : (s + 1) * 128] = gates[
                    c, s, z, :, width + k * 128 : width + (k + 1) * 128
                ].astype(F32)
        send(out_held.at[l], out_out.at[l])
        for s, c, z in places:
            at = s * 128 + (c * QUAD + z) * 16
            in_held[l, at : at + 16, :] = ins[c, s, z].astype(F32)
        send(in_held.at[l], in_out.at[l])
    for copy in copies:
        copy.wait()


INPUTS = tuple(
    dict(tokens=0, lengths=0, out_grad_far=0, gain=0, bias=0, decay=0, freq=0, lstep=0, b_in_far=0, c_out_far=0, skip=0, gmat_far=0, gbias=0)
)


def per_device(cfg, *args):
    rows, width, states, lanes = cfg.rows, cfg.width, cfg.states, cfg.lanes
    sections, chips = cfg.sections, cfg.dp // 2
    groups = chips // QUAD
    steps = rows // SUB
    vmem, dma = pltpu.VMEM, pltpu.SemaphoreType.DMA
    widths = (width + states, states) * 2
    outs = {f"full_{k}": ((2, sections, QUAD, 16, w), BF16) for k, w in enumerate(widths)}
    outs.update(
        small=((2, 24, 128), F32), mixed=((2, rows, 128), BF16), token_grad=((2, rows, 128), F32)
    )
    scratch = dict(
        sum_own=vmem((REDUCES, 24, 128), F32),
        sum_sibling=vmem((REDUCES, 24, 128), F32),
        sum_slots=vmem((REDUCES, chips, 24, 128), F32),
        sum_send=dma((REDUCES, chips)),
        sum_recv=dma((REDUCES, chips)),
        grad_send=dma((4, (2 + sections) * QUAD + groups)),
        grad_recv=dma((4, (2 + sections) * QUAD + groups)),
        fetch_sem=dma((4,)),
        b_in=vmem((2, width, states), BF16),
        c_out=vmem((2, states, width), BF16),
        gmat=vmem((2, width, width), BF16),
        out_grad=vmem((2, rows, width), BF16),
        widen=vmem((states, 2 * lanes), BF16),
        q=vmem((2, rows, 2 * lanes), F32),
        spread=vmem((rows, rows), BF16),
        gather=vmem((rows, rows), BF16),
        first_in=vmem((2, rows, width), BF16),
        out_grads=vmem((2, rows, width), BF16),
        second_in=vmem((2, rows, width), F32),
        grad_second=vmem((2, rows, width), BF16),
        valid=vmem((2, rows, 128), F32),
        keep_start=vmem((2, rows, 128), F32),
        keep_end=vmem((2, rows, 128), F32),
        par=vmem((SUB, lanes), F32),
        b_pad=vmem((2, width, 2 * lanes), BF16),
        c_pad=vmem((2, 2 * lanes, width), BF16),
        normed=vmem((2, 2, rows, width), F32),
        scaled=vmem((2, 2 * rows, width), BF16),
        drive=vmem((2, 2, rows, 2 * lanes), F32),
        state=vmem((2, 2, (steps + 1) * SUB, 2 * lanes), F32),
        joined=vmem((2, 2 * rows, 2 * lanes), BF16),
        work=vmem((rows, width), F32),
        active=vmem((2, 2, rows, width), F32),
        active_low=vmem((2, 2 * rows, width), BF16),
        slope=vmem((2, 2, rows, width), F32),
        sig=vmem((2, 2, rows, width), F32),
        through=vmem((rows, width), F32),
        grad_logits=vmem((2, 2 * rows, width), BF16),
        branch=vmem((2, 2 * rows, width), BF16),
        grad_drive=vmem((2, 2 * rows, states), BF16),
        grad_scaled=vmem((2, 2, rows, width), F32),
        state_sums=vmem((2, 2, 4, SUB, lanes), F32),
        narrow=vmem((rows, 128), BF16),
        narrow_rest=vmem((rows, 128), BF16),
        rows=vmem((SUB, width), F32),
    )
    for k, w in enumerate(widths):
        blocks = (2, QUAD), (QUAD,), (QUAD,), (QUAD,), (groups,)
        for part, block in zip(STAGES, blocks):
            scratch[f"{part}_{k}"] = vmem((*block, 16, w), BF16)
    in_vmem = pl.BlockSpec(memory_space=pltpu.VMEM)
    in_smem = pl.BlockSpec(memory_space=pltpu.SMEM)
    in_hbm = pl.BlockSpec(memory_space=pltpu.HBM)
    names = INPUTS + tuple(outs) + tuple(scratch)
    made = pl.pallas_call(
        partial(main_kernel, cfg, names),
        name="layers",
        out_shape=[vmem(*spec) for spec in outs.values()],
        in_specs=[
            in_smem if name == "lengths" else in_hbm if name.endswith("_far") else in_vmem
            for name in INPUTS
        ],
        out_specs=[in_vmem for name in outs],
        scratch_shapes=list(scratch.values()),
        compiler_params=pltpu.CompilerParams(
            collective_id=0, has_side_effects=True, vmem_limit_bytes=56 * 2**20
        ),
    )(*args)
    shapes = [
        ((2, rows, 128), BF16),
        ((2, rows, 128), F32),
        ((2, width), F32),
        ((2, width), F32),
        ((2, states // 2), F32),
        ((2, states // 2), F32),
        ((2, states // 2), F32),
        ((2, width, states), F32),
        ((2, states, width), F32),
        ((2, width), F32),
        ((2, width, width), F32),
        ((2, width), F32),
    ]
    by_copy = (7, 8, 10)
    return pl.pallas_call(
        partial(lay_out_kernel, cfg),
        name="lay_out",
        out_shape=[jax.ShapeDtypeStruct(*spec) for spec in shapes],
        in_specs=[in_vmem] * 7,
        out_specs=[in_hbm] * 12,
        scratch_shapes=[vmem(*shapes[k]) for k in by_copy]
        + [vmem((2, width), F32)] * 4
        + [vmem((2, states // 2), F32)] * 3
        + [dma((15,))],
        compiler_params=pltpu.CompilerParams(vmem_limit_bytes=24 * 2**20),
    )(*made)


def solution(mesh):
    sections, dp = mesh.shape["section"], mesh.shape["dp"]

    def run(*args):
        _, rows, width = args[0].shape
        states = args[8].shape[2]
        cfg = SimpleNamespace(
            rows=rows // dp,
            width=width,
            states=states,
            half=states // 2,
            lanes=-(-states // 256) * 128,
            sections=sections,
            dp=dp,
        )
        split = P(None, "dp", None)
        shared = P()
        placed = P(None, "dp", "section")
        return jax.shard_map(
            partial(per_device, cfg),
            mesh=mesh,
            in_specs=(split, P(None, "dp"), split) + (shared,) * 10,
            out_specs=(placed, placed) + (shared,) * 10,
            check_vma=False,
        )(*args)

    return run
```

```python
from functools import partial
from types import SimpleNamespace

import jax
import jax.numpy as jnp
from jax import lax
from jax.experimental import pallas as pl
from jax.experimental.pallas import tpu as pltpu
from jax.sharding import PartitionSpec as P

epsilon = 1e-05
MESH = pl.DeviceIdType.MESH
F32 = jnp.float32
BF16 = jnp.bfloat16
SUB = 8
QUAD = 4
LATE_STATES = 3
SUM_ROWS = (24, 8, 8, 8, 8, 16)


STAGES = tuple(dict(mine=0, theirs=0, chip=0, quad=0, group=0, full=0))


def matmul(left, right):
    return jnp.dot(left, right, preferred_element_type=F32)


def matmul_nt(left, right):
    return lax.dot_general(left, right, (((1,), (1,)), ((), ())), preferred_element_type=F32)


def matmul_tn(left, right):
    return lax.dot_general(left, right, (((0,), (0,)), ((), ())), preferred_element_type=F32)


def cmul(ar, ai, br, bi):
    return ar * br - ai * bi, ar * bi + ai * br


def sweep(count, body, carry):
    for t in range(count):
        carry = body(t, carry)
    return carry


def repeat_lanes(x, times):
    return jnp.concatenate([x] * times, axis=1)


def fold_rows(x):
    return jnp.sum(x.reshape(x.shape[0] // SUB, SUB, x.shape[1]), axis=0)


def unfold(total, first, count):
    return jnp.concatenate([total[first + k : first + k + 1, :] for k in range(count)], axis=1)


class SmallSum:
    def __init__(self, place, direct, own, sibling, slots, send_sems, recv_sems, index):
        self.place, self.direct = place, direct
        self.own, self.sibling, self.slots = own, sibling, slots
        self.send_sems, self.recv_sems, self.index = send_sems, recv_sems, index

    def remote(self, src, dst, step, device):
        copy = pltpu.make_async_remote_copy(
            src_ref=src,
            dst_ref=dst,
            send_sem=self.send_sems.at[self.index, step],
            recv_sem=self.recv_sems.at[self.index, step],
            device_id=(self.place.section, device),
            device_id_type=MESH,
        )
        copy.start()
        return copy

    def to_all(self, slot, members, peer):
        self.members = members
        block = self.slots.at[slot]
        self.copies = [self.remote(block, block, step, peer(step)) for step in range(1, members)]

    def start(self):
        at = self.place
        if self.direct:
            self.slots[at.dp] = self.own[...]
            self.to_all(at.dp, at.devices, at.dp_peer)
        else:
            self.copy = self.remote(self.own, self.sibling, 0, at.sibling)

    def turn(self):
        at = self.place
        if not self.direct:
            self.copy.wait()
            self.slots[at.chip] = self.own[...] + self.sibling[...]
            self.to_all(at.chip, at.chips, at.chip_peer)

    def total(self):
        for copy in self.copies:
            copy.wait()
        result = self.slots[0]
        for member in range(1, self.members):
            result = result + self.slots[member]
        return result


class GradSum:
    def __init__(self, place, refs, send_sems, recv_sems, index):
        self.place = place
        self.mine, self.theirs, self.chip_part, self.quad_in, self.group_in, self.full = refs
        self.send_sems, self.recv_sems, self.index = send_sems, recv_sems, index
        self.sem = 0

    def remote(self, src, dst, device):
        copy = pltpu.make_async_remote_copy(
            src_ref=src,
            dst_ref=dst,
            send_sem=self.send_sems.at[self.index, self.sem],
            recv_sem=self.recv_sems.at[self.index, self.sem],
            device_id=device,
            device_id_type=MESH,
        )
        self.sem += 1
        copy.start()
        return copy

    def to_core(self):
        at = self.place
        self.copy = self.remote(
            self.mine.at[1 - at.core], self.theirs, (at.section, at.sibling)
        )

    def to_quad(self):
        at = self.place
        self.copy.wait()
        for part in range(QUAD):
            both = self.mine[at.core, part].astype(F32) + self.theirs[part].astype(F32)
            self.chip_part[part] = both.astype(BF16)
        self.copies = []
        for step in range(1, QUAD):
            other = lax.rem(at.quad + step, QUAD)
            self.copies.append(
                self.remote(
                    self.chip_part.at[other],
                    self.quad_in.at[at.quad],
                    (at.section, at.quad_peer(step)),
                )
            )
        self.quad_in[at.quad] = self.chip_part[at.quad]

    def to_groups(self):
        at = self.place
        for copy in self.copies:
            copy.wait()
        total = self.quad_in[0].astype(F32)
        for part in range(1, QUAD):
            total = total + self.quad_in[part].astype(F32)
        if at.groups > 1:
            group = at.group
            self.group_in[group] = total.astype(BF16)
            copies = []
            for step in range(1, at.groups):
                copies.append(
                    self.remote(
                        self.group_in.at[group],
                        self.group_in.at[group],
                        (at.section, at.chip_peer(step * QUAD)),
                    )
                )
            for copy in copies:
                copy.wait()
            total = self.group_in[0].astype(F32)
            for other in range(1, at.groups):
                total = total + self.group_in[other].astype(F32)
        piece = self.full.at[at.core, at.section, at.quad]
        piece[...] = total.astype(BF16)
        self.copies = [
            self.remote(piece, piece, (at.section, at.quad_peer(step))) for step in range(1, QUAD)
        ]
        self.spread = [self.over_sections(at.quad)]

    def over_sections(self, quad):
        at = self.place
        piece = self.full.at[at.core, at.section, quad]
        return [
            self.remote(piece, piece, (lax.rem(at.section + step, at.sections), at.dp))
            for step in range(1, at.sections)
        ]

    def to_sections(self):
        at = self.place
        for step in range(1, QUAD):
            self.copies[step - 1].wait()
            self.spread.append(self.over_sections(lax.rem(at.quad + QUAD - step, QUAD)))
        piece = self.full.at[at.core, at.section]
        self.last = [self.remote(piece, piece, (at.section, at.sibling))]

    def to_sibling(self):
        at = self.place
        for step in range(1, at.sections):
            for copies in self.spread:
                copies[step - 1].wait()
            other = lax.rem(at.section + at.sections - step, at.sections)
            piece = self.full.at[at.core, other]
            self.last.append(self.remote(piece, piece, (at.section, at.sibling)))

    def end(self):
        for copy in self.last:
            copy.wait()


def main_kernel(cfg, names, *refs):
    r = SimpleNamespace(**dict(zip(names, refs)))
    rows, width, states, half, lanes = (
        cfg.rows,
        cfg.width,
        cfg.states,
        cfg.half,
        cfg.lanes,
    )
    steps = rows // SUB
    section = lax.axis_index("section")
    dp = lax.axis_index("dp")
    chips = cfg.dp // 2
    core, chip = lax.rem(dp, 2), lax.div(dp, 2)
    quad, group = lax.rem(chip, QUAD), lax.div(chip, QUAD)
    place = SimpleNamespace(
        section=section,
        sections=cfg.sections,
        dp=dp,
        core=core,
        chip=chip,
        chips=chips,
        quad=quad,
        group=group,
        groups=chips // QUAD,
        devices=cfg.dp,
        dp_peer=lambda step: lax.rem(dp + step, cfg.dp),
        sibling=dp + 1 - 2 * core,
        chip_peer=lambda step: lax.rem(chip + step, chips) * 2 + core,
        quad_peer=lambda step: (group * QUAD + lax.rem(quad + step, QUAD)) * 2 + core,
    )

    direct = cfg.dp <= 8
    if direct:
        peers = [(section, place.dp_peer(step)) for step in range(1, cfg.dp)]
    else:
        peers = [(section, place.sibling)]
        peers += [(section, place.chip_peer(step)) for step in range(1, chips)]
    peers += [(lax.rem(section + step, cfg.sections), dp) for step in range(1, cfg.sections)]
    barrier = pltpu.get_barrier_semaphore()
    for peer in peers:
        pl.semaphore_signal(barrier, inc=1, device_id=peer, device_id_type=MESH)

    small = [
        SmallSum(
            place,
            direct and k < len(SUM_ROWS) - 1,
            r.sum_own.at[k, 0:tall] if k < len(SUM_ROWS) - 1 else r.late_own.at[section],
            r.sum_sibling.at[k, 0:tall],
            r.sum_slots.at[k, :, 0:tall],
            r.sum_send,
            r.sum_recv,
            k,
        )
        for k, tall in enumerate(SUM_ROWS)
    ]
    first_sum = small[0]
    mid_sum = [small[1], small[2]]
    upper_sum = [small[3], small[4]]
    late_sum = small[5]
    batches = [
        GradSum(
            place,
            [getattr(r, f"{part}_{k}") for part in STAGES],
            r.grad_send,
            r.grad_recv,
            k,
        )
        for k in range(4)
    ]
    upper_gate, upper_in, lower_gate, lower_in = batches

    fetched = []
    for k, (held, given) in enumerate(
        (
            (r.b_in, r.b_in_far),
            (r.out_grad, r.out_grad_far),
            (r.c_out, r.c_out_far),
            (r.gmat, r.gmat_far),
        )
    ):
        fetched.append(pltpu.make_async_copy(given, held, r.fetch_sem.at[k]))
        fetched[k].start()

    first_len = [r.lengths[m, 0] for m in range(2)]
    total_len = [r.lengths[m, 0] + r.lengths[m, 1] for m in range(2)]

    def put(index, at, row):
        for k in range(row.shape[1] // 128):
            r.sum_own[index, at + k : at + k + 1, :] = row[:, k * 128 : (k + 1) * 128]

    def put_late(at, row):
        for k in range(cfg.sections):
            r.late_own[k, at : at + 1, :] = row[:, k * 128 : (k + 1) * 128]

    chunk = 32
    for m in range(2):

        def token_sums(t, carry, m=m):
            at = pl.ds(t * chunk, chunk)
            v = r.tokens[m, at, :].astype(F32)
            place_row = t * chunk + lax.broadcasted_iota(jnp.int32, (chunk, width), 0)
            kept = jnp.where(place_row < total_len[m], v, 0.0)
            return carry[0] + fold_rows(kept), carry[1] + fold_rows(kept * v)

        zero = jnp.zeros((SUB, width), F32)
        sums, squares = sweep(rows // chunk, token_sums, (zero, zero))
        put(0, 8 * m, jnp.sum(sums, axis=0, keepdims=True))
        put(0, 8 * m + 4, jnp.sum(squares, axis=0, keepdims=True))
        count = jnp.minimum(total_len[m], rows).astype(F32)
        r.sum_own[0, 16 + m : 17 + m, :] = jnp.full((1, 128), count, F32)

    pl.semaphore_wait(barrier, len(peers))
    first_sum.start()

    at_i = lax.broadcasted_iota(jnp.int32, (rows, rows), 0)
    at_r = lax.broadcasted_iota(jnp.int32, (rows, rows), 1)
    r.spread[...] = jnp.where(
        at_r == (at_i % SUB) * steps + at_i // SUB, 1.0, 0.0
    ).astype(BF16)
    r.gather[...] = jnp.where(
        at_i == (at_r % SUB) * steps + at_r // SUB, 1.0, 0.0
    ).astype(BF16)
    for m in range(2):
        r.first_in[m] = matmul(r.spread[...], r.tokens[m]).astype(BF16)
    first_sum.turn()
    fetched[1].wait()
    for m in range(2):
        r.out_grads[m] = matmul(r.spread[...], r.out_grad[m]).astype(BF16)
    held = lax.broadcasted_iota(jnp.int32, (rows, 128), 0)
    held = (held % SUB) * steps + held // SUB
    all_start, all_end = [], []
    for m in range(2):
        one, zero = jnp.float32(1.0), jnp.float32(0.0)
        past = held >= total_len[m]
        starts = (held == 0) | (held == first_len[m]) | past
        ends = (held == first_len[m] - 1) | (held == total_len[m] - 1) | past | (held == rows - 1)
        r.valid[m] = jnp.where(past, zero, one)
        r.keep_start[m] = jnp.where(starts, zero, one)
        r.keep_end[m] = jnp.where(ends, zero, one)
        for kept, mask in ((all_start, r.keep_start), (all_end, r.keep_end)):
            kept.append(jnp.min(mask[m].reshape(steps, SUB, 128), axis=0))

    r.par[...] = jnp.zeros((SUB, lanes), F32)
    r.par[0:2, :] = jnp.ones((2, lanes), F32)
    r.par[0:2, 0:half] = r.decay[...]
    r.par[2:4, 0:half] = r.freq[...]
    r.par[4:6, 0:half] = r.lstep[...]
    decay, spin = r.par[0:2, :], r.par[2:4, :]
    step_size = jnp.exp(r.par[4:6, :])
    damping = jnp.exp(-decay * step_size)
    bar_re = damping * jnp.cos(spin * step_size)
    bar_im = damping * jnp.sin(spin * step_size)
    modulus = decay * decay + spin * spin
    fac_re = ((bar_re - 1.0) * -decay + bar_im * spin) / modulus
    fac_im = (bar_im * -decay - (bar_re - 1.0) * spin) / modulus
    pow_re, pow_im = bar_re, bar_im
    power = 1
    while power < steps:
        pow_re, pow_im = cmul(pow_re, pow_im, pow_re, pow_im)
        power *= 2

    lane = lax.broadcasted_iota(jnp.int32, (1, 128), 1)
    low_lanes = lane < half - 128
    turn_by = half - 128

    from_column = lax.broadcasted_iota(jnp.int32, (states, 2 * lanes), 0)
    to_column = lax.broadcasted_iota(jnp.int32, (states, 2 * lanes), 1)
    moved_to = jnp.where(from_column < half, from_column, from_column + (lanes - half))
    r.widen[...] = jnp.where(to_column == moved_to, 1.0, 0.0).astype(BF16)
    for k in (0, 2, 3):
        fetched[k].wait()
    for l in range(2):
        r.b_pad[l] = matmul(r.b_in[l], r.widen[...]).astype(BF16)
        blank = jnp.zeros((lanes - half, width), BF16)
        r.c_pad[l, 0:half, :] = r.c_out[l, 0:half, :]
        r.c_pad[l, half:lanes, :] = blank
        r.c_pad[l, lanes : lanes + half, :] = r.c_out[l, half:states, :]
        r.c_pad[l, lanes + half : 2 * lanes, :] = blank

    def across(end, coef, reverse):
        end_re, end_im = end
        coef_re, coef_im = coef
        sub = lax.broadcasted_iota(jnp.int32, (SUB, lanes), 0)
        for by in (1, 2, 4):
            turn = SUB - by if reverse else by
            live = sub < SUB - by if reverse else sub >= by

            def moved(x):
                return jnp.where(live, pltpu.roll(x, turn, 0), 0.0)

            add_re, add_im = cmul(coef_re, coef_im, moved(end_re), moved(end_im))
            coef_re, coef_im = cmul(coef_re, coef_im, moved(coef_re), moved(coef_im))
            end_re, end_im = end_re + add_re, end_im + add_im
        turn = SUB - 1 if reverse else 1
        live = sub < SUB - 1 if reverse else sub >= 1
        return tuple(jnp.where(live, pltpu.roll(x, turn, 0), 0.0) for x in (end_re, end_im))

    def wide8(x, l):
        return jnp.broadcast_to(x[l : l + 1, :], (SUB, x.shape[1]))

    def group_rows(p):
        return pl.ds(p * SUB, SUB)

    def scan_coefs(l, m, reverse):
        keep = r.keep_end if reverse else r.keep_start
        all_kept = repeat_lanes((all_end if reverse else all_start)[m], lanes // 128)
        product = (all_kept * wide8(pow_re, l), all_kept * wide8(pow_im, l))
        return keep, wide8(bar_re, l), wide8(bar_im, l), product

    def advance(keep, m, at, br, bi, re, im, src_re, src_im):
        k = repeat_lanes(keep[m, at, :], lanes // 128)
        kr, ki = k * br, k * bi
        return kr * re - ki * im + src_re, kr * im + ki * re + src_im

    def scan_states(l, m):
        reverse = l == 1
        lead = 0 if reverse else 1
        keep, br, bi, product = scan_coefs(l, m, reverse)
        fr, fi = wide8(fac_re, l), wide8(fac_im, l)
        zero = jnp.zeros((SUB, lanes), F32)

        def ends(t, carry):
            p = steps - 1 - t if reverse else t
            at = group_rows(p)
            v = repeat_lanes(r.valid[m, at, :], lanes // 128)
            drive_re = r.drive[l, m, at, 0:lanes]
            drive_im = r.drive[l, m, at, lanes : 2 * lanes]
            src_re, src_im = cmul(fr, fi, v * drive_re, v * drive_im)
            r.state[l, m, group_rows(p + lead), 0:lanes] = src_re
            r.state[l, m, group_rows(p + lead), lanes : 2 * lanes] = src_im
            return advance(keep, m, at, br, bi, *carry, src_re, src_im)

        end = sweep(steps, ends, (zero, zero))
        enter = across(end, product, reverse)
        first = steps if reverse else 0
        r.state[l, m, first * SUB : (first + 1) * SUB, 0:lanes] = enter[0]
        r.state[l, m, first * SUB : (first + 1) * SUB, lanes : 2 * lanes] = enter[1]

        def fill(t, carry):
            done = []
            for k in range(2):
                p = steps - 1 - (2 * t + k) if reverse else 2 * t + k
                at, to = group_rows(p), group_rows(p + lead)
                src_re = r.state[l, m, to, 0:lanes]
                src_im = r.state[l, m, to, lanes : 2 * lanes]
                carry = advance(keep, m, at, br, bi, *carry, src_re, src_im)
                r.state[l, m, to, 0:lanes] = carry[0]
                r.state[l, m, to, lanes : 2 * lanes] = carry[1]
                done.append(jnp.concatenate([carry[0], -carry[1]], axis=1))
            pair = steps // 2 - 1 - t if reverse else t
            both = jnp.concatenate(done[::-1] if reverse else done, axis=0)
            to = pl.ds(m * rows + pair * 16, 16)
            r.joined[l, to, :] = both.astype(BF16)
            return carry

        sweep(steps // 2, fill, enter)

    def scan_grads(l, m):
        reverse = l == 0
        back = 1 if l == 1 else 0
        keep, br, bi, product = scan_coefs(l, m, reverse)
        keep_state = r.keep_start if l == 0 else r.keep_end
        fr, fi = 2.0 * wide8(fac_re, l), 2.0 * wide8(fac_im, l)
        zero = jnp.zeros((SUB, lanes), F32)

        def ends(t, carry):
            p = steps - 1 - t if reverse else t
            at = group_rows(p)
            q_re = r.q[m, at, 0:lanes]
            q_im = r.q[m, at, lanes : 2 * lanes]
            return advance(keep, m, at, br, bi, *carry, q_re, q_im)

        end = sweep(steps, ends, (zero, zero))
        enter = across(end, product, reverse)

        def fill(t, carry):
            w, bar_sum, fac_sum = carry
            done = []
            for k in range(2):
                p = steps - 1 - (2 * t + k) if reverse else 2 * t + k
                at, near = group_rows(p), group_rows(p + back)
                q_re = r.q[m, at, 0:lanes]
                q_im = r.q[m, at, lanes : 2 * lanes]
                w = advance(keep, m, at, br, bi, *w, q_re, q_im)
                kept = repeat_lanes(keep_state[m, at, :], lanes // 128)
                near_re = kept * r.state[l, m, near, 0:lanes]
                near_im = kept * r.state[l, m, near, lanes : 2 * lanes]
                term = cmul(*w, near_re, near_im)
                bar_sum = (bar_sum[0] + term[0], bar_sum[1] + term[1])
                v = repeat_lanes(r.valid[m, at, :], lanes // 128)
                vw = (v * w[0], v * w[1])
                drive_re = r.drive[l, m, at, 0:lanes]
                drive_im = r.drive[l, m, at, lanes : 2 * lanes]
                term = cmul(*vw, drive_re, drive_im)
                fac_sum = (fac_sum[0] + term[0], fac_sum[1] + term[1])
                gd_re, gd_im = cmul(fr, fi, *vw)
                im_low = pltpu.roll(-gd_im[:, 0:128], 64, 1)
                im_high = pltpu.roll(-gd_im[:, 128:256], 64, 1)
                done.append(
                    jnp.concatenate(
                        [
                            gd_re[:, 0:128],
                            jnp.where(low_lanes, gd_re[:, 128:256], im_low),
                            jnp.where(low_lanes, im_low, im_high),
                        ],
                        axis=1,
                    )
                )
            pair = steps // 2 - 1 - t if reverse else t
            both = jnp.concatenate(done[::-1] if reverse else done, axis=0)
            to = pl.ds(m * rows + pair * 16, 16)
            r.grad_drive[l, to, :] = both.astype(BF16)
            return w, bar_sum, fac_sum

        none = (zero, zero)
        _, bar_sum, fac_sum = sweep(steps // 2, fill, (enter, none, none))
        for k, part in enumerate((*bar_sum, *fac_sum)):
            r.state_sums[l, m, k] = part

    def row_of(ref, l):
        return ref[l : l + 1, :]

    def micro_rows(m):
        return slice(m * rows, (m + 1) * rows)

    gelu_chunk = 16

    def mixer(l, m, center, inv, hook=None):
        gain, bias, skip = row_of(r.gain, l), row_of(r.bias, l), row_of(r.skip, l)

        def normalise(t, carry):
            at = pl.ds(t * chunk, chunk)
            if l == 0:
                v = r.first_in[m, at, :].astype(F32)
            else:
                v = r.second_in[m, at, :]
            normed = (v - center) * inv
            r.normed[l, m, at, :] = normed
            to = pl.ds(m * rows + t * chunk, chunk)
            r.scaled[l, to, :] = (normed * gain + bias).astype(BF16)
            return carry

        sweep(rows // chunk, normalise, 0)
        r.drive[l, m] = matmul(r.scaled[l, micro_rows(m), :], r.b_pad[l])
        scan_states(l, m)
        if hook is not None:
            hook()
        r.work[...] = matmul(r.joined[l, micro_rows(m), :], r.c_pad[l])

        def activate(t, carry):
            at = pl.ds(t * gelu_chunk, gelu_chunk)
            scaled = r.normed[l, m, at, :] * gain + bias
            y = (2.0 * r.work[at, :] + skip * scaled).astype(BF16).astype(F32)
            below = 0.5 + 0.5 * lax.erf(y * 0.7071067811865476)
            density = jnp.exp(-0.5 * y * y) * 0.3989422804014327
            active = y * below
            r.active[l, m, at, :] = active
            r.slope[l, m, at, :] = below + y * density
            to = pl.ds(m * rows + t * gelu_chunk, gelu_chunk)
            r.active_low[l, to, :] = active.astype(BF16)
            return carry

        sweep(rows // gelu_chunk, activate, 0)
        r.work[...] = matmul(r.active_low[l, micro_rows(m), :], r.gmat[l])

    def first_gate(m):
        gbias = row_of(r.gbias, 0)

        def gate(t, carry):
            at = pl.ds(t * gelu_chunk, gelu_chunk)
            opened = jax.nn.sigmoid(r.work[at, :] + gbias)
            r.sig[0, m, at, :] = opened
            v = repeat_lanes(r.valid[m, at, :], width // 128)
            gated = v * r.active[0, m, at, :] * opened
            second = r.first_in[m, at, :].astype(F32) + gated.astype(BF16).astype(F32)
            r.second_in[m, at, :] = second
            kept = v * second
            return carry[0] + fold_rows(kept), carry[1] + fold_rows(kept * second)

        zero = jnp.zeros((SUB, width), F32)
        sums, squares = sweep(rows // gelu_chunk, gate, (zero, zero))
        put(1 + m, 0, jnp.sum(sums, axis=0, keepdims=True))
        put(1 + m, 4, jnp.sum(squares, axis=0, keepdims=True))

    bias_sums = {}
    skip_sums = {}

    def gate_grad(l, m, grad_of):
        gbias = row_of(r.gbias, l)

        def gate(t, carry):
            at = pl.ds(t * gelu_chunk, gelu_chunk)
            if l == 1:
                opened = jax.nn.sigmoid(r.work[at, :] + gbias)
                r.sig[1, m, at, :] = opened
            else:
                opened = r.sig[0, m, at, :]
            v = repeat_lanes(r.valid[m, at, :], width // 128)
            masked = v * grad_of(at, v)
            through = masked * opened
            r.through[at, :] = through
            grad_logits = through * r.active[l, m, at, :] * (1.0 - opened)
            to = pl.ds(m * rows + t * gelu_chunk, gelu_chunk)
            r.grad_logits[l, to, :] = grad_logits.astype(BF16)
            return carry + fold_rows(grad_logits)

        zero = jnp.zeros((SUB, width), F32)
        bias_sums[l, m] = sweep(rows // gelu_chunk, gate, zero)

    def branch_grad(l, m):
        gain, bias = row_of(r.gain, l), row_of(r.bias, l)
        r.work[...] = matmul_nt(r.grad_logits[l, micro_rows(m), :], r.gmat[l])

        def branch(t, carry):
            at = pl.ds(t * chunk, chunk)
            grad_active = r.through[at, :] + r.work[at, :]
            g = (r.slope[l, m, at, :] * grad_active).astype(BF16)
            to = pl.ds(m * rows + t * chunk, chunk)
            r.branch[l, to, :] = g
            scaled = r.normed[l, m, at, :] * gain + bias
            return carry + fold_rows(g.astype(F32) * scaled)

        zero = jnp.zeros((SUB, width), F32)
        skip_sums[l, m] = sweep(rows // chunk, branch, zero)
        r.q[m] = matmul_nt(r.branch[l, micro_rows(m), :], r.c_pad[l])

    def mixer_grad(l, m, hook=None):
        skip = row_of(r.skip, l)
        scan_grads(l, m)
        if hook is not None:
            hook()
        r.work[...] = matmul_nt(r.grad_drive[l, micro_rows(m), :], r.b_in[l])

        def scaled_grad(t, carry):
            at = pl.ds(t * chunk, chunk)
            to = pl.ds(m * rows + t * chunk, chunk)
            grad = r.work[at, :] + skip * r.branch[l, to, :].astype(F32)
            r.grad_scaled[l, m, at, :] = grad
            normed = r.normed[l, m, at, :]
            return carry[0] + fold_rows(grad), carry[1] + fold_rows(grad * normed)

        zero = jnp.zeros((SUB, width), F32)
        sums, products = sweep(rows // chunk, scaled_grad, (zero, zero))
        sums = jnp.sum(sums, axis=0, keepdims=True)
        products = jnp.sum(products, axis=0, keepdims=True)
        if l == 1:
            put(3 + m, 0, sums)
            put(3 + m, 4, products)
        else:
            put_late(2 * m, sums)
            put_late(2 * m + 1, products)

    def moments(total, at, count):
        center = unfold(total, at, 4) / count
        return center, lax.rsqrt(unfold(total, at + 4, 4) / count - center * center + epsilon)

    own_columns = pl.ds(pl.multiple_of(section * 128, 128), 128)

    def gate_weights(l, ref):
        grad = matmul_tn(r.active_low[l, :, own_columns], r.grad_logits[l])
        ref[:, :, :, 0:width] = grad.astype(BF16).reshape(2, QUAD, 16, width)

    def out_weights(l, ref, at):
        grad = 2.0 * matmul_tn(r.joined[l], r.branch[l, :, own_columns])
        grad = jnp.concatenate([grad[0:half, :], grad[lanes : lanes + half, :]], axis=0)
        tall = states // (2 * QUAD)
        for k in range(tall // 16):
            for c in range(2):
                for z in range(QUAD):
                    first = (c * QUAD + z) * tall + 16 * k
                    ref[c, z, :, at + 128 * k : at + 128 * (k + 1)] = grad[
                        first : first + 16, :
                    ].astype(BF16)

    def in_weights(l, ref, at):
        grad = matmul_tn(r.scaled[l, :, own_columns], r.grad_drive[l])
        ref[:, :, :, at : at + states] = grad.astype(BF16).reshape(2, QUAD, 16, states)

    def layer_rows(l):
        def both(sums):
            return jnp.sum(sums[l, 0] + sums[l, 1], axis=0, keepdims=True)

        put_late(4 + 2 * l, both(skip_sums))
        put_late(5 + 2 * l, both(bias_sums))
        part = [
            jnp.sum(r.state_sums[l, 0, k] + r.state_sums[l, 1, k], axis=0, keepdims=True)
            for k in range(4)
        ]
        gb_re, gb_im = 2.0 * part[0], -2.0 * part[1]
        gf_re, gf_im = 2.0 * part[2], -2.0 * part[3]
        one = slice(l, l + 1)
        lam_re, lam_im, size = -decay[one], spin[one], step_size[one]
        b_re, b_im, f_re, f_im = bar_re[one], bar_im[one], fac_re[one], fac_im[one]
        top_re, top_im = size * b_re - f_re, size * b_im - f_im
        square = modulus[one]
        d_re = (top_re * lam_re + top_im * lam_im) / square
        d_im = (top_im * lam_re - top_re * lam_im) / square
        gl_re = size * (b_re * gb_re + b_im * gb_im) + (d_re * gf_re + d_im * gf_im)
        gl_im = size * (b_re * gb_im - b_im * gb_re) + (d_re * gf_im - d_im * gf_re)
        e_re, e_im = cmul(lam_re, lam_im, b_re, b_im)
        g_step = size * ((e_re * gb_re + e_im * gb_im) + (b_re * gf_re + b_im * gf_im))
        parts = [
            row[:, k : k + 128] for row in (-gl_re, gl_im, g_step) for k in range(0, lanes, 128)
        ]
        for k, row in enumerate(parts):
            k += l * len(parts)
            at = 8 + k % LATE_STATES
            r.late_own[k // LATE_STATES, at : at + 1, :] = row

    def mixed_rows(m):
        def mix(t, carry):
            at = pl.ds(t * chunk, chunk)
            gated = (
                r.valid[m, at, :]
                * r.active[1, m, at, own_columns]
                * r.sig[1, m, at, own_columns]
            )
            stream = r.second_in[m, at, own_columns].astype(BF16).astype(F32)
            r.narrow[at, :] = (stream + gated).astype(BF16)
            return carry

        sweep(rows // chunk, mix, 0)
        r.mixed[m] = matmul(r.gather[...], r.narrow[...]).astype(BF16)

    def stream_grad(l, m, total, count, inv):
        gain = row_of(r.gain, l)
        first = gain * unfold(total, 0, 4) / count
        second = gain * unfold(total, 4, 4) / count
        return gain, first, second, inv

    total0 = first_sum.total()
    counts = [repeat_lanes(total0[16 + m : 17 + m, :], width // 128) for m in range(2)]
    norm0 = [moments(total0, 8 * m, counts[m]) for m in range(2)]

    mixer(0, 0, *norm0[0])
    first_gate(0)
    mid_sum[0].start()
    mixer(0, 1, *norm0[1], hook=mid_sum[0].turn)
    first_gate(1)
    mid_sum[1].start()

    norm1 = [None, None]
    for m in range(2):
        norm1[m] = moments(mid_sum[m].total(), 0, counts[m])
        hook = mid_sum[1].turn if m == 0 else None
        mixer(1, m, *norm1[m], hook=hook)
        gate_grad(1, m, lambda at, v, m=m: r.out_grads[m, at, :].astype(F32))
        branch_grad(1, m)
        if m == 1:
            gate_weights(1, r.mine_0)
            out_weights(1, r.mine_0, width)
            upper_gate.to_core()
        mixer_grad(1, m)
        upper_sum[m].start()
        upper_sum[m].turn()

    in_weights(1, r.mine_1, 0)
    upper_in.to_core()
    upper_gate.to_quad()
    layer_rows(1)

    def second_grad(m, total):
        gain, first, second, inv = stream_grad(1, m, total, counts[m], norm1[m][1])

        def grad_of(at, v):
            grad_normed = r.grad_scaled[1, m, at, :] * gain
            normed = r.normed[1, m, at, :]
            grad_stream = inv * (grad_normed - v * (first + normed * second))
            out_grad = r.out_grads[m, at, :].astype(F32)
            grad = (out_grad + grad_stream.astype(BF16).astype(F32)).astype(BF16)
            r.grad_second[m, at, :] = grad
            return grad.astype(F32)

        return grad_of

    upper_total = [upper_sum[0].total()]
    gate_grad(0, 0, second_grad(0, upper_total[0]))
    upper_in.to_quad()
    branch_grad(0, 0)
    mixer_grad(0, 0)
    upper_total.append(upper_sum[1].total())
    gate_grad(0, 1, second_grad(1, upper_total[1]))
    branch_grad(0, 1)
    upper_gate.to_groups()
    gate_weights(0, r.mine_2)
    out_weights(0, r.mine_2, width)
    lower_gate.to_core()
    mixer_grad(0, 1)
    lower_gate.to_quad()
    in_weights(0, r.mine_3, 0)
    lower_in.to_core()
    layer_rows(0)
    late_sum.start()
    upper_in.to_groups()
    lower_in.to_quad()
    late_sum.turn()
    mixed_rows(0)
    mixed_rows(1)
    upper_gate.to_sections()
    lower_gate.to_groups()
    lower_in.to_groups()
    upper_in.to_sections()
    lower_gate.to_sections()
    lower_in.to_sections()
    upper_gate.to_sibling()
    upper_in.to_sibling()

    late = late_sum.total()
    r.late[section] = late
    to_sections = [
        pltpu.make_async_remote_copy(
            src_ref=r.late.at[section],
            dst_ref=r.late.at[section],
            send_sem=r.late_send.at[step],
            recv_sem=r.late_recv.at[step],
            device_id=(lax.rem(section + step, cfg.sections), dp),
            device_id_type=MESH,
        )
        for step in range(1, cfg.sections)
    ]
    for copy in to_sections:
        copy.start()
    own_gain = r.gain[0:1, own_columns]
    for m in range(2):
        count = counts[m][:, 0:128]
        first = own_gain * late[2 * m : 2 * m + 1, :] / count
        second = own_gain * late[2 * m + 1 : 2 * m + 2, :] / count
        r.rows[m : m + 1, :] = norm0[m][1]
        inv = r.rows[m : m + 1, own_columns]

        def token_grad(t, carry, m=m, first=first, second=second, inv=inv):
            at = pl.ds(t * chunk, chunk)
            grad_normed = r.grad_scaled[0, m, at, own_columns] * own_gain
            normed = r.normed[0, m, at, own_columns]
            grad_stream = inv * (grad_normed - r.valid[m, at, :] * (first + normed * second))
            grad = r.grad_second[m, at, own_columns].astype(F32) + grad_stream
            high = grad.astype(BF16)
            r.narrow[at, :] = high
            r.narrow_rest[at, :] = (grad - high.astype(F32)).astype(BF16)
            return carry

        sweep(rows // chunk, token_grad, 0)
        r.token_grad[m] = matmul(r.gather[...], r.narrow[...]) + matmul(
            r.gather[...], r.narrow_rest[...]
        )
    r.upper_norm[...] = upper_total[0] + upper_total[1]
    for copy in to_sections:
        copy.wait()
    lower_gate.to_sibling()
    lower_in.to_sibling()
    for batch in batches:
        batch.end()


def lay_out_kernel(cfg, *refs):
    full = refs[0:4]
    late, upper_norm, mixed, token_grad = refs[4:8]
    (
        mixed_out,
        token_grad_out,
        gain_out,
        bias_out,
        decay_out,
        freq_out,
        step_out,
        in_out,
        out_out,
        skip_out,
        gate_out,
        gbias_out,
    ) = refs[8:20]
    in_held, out_held, gate_held = refs[20:23]
    rows_held, sems = refs[23:30], refs[30]
    width, states, half = cfg.width, cfg.states, cfg.half
    tall = states // (2 * QUAD)
    copies = []

    def send(held, out):
        copies.append(pltpu.make_async_copy(held, out, sems.at[len(copies)]))
        copies[-1].start()

    send(mixed, mixed_out)
    send(token_grad, token_grad_out)
    def columns(at):
        return jnp.concatenate([late[s, at : at + 1, :] for s in range(cfg.sections)], axis=1)

    row_outs = (bias_out, gain_out, skip_out, gbias_out, decay_out, freq_out, step_out)
    values = [
        (columns(0) + columns(2), unfold(upper_norm, 0, 4)),
        (columns(1) + columns(3), unfold(upper_norm, 4, 4)),
        (columns(4), columns(6)),
        (columns(5), columns(7)),
    ]
    for k in range(3):
        places = [(6 * l + 2 * k + part) for l in range(2) for part in range(2)]
        row = [late[p // LATE_STATES, 8 + p % LATE_STATES, :][None] for p in places]
        values.append([jnp.concatenate(row[2 * l : 2 * l + 2], axis=1)[:, 0:half] for l in range(2)])
    for held, out, value in zip(rows_held, row_outs, values):
        for l in range(2):
            held[l : l + 1, :] = value[l]
        send(held, out)

    places = [(s, c, z) for s in range(cfg.sections) for c in range(2) for z in range(QUAD)]
    for l in (1, 0):
        gates, ins = full[2 - 2 * l], full[3 - 2 * l]
        for s, c, z in places:
            at = s * 128 + (c * QUAD + z) * 16
            gate_held[l, at : at + 16, :] = gates[c, s, z, :, 0:width].astype(F32)
        send(gate_held.at[l], gate_out.at[l])
        for s, c, z in places:
            for k in range(tall // 16):
                first = (c * QUAD + z) * tall + 16 * k
                out_held[l, first : first + 16, s * 128 : (s + 1) * 128] = gates[
                    c, s, z, :, width + k * 128 : width + (k + 1) * 128
                ].astype(F32)
        send(out_held.at[l], out_out.at[l])
        for s, c, z in places:
            at = s * 128 + (c * QUAD + z) * 16
            in_held[l, at : at + 16, :] = ins[c, s, z].astype(F32)
        send(in_held.at[l], in_out.at[l])
    for copy in copies:
        copy.wait()


INPUTS = tuple(
    dict(tokens=0, lengths=0, out_grad_far=0, gain=0, bias=0, decay=0, freq=0, lstep=0, b_in_far=0, c_out_far=0, skip=0, gmat_far=0, gbias=0)
)


def per_device(cfg, *args):
    rows, width, states, lanes = cfg.rows, cfg.width, cfg.states, cfg.lanes
    sections, dp, chips = cfg.sections, cfg.dp, cfg.dp // 2
    groups = chips // QUAD
    steps = rows // SUB
    vmem, dma = pltpu.VMEM, pltpu.SemaphoreType.DMA
    widths = (width + states, states) * 2
    outs = {f"full_{k}": ((2, sections, QUAD, 16, w), BF16) for k, w in enumerate(widths)}
    outs.update(
        late=((sections, 16, 128), F32), upper_norm=((8, 128), F32), mixed=((2, rows, 128), BF16), token_grad=((2, rows, 128), F32)
    )
    scratch = dict(
        sum_own=vmem((len(SUM_ROWS), 24, 128), F32),
        sum_sibling=vmem((len(SUM_ROWS), 24, 128), F32),
        sum_slots=vmem((len(SUM_ROWS), min(dp, max(chips, 8)), 24, 128), F32),
        late_own=vmem((sections, 16, 128), F32),
        late_send=dma((sections,)),
        late_recv=dma((sections,)),
        sum_send=dma((len(SUM_ROWS), max(chips, 8))),
        sum_recv=dma((len(SUM_ROWS), max(chips, 8))),
        grad_send=dma((4, (2 + sections) * QUAD + groups)),
        grad_recv=dma((4, (2 + sections) * QUAD + groups)),
        fetch_sem=dma((4,)),
        b_in=vmem((2, width, states), BF16),
        c_out=vmem((2, states, width), BF16),
        gmat=vmem((2, width, width), BF16),
        out_grad=vmem((2, rows, width), BF16),
        widen=vmem((states, 2 * lanes), BF16),
        q=vmem((2, rows, 2 * lanes), F32),
        spread=vmem((rows, rows), BF16),
        gather=vmem((rows, rows), BF16),
        first_in=vmem((2, rows, width), BF16),
        out_grads=vmem((2, rows, width), BF16),
        second_in=vmem((2, rows, width), F32),
        grad_second=vmem((2, rows, width), BF16),
        valid=vmem((2, rows, 128), F32),
        keep_start=vmem((2, rows, 128), F32),
        keep_end=vmem((2, rows, 128), F32),
        par=vmem((SUB, lanes), F32),
        b_pad=vmem((2, width, 2 * lanes), BF16),
        c_pad=vmem((2, 2 * lanes, width), BF16),
        normed=vmem((2, 2, rows, width), F32),
        scaled=vmem((2, 2 * rows, width), BF16),
        drive=vmem((2, 2, rows, 2 * lanes), F32),
        state=vmem((2, 2, (steps + 1) * SUB, 2 * lanes), F32),
        joined=vmem((2, 2 * rows, 2 * lanes), BF16),
        work=vmem((rows, width), F32),
        active=vmem((2, 2, rows, width), F32),
        active_low=vmem((2, 2 * rows, width), BF16),
        slope=vmem((2, 2, rows, width), F32),
        sig=vmem((2, 2, rows, width), F32),
        through=vmem((rows, width), F32),
        grad_logits=vmem((2, 2 * rows, width), BF16),
        branch=vmem((2, 2 * rows, width), BF16),
        grad_drive=vmem((2, 2 * rows, states), BF16),
        grad_scaled=vmem((2, 2, rows, width), F32),
        state_sums=vmem((2, 2, 4, SUB, lanes), F32),
        narrow=vmem((rows, 128), BF16),
        narrow_rest=vmem((rows, 128), BF16),
        rows=vmem((SUB, width), F32),
    )
    for k, w in enumerate(widths):
        blocks = (2, QUAD), (QUAD,), (QUAD,), (QUAD,), (groups,)
        for part, block in zip(STAGES, blocks):
            scratch[f"{part}_{k}"] = vmem((*block, 16, w), BF16)
    in_vmem = pl.BlockSpec(memory_space=pltpu.VMEM)
    in_smem = pl.BlockSpec(memory_space=pltpu.SMEM)
    in_hbm = pl.BlockSpec(memory_space=pltpu.HBM)
    names = INPUTS + tuple(outs) + tuple(scratch)
    made = pl.pallas_call(
        partial(main_kernel, cfg, names),
        name="layers",
        out_shape=[vmem(*spec) for spec in outs.values()],
        in_specs=[
            in_smem if name == "lengths" else in_hbm if name.endswith("_far") else in_vmem
            for name in INPUTS
        ],
        out_specs=[in_vmem for name in outs],
        scratch_shapes=list(scratch.values()),
        compiler_params=pltpu.CompilerParams(
            collective_id=0, has_side_effects=True, vmem_limit_bytes=56 * 2**20
        ),
    )(*args)
    shapes = [
        ((2, rows, 128), BF16),
        ((2, rows, 128), F32),
        ((2, width), F32),
        ((2, width), F32),
        ((2, states // 2), F32),
        ((2, states // 2), F32),
        ((2, states // 2), F32),
        ((2, width, states), F32),
        ((2, states, width), F32),
        ((2, width), F32),
        ((2, width, width), F32),
        ((2, width), F32),
    ]
    by_copy = (7, 8, 10)
    return pl.pallas_call(
        partial(lay_out_kernel, cfg),
        name="lay_out",
        out_shape=[jax.ShapeDtypeStruct(*spec) for spec in shapes],
        in_specs=[in_vmem] * 8,
        out_specs=[in_hbm] * 12,
        scratch_shapes=[vmem(*shapes[k]) for k in by_copy]
        + [vmem((2, width), F32)] * 4
        + [vmem((2, states // 2), F32)] * 3
        + [dma((15,))],
        compiler_params=pltpu.CompilerParams(vmem_limit_bytes=24 * 2**20),
    )(*made)


def solution(mesh):
    sections, dp = mesh.shape["section"], mesh.shape["dp"]

    def run(*args):
        _, rows, width = args[0].shape
        states = args[8].shape[2]
        cfg = SimpleNamespace(
            rows=rows // dp,
            width=width,
            states=states,
            half=states // 2,
            lanes=-(-states // 256) * 128,
            sections=sections,
            dp=dp,
        )
        split = P(None, "dp", None)
        shared = P()
        placed = P(None, "dp", "section")
        return jax.shard_map(
            partial(per_device, cfg),
            mesh=mesh,
            in_specs=(split, P(None, "dp"), split) + (shared,) * 10,
            out_specs=(placed, placed) + (shared,) * 10,
            check_vma=False,
        )(*args)

    return run
```

```python
from functools import partial
from types import SimpleNamespace

import jax
import jax.numpy as jnp
from jax import lax
from jax.experimental import pallas as pl
from jax.experimental.pallas import tpu as pltpu
from jax.sharding import PartitionSpec as P

epsilon = 1e-05
MESH = pl.DeviceIdType.MESH
F32 = jnp.float32
BF16 = jnp.bfloat16
SUB = 8
QUAD = 4
LATE_STATES = 3
SUM_ROWS = (24, 8, 8, 8, 8, 16)


STAGES = tuple(dict(mine=0, theirs=0, chip=0, quad=0, group=0, full=0))


def matmul(left, right):
    return jnp.dot(left, right, preferred_element_type=F32)


def matmul_nt(left, right):
    return lax.dot_general(left, right, (((1,), (1,)), ((), ())), preferred_element_type=F32)


def matmul_tn(left, right):
    return lax.dot_general(left, right, (((0,), (0,)), ((), ())), preferred_element_type=F32)


def cmul(ar, ai, br, bi):
    return ar * br - ai * bi, ar * bi + ai * br


def sweep(count, body, carry):
    for t in range(count):
        carry = body(t, carry)
    return carry


def repeat_lanes(x, times):
    return jnp.concatenate([x] * times, axis=1)


def fold_rows(x):
    return jnp.sum(x.reshape(x.shape[0] // SUB, SUB, x.shape[1]), axis=0)


def unfold(total, first, count):
    return jnp.concatenate([total[first + k : first + k + 1, :] for k in range(count)], axis=1)


def landed(block, sem):
    pltpu.make_async_copy(block, block, sem).wait()


def remote(src, dst, send_sem, recv_sem, device):
    pltpu.make_async_remote_copy(
        src_ref=src,
        dst_ref=dst,
        send_sem=send_sem,
        recv_sem=recv_sem,
        device_id=device,
        device_id_type=MESH,
    ).start()


class SmallSum:
    def __init__(self, place, direct, own, sibling, slots, send_sems, recv_sems):
        self.place, self.direct = place, direct
        self.own, self.sibling, self.slots = own, sibling, slots
        self.send_sems, self.recv_sems = send_sems, recv_sems

    def to_all(self, slot, members, peer):
        self.members = members
        block = self.slots.at[slot]
        for step in range(1, members):
            to = (self.place.section, peer(step))
            remote(block, block, self.send_sems.at[1], self.recv_sems.at[1], to)

    def start(self):
        at = self.place
        if self.direct:
            self.slots[at.dp] = self.own[...]
            self.to_all(at.dp, at.devices, at.dp_peer)
        else:
            to = (at.section, at.sibling)
            remote(self.own, self.sibling, self.send_sems.at[0], self.recv_sems.at[0], to)

    def turn(self):
        at = self.place
        if not self.direct:
            landed(self.sibling, self.recv_sems.at[0])
            self.slots[at.chip] = self.own[...] + self.sibling[...]
            self.to_all(at.chip, at.chips, at.chip_peer)

    def total(self):
        landed(self.slots.at[0 : self.members - 1], self.recv_sems.at[1])
        result = self.slots[0]
        for member in range(1, self.members):
            result = result + self.slots[member]
        return result

    def end(self):
        if not self.direct:
            landed(self.own, self.send_sems.at[0])
        landed(self.slots.at[0 : self.members - 1], self.send_sems.at[1])


class GradSum:
    def __init__(self, place, refs, send_sems, recv_sems):
        self.place = place
        self.mine, self.theirs, self.chip_part, self.quad_in, self.group_in, self.full = refs
        self.send_sems, self.recv_sems = send_sems, recv_sems

    def send(self, src, dst, send, recv, device):
        remote(src, dst, self.send_sems.at[send], self.recv_sems.at[recv], device)

    def to_core(self):
        at = self.place
        self.send(self.mine.at[1 - at.core], self.theirs, 0, 0, (at.section, at.sibling))

    def to_quad(self):
        at = self.place
        landed(self.theirs, self.recv_sems.at[0])
        for part in range(QUAD):
            both = self.mine[at.core, part].astype(F32) + self.theirs[part].astype(F32)
            self.chip_part[part] = both.astype(BF16)
        for step in range(1, QUAD):
            other = lax.rem(at.quad + step, QUAD)
            to = (at.section, at.quad_peer(step))
            self.send(self.chip_part.at[other], self.quad_in.at[at.quad], 1, 1, to)
        self.quad_in[at.quad] = self.chip_part[at.quad]

    def to_groups(self):
        at = self.place
        landed(self.quad_in.at[0 : QUAD - 1], self.recv_sems.at[1])
        total = self.quad_in[0].astype(F32)
        for part in range(1, QUAD):
            total = total + self.quad_in[part].astype(F32)
        if at.groups > 1:
            mine = self.group_in.at[at.group]
            mine[...] = total.astype(BF16)
            for step in range(1, at.groups):
                self.send(mine, mine, 5, 9, (at.section, at.chip_peer(step * QUAD)))
            landed(self.group_in.at[0 : at.groups - 1], self.recv_sems.at[9])
            total = self.group_in[0].astype(F32)
            for other in range(1, at.groups):
                total = total + self.group_in[other].astype(F32)
        piece = self.full.at[at.core, at.section, at.quad]
        piece[...] = total.astype(BF16)
        for step in range(1, QUAD):
            self.send(piece, piece, 2, 1 + step, (at.section, at.quad_peer(step)))
        self.over_sections(at.quad)

    def over_sections(self, quad):
        at = self.place
        piece = self.full.at[at.core, at.section, quad]
        for step in range(1, at.sections):
            to = (lax.rem(at.section + step, at.sections), at.dp)
            self.send(piece, piece, 3, 4 + step, to)

    def to_sections(self):
        at = self.place
        for step in range(1, QUAD):
            other = lax.rem(at.quad + QUAD - step, QUAD)
            landed(self.full.at[at.core, at.section, other], self.recv_sems.at[1 + step])
            self.over_sections(other)
        piece = self.full.at[at.core, at.section]
        self.send(piece, piece, 4, 8, (at.section, at.sibling))

    def to_sibling(self):
        at = self.place
        for step in range(1, at.sections):
            other = lax.rem(at.section + at.sections - step, at.sections)
            piece = self.full.at[at.core, other]
            landed(piece, self.recv_sems.at[4 + step])
            self.send(piece, piece, 4, 8, (at.section, at.sibling))

    def end(self):
        at = self.place
        landed(self.full.at[1 - at.core], self.recv_sems.at[8])
        landed(self.theirs, self.send_sems.at[0])
        landed(self.quad_in.at[0 : QUAD - 1], self.send_sems.at[1])
        landed(self.quad_in.at[0 : QUAD - 1], self.send_sems.at[2])
        landed(self.full.at[at.core, 0 : at.sections - 1], self.send_sems.at[3])
        landed(self.full.at[at.core], self.send_sems.at[4])
        if at.groups > 1:
            landed(self.group_in.at[0 : at.groups - 1], self.send_sems.at[5])


def main_kernel(cfg, names, *refs):
    r = SimpleNamespace(**dict(zip(names, refs)))
    rows, width, states, half, lanes = (
        cfg.rows,
        cfg.width,
        cfg.states,
        cfg.half,
        cfg.lanes,
    )
    steps = rows // SUB
    section = lax.axis_index("section")
    dp = lax.axis_index("dp")
    chips = cfg.dp // 2
    core, chip = lax.rem(dp, 2), lax.div(dp, 2)
    quad, group = lax.rem(chip, QUAD), lax.div(chip, QUAD)
    place = SimpleNamespace(
        section=section,
        sections=cfg.sections,
        dp=dp,
        core=core,
        chip=chip,
        chips=chips,
        quad=quad,
        group=group,
        groups=chips // QUAD,
        devices=cfg.dp,
        dp_peer=lambda step: lax.rem(dp + step, cfg.dp),
        sibling=dp + 1 - 2 * core,
        chip_peer=lambda step: lax.rem(chip + step, chips) * 2 + core,
        quad_peer=lambda step: (group * QUAD + lax.rem(quad + step, QUAD)) * 2 + core,
    )

    direct = cfg.dp <= 8
    if direct:
        peers = [(section, place.dp_peer(step)) for step in range(1, cfg.dp)]
    else:
        peers = [(section, place.sibling)]
        peers += [(section, place.chip_peer(step)) for step in range(1, chips)]
    peers += [(lax.rem(section + step, cfg.sections), dp) for step in range(1, cfg.sections)]
    barrier = pltpu.get_barrier_semaphore()
    for peer in peers:
        pl.semaphore_signal(barrier, inc=1, device_id=peer, device_id_type=MESH)

    small = [
        SmallSum(
            place,
            direct and k < len(SUM_ROWS) - 1,
            r.sum_own.at[k, 0:tall] if k < len(SUM_ROWS) - 1 else r.late_own.at[section],
            r.sum_sibling.at[k, 0:tall],
            r.sum_slots.at[k, :, 0:tall],
            r.sum_send.at[k],
            r.sum_recv.at[k],
        )
        for k, tall in enumerate(SUM_ROWS)
    ]
    first_sum = small[0]
    mid_sum = [small[1], small[2]]
    upper_sum = [small[3], small[4]]
    late_sum = small[5]
    batches = [
        GradSum(
            place,
            [getattr(r, f"{part}_{k}") for part in STAGES],
            r.grad_send.at[k],
            r.grad_recv.at[k],
        )
        for k in range(5)
    ]
    upper_gate, upper_in, lower_gate, lower_out, lower_in = batches

    fetched = []
    for k, (held, given) in enumerate(
        (
            (r.b_in, r.b_in_far),
            (r.out_grad, r.out_grad_far),
            (r.c_out, r.c_out_far),
            (r.gmat, r.gmat_far),
        )
    ):
        fetched.append(pltpu.make_async_copy(given, held, r.fetch_sem.at[k]))
        fetched[k].start()

    first_len = [r.lengths[m, 0] for m in range(2)]
    total_len = [r.lengths[m, 0] + r.lengths[m, 1] for m in range(2)]

    def put(index, at, row):
        for k in range(row.shape[1] // 128):
            r.sum_own[index, at + k : at + k + 1, :] = row[:, k * 128 : (k + 1) * 128]

    def put_late(at, row):
        for k in range(cfg.sections):
            r.late_own[k, at : at + 1, :] = row[:, k * 128 : (k + 1) * 128]

    chunk = 32
    for m in range(2):

        def token_sums(t, carry, m=m):
            at = pl.ds(t * chunk, chunk)
            v = r.tokens[m, at, :].astype(F32)
            place_row = t * chunk + lax.broadcasted_iota(jnp.int32, (chunk, width), 0)
            kept = jnp.where(place_row < total_len[m], v, 0.0)
            return carry[0] + fold_rows(kept), carry[1] + fold_rows(kept * v)

        zero = jnp.zeros((SUB, width), F32)
        sums, squares = sweep(rows // chunk, token_sums, (zero, zero))
        put(0, 8 * m, jnp.sum(sums, axis=0, keepdims=True))
        put(0, 8 * m + 4, jnp.sum(squares, axis=0, keepdims=True))
        count = jnp.minimum(total_len[m], rows).astype(F32)
        r.sum_own[0, 16 + m : 17 + m, :] = jnp.full((1, 128), count, F32)

    pl.semaphore_wait(barrier, len(peers))
    first_sum.start()

    at_i = lax.broadcasted_iota(jnp.int32, (rows, rows), 0)
    at_r = lax.broadcasted_iota(jnp.int32, (rows, rows), 1)
    r.spread[...] = jnp.where(
        at_r == (at_i % SUB) * steps + at_i // SUB, 1.0, 0.0
    ).astype(BF16)
    r.gather[...] = jnp.where(
        at_i == (at_r % SUB) * steps + at_r // SUB, 1.0, 0.0
    ).astype(BF16)
    for m in range(2):
        r.first_in[m] = matmul(r.spread[...], r.tokens[m]).astype(BF16)
    first_sum.turn()
    fetched[1].wait()
    for m in range(2):
        r.out_grads[m] = matmul(r.spread[...], r.out_grad[m]).astype(BF16)
    held = lax.broadcasted_iota(jnp.int32, (rows, 128), 0)
    held = (held % SUB) * steps + held // SUB
    all_start, all_end = [], []
    for m in range(2):
        one, zero = jnp.float32(1.0), jnp.float32(0.0)
        past = held >= total_len[m]
        starts = (held == 0) | (held == first_len[m]) | past
        ends = (held == first_len[m] - 1) | (held == total_len[m] - 1) | past | (held == rows - 1)
        r.valid[m] = jnp.where(past, zero, one)
        r.keep_start[m] = jnp.where(starts, zero, one)
        r.keep_end[m] = jnp.where(ends, zero, one)
        for kept, mask in ((all_start, r.keep_start), (all_end, r.keep_end)):
            kept.append(jnp.min(mask[m].reshape(steps, SUB, 128), axis=0))

    r.par[...] = jnp.zeros((SUB, lanes), F32)
    r.par[0:2, :] = jnp.ones((2, lanes), F32)
    r.par[0:2, 0:half] = r.decay[...]
    r.par[2:4, 0:half] = r.freq[...]
    r.par[4:6, 0:half] = r.lstep[...]
    decay, spin = r.par[0:2, :], r.par[2:4, :]
    step_size = jnp.exp(r.par[4:6, :])
    damping = jnp.exp(-decay * step_size)
    bar_re = damping * jnp.cos(spin * step_size)
    bar_im = damping * jnp.sin(spin * step_size)
    modulus = decay * decay + spin * spin
    fac_re = ((bar_re - 1.0) * -decay + bar_im * spin) / modulus
    fac_im = (bar_im * -decay - (bar_re - 1.0) * spin) / modulus
    pow_re, pow_im = bar_re, bar_im
    power = 1
    while power < steps:
        pow_re, pow_im = cmul(pow_re, pow_im, pow_re, pow_im)
        power *= 2

    lane = lax.broadcasted_iota(jnp.int32, (1, 128), 1)
    low_lanes = lane < half - 128
    turn_by = half - 128

    from_column = lax.broadcasted_iota(jnp.int32, (states, 2 * lanes), 0)
    to_column = lax.broadcasted_iota(jnp.int32, (states, 2 * lanes), 1)
    moved_to = jnp.where(from_column < half, from_column, from_column + (lanes - half))
    r.widen[...] = jnp.where(to_column == moved_to, 1.0, 0.0).astype(BF16)
    for k in (0, 2, 3):
        fetched[k].wait()
    for l in range(2):
        r.b_pad[l] = matmul(r.b_in[l], r.widen[...]).astype(BF16)
        blank = jnp.zeros((lanes - half, width), BF16)
        r.c_pad[l, 0:half, :] = r.c_out[l, 0:half, :]
        r.c_pad[l, half:lanes, :] = blank
        r.c_pad[l, lanes : lanes + half, :] = r.c_out[l, half:states, :]
        r.c_pad[l, lanes + half : 2 * lanes, :] = blank

    def across(end, coef, reverse):
        end_re, end_im = end
        coef_re, coef_im = coef
        sub = lax.broadcasted_iota(jnp.int32, (SUB, lanes), 0)
        for by in (1, 2, 4):
            turn = SUB - by if reverse else by
            live = sub < SUB - by if reverse else sub >= by

            def moved(x):
                return jnp.where(live, pltpu.roll(x, turn, 0), 0.0)

            add_re, add_im = cmul(coef_re, coef_im, moved(end_re), moved(end_im))
            coef_re, coef_im = cmul(coef_re, coef_im, moved(coef_re), moved(coef_im))
            end_re, end_im = end_re + add_re, end_im + add_im
        turn = SUB - 1 if reverse else 1
        live = sub < SUB - 1 if reverse else sub >= 1
        return tuple(jnp.where(live, pltpu.roll(x, turn, 0), 0.0) for x in (end_re, end_im))

    def wide8(x, l):
        return jnp.broadcast_to(x[l : l + 1, :], (SUB, x.shape[1]))

    def group_rows(p):
        return pl.ds(p * SUB, SUB)

    def scan_coefs(l, m, reverse):
        keep = r.keep_end if reverse else r.keep_start
        all_kept = repeat_lanes((all_end if reverse else all_start)[m], lanes // 128)
        product = (all_kept * wide8(pow_re, l), all_kept * wide8(pow_im, l))
        return keep, wide8(bar_re, l), wide8(bar_im, l), product

    def advance(keep, m, at, br, bi, re, im, src_re, src_im):
        k = repeat_lanes(keep[m, at, :], lanes // 128)
        kr, ki = k * br, k * bi
        return kr * re - ki * im + src_re, kr * im + ki * re + src_im

    def scan_states(l, m):
        reverse = l == 1
        lead = 0 if reverse else 1
        keep, br, bi, product = scan_coefs(l, m, reverse)
        fr, fi = wide8(fac_re, l), wide8(fac_im, l)
        zero = jnp.zeros((SUB, lanes), F32)

        def ends(t, carry):
            p = steps - 1 - t if reverse else t
            at = group_rows(p)
            v = repeat_lanes(r.valid[m, at, :], lanes // 128)
            drive_re = r.drive[l, m, at, 0:lanes]
            drive_im = r.drive[l, m, at, lanes : 2 * lanes]
            src_re, src_im = cmul(fr, fi, v * drive_re, v * drive_im)
            r.state[l, m, group_rows(p + lead), 0:lanes] = src_re
            r.state[l, m, group_rows(p + lead), lanes : 2 * lanes] = src_im
            return advance(keep, m, at, br, bi, *carry, src_re, src_im)

        end = sweep(steps, ends, (zero, zero))
        enter = across(end, product, reverse)
        first = steps if reverse else 0
        r.state[l, m, first * SUB : (first + 1) * SUB, 0:lanes] = enter[0]
        r.state[l, m, first * SUB : (first + 1) * SUB, lanes : 2 * lanes] = enter[1]

        def fill(t, carry):
            done = []
            for k in range(2):
                p = steps - 1 - (2 * t + k) if reverse else 2 * t + k
                at, to = group_rows(p), group_rows(p + lead)
                src_re = r.state[l, m, to, 0:lanes]
                src_im = r.state[l, m, to, lanes : 2 * lanes]
                carry = advance(keep, m, at, br, bi, *carry, src_re, src_im)
                r.state[l, m, to, 0:lanes] = carry[0]
                r.state[l, m, to, lanes : 2 * lanes] = carry[1]
                done.append(jnp.concatenate([carry[0], -carry[1]], axis=1))
            pair = steps // 2 - 1 - t if reverse else t
            both = jnp.concatenate(done[::-1] if reverse else done, axis=0)
            to = pl.ds(m * rows + pair * 16, 16)
            r.joined[l, to, :] = both.astype(BF16)
            return carry

        sweep(steps // 2, fill, enter)

    def scan_grads(l, m):
        reverse = l == 0
        back = 1 if l == 1 else 0
        keep, br, bi, product = scan_coefs(l, m, reverse)
        keep_state = r.keep_start if l == 0 else r.keep_end
        fr, fi = 2.0 * wide8(fac_re, l), 2.0 * wide8(fac_im, l)
        zero = jnp.zeros((SUB, lanes), F32)

        def ends(t, carry):
            p = steps - 1 - t if reverse else t
            at = group_rows(p)
            q_re = r.q[m, at, 0:lanes]
            q_im = r.q[m, at, lanes : 2 * lanes]
            return advance(keep, m, at, br, bi, *carry, q_re, q_im)

        end = sweep(steps, ends, (zero, zero))
        enter = across(end, product, reverse)

        def fill(t, carry):
            w, bar_sum, fac_sum = carry
            done = []
            for k in range(2):
                p = steps - 1 - (2 * t + k) if reverse else 2 * t + k
                at, near = group_rows(p), group_rows(p + back)
                q_re = r.q[m, at, 0:lanes]
                q_im = r.q[m, at, lanes : 2 * lanes]
                w = advance(keep, m, at, br, bi, *w, q_re, q_im)
                kept = repeat_lanes(keep_state[m, at, :], lanes // 128)
                near_re = kept * r.state[l, m, near, 0:lanes]
                near_im = kept * r.state[l, m, near, lanes : 2 * lanes]
                term = cmul(*w, near_re, near_im)
                bar_sum = (bar_sum[0] + term[0], bar_sum[1] + term[1])
                v = repeat_lanes(r.valid[m, at, :], lanes // 128)
                vw = (v * w[0], v * w[1])
                drive_re = r.drive[l, m, at, 0:lanes]
                drive_im = r.drive[l, m, at, lanes : 2 * lanes]
                term = cmul(*vw, drive_re, drive_im)
                fac_sum = (fac_sum[0] + term[0], fac_sum[1] + term[1])
                gd_re, gd_im = cmul(fr, fi, *vw)
                im_low = pltpu.roll(-gd_im[:, 0:128], 64, 1)
                im_high = pltpu.roll(-gd_im[:, 128:256], 64, 1)
                done.append(
                    jnp.concatenate(
                        [
                            gd_re[:, 0:128],
                            jnp.where(low_lanes, gd_re[:, 128:256], im_low),
                            jnp.where(low_lanes, im_low, im_high),
                        ],
                        axis=1,
                    )
                )
            pair = steps // 2 - 1 - t if reverse else t
            both = jnp.concatenate(done[::-1] if reverse else done, axis=0)
            to = pl.ds(m * rows + pair * 16, 16)
            r.grad_drive[l, to, :] = both.astype(BF16)
            return w, bar_sum, fac_sum

        none = (zero, zero)
        _, bar_sum, fac_sum = sweep(steps // 2, fill, (enter, none, none))
        for k, part in enumerate((*bar_sum, *fac_sum)):
            r.state_sums[l, m, k] = part

    def row_of(ref, l):
        return ref[l : l + 1, :]

    def micro_rows(m):
        return slice(m * rows, (m + 1) * rows)

    gelu_chunk = 16

    def mixer(l, m, center, inv, hook=None):
        gain, bias, skip = row_of(r.gain, l), row_of(r.bias, l), row_of(r.skip, l)

        def normalise(t, carry):
            at = pl.ds(t * chunk, chunk)
            if l == 0:
                v = r.first_in[m, at, :].astype(F32)
            else:
                v = r.second_in[m, at, :]
            normed = (v - center) * inv
            r.normed[l, m, at, :] = normed
            to = pl.ds(m * rows + t * chunk, chunk)
            r.scaled[l, to, :] = (normed * gain + bias).astype(BF16)
            return carry

        sweep(rows // chunk, normalise, 0)
        r.drive[l, m] = matmul(r.scaled[l, micro_rows(m), :], r.b_pad[l])
        scan_states(l, m)
        if hook is not None:
            hook()
        r.work[...] = matmul(r.joined[l, micro_rows(m), :], r.c_pad[l])

        def activate(t, carry):
            at = pl.ds(t * gelu_chunk, gelu_chunk)
            scaled = r.normed[l, m, at, :] * gain + bias
            y = (2.0 * r.work[at, :] + skip * scaled).astype(BF16).astype(F32)
            below = 0.5 + 0.5 * lax.erf(y * 0.7071067811865476)
            density = jnp.exp(-0.5 * y * y) * 0.3989422804014327
            active = y * below
            r.active[l, m, at, :] = active
            r.slope[l, m, at, :] = below + y * density
            to = pl.ds(m * rows + t * gelu_chunk, gelu_chunk)
            r.active_low[l, to, :] = active.astype(BF16)
            return carry

        sweep(rows // gelu_chunk, activate, 0)
        r.work[...] = matmul(r.active_low[l, micro_rows(m), :], r.gmat[l])

    def first_gate(m):
        gbias = row_of(r.gbias, 0)

        def gate(t, carry):
            at = pl.ds(t * gelu_chunk, gelu_chunk)
            opened = jax.nn.sigmoid(r.work[at, :] + gbias)
            r.sig[0, m, at, :] = opened
            v = repeat_lanes(r.valid[m, at, :], width // 128)
            gated = v * r.active[0, m, at, :] * opened
            second = r.first_in[m, at, :].astype(F32) + gated.astype(BF16).astype(F32)
            r.second_in[m, at, :] = second
            kept = v * second
            return carry[0] + fold_rows(kept), carry[1] + fold_rows(kept * second)

        zero = jnp.zeros((SUB, width), F32)
        sums, squares = sweep(rows // gelu_chunk, gate, (zero, zero))
        put(1 + m, 0, jnp.sum(sums, axis=0, keepdims=True))
        put(1 + m, 4, jnp.sum(squares, axis=0, keepdims=True))

    bias_sums = {}
    skip_sums = {}

    def gate_grad(l, m, grad_of):
        gbias = row_of(r.gbias, l)

        def gate(t, carry):
            at = pl.ds(t * gelu_chunk, gelu_chunk)
            if l == 1:
                opened = jax.nn.sigmoid(r.work[at, :] + gbias)
                r.sig[1, m, at, :] = opened
            else:
                opened = r.sig[0, m, at, :]
            v = repeat_lanes(r.valid[m, at, :], width // 128)
            masked = v * grad_of(at, v)
            through = masked * opened
            r.through[at, :] = through
            grad_logits = through * r.active[l, m, at, :] * (1.0 - opened)
            to = pl.ds(m * rows + t * gelu_chunk, gelu_chunk)
            r.grad_logits[l, to, :] = grad_logits.astype(BF16)
            return carry + fold_rows(grad_logits)

        zero = jnp.zeros((SUB, width), F32)
        bias_sums[l, m] = sweep(rows // gelu_chunk, gate, zero)

    def branch_grad(l, m):
        gain, bias = row_of(r.gain, l), row_of(r.bias, l)
        r.work[...] = matmul_nt(r.grad_logits[l, micro_rows(m), :], r.gmat[l])

        def branch(t, carry):
            at = pl.ds(t * chunk, chunk)
            grad_active = r.through[at, :] + r.work[at, :]
            g = (r.slope[l, m, at, :] * grad_active).astype(BF16)
            to = pl.ds(m * rows + t * chunk, chunk)
            r.branch[l, to, :] = g
            scaled = r.normed[l, m, at, :] * gain + bias
            return carry + fold_rows(g.astype(F32) * scaled)

        zero = jnp.zeros((SUB, width), F32)
        skip_sums[l, m] = sweep(rows // chunk, branch, zero)
        r.q[m] = matmul_nt(r.branch[l, micro_rows(m), :], r.c_pad[l])

    def mixer_grad(l, m, hook=None):
        skip = row_of(r.skip, l)
        scan_grads(l, m)
        if hook is not None:
            hook()
        r.work[...] = matmul_nt(r.grad_drive[l, micro_rows(m), :], r.b_in[l])

        def scaled_grad(t, carry):
            at = pl.ds(t * chunk, chunk)
            to = pl.ds(m * rows + t * chunk, chunk)
            grad = r.work[at, :] + skip * r.branch[l, to, :].astype(F32)
            r.grad_scaled[l, m, at, :] = grad
            normed = r.normed[l, m, at, :]
            return carry[0] + fold_rows(grad), carry[1] + fold_rows(grad * normed)

        zero = jnp.zeros((SUB, width), F32)
        sums, products = sweep(rows // chunk, scaled_grad, (zero, zero))
        sums = jnp.sum(sums, axis=0, keepdims=True)
        products = jnp.sum(products, axis=0, keepdims=True)
        if l == 1:
            put(3 + m, 0, sums)
            put(3 + m, 4, products)
        else:
            put_late(2 * m, sums)
            put_late(2 * m + 1, products)

    def moments(total, at, count):
        center = unfold(total, at, 4) / count
        return center, lax.rsqrt(unfold(total, at + 4, 4) / count - center * center + epsilon)

    own_columns = pl.ds(pl.multiple_of(section * 128, 128), 128)

    def gate_weights(l, ref):
        grad = matmul_tn(r.active_low[l, :, own_columns], r.grad_logits[l])
        ref[:, :, :, 0:width] = grad.astype(BF16).reshape(2, QUAD, 16, width)

    def out_weights(l, ref, at):
        grad = 2.0 * matmul_tn(r.joined[l], r.branch[l, :, own_columns])
        grad = jnp.concatenate([grad[0:half, :], grad[lanes : lanes + half, :]], axis=0)
        tall = states // (2 * QUAD)
        for k in range(tall // 16):
            for c in range(2):
                for z in range(QUAD):
                    first = (c * QUAD + z) * tall + 16 * k
                    ref[c, z, :, at + 128 * k : at + 128 * (k + 1)] = grad[
                        first : first + 16, :
                    ].astype(BF16)

    def in_weights(l, ref, at):
        grad = matmul_tn(r.scaled[l, :, own_columns], r.grad_drive[l])
        ref[:, :, :, at : at + states] = grad.astype(BF16).reshape(2, QUAD, 16, states)

    def layer_rows(l):
        def both(sums):
            return jnp.sum(sums[l, 0] + sums[l, 1], axis=0, keepdims=True)

        put_late(4 + 2 * l, both(skip_sums))
        put_late(5 + 2 * l, both(bias_sums))
        part = [
            jnp.sum(r.state_sums[l, 0, k] + r.state_sums[l, 1, k], axis=0, keepdims=True)
            for k in range(4)
        ]
        gb_re, gb_im = 2.0 * part[0], -2.0 * part[1]
        gf_re, gf_im = 2.0 * part[2], -2.0 * part[3]
        one = slice(l, l + 1)
        lam_re, lam_im, size = -decay[one], spin[one], step_size[one]
        b_re, b_im, f_re, f_im = bar_re[one], bar_im[one], fac_re[one], fac_im[one]
        top_re, top_im = size * b_re - f_re, size * b_im - f_im
        square = modulus[one]
        d_re = (top_re * lam_re + top_im * lam_im) / square
        d_im = (top_im * lam_re - top_re * lam_im) / square
        gl_re = size * (b_re * gb_re + b_im * gb_im) + (d_re * gf_re + d_im * gf_im)
        gl_im = size * (b_re * gb_im - b_im * gb_re) + (d_re * gf_im - d_im * gf_re)
        e_re, e_im = cmul(lam_re, lam_im, b_re, b_im)
        g_step = size * ((e_re * gb_re + e_im * gb_im) + (b_re * gf_re + b_im * gf_im))
        parts = [
            row[:, k : k + 128] for row in (-gl_re, gl_im, g_step) for k in range(0, lanes, 128)
        ]
        for k, row in enumerate(parts):
            k += l * len(parts)
            at = 8 + k % LATE_STATES
            r.late_own[k // LATE_STATES, at : at + 1, :] = row

    def mixed_rows(m):
        def mix(t, carry):
            at = pl.ds(t * chunk, chunk)
            gated = (
                r.valid[m, at, :]
                * r.active[1, m, at, own_columns]
                * r.sig[1, m, at, own_columns]
            )
            stream = r.second_in[m, at, own_columns].astype(BF16).astype(F32)
            r.narrow[at, :] = (stream + gated).astype(BF16)
            return carry

        sweep(rows // chunk, mix, 0)
        r.mixed[m] = matmul(r.gather[...], r.narrow[...]).astype(BF16)

    def stream_grad(l, m, total, count, inv):
        gain = row_of(r.gain, l)
        first = gain * unfold(total, 0, 4) / count
        second = gain * unfold(total, 4, 4) / count
        return gain, first, second, inv

    total0 = first_sum.total()
    counts = [repeat_lanes(total0[16 + m : 17 + m, :], width // 128) for m in range(2)]
    norm0 = [moments(total0, 8 * m, counts[m]) for m in range(2)]

    mixer(0, 0, *norm0[0])
    first_gate(0)
    mid_sum[0].start()
    mixer(0, 1, *norm0[1], hook=mid_sum[0].turn)
    first_gate(1)
    mid_sum[1].start()

    norm1 = [None, None]
    for m in range(2):
        norm1[m] = moments(mid_sum[m].total(), 0, counts[m])
        hook = mid_sum[1].turn if m == 0 else None
        mixer(1, m, *norm1[m], hook=hook)
        gate_grad(1, m, lambda at, v, m=m: r.out_grads[m, at, :].astype(F32))
        branch_grad(1, m)
        if m == 1:
            gate_weights(1, r.mine_0)
            out_weights(1, r.mine_0, width)
            upper_gate.to_core()
        mixer_grad(1, m)
        upper_sum[m].start()
        upper_sum[m].turn()

    in_weights(1, r.mine_1, 0)
    upper_in.to_core()
    upper_gate.to_quad()
    layer_rows(1)

    def second_grad(m, total):
        gain, first, second, inv = stream_grad(1, m, total, counts[m], norm1[m][1])

        def grad_of(at, v):
            grad_normed = r.grad_scaled[1, m, at, :] * gain
            normed = r.normed[1, m, at, :]
            grad_stream = inv * (grad_normed - v * (first + normed * second))
            out_grad = r.out_grads[m, at, :].astype(F32)
            grad = (out_grad + grad_stream.astype(BF16).astype(F32)).astype(BF16)
            r.grad_second[m, at, :] = grad
            return grad.astype(F32)

        return grad_of

    upper_total = [upper_sum[0].total()]
    gate_grad(0, 0, second_grad(0, upper_total[0]))
    upper_in.to_quad()
    branch_grad(0, 0)
    mixer_grad(0, 0)
    upper_total.append(upper_sum[1].total())
    gate_grad(0, 1, second_grad(1, upper_total[1]))
    gate_weights(0, r.mine_2)
    lower_gate.to_core()
    upper_gate.to_groups()
    branch_grad(0, 1)
    out_weights(0, r.mine_3, 0)
    lower_out.to_core()
    upper_in.to_groups()
    lower_gate.to_quad()
    mixer_grad(0, 1)
    lower_out.to_quad()
    in_weights(0, r.mine_4, 0)
    lower_in.to_core()
    layer_rows(0)
    late_sum.start()
    upper_gate.to_sections()
    lower_in.to_quad()
    late_sum.turn()
    mixed_rows(0)
    mixed_rows(1)
    lower_gate.to_groups()
    upper_in.to_sections()
    lower_out.to_groups()
    lower_in.to_groups()
    lower_gate.to_sections()
    upper_gate.to_sibling()
    upper_in.to_sibling()
    lower_out.to_sections()
    lower_in.to_sections()

    late = late_sum.total()
    r.late[section] = late
    block = r.late.at[section]
    for step in range(1, cfg.sections):
        to = (lax.rem(section + step, cfg.sections), dp)
        remote(block, block, r.late_sem.at[0], r.late_sem.at[1], to)
    own_gain = r.gain[0:1, own_columns]
    for m in range(2):
        count = counts[m][:, 0:128]
        first = own_gain * late[2 * m : 2 * m + 1, :] / count
        second = own_gain * late[2 * m + 1 : 2 * m + 2, :] / count
        r.rows[m : m + 1, :] = norm0[m][1]
        inv = r.rows[m : m + 1, own_columns]

        def token_grad(t, carry, m=m, first=first, second=second, inv=inv):
            at = pl.ds(t * chunk, chunk)
            grad_normed = r.grad_scaled[0, m, at, own_columns] * own_gain
            normed = r.normed[0, m, at, own_columns]
            grad_stream = inv * (grad_normed - r.valid[m, at, :] * (first + normed * second))
            grad = r.grad_second[m, at, own_columns].astype(F32) + grad_stream
            high = grad.astype(BF16)
            r.narrow[at, :] = high
            r.narrow_rest[at, :] = (grad - high.astype(F32)).astype(BF16)
            return carry

        sweep(rows // chunk, token_grad, 0)
        r.token_grad[m] = matmul(r.gather[...], r.narrow[...]) + matmul(
            r.gather[...], r.narrow_rest[...]
        )
    r.upper_norm[...] = upper_total[0] + upper_total[1]
    for k in range(2):
        landed(r.late.at[0 : cfg.sections - 1], r.late_sem.at[k])
    lower_gate.to_sibling()
    lower_out.to_sibling()
    lower_in.to_sibling()
    for batch in batches:
        batch.end()
    for each in small:
        each.end()


def lay_out_kernel(cfg, *refs):
    full = refs[0:5]
    late, upper_norm, mixed, token_grad = refs[5:9]
    (
        mixed_out,
        token_grad_out,
        gain_out,
        bias_out,
        decay_out,
        freq_out,
        step_out,
        in_out,
        out_out,
        skip_out,
        gate_out,
        gbias_out,
    ) = refs[9:21]
    in_held, out_held, gate_held = refs[21:24]
    rows_held, sems = refs[24:31], refs[31]
    width, states, half = cfg.width, cfg.states, cfg.half
    tall = states // (2 * QUAD)
    copies = []

    def send(held, out, sem=None):
        copy = pltpu.make_async_copy(held, out, sems.at[3 + len(copies) if sem is None else sem])
        copy.start()
        if sem is None:
            copies.append(copy)

    send(mixed, mixed_out)
    send(token_grad, token_grad_out)
    def columns(at):
        return jnp.concatenate([late[s, at : at + 1, :] for s in range(cfg.sections)], axis=1)

    row_outs = (bias_out, gain_out, skip_out, gbias_out, decay_out, freq_out, step_out)
    values = [
        (columns(0) + columns(2), unfold(upper_norm, 0, 4)),
        (columns(1) + columns(3), unfold(upper_norm, 4, 4)),
        (columns(4), columns(6)),
        (columns(5), columns(7)),
    ]
    for k in range(3):
        places = [(6 * l + 2 * k + part) for l in range(2) for part in range(2)]
        row = [late[p // LATE_STATES, 8 + p % LATE_STATES, :][None] for p in places]
        values.append([jnp.concatenate(row[2 * l : 2 * l + 2], axis=1)[:, 0:half] for l in range(2)])
    for held, out, value in zip(rows_held, row_outs, values):
        for l in range(2):
            held[l : l + 1, :] = value[l]
        send(held, out)

    for l in (1, 0):
        parts = ((full[0], 0), (full[0], width), (full[1], 0))
        if l == 0:
            parts = ((full[2], 0), (full[3], 0), (full[4], 0))
        for s in range(cfg.sections):
            mine = slice(s * 128, (s + 1) * 128)
            members = [(c, z) for c in range(2) for z in range(QUAD)]
            for (part, begin), held, out, wide, sem in (
                (parts[0], gate_held, gate_out, width, 0),
                (parts[2], in_held, in_out, states, 1),
            ):
                for c, z in members:
                    at = s * 128 + (c * QUAD + z) * 16
                    held[l, at : at + 16, :] = part[c, s, z, :, begin : begin + wide].astype(F32)
                send(held.at[l, mine], out.at[l, mine], sem)
            part, begin = parts[1]
            for c, z in members:
                for k in range(tall // 16):
                    first = (c * QUAD + z) * tall + 16 * k
                    out_held[l, first : first + 16, mine] = part[
                        c, s, z, :, begin + k * 128 : begin + (k + 1) * 128
                    ].astype(F32)
        send(out_held.at[l], out_out.at[l], 2)
    for copy in copies:
        copy.wait()
    for sem, out in enumerate((gate_out, in_out, out_out)):
        landed(out, sems.at[sem])


INPUTS = tuple(
    dict(tokens=0, lengths=0, out_grad_far=0, gain=0, bias=0, decay=0, freq=0, lstep=0, b_in_far=0, c_out_far=0, skip=0, gmat_far=0, gbias=0)
)


def per_device(cfg, *args):
    rows, width, states, lanes = cfg.rows, cfg.width, cfg.states, cfg.lanes
    sections, dp, chips = cfg.sections, cfg.dp, cfg.dp // 2
    groups = chips // QUAD
    steps = rows // SUB
    vmem, dma = pltpu.VMEM, pltpu.SemaphoreType.DMA
    widths = (width + states, states, width, states, states)
    outs = {f"full_{k}": ((2, sections, QUAD, 16, w), BF16) for k, w in enumerate(widths)}
    outs.update(
        late=((sections, 16, 128), F32), upper_norm=((8, 128), F32), mixed=((2, rows, 128), BF16), token_grad=((2, rows, 128), F32)
    )
    scratch = dict(
        sum_own=vmem((len(SUM_ROWS), 24, 128), F32),
        sum_sibling=vmem((len(SUM_ROWS), 24, 128), F32),
        sum_slots=vmem((len(SUM_ROWS), min(dp, max(chips, 8)), 24, 128), F32),
        late_own=vmem((sections, 16, 128), F32),
        late_sem=dma((2,)),
        sum_send=dma((len(SUM_ROWS), 2)),
        sum_recv=dma((len(SUM_ROWS), 2)),
        grad_send=dma((5, 5 + (groups > 1))),
        grad_recv=dma((5, 9 + (groups > 1))),
        fetch_sem=dma((4,)),
        b_in=vmem((2, width, states), BF16),
        c_out=vmem((2, states, width), BF16),
        gmat=vmem((2, width, width), BF16),
        out_grad=vmem((2, rows, width), BF16),
        widen=vmem((states, 2 * lanes), BF16),
        q=vmem((2, rows, 2 * lanes), F32),
        spread=vmem((rows, rows), BF16),
        gather=vmem((rows, rows), BF16),
        first_in=vmem((2, rows, width), BF16),
        out_grads=vmem((2, rows, width), BF16),
        second_in=vmem((2, rows, width), F32),
        grad_second=vmem((2, rows, width), BF16),
        valid=vmem((2, rows, 128), F32),
        keep_start=vmem((2, rows, 128), F32),
        keep_end=vmem((2, rows, 128), F32),
        par=vmem((SUB, lanes), F32),
        b_pad=vmem((2, width, 2 * lanes), BF16),
        c_pad=vmem((2, 2 * lanes, width), BF16),
        normed=vmem((2, 2, rows, width), F32),
        scaled=vmem((2, 2 * rows, width), BF16),
        drive=vmem((2, 2, rows, 2 * lanes), F32),
        state=vmem((2, 2, (steps + 1) * SUB, 2 * lanes), F32),
        joined=vmem((2, 2 * rows, 2 * lanes), BF16),
        work=vmem((rows, width), F32),
        active=vmem((2, 2, rows, width), F32),
        active_low=vmem((2, 2 * rows, width), BF16),
        slope=vmem((2, 2, rows, width), F32),
        sig=vmem((2, 2, rows, width), F32),
        through=vmem((rows, width), F32),
        grad_logits=vmem((2, 2 * rows, width), BF16),
        branch=vmem((2, 2 * rows, width), BF16),
        grad_drive=vmem((2, 2 * rows, states), BF16),
        grad_scaled=vmem((2, 2, rows, width), F32),
        state_sums=vmem((2, 2, 4, SUB, lanes), F32),
        narrow=vmem((rows, 128), BF16),
        narrow_rest=vmem((rows, 128), BF16),
        rows=vmem((SUB, width), F32),
    )
    for k, w in enumerate(widths):
        blocks = (2, QUAD), (QUAD,), (QUAD,), (QUAD,), (groups,)
        for part, block in zip(STAGES, blocks):
            scratch[f"{part}_{k}"] = vmem((*block, 16, w), BF16)
    in_vmem = pl.BlockSpec(memory_space=pltpu.VMEM)
    in_smem = pl.BlockSpec(memory_space=pltpu.SMEM)
    in_hbm = pl.BlockSpec(memory_space=pltpu.HBM)
    names = INPUTS + tuple(outs) + tuple(scratch)
    made = pl.pallas_call(
        partial(main_kernel, cfg, names),
        name="layers",
        out_shape=[vmem(*spec) for spec in outs.values()],
        in_specs=[
            in_smem if name == "lengths" else in_hbm if name.endswith("_far") else in_vmem
            for name in INPUTS
        ],
        out_specs=[in_vmem for name in outs],
        scratch_shapes=list(scratch.values()),
        compiler_params=pltpu.CompilerParams(
            collective_id=0, has_side_effects=True, vmem_limit_bytes=56 * 2**20
        ),
    )(*args)
    shapes = [
        ((2, rows, 128), BF16),
        ((2, rows, 128), F32),
        ((2, width), F32),
        ((2, width), F32),
        ((2, states // 2), F32),
        ((2, states // 2), F32),
        ((2, states // 2), F32),
        ((2, width, states), F32),
        ((2, states, width), F32),
        ((2, width), F32),
        ((2, width, width), F32),
        ((2, width), F32),
    ]
    by_copy = (7, 8, 10)
    return pl.pallas_call(
        partial(lay_out_kernel, cfg),
        name="lay_out",
        out_shape=[jax.ShapeDtypeStruct(*spec) for spec in shapes],
        in_specs=[in_vmem] * 9,
        out_specs=[in_hbm] * 12,
        scratch_shapes=[vmem(*shapes[k]) for k in by_copy]
        + [vmem((2, width), F32)] * 4
        + [vmem((2, states // 2), F32)] * 3
        + [dma((12,))],
        compiler_params=pltpu.CompilerParams(vmem_limit_bytes=24 * 2**20),
    )(*made)


def solution(mesh):
    sections, dp = mesh.shape["section"], mesh.shape["dp"]

    def run(*args):
        _, rows, width = args[0].shape
        states = args[8].shape[2]
        cfg = SimpleNamespace(
            rows=rows // dp,
            width=width,
            states=states,
            half=states // 2,
            lanes=-(-states // 256) * 128,
            sections=sections,
            dp=dp,
        )
        split = P(None, "dp", None)
        shared = P()
        placed = P(None, "dp", "section")
        return jax.shard_map(
            partial(per_device, cfg),
            mesh=mesh,
            in_specs=(split, P(None, "dp"), split) + (shared,) * 10,
            out_specs=(placed, placed) + (shared,) * 10,
            check_vma=False,
        )(*args)

    return run
```

```python
from functools import partial
from types import SimpleNamespace

import jax
import jax.numpy as jnp
from jax import lax
from jax.experimental import pallas as pl
from jax.experimental.pallas import tpu as pltpu
from jax.sharding import PartitionSpec as P

epsilon = 1e-05
MESH = pl.DeviceIdType.MESH
F32 = jnp.float32
BF16 = jnp.bfloat16
SUB = 8
QUAD = 4
LATE_STATES = 3
SUM_ROWS = (18, 8, 8, 8, 8, 16)


STAGES = tuple(dict(mine=0, theirs=0, chip=0, quad=0, group=0, full=0))


def matmul(left, right):
    return jnp.dot(left, right, preferred_element_type=F32)


def matmul_nt(left, right):
    return lax.dot_general(left, right, (((1,), (1,)), ((), ())), preferred_element_type=F32)


def matmul_tn(left, right):
    return lax.dot_general(left, right, (((0,), (0,)), ((), ())), preferred_element_type=F32)


def cmul(ar, ai, br, bi):
    return ar * br - ai * bi, ar * bi + ai * br


def sweep(count, body, carry):
    for t in range(count):
        carry = body(t, carry)
    return carry


def repeat_lanes(x, times):
    return jnp.concatenate([x] * times, axis=1)


def fold_rows(x):
    return jnp.sum(x.reshape(x.shape[0] // SUB, SUB, x.shape[1]), axis=0)


def unfold(total, first, count):
    return jnp.concatenate([total[first + k : first + k + 1, :] for k in range(count)], axis=1)


def landed(block, sem):
    pltpu.make_async_copy(block, block, sem).wait()


def remote(src, dst, send_sem, recv_sem, device):
    pltpu.make_async_remote_copy(
        src_ref=src,
        dst_ref=dst,
        send_sem=send_sem,
        recv_sem=recv_sem,
        device_id=device,
        device_id_type=MESH,
    ).start()


class SmallSum:
    def __init__(self, place, direct, own, sibling, slots, send_sems, recv_sems):
        self.place, self.direct = place, direct
        self.own, self.sibling, self.slots = own, sibling, slots
        self.send_sems, self.recv_sems = send_sems, recv_sems

    def to_all(self, slot, members, peer):
        self.members = members
        block = self.slots.at[slot]
        for step in range(1, members):
            to = (self.place.section, peer(step))
            remote(block, block, self.send_sems.at[1], self.recv_sems.at[1], to)

    def start(self):
        at = self.place
        if self.direct:
            self.slots[at.dp] = self.own[...]
            self.to_all(at.dp, at.devices, at.dp_peer)
        else:
            to = (at.section, at.sibling)
            remote(self.own, self.sibling, self.send_sems.at[0], self.recv_sems.at[0], to)

    def turn(self):
        at = self.place
        if not self.direct:
            landed(self.sibling, self.recv_sems.at[0])
            self.slots[at.chip] = self.own[...] + self.sibling[...]
            self.to_all(at.chip, at.chips, at.chip_peer)

    def total(self):
        landed(self.slots.at[0 : self.members - 1], self.recv_sems.at[1])
        result = self.slots[0]
        for member in range(1, self.members):
            result = result + self.slots[member]
        return result

    def end(self):
        if not self.direct:
            landed(self.own, self.send_sems.at[0])
        landed(self.slots.at[0 : self.members - 1], self.send_sems.at[1])


class GradSum:
    def __init__(self, place, refs, send_sems, recv_sems):
        self.place = place
        self.mine, self.theirs, self.chip_part, self.quad_in, self.group_in, self.full = refs
        self.send_sems, self.recv_sems = send_sems, recv_sems

    def send(self, src, dst, send, recv, device):
        remote(src, dst, self.send_sems.at[send], self.recv_sems.at[recv], device)

    def to_core(self):
        at = self.place
        self.send(self.mine.at[1 - at.core], self.theirs, 0, 0, (at.section, at.sibling))

    def add_cores(self):
        landed(self.theirs, self.recv_sems.at[0])
        for part in range(QUAD):
            both = self.mine[self.place.core, part].astype(F32) + self.theirs[part].astype(F32)
            self.chip_part[part] = both.astype(BF16)

    def to_quad(self):
        at = self.place
        self.add_cores()
        for step in range(1, QUAD):
            other = lax.rem(at.quad + step, QUAD)
            to = (at.section, at.quad_peer(step))
            self.send(self.chip_part.at[other], self.quad_in.at[at.quad], 1, 1, to)
        self.quad_in[at.quad] = self.chip_part[at.quad]

    def to_groups(self):
        at = self.place
        landed(self.quad_in.at[0 : QUAD - 1], self.recv_sems.at[1])
        total = self.quad_in[0].astype(F32)
        for part in range(1, QUAD):
            total = total + self.quad_in[part].astype(F32)
        self.own_piece(total)
        self.to_members()
        self.over_sections(at.quad)

    def to_members(self):
        at = self.place
        piece = self.full.at[at.core, at.section, at.quad]
        for step in range(1, QUAD):
            self.send(piece, piece, 2, 1 + step, (at.section, at.quad_peer(step)))

    def own_piece(self, total):
        at = self.place
        if at.groups > 1:
            mine = self.group_in.at[at.group]
            mine[...] = total.astype(BF16)
            for step in range(1, at.groups):
                self.send(mine, mine, 5, 9, (at.section, at.chip_peer(step * QUAD)))
            landed(self.group_in.at[0 : at.groups - 1], self.recv_sems.at[9])
            total = self.group_in[0].astype(F32)
            for other in range(1, at.groups):
                total = total + self.group_in[other].astype(F32)
        self.full[at.core, at.section, at.quad] = total.astype(BF16)

    def over_sections(self, quad):
        at = self.place
        piece = self.full.at[at.core, at.section, quad]
        for k in (1, 2, 3):
            self.send(piece, piece, 3, 4 + k, (at.beyond(k), at.dp))

    def to_sections(self):
        at = self.place
        for step in range(1, QUAD):
            other = lax.rem(at.quad + QUAD - step, QUAD)
            landed(self.full.at[at.core, at.section, other], self.recv_sems.at[1 + step])
            self.over_sections(other)
        block = self.full.at[at.core, at.section]
        self.send(block, block, 4, 8, (at.section, at.sibling))

    def to_sibling(self):
        at = self.place
        for k in (1, 2, 3):
            block = self.full.at[at.core, at.beyond(k)]
            landed(block, self.recv_sems.at[4 + k])
            self.send(block, block, 4, 8, (at.section, at.sibling))

    def end(self):
        at = self.place
        landed(self.full.at[1 - at.core], self.recv_sems.at[8])
        landed(self.theirs, self.send_sems.at[0])
        landed(self.quad_in.at[0 : QUAD - 1], self.send_sems.at[1])
        landed(self.quad_in.at[0 : QUAD - 1], self.send_sems.at[2])
        landed(self.full.at[at.core, 0 : at.sections - 1], self.send_sems.at[3])
        landed(self.full.at[at.core], self.send_sems.at[4])
        if at.groups > 1:
            landed(self.group_in.at[0 : at.groups - 1], self.send_sems.at[5])


class RelaySum(GradSum):
    def to_members(self):
        at = self.place
        piece = self.full.at[at.core, at.section, at.quad]
        self.send(piece, piece, 2, 2, (at.section, at.apart(2)))
        self.send(piece, piece, 2, 3, (at.section, at.apart(1)))

    def to_near(self):
        at = self.place
        far = 2 * (1 - at.high) + at.low
        piece = self.full.at[at.core, at.section, far]
        landed(piece, self.recv_sems.at[2])
        self.send(piece, piece, 2, 4, (at.section, at.apart(1)))
        self.over_sections(far)
        near = 2 * at.high + 1 - at.low
        landed(self.full.at[at.core, at.section, near], self.recv_sems.at[3])
        self.over_sections(near)

    def to_sections(self):
        at = self.place
        last = 2 * (1 - at.high) + 1 - at.low
        landed(self.full.at[at.core, at.section, last], self.recv_sems.at[4])
        self.over_sections(last)
        block = self.full.at[at.core, at.section]
        self.send(block, block, 4, 8, (at.section, at.sibling))


def main_kernel(cfg, names, *refs):
    r = SimpleNamespace(**dict(zip(names, refs)))
    rows, width, states, half, lanes = (
        cfg.rows,
        cfg.width,
        cfg.states,
        cfg.half,
        cfg.lanes,
    )
    steps = rows // SUB
    section = lax.axis_index("section")
    dp = lax.axis_index("dp")
    chips = cfg.dp // 2
    core, chip = lax.rem(dp, 2), lax.div(dp, 2)
    quad, group = lax.rem(chip, QUAD), lax.div(chip, QUAD)
    beyond = {
        1: section + 1 - 2 * lax.rem(section, 2),
        2: section + 2 - 4 * lax.div(section, 2),
        3: 3 - section,
    }
    place = SimpleNamespace(
        section=section,
        beyond=lambda k: beyond[k],
        sections=cfg.sections,
        dp=dp,
        core=core,
        chip=chip,
        chips=chips,
        quad=quad,
        group=group,
        groups=chips // QUAD,
        devices=cfg.dp,
        dp_peer=lambda step: lax.rem(dp + step, cfg.dp),
        sibling=dp + 1 - 2 * core,
        chip_peer=lambda step: lax.rem(chip + step, chips) * 2 + core,
        high=lax.div(quad, 2),
        low=lax.rem(quad, 2),
        apart=lambda by: (
            chip + by * (1 - 2 * (lax.rem(quad, 2) if by == 1 else lax.div(quad, 2)))
        )
        * 2
        + core,
        quad_peer=lambda step: (group * QUAD + lax.rem(quad + step, QUAD)) * 2 + core,
    )

    direct = cfg.dp <= 8
    if direct:
        peers = [(section, place.dp_peer(step)) for step in range(1, cfg.dp)]
    else:
        peers = [(section, place.sibling)]
        peers += [(section, place.chip_peer(step)) for step in range(1, chips)]
    peers += [(beyond[k], dp) for k in (1, 2, 3)]
    barrier = pltpu.get_barrier_semaphore()
    for peer in peers:
        pl.semaphore_signal(barrier, inc=1, device_id=peer, device_id_type=MESH)

    small = [
        SmallSum(
            place,
            direct and k < len(SUM_ROWS) - 1,
            r.sum_own.at[k, 0:tall] if k < len(SUM_ROWS) - 1 else r.late_own.at[section],
            r.sum_sibling.at[k, 0:tall],
            r.sum_slots.at[k, :, 0:tall],
            r.sum_send.at[k],
            r.sum_recv.at[k],
        )
        for k, tall in enumerate(SUM_ROWS)
    ]
    first_sum = small[0]
    mid_sum = [small[1], small[2]]
    upper_sum = [small[3], small[4]]
    late_sum = small[5]
    batches = [
        (RelaySum if k < 2 else GradSum)(
            place,
            [getattr(r, f"{part}_{k}") for part in STAGES],
            r.grad_send.at[k],
            r.grad_recv.at[k],
        )
        for k in range(4)
    ]
    upper_gate, upper_in, lower_gate, lower_rest = batches

    r.gain, r.bias, r.skip, r.gbias = [r.wide_par.at[k] for k in range(4)]
    r.decay, r.freq, r.lstep = [r.state_par.at[k] for k in range(3)]
    wide_far = (r.gain_far, r.bias_far, r.skip_far, r.gbias_far)
    state_far = (r.decay_far, r.freq_far, r.lstep_far)
    fetches = [[(r.lengths_far, r.lengths)]]
    fetches += [[(r.tokens_far.at[m], r.tokens.at[m])] for m in range(2)]
    fetches += [[(far, r.state_par.at[k]) for k, far in enumerate(state_far)]]
    fetches += [[(r.b_in_far, r.b_in)], [(r.out_grad_far, r.out_grad)], [(r.c_out_far, r.c_out)]]
    fetches += [[(far, r.wide_par.at[k]) for k, far in enumerate(wide_far)]]
    fetches += [[(r.gmat_far, r.gmat)]]
    for k, group_of in enumerate(fetches):
        for far, held in group_of:
            pltpu.make_async_copy(far, held, r.fetch_sem.at[k]).start()
    landed(r.lengths, r.fetch_sem.at[0])

    first_len = [r.lengths[m, 0] for m in range(2)]
    total_len = [r.lengths[m, 0] + r.lengths[m, 1] for m in range(2)]

    def put(index, at, row):
        for k in range(row.shape[1] // 128):
            r.sum_own[index, at + k : at + k + 1, :] = row[:, k * 128 : (k + 1) * 128]

    def put_late(at, row):
        for k in range(cfg.sections):
            r.late_own[k, at : at + 1, :] = row[:, k * 128 : (k + 1) * 128]

    chunk = 32
    for m in range(2):

        landed(r.tokens.at[m], r.fetch_sem.at[1 + m])

        def token_sums(t, carry, m=m):
            at = pl.ds(t * chunk, chunk)
            v = r.tokens[m, at, :].astype(F32)
            place_row = t * chunk + lax.broadcasted_iota(jnp.int32, (chunk, width), 0)
            kept = jnp.where(place_row < total_len[m], v, 0.0)
            return carry[0] + fold_rows(kept), carry[1] + fold_rows(kept * v)

        zero = jnp.zeros((SUB, width), F32)
        sums, squares = sweep(rows // chunk, token_sums, (zero, zero))
        put(0, 8 * m, jnp.sum(sums, axis=0, keepdims=True))
        put(0, 8 * m + 4, jnp.sum(squares, axis=0, keepdims=True))
        count = jnp.minimum(total_len[m], rows).astype(F32)
        r.sum_own[0, 16 + m : 17 + m, :] = jnp.full((1, 128), count, F32)

    pl.semaphore_wait(barrier, len(peers))
    first_sum.start()

    at_i = lax.broadcasted_iota(jnp.int32, (rows, rows), 0)
    at_r = lax.broadcasted_iota(jnp.int32, (rows, rows), 1)
    r.spread[...] = jnp.where(
        at_r == (at_i % SUB) * steps + at_i // SUB, 1.0, 0.0
    ).astype(BF16)
    r.gather[...] = jnp.where(
        at_i == (at_r % SUB) * steps + at_r // SUB, 1.0, 0.0
    ).astype(BF16)
    for m in range(2):
        r.first_in[m] = matmul(r.spread[...], r.tokens[m]).astype(BF16)
    first_sum.turn()
    landed(r.out_grad, r.fetch_sem.at[5])
    for m in range(2):
        r.out_grads[m] = matmul(r.spread[...], r.out_grad[m]).astype(BF16)
    held = lax.broadcasted_iota(jnp.int32, (rows, 128), 0)
    held = (held % SUB) * steps + held // SUB
    all_start, all_end = [], []
    for m in range(2):
        one, zero = jnp.float32(1.0), jnp.float32(0.0)
        past = held >= total_len[m]
        starts = (held == 0) | (held == first_len[m]) | past
        ends = (held == first_len[m] - 1) | (held == total_len[m] - 1) | past | (held == rows - 1)
        r.valid[m] = jnp.where(past, zero, one)
        r.keep_start[m] = jnp.where(starts, zero, one)
        r.keep_end[m] = jnp.where(ends, zero, one)
        for kept, mask in ((all_start, r.keep_start), (all_end, r.keep_end)):
            kept.append(jnp.min(mask[m].reshape(steps, SUB, 128), axis=0))

    r.par[...] = jnp.zeros((SUB, lanes), F32)
    r.par[0:2, :] = jnp.ones((2, lanes), F32)
    landed(r.state_par, r.fetch_sem.at[3])
    r.par[0:2, 0:half] = r.decay[...]
    r.par[2:4, 0:half] = r.freq[...]
    r.par[4:6, 0:half] = r.lstep[...]
    decay, spin = r.par[0:2, :], r.par[2:4, :]
    step_size = jnp.exp(r.par[4:6, :])
    damping = jnp.exp(-decay * step_size)
    bar_re = damping * jnp.cos(spin * step_size)
    bar_im = damping * jnp.sin(spin * step_size)
    modulus = decay * decay + spin * spin
    fac_re = ((bar_re - 1.0) * -decay + bar_im * spin) / modulus
    fac_im = (bar_im * -decay - (bar_re - 1.0) * spin) / modulus
    pow_re, pow_im = bar_re, bar_im
    power = 1
    while power < steps:
        pow_re, pow_im = cmul(pow_re, pow_im, pow_re, pow_im)
        power *= 2

    lane = lax.broadcasted_iota(jnp.int32, (1, 128), 1)
    low_lanes = lane < half - 128
    turn_by = half - 128

    from_column = lax.broadcasted_iota(jnp.int32, (states, 2 * lanes), 0)
    to_column = lax.broadcasted_iota(jnp.int32, (states, 2 * lanes), 1)
    moved_to = jnp.where(from_column < half, from_column, from_column + (lanes - half))
    r.widen[...] = jnp.where(to_column == moved_to, 1.0, 0.0).astype(BF16)
    for held, k in ((r.b_in, 4), (r.c_out, 6), (r.wide_par, 7), (r.gmat, 8)):
        landed(held, r.fetch_sem.at[k])
    for l in range(2):
        r.b_pad[l] = matmul(r.b_in[l], r.widen[...]).astype(BF16)
        blank = jnp.zeros((lanes - half, width), BF16)
        r.c_pad[l, 0:half, :] = r.c_out[l, 0:half, :]
        r.c_pad[l, half:lanes, :] = blank
        r.c_pad[l, lanes : lanes + half, :] = r.c_out[l, half:states, :]
        r.c_pad[l, lanes + half : 2 * lanes, :] = blank

    def across(end, coef, reverse):
        end_re, end_im = end
        coef_re, coef_im = coef
        sub = lax.broadcasted_iota(jnp.int32, (SUB, lanes), 0)
        for by in (1, 2, 4):
            turn = SUB - by if reverse else by
            live = sub < SUB - by if reverse else sub >= by

            def moved(x):
                return jnp.where(live, pltpu.roll(x, turn, 0), 0.0)

            add_re, add_im = cmul(coef_re, coef_im, moved(end_re), moved(end_im))
            coef_re, coef_im = cmul(coef_re, coef_im, moved(coef_re), moved(coef_im))
            end_re, end_im = end_re + add_re, end_im + add_im
        turn = SUB - 1 if reverse else 1
        live = sub < SUB - 1 if reverse else sub >= 1
        return tuple(jnp.where(live, pltpu.roll(x, turn, 0), 0.0) for x in (end_re, end_im))

    def wide8(x, l):
        return jnp.broadcast_to(x[l : l + 1, :], (SUB, x.shape[1]))

    def group_rows(p):
        return pl.ds(p * SUB, SUB)

    def scan_coefs(l, m, reverse):
        keep = r.keep_end if reverse else r.keep_start
        all_kept = repeat_lanes((all_end if reverse else all_start)[m], lanes // 128)
        product = (all_kept * wide8(pow_re, l), all_kept * wide8(pow_im, l))
        return keep, wide8(bar_re, l), wide8(bar_im, l), product

    def advance(keep, m, at, br, bi, re, im, src_re, src_im):
        k = repeat_lanes(keep[m, at, :], lanes // 128)
        kr, ki = k * br, k * bi
        return kr * re - ki * im + src_re, kr * im + ki * re + src_im

    def scan_states(l, m):
        reverse = l == 1
        lead = 0 if reverse else 1
        keep, br, bi, product = scan_coefs(l, m, reverse)
        fr, fi = wide8(fac_re, l), wide8(fac_im, l)
        zero = jnp.zeros((SUB, lanes), F32)

        def ends(t, carry):
            p = steps - 1 - t if reverse else t
            at = group_rows(p)
            v = repeat_lanes(r.valid[m, at, :], lanes // 128)
            drive_re = r.drive[l, m, at, 0:lanes]
            drive_im = r.drive[l, m, at, lanes : 2 * lanes]
            src_re, src_im = cmul(fr, fi, v * drive_re, v * drive_im)
            r.state[l, m, group_rows(p + lead), 0:lanes] = src_re
            r.state[l, m, group_rows(p + lead), lanes : 2 * lanes] = src_im
            return advance(keep, m, at, br, bi, *carry, src_re, src_im)

        end = sweep(steps, ends, (zero, zero))
        enter = across(end, product, reverse)
        first = steps if reverse else 0
        r.state[l, m, first * SUB : (first + 1) * SUB, 0:lanes] = enter[0]
        r.state[l, m, first * SUB : (first + 1) * SUB, lanes : 2 * lanes] = enter[1]

        def fill(t, carry):
            done = []
            for k in range(2):
                p = steps - 1 - (2 * t + k) if reverse else 2 * t + k
                at, to = group_rows(p), group_rows(p + lead)
                src_re = r.state[l, m, to, 0:lanes]
                src_im = r.state[l, m, to, lanes : 2 * lanes]
                carry = advance(keep, m, at, br, bi, *carry, src_re, src_im)
                r.state[l, m, to, 0:lanes] = carry[0]
                r.state[l, m, to, lanes : 2 * lanes] = carry[1]
                done.append(jnp.concatenate([carry[0], -carry[1]], axis=1))
            pair = steps // 2 - 1 - t if reverse else t
            both = jnp.concatenate(done[::-1] if reverse else done, axis=0)
            to = pl.ds(m * rows + pair * 16, 16)
            r.joined[l, to, :] = both.astype(BF16)
            return carry

        sweep(steps // 2, fill, enter)

    def scan_grads(l, m):
        reverse = l == 0
        back = 1 if l == 1 else 0
        keep, br, bi, product = scan_coefs(l, m, reverse)
        keep_state = r.keep_start if l == 0 else r.keep_end
        fr, fi = 2.0 * wide8(fac_re, l), 2.0 * wide8(fac_im, l)
        zero = jnp.zeros((SUB, lanes), F32)

        def ends(t, carry):
            p = steps - 1 - t if reverse else t
            at = group_rows(p)
            q_re = r.q[m, at, 0:lanes]
            q_im = r.q[m, at, lanes : 2 * lanes]
            return advance(keep, m, at, br, bi, *carry, q_re, q_im)

        end = sweep(steps, ends, (zero, zero))
        enter = across(end, product, reverse)

        def fill(t, carry):
            w, bar_sum, fac_sum = carry
            done = []
            for k in range(2):
                p = steps - 1 - (2 * t + k) if reverse else 2 * t + k
                at, near = group_rows(p), group_rows(p + back)
                q_re = r.q[m, at, 0:lanes]
                q_im = r.q[m, at, lanes : 2 * lanes]
                w = advance(keep, m, at, br, bi, *w, q_re, q_im)
                kept = repeat_lanes(keep_state[m, at, :], lanes // 128)
                near_re = kept * r.state[l, m, near, 0:lanes]
                near_im = kept * r.state[l, m, near, lanes : 2 * lanes]
                term = cmul(*w, near_re, near_im)
                bar_sum = (bar_sum[0] + term[0], bar_sum[1] + term[1])
                v = repeat_lanes(r.valid[m, at, :], lanes // 128)
                vw = (v * w[0], v * w[1])
                drive_re = r.drive[l, m, at, 0:lanes]
                drive_im = r.drive[l, m, at, lanes : 2 * lanes]
                term = cmul(*vw, drive_re, drive_im)
                fac_sum = (fac_sum[0] + term[0], fac_sum[1] + term[1])
                gd_re, gd_im = cmul(fr, fi, *vw)
                im_low = pltpu.roll(-gd_im[:, 0:128], 64, 1)
                im_high = pltpu.roll(-gd_im[:, 128:256], 64, 1)
                done.append(
                    jnp.concatenate(
                        [
                            gd_re[:, 0:128],
                            jnp.where(low_lanes, gd_re[:, 128:256], im_low),
                            jnp.where(low_lanes, im_low, im_high),
                        ],
                        axis=1,
                    )
                )
            pair = steps // 2 - 1 - t if reverse else t
            both = jnp.concatenate(done[::-1] if reverse else done, axis=0)
            to = pl.ds(m * rows + pair * 16, 16)
            r.grad_drive[l, to, :] = both.astype(BF16)
            return w, bar_sum, fac_sum

        none = (zero, zero)
        _, bar_sum, fac_sum = sweep(steps // 2, fill, (enter, none, none))
        for k, part in enumerate((*bar_sum, *fac_sum)):
            r.state_sums[l, m, k] = part

    def row_of(ref, l):
        return ref[l : l + 1, :]

    def micro_rows(m):
        return slice(m * rows, (m + 1) * rows)

    gelu_chunk = 16

    def mixer(l, m, center, inv, hook=None):
        gain, bias, skip = row_of(r.gain, l), row_of(r.bias, l), row_of(r.skip, l)

        def normalise(t, carry):
            at = pl.ds(t * chunk, chunk)
            if l == 0:
                v = r.first_in[m, at, :].astype(F32)
            else:
                v = r.second_in[m, at, :]
            normed = (v - center) * inv
            r.normed[l, m, at, :] = normed
            to = pl.ds(m * rows + t * chunk, chunk)
            r.scaled[l, to, :] = (normed * gain + bias).astype(BF16)
            return carry

        sweep(rows // chunk, normalise, 0)
        r.drive[l, m] = matmul(r.scaled[l, micro_rows(m), :], r.b_pad[l])
        scan_states(l, m)
        if hook is not None:
            hook()
        r.work[...] = matmul(r.joined[l, micro_rows(m), :], r.c_pad[l])

        def activate(t, carry):
            at = pl.ds(t * gelu_chunk, gelu_chunk)
            scaled = r.normed[l, m, at, :] * gain + bias
            y = (2.0 * r.work[at, :] + skip * scaled).astype(BF16).astype(F32)
            below = 0.5 + 0.5 * lax.erf(y * 0.7071067811865476)
            density = jnp.exp(-0.5 * y * y) * 0.3989422804014327
            active = y * below
            r.active[l, m, at, :] = active
            r.slope[l, m, at, :] = below + y * density
            to = pl.ds(m * rows + t * gelu_chunk, gelu_chunk)
            r.active_low[l, to, :] = active.astype(BF16)
            return carry

        sweep(rows // gelu_chunk, activate, 0)
        r.work[...] = matmul(r.active_low[l, micro_rows(m), :], r.gmat[l])

    def first_gate(m):
        gbias = row_of(r.gbias, 0)

        def gate(t, carry):
            at = pl.ds(t * gelu_chunk, gelu_chunk)
            opened = jax.nn.sigmoid(r.work[at, :] + gbias)
            r.sig[0, m, at, :] = opened
            v = repeat_lanes(r.valid[m, at, :], width // 128)
            gated = v * r.active[0, m, at, :] * opened
            second = r.first_in[m, at, :].astype(F32) + gated.astype(BF16).astype(F32)
            r.second_in[m, at, :] = second
            kept = v * second
            return carry[0] + fold_rows(kept), carry[1] + fold_rows(kept * second)

        zero = jnp.zeros((SUB, width), F32)
        sums, squares = sweep(rows // gelu_chunk, gate, (zero, zero))
        put(1 + m, 0, jnp.sum(sums, axis=0, keepdims=True))
        put(1 + m, 4, jnp.sum(squares, axis=0, keepdims=True))

    bias_sums = {}
    skip_sums = {}

    def gate_grad(l, m, grad_of):
        gbias = row_of(r.gbias, l)

        def gate(t, carry):
            at = pl.ds(t * gelu_chunk, gelu_chunk)
            if l == 1:
                opened = jax.nn.sigmoid(r.work[at, :] + gbias)
                r.sig[1, m, at, :] = opened
            else:
                opened = r.sig[0, m, at, :]
            v = repeat_lanes(r.valid[m, at, :], width // 128)
            masked = v * grad_of(at, v)
            through = masked * opened
            r.through[at, :] = through
            grad_logits = through * r.active[l, m, at, :] * (1.0 - opened)
            to = pl.ds(m * rows + t * gelu_chunk, gelu_chunk)
            r.grad_logits[l, to, :] = grad_logits.astype(BF16)
            return carry + fold_rows(grad_logits)

        zero = jnp.zeros((SUB, width), F32)
        bias_sums[l, m] = sweep(rows // gelu_chunk, gate, zero)

    def branch_grad(l, m):
        gain, bias = row_of(r.gain, l), row_of(r.bias, l)
        r.work[...] = matmul_nt(r.grad_logits[l, micro_rows(m), :], r.gmat[l])

        def branch(t, carry):
            at = pl.ds(t * chunk, chunk)
            grad_active = r.through[at, :] + r.work[at, :]
            g = (r.slope[l, m, at, :] * grad_active).astype(BF16)
            to = pl.ds(m * rows + t * chunk, chunk)
            r.branch[l, to, :] = g
            scaled = r.normed[l, m, at, :] * gain + bias
            return carry + fold_rows(g.astype(F32) * scaled)

        zero = jnp.zeros((SUB, width), F32)
        skip_sums[l, m] = sweep(rows // chunk, branch, zero)
        r.q[m] = matmul_nt(r.branch[l, micro_rows(m), :], r.c_pad[l])

    def mixer_grad(l, m, hook=None):
        skip = row_of(r.skip, l)
        scan_grads(l, m)
        if hook is not None:
            hook()
        r.work[...] = matmul_nt(r.grad_drive[l, micro_rows(m), :], r.b_in[l])

        def scaled_grad(t, carry):
            at = pl.ds(t * chunk, chunk)
            to = pl.ds(m * rows + t * chunk, chunk)
            grad = r.work[at, :] + skip * r.branch[l, to, :].astype(F32)
            r.grad_scaled[l, m, at, :] = grad
            normed = r.normed[l, m, at, :]
            return carry[0] + fold_rows(grad), carry[1] + fold_rows(grad * normed)

        zero = jnp.zeros((SUB, width), F32)
        sums, products = sweep(rows // chunk, scaled_grad, (zero, zero))
        sums = jnp.sum(sums, axis=0, keepdims=True)
        products = jnp.sum(products, axis=0, keepdims=True)
        if l == 1:
            put(3 + m, 0, sums)
            put(3 + m, 4, products)
        else:
            put_late(2 * m, sums)
            put_late(2 * m + 1, products)

    def moments(total, at, count):
        center = unfold(total, at, 4) / count
        return center, lax.rsqrt(unfold(total, at + 4, 4) / count - center * center + epsilon)

    own_columns = pl.ds(pl.multiple_of(section * 128, 128), 128)

    def gate_weights(l, ref):
        grad = matmul_tn(r.active_low[l, :, own_columns], r.grad_logits[l])
        ref[:, :, :, 0:width] = grad.astype(BF16).reshape(2, QUAD, 16, width)

    def out_weights(l, ref, at):
        grad = 2.0 * matmul_tn(r.joined[l], r.branch[l, :, own_columns])
        grad = jnp.concatenate([grad[0:half, :], grad[lanes : lanes + half, :]], axis=0)
        tall = states // (2 * QUAD)
        for k in range(tall // 16):
            for c in range(2):
                for z in range(QUAD):
                    first = (c * QUAD + z) * tall + 16 * k
                    ref[c, z, :, at + 128 * k : at + 128 * (k + 1)] = grad[
                        first : first + 16, :
                    ].astype(BF16)

    def in_weights(l, ref, at):
        grad = matmul_tn(r.scaled[l, :, own_columns], r.grad_drive[l])
        ref[:, :, :, at : at + states] = grad.astype(BF16).reshape(2, QUAD, 16, states)

    def layer_rows(l):
        def both(sums):
            return jnp.sum(sums[l, 0] + sums[l, 1], axis=0, keepdims=True)

        put_late(4 + 2 * l, both(skip_sums))
        put_late(5 + 2 * l, both(bias_sums))
        part = [
            jnp.sum(r.state_sums[l, 0, k] + r.state_sums[l, 1, k], axis=0, keepdims=True)
            for k in range(4)
        ]
        gb_re, gb_im = 2.0 * part[0], -2.0 * part[1]
        gf_re, gf_im = 2.0 * part[2], -2.0 * part[3]
        one = slice(l, l + 1)
        lam_re, lam_im, size = -decay[one], spin[one], step_size[one]
        b_re, b_im, f_re, f_im = bar_re[one], bar_im[one], fac_re[one], fac_im[one]
        top_re, top_im = size * b_re - f_re, size * b_im - f_im
        square = modulus[one]
        d_re = (top_re * lam_re + top_im * lam_im) / square
        d_im = (top_im * lam_re - top_re * lam_im) / square
        gl_re = size * (b_re * gb_re + b_im * gb_im) + (d_re * gf_re + d_im * gf_im)
        gl_im = size * (b_re * gb_im - b_im * gb_re) + (d_re * gf_im - d_im * gf_re)
        e_re, e_im = cmul(lam_re, lam_im, b_re, b_im)
        g_step = size * ((e_re * gb_re + e_im * gb_im) + (b_re * gf_re + b_im * gf_im))
        parts = [
            row[:, k : k + 128] for row in (-gl_re, gl_im, g_step) for k in range(0, lanes, 128)
        ]
        for k, row in enumerate(parts):
            k += l * len(parts)
            at = 8 + k % LATE_STATES
            r.late_own[k // LATE_STATES, at : at + 1, :] = row

    def mixed_rows(m):
        def mix(t, carry):
            at = pl.ds(t * chunk, chunk)
            gated = (
                r.valid[m, at, :]
                * r.active[1, m, at, own_columns]
                * r.sig[1, m, at, own_columns]
            )
            stream = r.second_in[m, at, own_columns].astype(BF16).astype(F32)
            r.narrow[at, :] = (stream + gated).astype(BF16)
            return carry

        sweep(rows // chunk, mix, 0)
        r.mixed[m] = matmul(r.gather[...], r.narrow[...]).astype(BF16)

    def stream_grad(l, m, total, count, inv):
        gain = row_of(r.gain, l)
        first = gain * unfold(total, 0, 4) / count
        second = gain * unfold(total, 4, 4) / count
        return gain, first, second, inv

    total0 = first_sum.total()
    counts = [repeat_lanes(total0[16 + m : 17 + m, :], width // 128) for m in range(2)]
    norm0 = [moments(total0, 8 * m, counts[m]) for m in range(2)]

    mixer(0, 0, *norm0[0])
    first_gate(0)
    mid_sum[0].start()
    mixer(0, 1, *norm0[1], hook=mid_sum[0].turn)
    first_gate(1)
    mid_sum[1].start()

    norm1 = [None, None]
    for m in range(2):
        norm1[m] = moments(mid_sum[m].total(), 0, counts[m])
        hook = mid_sum[1].turn if m == 0 else None
        mixer(1, m, *norm1[m], hook=hook)
        gate_grad(1, m, lambda at, v, m=m: r.out_grads[m, at, :].astype(F32))
        branch_grad(1, m)
        if m == 1:
            gate_weights(1, r.mine_0)
            out_weights(1, r.mine_0, width)
            upper_gate.to_core()
        mixer_grad(1, m)
        upper_sum[m].start()
        upper_sum[m].turn()

    in_weights(1, r.mine_1, 0)
    upper_in.to_core()
    upper_gate.to_quad()
    layer_rows(1)

    def second_grad(m, total):
        gain, first, second, inv = stream_grad(1, m, total, counts[m], norm1[m][1])

        def grad_of(at, v):
            grad_normed = r.grad_scaled[1, m, at, :] * gain
            normed = r.normed[1, m, at, :]
            grad_stream = inv * (grad_normed - v * (first + normed * second))
            out_grad = r.out_grads[m, at, :].astype(F32)
            grad = (out_grad + grad_stream.astype(BF16).astype(F32)).astype(BF16)
            r.grad_second[m, at, :] = grad
            return grad.astype(F32)

        return grad_of

    upper_total = [upper_sum[0].total()]
    gate_grad(0, 0, second_grad(0, upper_total[0]))
    upper_in.to_quad()
    branch_grad(0, 0)
    mixer_grad(0, 0)
    upper_total.append(upper_sum[1].total())
    gate_grad(0, 1, second_grad(1, upper_total[1]))
    gate_weights(0, r.mine_2)
    lower_gate.to_core()
    branch_grad(0, 1)
    upper_gate.to_groups()
    out_weights(0, r.mine_3, 0)
    lower_gate.to_quad()
    upper_in.to_groups()
    mixer_grad(0, 1)
    in_weights(0, r.mine_3, states)
    lower_rest.to_core()
    layer_rows(0)
    late_sum.start()
    mixed_rows(0)
    lower_rest.to_quad()
    late_sum.turn()
    upper_gate.to_near()
    mixed_rows(1)
    upper_in.to_near()
    lower_gate.to_groups()
    upper_gate.to_sections()

    late = late_sum.total()
    r.late[section] = late
    block = r.late.at[section]
    for k in (1, 2, 3):
        remote(block, block, r.late_sem.at[0], r.late_sem.at[1], (beyond[k], dp))
    lower_rest.to_groups()
    upper_in.to_sections()
    own_gain = r.gain[0:1, own_columns]
    for m in range(2):
        count = counts[m][:, 0:128]
        first = own_gain * late[2 * m : 2 * m + 1, :] / count
        second = own_gain * late[2 * m + 1 : 2 * m + 2, :] / count
        r.rows[m : m + 1, :] = norm0[m][1]
        inv = r.rows[m : m + 1, own_columns]

        def token_grad(t, carry, m=m, first=first, second=second, inv=inv):
            at = pl.ds(t * chunk, chunk)
            grad_normed = r.grad_scaled[0, m, at, own_columns] * own_gain
            normed = r.normed[0, m, at, own_columns]
            grad_stream = inv * (grad_normed - r.valid[m, at, :] * (first + normed * second))
            grad = r.grad_second[m, at, own_columns].astype(F32) + grad_stream
            high = grad.astype(BF16)
            r.narrow[at, :] = high
            r.narrow_rest[at, :] = (grad - high.astype(F32)).astype(BF16)
            return carry

        sweep(rows // chunk, token_grad, 0)
        r.token_grad[m] = matmul(r.gather[...], r.narrow[...]) + matmul(
            r.gather[...], r.narrow_rest[...]
        )
    r.upper_norm[...] = upper_total[0] + upper_total[1]
    lower_gate.to_sections()
    lower_rest.to_sections()
    upper_gate.to_sibling()
    upper_in.to_sibling()
    lower_gate.to_sibling()
    lower_rest.to_sibling()
    for k in range(2):
        landed(r.late.at[0 : cfg.sections - 1], r.late_sem.at[k])
    for batch in batches:
        batch.end()
    for each in small:
        each.end()


def lay_out_kernel(cfg, *refs):
    full = refs[0:4]
    late, upper_norm, mixed, token_grad = refs[4:8]
    (
        mixed_out,
        token_grad_out,
        gain_out,
        bias_out,
        decay_out,
        freq_out,
        step_out,
        in_out,
        out_out,
        skip_out,
        gate_out,
        gbias_out,
    ) = refs[8:20]
    in_held, out_held, gate_held = refs[20:23]
    rows_held, sems = refs[23:30], refs[30]
    width, states, half = cfg.width, cfg.states, cfg.half
    tall = states // (2 * QUAD)
    copies = []

    def send(held, out, sem=None):
        copy = pltpu.make_async_copy(held, out, sems.at[3 + len(copies) if sem is None else sem])
        copy.start()
        if sem is None:
            copies.append(copy)

    send(mixed, mixed_out)
    send(token_grad, token_grad_out)
    def columns(at):
        return jnp.concatenate([late[s, at : at + 1, :] for s in range(cfg.sections)], axis=1)

    row_outs = (bias_out, gain_out, skip_out, gbias_out, decay_out, freq_out, step_out)
    values = [
        (columns(0) + columns(2), unfold(upper_norm, 0, 4)),
        (columns(1) + columns(3), unfold(upper_norm, 4, 4)),
        (columns(4), columns(6)),
        (columns(5), columns(7)),
    ]
    for k in range(3):
        places = [(6 * l + 2 * k + part) for l in range(2) for part in range(2)]
        row = [late[p // LATE_STATES, 8 + p % LATE_STATES, :][None] for p in places]
        values.append([jnp.concatenate(row[2 * l : 2 * l + 2], axis=1)[:, 0:half] for l in range(2)])
    for held, out, value in zip(rows_held, row_outs, values):
        for l in range(2):
            held[l : l + 1, :] = value[l]
        send(held, out)

    for l in (1, 0):
        parts = ((full[0], 0), (full[0], width), (full[1], 0))
        if l == 0:
            parts = ((full[2], 0), (full[3], 0), (full[3], states))
        for s in range(cfg.sections):
            mine = slice(s * 128, (s + 1) * 128)
            members = [(c, z) for c in range(2) for z in range(QUAD)]
            for (part, begin), held, out, wide, sem in (
                (parts[0], gate_held, gate_out, width, 0),
                (parts[2], in_held, in_out, states, 1),
            ):
                for c, z in members:
                    at = s * 128 + (c * QUAD + z) * 16
                    held[l, at : at + 16, :] = part[c, s, z, :, begin : begin + wide].astype(F32)
                send(held.at[l, mine], out.at[l, mine], sem)
            part, begin = parts[1]
            for c, z in members:
                for k in range(tall // 16):
                    first = (c * QUAD + z) * tall + 16 * k
                    out_held[l, first : first + 16, mine] = part[
                        c, s, z, :, begin + k * 128 : begin + (k + 1) * 128
                    ].astype(F32)
        send(out_held.at[l], out_out.at[l], 2)
    for copy in copies:
        copy.wait()
    for sem, out in enumerate((gate_out, in_out, out_out)):
        landed(out, sems.at[sem])


INPUTS = tuple(
    dict(
        tokens=0,
        lengths=0,
        out_grad=0,
        gain=0,
        bias=0,
        decay=0,
        freq=0,
        lstep=0,
        b_in=0,
        c_out=0,
        skip=0,
        gmat=0,
        gbias=0,
    )
)


def per_device(cfg, *args):
    rows, width, states, lanes = cfg.rows, cfg.width, cfg.states, cfg.lanes
    sections, dp, chips = cfg.sections, cfg.dp, cfg.dp // 2
    groups = chips // QUAD
    steps = rows // SUB
    vmem, dma = pltpu.VMEM, pltpu.SemaphoreType.DMA
    widths = (width + states, states, width, 2 * states)
    outs = {f"full_{k}": ((2, sections, QUAD, 16, w), BF16) for k, w in enumerate(widths)}
    outs.update(
        late=((sections, 16, 128), F32), upper_norm=((8, 128), F32), mixed=((2, rows, 128), BF16), token_grad=((2, rows, 128), F32)
    )
    scratch = dict(
        sum_own=vmem((len(SUM_ROWS), 24, 128), F32),
        sum_sibling=vmem((len(SUM_ROWS), 24, 128), F32),
        sum_slots=vmem((len(SUM_ROWS), min(dp, max(chips, 8)), 24, 128), F32),
        late_own=vmem((sections, 16, 128), F32),
        late_sem=dma((2,)),
        sum_send=dma((len(SUM_ROWS), 2)),
        sum_recv=dma((len(SUM_ROWS), 2)),
        grad_send=dma((4, 5 + (groups > 1))),
        grad_recv=dma((4, 9 + (groups > 1))),
        fetch_sem=dma((9,)),
        lengths=pltpu.SMEM((2, 2), jnp.int32),
        tokens=vmem((2, rows, width), BF16),
        wide_par=vmem((4, 2, width), F32),
        state_par=vmem((3, 2, states // 2), F32),
        b_in=vmem((2, width, states), BF16),
        c_out=vmem((2, states, width), BF16),
        gmat=vmem((2, width, width), BF16),
        out_grad=vmem((2, rows, width), BF16),
        widen=vmem((states, 2 * lanes), BF16),
        q=vmem((2, rows, 2 * lanes), F32),
        spread=vmem((rows, rows), BF16),
        gather=vmem((rows, rows), BF16),
        first_in=vmem((2, rows, width), BF16),
        out_grads=vmem((2, rows, width), BF16),
        second_in=vmem((2, rows, width), F32),
        grad_second=vmem((2, rows, width), BF16),
        valid=vmem((2, rows, 128), F32),
        keep_start=vmem((2, rows, 128), F32),
        keep_end=vmem((2, rows, 128), F32),
        par=vmem((SUB, lanes), F32),
        b_pad=vmem((2, width, 2 * lanes), BF16),
        c_pad=vmem((2, 2 * lanes, width), BF16),
        normed=vmem((2, 2, rows, width), F32),
        scaled=vmem((2, 2 * rows, width), BF16),
        drive=vmem((2, 2, rows, 2 * lanes), F32),
        state=vmem((2, 2, (steps + 1) * SUB, 2 * lanes), F32),
        joined=vmem((2, 2 * rows, 2 * lanes), BF16),
        work=vmem((rows, width), F32),
        active=vmem((2, 2, rows, width), F32),
        active_low=vmem((2, 2 * rows, width), BF16),
        slope=vmem((2, 2, rows, width), F32),
        sig=vmem((2, 2, rows, width), F32),
        through=vmem((rows, width), F32),
        grad_logits=vmem((2, 2 * rows, width), BF16),
        branch=vmem((2, 2 * rows, width), BF16),
        grad_drive=vmem((2, 2 * rows, states), BF16),
        grad_scaled=vmem((2, 2, rows, width), F32),
        state_sums=vmem((2, 2, 4, SUB, lanes), F32),
        narrow=vmem((rows, 128), BF16),
        narrow_rest=vmem((rows, 128), BF16),
        rows=vmem((SUB, width), F32),
    )
    for k, w in enumerate(widths):
        blocks = (2, QUAD), (QUAD,), (QUAD,), (QUAD,), (groups,)
        for part, block in zip(STAGES, blocks):
            scratch[f"{part}_{k}"] = vmem((*block, 16, w), BF16)
    in_vmem = pl.BlockSpec(memory_space=pltpu.VMEM)
    in_hbm = pl.BlockSpec(memory_space=pltpu.HBM)
    names = tuple(f"{name}_far" for name in INPUTS) + tuple(outs) + tuple(scratch)
    made = pl.pallas_call(
        partial(main_kernel, cfg, names),
        name="layers",
        out_shape=[vmem(*spec) for spec in outs.values()],
        in_specs=[in_hbm for name in INPUTS],
        out_specs=[in_vmem for name in outs],
        scratch_shapes=list(scratch.values()),
        compiler_params=pltpu.CompilerParams(
            collective_id=0, has_side_effects=True, vmem_limit_bytes=56 * 2**20
        ),
    )(*args)
    shapes = [
        ((2, rows, 128), BF16),
        ((2, rows, 128), F32),
        ((2, width), F32),
        ((2, width), F32),
        ((2, states // 2), F32),
        ((2, states // 2), F32),
        ((2, states // 2), F32),
        ((2, width, states), F32),
        ((2, states, width), F32),
        ((2, width), F32),
        ((2, width, width), F32),
        ((2, width), F32),
    ]
    by_copy = (7, 8, 10)
    return pl.pallas_call(
        partial(lay_out_kernel, cfg),
        name="lay_out",
        out_shape=[jax.ShapeDtypeStruct(*spec) for spec in shapes],
        in_specs=[in_vmem] * 8,
        out_specs=[in_hbm] * 12,
        scratch_shapes=[vmem(*shapes[k]) for k in by_copy]
        + [vmem((2, width), F32)] * 4
        + [vmem((2, states // 2), F32)] * 3
        + [dma((12,))],
        compiler_params=pltpu.CompilerParams(vmem_limit_bytes=24 * 2**20),
    )(*made)


def solution(mesh):
    sections, dp = mesh.shape["section"], mesh.shape["dp"]

    def run(*args):
        _, rows, width = args[0].shape
        states = args[8].shape[2]
        cfg = SimpleNamespace(
            rows=rows // dp,
            width=width,
            states=states,
            half=states // 2,
            lanes=-(-states // 256) * 128,
            sections=sections,
            dp=dp,
        )
        split = P(None, "dp", None)
        shared = P()
        placed = P(None, "dp", "section")
        return jax.shard_map(
            partial(per_device, cfg),
            mesh=mesh,
            in_specs=(split, P(None, "dp"), split) + (shared,) * 10,
            out_specs=(placed, placed) + (shared,) * 10,
            check_vma=False,
        )(*args)

    return run
```

```python
from functools import partial
from types import SimpleNamespace

import jax
import jax.numpy as jnp
from jax import lax
from jax.experimental import pallas as pl
from jax.experimental.pallas import tpu as pltpu
from jax.sharding import PartitionSpec as P

epsilon = 1e-05
MESH = pl.DeviceIdType.MESH
F32 = jnp.float32
BF16 = jnp.bfloat16
SUB = 8
QUAD = 4
PART_SEMS = 8
LATE_STATES = 3
SUM_ROWS = (10, 8, 8, 8, 8, 8, 16)


STAGES = tuple(dict(mine=0, theirs=0, chip=0, quad=0, group=0, full=0))


def matmul(left, right):
    return jnp.dot(left, right, preferred_element_type=F32)


def matmul_nt(left, right):
    return lax.dot_general(left, right, (((1,), (1,)), ((), ())), preferred_element_type=F32)


def matmul_tn(left, right):
    return lax.dot_general(left, right, (((0,), (0,)), ((), ())), preferred_element_type=F32)


def cmul(ar, ai, br, bi):
    return ar * br - ai * bi, ar * bi + ai * br


def sweep(count, body, carry):
    for t in range(count):
        carry = body(t, carry)
    return carry


def repeat_lanes(x, times):
    return jnp.concatenate([x] * times, axis=1)


def fold_rows(x):
    return jnp.sum(x.reshape(x.shape[0] // SUB, SUB, x.shape[1]), axis=0)


def unfold(total, first, count):
    return jnp.concatenate([total[first + k : first + k + 1, :] for k in range(count)], axis=1)


def landed(block, sem):
    pltpu.make_async_copy(block, block, sem).wait()


def remote(src, dst, send_sem, recv_sem, device):
    pltpu.make_async_remote_copy(
        src_ref=src,
        dst_ref=dst,
        send_sem=send_sem,
        recv_sem=recv_sem,
        device_id=device,
        device_id_type=MESH,
    ).start()


def first_sems(cfg):
    begins = [0]
    for k in range(len(SUM_ROWS)):
        begins.append(begins[-1] + (2 if cfg.dp <= 8 and k < len(SUM_ROWS) - 1 else 4))
    return begins


class SmallSum:
    def __init__(self, place, direct, own, sibling, slots, sems):
        self.place, self.direct = place, direct
        self.own, self.sibling, self.slots, self.sems = own, sibling, slots, sems

    def to_all(self, slot, members, peer):
        self.members = members
        block = self.slots.at[slot]
        for step in range(1, members):
            to = (self.place.section, peer(step))
            remote(block, block, self.sems.at[0], self.sems.at[1], to)

    def start(self):
        at = self.place
        if self.direct:
            self.slots[at.dp] = self.own[...]
            self.to_all(at.dp, at.devices, at.dp_peer)
        else:
            to = (at.section, at.sibling)
            remote(self.own, self.sibling, self.sems.at[2], self.sems.at[3], to)

    def turn(self):
        at = self.place
        if not self.direct:
            landed(self.sibling, self.sems.at[3])
            self.slots[at.chip] = self.own[...] + self.sibling[...]
            self.to_all(at.chip, at.chips, at.chip_peer)

    def total(self):
        landed(self.slots.at[0 : self.members - 1], self.sems.at[1])
        result = self.slots[0]
        for member in range(1, self.members):
            result = result + self.slots[member]
        return result

    def end(self):
        if not self.direct:
            landed(self.own, self.sems.at[2])
        landed(self.slots.at[0 : self.members - 1], self.sems.at[0])


class GradSum:
    def __init__(self, place, parts, refs, send_sems, recv_sems):
        self.place, self.parts = place, parts
        self.mine, self.theirs, self.chip_part, self.quad_in, self.group_in, self.full = refs
        self.send_sems, self.recv_sems = send_sems, recv_sems

    def recv(self, part, k):
        if k == PART_SEMS:
            return self.recv_sems.at[1 + 3 * PART_SEMS + part]
        return self.recv_sems.at[1 + part * PART_SEMS + k]

    def send(self, part, src, dst, send, recv, device):
        columns = self.parts[part]
        sem = self.recv_sems.at[0] if recv is None else self.recv(part, recv)
        remote(src.at[..., columns], dst.at[..., columns], self.send_sems.at[send], sem, device)

    def landed(self, part, block, k):
        landed(block.at[..., self.parts[part]], self.recv(part, k))

    def to_core(self, part):
        at = self.place
        self.send(part, self.mine.at[1 - at.core], self.theirs, 0, 0, (at.section, at.sibling))

    def to_quad(self, part):
        at, columns = self.place, self.parts[part]
        self.landed(part, self.theirs, 0)
        for k in range(QUAD):
            both = self.mine[at.core, k, :, columns].astype(F32)
            both = both + self.theirs[k, :, columns].astype(F32)
            self.chip_part[k, :, columns] = both.astype(BF16)
        for step in range(1, QUAD):
            other = lax.rem(at.quad + step, QUAD)
            to = (at.section, at.quad_peer(step))
            self.send(part, self.chip_part.at[other], self.quad_in.at[at.quad], 1, 1, to)
        self.quad_in[at.quad, :, columns] = self.chip_part[at.quad, :, columns]

    def to_groups(self, part):
        at, columns = self.place, self.parts[part]
        self.landed(part, self.quad_in.at[0 : QUAD - 1], 1)
        total = self.quad_in[0, :, columns].astype(F32)
        for k in range(1, QUAD):
            total = total + self.quad_in[k, :, columns].astype(F32)
        if at.groups > 1:
            mine = self.group_in.at[at.group]
            mine[:, columns] = total.astype(BF16)
            for step in range(1, at.groups):
                self.send(part, mine, mine, 5, 8, (at.section, at.chip_peer(step * QUAD)))
            self.landed(part, self.group_in.at[0 : at.groups - 1], 8)
            total = self.group_in[0, :, columns].astype(F32)
            for other in range(1, at.groups):
                total = total + self.group_in[other, :, columns].astype(F32)
        piece = self.full.at[at.core, at.section, at.quad]
        piece[:, columns] = total.astype(BF16)
        self.to_members(part)
        self.over_sections(part, at.quad)

    def to_members(self, part):
        at = self.place
        piece = self.full.at[at.core, at.section, at.quad]
        for step in range(1, QUAD):
            self.send(part, piece, piece, 2, 1 + step, (at.section, at.quad_peer(step)))

    def over_sections(self, part, quad):
        at = self.place
        piece = self.full.at[at.core, at.section, quad]
        for k in (1, 2, 3):
            self.send(part, piece, piece, 3, 4 + k, (at.beyond(k), at.dp))

    def to_sections(self, part):
        at = self.place
        for step in range(1, QUAD):
            other = lax.rem(at.quad + QUAD - step, QUAD)
            self.landed(part, self.full.at[at.core, at.section, other], 1 + step)
            self.over_sections(part, other)
        self.to_other(part, at.section)

    def to_other(self, part, section):
        at = self.place
        block = self.full.at[at.core, section]
        self.send(part, block, block, 4, None, (at.section, at.sibling))

    def to_sibling(self, part):
        at = self.place
        for k in (1, 2, 3):
            self.landed(part, self.full.at[at.core, at.beyond(k)], 4 + k)
            self.to_other(part, at.beyond(k))

    def end(self):
        at = self.place
        landed(self.full.at[1 - at.core], self.recv_sems.at[0])
        landed(self.theirs, self.send_sems.at[0])
        landed(self.quad_in.at[0 : QUAD - 1], self.send_sems.at[1])
        landed(self.quad_in.at[0 : QUAD - 1], self.send_sems.at[2])
        landed(self.full.at[at.core, 0 : at.sections - 1], self.send_sems.at[3])
        landed(self.full.at[at.core], self.send_sems.at[4])
        if at.groups > 1:
            landed(self.group_in.at[0 : at.groups - 1], self.send_sems.at[5])


class RelaySum(GradSum):
    def to_members(self, part):
        at = self.place
        piece = self.full.at[at.core, at.section, at.quad]
        self.send(part, piece, piece, 2, 2, (at.section, at.apart(2)))
        self.send(part, piece, piece, 2, 3, (at.section, at.apart(1)))

    def to_near(self, part):
        at = self.place
        far = 2 * (1 - at.high) + at.low
        piece = self.full.at[at.core, at.section, far]
        self.landed(part, piece, 2)
        self.send(part, piece, piece, 2, 4, (at.section, at.apart(1)))
        self.over_sections(part, far)
        near = 2 * at.high + 1 - at.low
        self.landed(part, self.full.at[at.core, at.section, near], 3)
        self.over_sections(part, near)

    def to_sections(self, part):
        at = self.place
        last = 2 * (1 - at.high) + 1 - at.low
        self.landed(part, self.full.at[at.core, at.section, last], 4)
        self.over_sections(part, last)
        self.to_other(part, at.section)


def main_kernel(cfg, names, *refs):
    r = SimpleNamespace(**dict(zip(names, refs)))
    rows, width, states, half, lanes = (
        cfg.rows,
        cfg.width,
        cfg.states,
        cfg.half,
        cfg.lanes,
    )
    steps = rows // SUB
    section = lax.axis_index("section")
    dp = lax.axis_index("dp")
    chips = cfg.dp // 2
    core, chip = lax.rem(dp, 2), lax.div(dp, 2)
    quad, group = lax.rem(chip, QUAD), lax.div(chip, QUAD)
    beyond = {
        1: section + 1 - 2 * lax.rem(section, 2),
        2: section + 2 - 4 * lax.div(section, 2),
        3: 3 - section,
    }
    place = SimpleNamespace(
        section=section,
        beyond=lambda k: beyond[k],
        sections=cfg.sections,
        dp=dp,
        core=core,
        chip=chip,
        chips=chips,
        quad=quad,
        group=group,
        groups=chips // QUAD,
        devices=cfg.dp,
        dp_peer=lambda step: lax.rem(dp + step, cfg.dp),
        sibling=dp + 1 - 2 * core,
        chip_peer=lambda step: lax.rem(chip + step, chips) * 2 + core,
        high=lax.div(quad, 2),
        low=lax.rem(quad, 2),
        apart=lambda by: (
            chip + by * (1 - 2 * (lax.rem(quad, 2) if by == 1 else lax.div(quad, 2)))
        )
        * 2
        + core,
        quad_peer=lambda step: (group * QUAD + lax.rem(quad + step, QUAD)) * 2 + core,
    )

    direct = cfg.dp <= 8
    if direct:
        peers = [(section, place.dp_peer(step)) for step in range(1, cfg.dp)]
    else:
        peers = [(section, place.sibling)]
        peers += [(section, place.chip_peer(step)) for step in range(1, chips)]
    peers += [(beyond[k], dp) for k in (1, 2, 3)]
    barrier = pltpu.get_barrier_semaphore()
    for peer in peers:
        pl.semaphore_signal(barrier, inc=1, device_id=peer, device_id_type=MESH)

    sum_sems = first_sems(cfg)
    small = [
        SmallSum(
            place,
            direct and k < len(SUM_ROWS) - 1,
            r.sum_own.at[k, 0:tall] if k < len(SUM_ROWS) - 1 else r.late_own.at[section],
            r.sum_sibling.at[k, 0:tall],
            r.sum_slots.at[k, :, 0:tall],
            r.sum_sem.at[sum_sems[k] : sum_sems[k + 1]],
        )
        for k, tall in enumerate(SUM_ROWS)
    ]
    first_sum, mid_sum, upper_sum = small[0:2], small[2:4], small[4:6]
    late_sum = small[6]
    gate_part, out_part, in_part = range(3)
    bounds = (0, width, width + states, width + 2 * states)
    batches = [
        (RelaySum if k == 0 else GradSum)(
            place,
            [slice(*bounds[k : k + 2]) for k in range(3)],
            [getattr(r, f"{part}_{k}") for part in STAGES],
            r.grad_send.at[k],
            r.grad_recv.at[k],
        )
        for k in range(2)
    ]
    upper, lower = batches

    r.gain, r.bias, r.skip, r.gbias = [r.wide_par.at[k] for k in range(4)]
    r.decay, r.freq, r.lstep = [r.state_par.at[k] for k in range(3)]
    wide_far = (r.gain_far, r.bias_far, r.skip_far, r.gbias_far)
    state_far = (r.decay_far, r.freq_far, r.lstep_far)
    fetches = [[(r.lengths_far, r.lengths)]]
    fetches += [[(r.tokens_far.at[m], r.tokens.at[m])] for m in range(2)]
    fetches += [[(far, r.state_par.at[k]) for k, far in enumerate(state_far)]]
    fetches += [[(r.b_in_far, r.b_in)], [(r.out_grad_far, r.out_grad)], [(r.c_out_far, r.c_out)]]
    fetches += [[(far, r.wide_par.at[k]) for k, far in enumerate(wide_far)]]
    fetches += [[(r.gmat_far, r.gmat)]]
    for k, group_of in enumerate(fetches):
        for far, held in group_of:
            pltpu.make_async_copy(far, held, r.fetch_sem.at[k]).start()
    landed(r.lengths, r.fetch_sem.at[0])

    first_len = [r.lengths[m, 0] for m in range(2)]
    total_len = [r.lengths[m, 0] + r.lengths[m, 1] for m in range(2)]

    def put(index, at, row):
        for k in range(row.shape[1] // 128):
            r.sum_own[index, at + k : at + k + 1, :] = row[:, k * 128 : (k + 1) * 128]

    def put_late(at, row):
        for k in range(cfg.sections):
            r.late_own[k, at : at + 1, :] = row[:, k * 128 : (k + 1) * 128]

    chunk = 32
    for m in range(2):

        landed(r.tokens.at[m], r.fetch_sem.at[1 + m])

        def token_sums(t, carry, m=m):
            at = pl.ds(t * chunk, chunk)
            v = r.tokens[m, at, :].astype(F32)
            place_row = t * chunk + lax.broadcasted_iota(jnp.int32, (chunk, width), 0)
            kept = jnp.where(place_row < total_len[m], v, 0.0)
            return carry[0] + fold_rows(kept), carry[1] + fold_rows(kept * v)

        zero = jnp.zeros((SUB, width), F32)
        sums, squares = sweep(rows // chunk, token_sums, (zero, zero))
        put(m, 0, jnp.sum(sums, axis=0, keepdims=True))
        put(m, 4, jnp.sum(squares, axis=0, keepdims=True))
        if m == 0:
            for k in range(2):
                count = jnp.minimum(total_len[k], rows).astype(F32)
                r.sum_own[0, 8 + k : 9 + k, :] = jnp.full((1, 128), count, F32)
            pl.semaphore_wait(barrier, len(peers))
        first_sum[m].start()

    at_i = lax.broadcasted_iota(jnp.int32, (rows, rows), 0)
    at_r = lax.broadcasted_iota(jnp.int32, (rows, rows), 1)
    r.spread[...] = jnp.where(
        at_r == (at_i % SUB) * steps + at_i // SUB, 1.0, 0.0
    ).astype(BF16)
    r.gather[...] = jnp.where(
        at_i == (at_r % SUB) * steps + at_r // SUB, 1.0, 0.0
    ).astype(BF16)
    for m in range(2):
        r.first_in[m] = matmul(r.spread[...], r.tokens[m]).astype(BF16)
    for m in range(2):
        first_sum[m].turn()
    landed(r.out_grad, r.fetch_sem.at[5])
    for m in range(2):
        r.out_grads[m] = matmul(r.spread[...], r.out_grad[m]).astype(BF16)
    held = lax.broadcasted_iota(jnp.int32, (rows, 128), 0)
    held = (held % SUB) * steps + held // SUB
    all_start, all_end = [], []
    for m in range(2):
        one, zero = jnp.float32(1.0), jnp.float32(0.0)
        past = held >= total_len[m]
        starts = (held == 0) | (held == first_len[m]) | past
        ends = (held == first_len[m] - 1) | (held == total_len[m] - 1) | past | (held == rows - 1)
        r.valid[m] = jnp.where(past, zero, one)
        r.keep_start[m] = jnp.where(starts, zero, one)
        r.keep_end[m] = jnp.where(ends, zero, one)
        for kept, mask in ((all_start, r.keep_start), (all_end, r.keep_end)):
            kept.append(jnp.min(mask[m].reshape(steps, SUB, 128), axis=0))

    r.par[...] = jnp.zeros((SUB, lanes), F32)
    r.par[0:2, :] = jnp.ones((2, lanes), F32)
    landed(r.state_par, r.fetch_sem.at[3])
    r.par[0:2, 0:half] = r.decay[...]
    r.par[2:4, 0:half] = r.freq[...]
    r.par[4:6, 0:half] = r.lstep[...]
    decay, spin = r.par[0:2, :], r.par[2:4, :]
    step_size = jnp.exp(r.par[4:6, :])
    damping = jnp.exp(-decay * step_size)
    bar_re = damping * jnp.cos(spin * step_size)
    bar_im = damping * jnp.sin(spin * step_size)
    modulus = decay * decay + spin * spin
    fac_re = ((bar_re - 1.0) * -decay + bar_im * spin) / modulus
    fac_im = (bar_im * -decay - (bar_re - 1.0) * spin) / modulus
    pow_re, pow_im = bar_re, bar_im
    power = 1
    while power < steps:
        pow_re, pow_im = cmul(pow_re, pow_im, pow_re, pow_im)
        power *= 2

    lane = lax.broadcasted_iota(jnp.int32, (1, 128), 1)
    low_lanes = lane < half - 128
    turn_by = half - 128

    from_column = lax.broadcasted_iota(jnp.int32, (states, 2 * lanes), 0)
    to_column = lax.broadcasted_iota(jnp.int32, (states, 2 * lanes), 1)
    moved_to = jnp.where(from_column < half, from_column, from_column + (lanes - half))
    r.widen[...] = jnp.where(to_column == moved_to, 1.0, 0.0).astype(BF16)
    for held, k in ((r.b_in, 4), (r.c_out, 6), (r.wide_par, 7), (r.gmat, 8)):
        landed(held, r.fetch_sem.at[k])
    for l in range(2):
        r.b_pad[l] = matmul(r.b_in[l], r.widen[...]).astype(BF16)
        blank = jnp.zeros((lanes - half, width), BF16)
        r.c_pad[l, 0:half, :] = r.c_out[l, 0:half, :]
        r.c_pad[l, half:lanes, :] = blank
        r.c_pad[l, lanes : lanes + half, :] = r.c_out[l, half:states, :]
        r.c_pad[l, lanes + half : 2 * lanes, :] = blank

    def across(end, coef, reverse):
        end_re, end_im = end
        coef_re, coef_im = coef
        sub = lax.broadcasted_iota(jnp.int32, (SUB, lanes), 0)
        for by in (1, 2, 4):
            turn = SUB - by if reverse else by
            live = sub < SUB - by if reverse else sub >= by

            def moved(x):
                return jnp.where(live, pltpu.roll(x, turn, 0), 0.0)

            add_re, add_im = cmul(coef_re, coef_im, moved(end_re), moved(end_im))
            coef_re, coef_im = cmul(coef_re, coef_im, moved(coef_re), moved(coef_im))
            end_re, end_im = end_re + add_re, end_im + add_im
        turn = SUB - 1 if reverse else 1
        live = sub < SUB - 1 if reverse else sub >= 1
        return tuple(jnp.where(live, pltpu.roll(x, turn, 0), 0.0) for x in (end_re, end_im))

    def wide8(x, l):
        return jnp.broadcast_to(x[l : l + 1, :], (SUB, x.shape[1]))

    def group_rows(p):
        return pl.ds(p * SUB, SUB)

    def scan_coefs(l, m, reverse):
        keep = r.keep_end if reverse else r.keep_start
        all_kept = repeat_lanes((all_end if reverse else all_start)[m], lanes // 128)
        product = (all_kept * wide8(pow_re, l), all_kept * wide8(pow_im, l))
        return keep, wide8(bar_re, l), wide8(bar_im, l), product

    def advance(keep, m, at, br, bi, re, im, src_re, src_im):
        k = repeat_lanes(keep[m, at, :], lanes // 128)
        kr, ki = k * br, k * bi
        return kr * re - ki * im + src_re, kr * im + ki * re + src_im

    def scan_states(l, m):
        reverse = l == 1
        lead = 0 if reverse else 1
        keep, br, bi, product = scan_coefs(l, m, reverse)
        fr, fi = wide8(fac_re, l), wide8(fac_im, l)
        zero = jnp.zeros((SUB, lanes), F32)

        def ends(t, carry):
            p = steps - 1 - t if reverse else t
            at = group_rows(p)
            v = repeat_lanes(r.valid[m, at, :], lanes // 128)
            drive_re = r.drive[l, m, at, 0:lanes]
            drive_im = r.drive[l, m, at, lanes : 2 * lanes]
            src_re, src_im = cmul(fr, fi, v * drive_re, v * drive_im)
            r.state[l, m, group_rows(p + lead), 0:lanes] = src_re
            r.state[l, m, group_rows(p + lead), lanes : 2 * lanes] = src_im
            return advance(keep, m, at, br, bi, *carry, src_re, src_im)

        end = sweep(steps, ends, (zero, zero))
        enter = across(end, product, reverse)
        first = steps if reverse else 0
        r.state[l, m, first * SUB : (first + 1) * SUB, 0:lanes] = enter[0]
        r.state[l, m, first * SUB : (first + 1) * SUB, lanes : 2 * lanes] = enter[1]

        def fill(t, carry):
            done = []
            for k in range(2):
                p = steps - 1 - (2 * t + k) if reverse else 2 * t + k
                at, to = group_rows(p), group_rows(p + lead)
                src_re = r.state[l, m, to, 0:lanes]
                src_im = r.state[l, m, to, lanes : 2 * lanes]
                carry = advance(keep, m, at, br, bi, *carry, src_re, src_im)
                r.state[l, m, to, 0:lanes] = carry[0]
                r.state[l, m, to, lanes : 2 * lanes] = carry[1]
                done.append(jnp.concatenate([carry[0], -carry[1]], axis=1))
            pair = steps // 2 - 1 - t if reverse else t
            both = jnp.concatenate(done[::-1] if reverse else done, axis=0)
            to = pl.ds(m * rows + pair * 16, 16)
            r.joined[l, to, :] = both.astype(BF16)
            return carry

        sweep(steps // 2, fill, enter)

    def scan_grads(l, m):
        reverse = l == 0
        back = 1 if l == 1 else 0
        keep, br, bi, product = scan_coefs(l, m, reverse)
        keep_state = r.keep_start if l == 0 else r.keep_end
        fr, fi = 2.0 * wide8(fac_re, l), 2.0 * wide8(fac_im, l)
        zero = jnp.zeros((SUB, lanes), F32)

        def ends(t, carry):
            p = steps - 1 - t if reverse else t
            at = group_rows(p)
            q_re = r.q[m, at, 0:lanes]
            q_im = r.q[m, at, lanes : 2 * lanes]
            return advance(keep, m, at, br, bi, *carry, q_re, q_im)

        end = sweep(steps, ends, (zero, zero))
        enter = across(end, product, reverse)

        def fill(t, carry):
            w, bar_sum, fac_sum = carry
            done = []
            for k in range(2):
                p = steps - 1 - (2 * t + k) if reverse else 2 * t + k
                at, near = group_rows(p), group_rows(p + back)
                q_re = r.q[m, at, 0:lanes]
                q_im = r.q[m, at, lanes : 2 * lanes]
                w = advance(keep, m, at, br, bi, *w, q_re, q_im)
                kept = repeat_lanes(keep_state[m, at, :], lanes // 128)
                near_re = kept * r.state[l, m, near, 0:lanes]
                near_im = kept * r.state[l, m, near, lanes : 2 * lanes]
                term = cmul(*w, near_re, near_im)
                bar_sum = (bar_sum[0] + term[0], bar_sum[1] + term[1])
                v = repeat_lanes(r.valid[m, at, :], lanes // 128)
                vw = (v * w[0], v * w[1])
                drive_re = r.drive[l, m, at, 0:lanes]
                drive_im = r.drive[l, m, at, lanes : 2 * lanes]
                term = cmul(*vw, drive_re, drive_im)
                fac_sum = (fac_sum[0] + term[0], fac_sum[1] + term[1])
                gd_re, gd_im = cmul(fr, fi, *vw)
                im_low = pltpu.roll(-gd_im[:, 0:128], 64, 1)
                im_high = pltpu.roll(-gd_im[:, 128:256], 64, 1)
                done.append(
                    jnp.concatenate(
                        [
                            gd_re[:, 0:128],
                            jnp.where(low_lanes, gd_re[:, 128:256], im_low),
                            jnp.where(low_lanes, im_low, im_high),
                        ],
                        axis=1,
                    )
                )
            pair = steps // 2 - 1 - t if reverse else t
            both = jnp.concatenate(done[::-1] if reverse else done, axis=0)
            to = pl.ds(m * rows + pair * 16, 16)
            r.grad_drive[l, to, :] = both.astype(BF16)
            return w, bar_sum, fac_sum

        none = (zero, zero)
        _, bar_sum, fac_sum = sweep(steps // 2, fill, (enter, none, none))
        for k, part in enumerate((*bar_sum, *fac_sum)):
            r.state_sums[l, m, k] = part

    def row_of(ref, l):
        return ref[l : l + 1, :]

    def micro_rows(m):
        return slice(m * rows, (m + 1) * rows)

    gelu_chunk = 16

    def mixer(l, m, center, inv):
        gain, bias, skip = row_of(r.gain, l), row_of(r.bias, l), row_of(r.skip, l)

        def normalise(t, carry):
            at = pl.ds(t * chunk, chunk)
            if l == 0:
                v = r.first_in[m, at, :].astype(F32)
            else:
                v = r.second_in[m, at, :]
            normed = (v - center) * inv
            r.normed[l, m, at, :] = normed
            to = pl.ds(m * rows + t * chunk, chunk)
            r.scaled[l, to, :] = (normed * gain + bias).astype(BF16)
            return carry

        sweep(rows // chunk, normalise, 0)
        yield
        r.drive[l, m] = matmul(r.scaled[l, micro_rows(m), :], r.b_pad[l])
        yield
        scan_states(l, m)
        yield
        r.work[m] = matmul(r.joined[l, micro_rows(m), :], r.c_pad[l])

        yield

        def activate(t, carry):
            at = pl.ds(t * gelu_chunk, gelu_chunk)
            scaled = r.normed[l, m, at, :] * gain + bias
            y = (2.0 * r.work[m, at, :] + skip * scaled).astype(BF16).astype(F32)
            below = 0.5 + 0.5 * lax.erf(y * 0.7071067811865476)
            density = jnp.exp(-0.5 * y * y) * 0.3989422804014327
            active = y * below
            r.active[l, m, at, :] = active
            r.slope[l, m, at, :] = below + y * density
            to = pl.ds(m * rows + t * gelu_chunk, gelu_chunk)
            r.active_low[l, to, :] = active.astype(BF16)
            return carry

        sweep(rows // gelu_chunk, activate, 0)
        yield
        r.work[m] = matmul(r.active_low[l, micro_rows(m), :], r.gmat[l])

    def first_gate(m):
        gbias = row_of(r.gbias, 0)

        def gate(t, carry):
            at = pl.ds(t * gelu_chunk, gelu_chunk)
            opened = jax.nn.sigmoid(r.work[m, at, :] + gbias)
            r.sig[0, m, at, :] = opened
            v = repeat_lanes(r.valid[m, at, :], width // 128)
            gated = v * r.active[0, m, at, :] * opened
            second = r.first_in[m, at, :].astype(F32) + gated.astype(BF16).astype(F32)
            r.second_in[m, at, :] = second
            kept = v * second
            return carry[0] + fold_rows(kept), carry[1] + fold_rows(kept * second)

        zero = jnp.zeros((SUB, width), F32)
        sums, squares = sweep(rows // gelu_chunk, gate, (zero, zero))
        put(2 + m, 0, jnp.sum(sums, axis=0, keepdims=True))
        put(2 + m, 4, jnp.sum(squares, axis=0, keepdims=True))

    bias_sums = {}
    skip_sums = {}

    def gate_grad(l, m, grad_of):
        gbias = row_of(r.gbias, l)

        def gate(t, carry):
            at = pl.ds(t * gelu_chunk, gelu_chunk)
            if l == 1:
                opened = jax.nn.sigmoid(r.work[m, at, :] + gbias)
                r.sig[1, m, at, :] = opened
            else:
                opened = r.sig[0, m, at, :]
            v = repeat_lanes(r.valid[m, at, :], width // 128)
            masked = v * grad_of(at, v)
            through = masked * opened
            r.through[m, at, :] = through
            grad_logits = through * r.active[l, m, at, :] * (1.0 - opened)
            to = pl.ds(m * rows + t * gelu_chunk, gelu_chunk)
            r.grad_logits[l, to, :] = grad_logits.astype(BF16)
            return carry + fold_rows(grad_logits)

        zero = jnp.zeros((SUB, width), F32)
        bias_sums[l, m] = sweep(rows // gelu_chunk, gate, zero)
        yield

    def branch_grad(l, m):
        gain, bias = row_of(r.gain, l), row_of(r.bias, l)
        r.work[m] = matmul_nt(r.grad_logits[l, micro_rows(m), :], r.gmat[l])
        yield

        def branch(t, carry):
            at = pl.ds(t * chunk, chunk)
            grad_active = r.through[m, at, :] + r.work[m, at, :]
            g = (r.slope[l, m, at, :] * grad_active).astype(BF16)
            to = pl.ds(m * rows + t * chunk, chunk)
            r.branch[l, to, :] = g
            scaled = r.normed[l, m, at, :] * gain + bias
            return carry + fold_rows(g.astype(F32) * scaled)

        zero = jnp.zeros((SUB, width), F32)
        skip_sums[l, m] = sweep(rows // chunk, branch, zero)
        yield
        r.q[m] = matmul_nt(r.branch[l, micro_rows(m), :], r.c_pad[l])
        yield

    def mixer_grad(l, m):
        skip = row_of(r.skip, l)
        scan_grads(l, m)
        yield
        r.work[m] = matmul_nt(r.grad_drive[l, micro_rows(m), :], r.b_in[l])
        yield

        def scaled_grad(t, carry):
            at = pl.ds(t * chunk, chunk)
            to = pl.ds(m * rows + t * chunk, chunk)
            grad = r.work[m, at, :] + skip * r.branch[l, to, :].astype(F32)
            r.grad_scaled[l, m, at, :] = grad
            normed = r.normed[l, m, at, :]
            return carry[0] + fold_rows(grad), carry[1] + fold_rows(grad * normed)

        zero = jnp.zeros((SUB, width), F32)
        sums, products = sweep(rows // chunk, scaled_grad, (zero, zero))
        sums = jnp.sum(sums, axis=0, keepdims=True)
        products = jnp.sum(products, axis=0, keepdims=True)
        if l == 1:
            put(4 + m, 0, sums)
            put(4 + m, 4, products)
        else:
            put_late(2 * m, sums)
            put_late(2 * m + 1, products)

    def moments(total, at, count):
        center = unfold(total, at, 4) / count
        return center, lax.rsqrt(unfold(total, at + 4, 4) / count - center * center + epsilon)

    own_columns = pl.ds(pl.multiple_of(section * 128, 128), 128)

    def gate_weights(l, ref):
        grad = matmul_tn(r.active_low[l, :, own_columns], r.grad_logits[l])
        ref[:, :, :, 0:width] = grad.astype(BF16).reshape(2, QUAD, 16, width)

    def out_weights(l, ref, at):
        grad = 2.0 * matmul_tn(r.joined[l], r.branch[l, :, own_columns])
        grad = jnp.concatenate([grad[0:half, :], grad[lanes : lanes + half, :]], axis=0)
        tall = states // (2 * QUAD)
        for k in range(tall // 16):
            for c in range(2):
                for z in range(QUAD):
                    first = (c * QUAD + z) * tall + 16 * k
                    ref[c, z, :, at + 128 * k : at + 128 * (k + 1)] = grad[
                        first : first + 16, :
                    ].astype(BF16)

    def in_weights(l, ref, at):
        grad = matmul_tn(r.scaled[l, :, own_columns], r.grad_drive[l])
        ref[:, :, :, at : at + states] = grad.astype(BF16).reshape(2, QUAD, 16, states)

    def layer_rows(l):
        def both(sums):
            return jnp.sum(sums[l, 0] + sums[l, 1], axis=0, keepdims=True)

        put_late(4 + 2 * l, both(skip_sums))
        put_late(5 + 2 * l, both(bias_sums))
        part = [
            jnp.sum(r.state_sums[l, 0, k] + r.state_sums[l, 1, k], axis=0, keepdims=True)
            for k in range(4)
        ]
        gb_re, gb_im = 2.0 * part[0], -2.0 * part[1]
        gf_re, gf_im = 2.0 * part[2], -2.0 * part[3]
        one = slice(l, l + 1)
        lam_re, lam_im, size = -decay[one], spin[one], step_size[one]
        b_re, b_im, f_re, f_im = bar_re[one], bar_im[one], fac_re[one], fac_im[one]
        top_re, top_im = size * b_re - f_re, size * b_im - f_im
        square = modulus[one]
        d_re = (top_re * lam_re + top_im * lam_im) / square
        d_im = (top_im * lam_re - top_re * lam_im) / square
        gl_re = size * (b_re * gb_re + b_im * gb_im) + (d_re * gf_re + d_im * gf_im)
        gl_im = size * (b_re * gb_im - b_im * gb_re) + (d_re * gf_im - d_im * gf_re)
        e_re, e_im = cmul(lam_re, lam_im, b_re, b_im)
        g_step = size * ((e_re * gb_re + e_im * gb_im) + (b_re * gf_re + b_im * gf_im))
        parts = [
            row[:, k : k + 128] for row in (-gl_re, gl_im, g_step) for k in range(0, lanes, 128)
        ]
        for k, row in enumerate(parts):
            k += l * len(parts)
            at = 8 + k % LATE_STATES
            r.late_own[k // LATE_STATES, at : at + 1, :] = row

    def mixed_rows(m):
        def mix(t, carry):
            at = pl.ds(t * chunk, chunk)
            gated = (
                r.valid[m, at, :]
                * r.active[1, m, at, own_columns]
                * r.sig[1, m, at, own_columns]
            )
            stream = r.second_in[m, at, own_columns].astype(BF16).astype(F32)
            r.narrow[at, :] = (stream + gated).astype(BF16)
            return carry

        sweep(rows // chunk, mix, 0)
        r.mixed[m] = matmul(r.gather[...], r.narrow[...]).astype(BF16)

    def stream_grad(l, m, total, count, inv):
        gain = row_of(r.gain, l)
        first = gain * unfold(total, 0, 4) / count
        second = gain * unfold(total, 4, 4) / count
        return gain, first, second, inv

    def take(steps):
        for _ in steps:
            pass

    counts, norm0 = [None, None], [None, None]
    for m in range(2):
        total = first_sum[m].total()
        if m == 0:
            counts = [repeat_lanes(total[8 + k : 9 + k, :], width // 128) for k in range(2)]
        norm0[m] = moments(total, 0, counts[m])
        take(mixer(0, m, *norm0[m]))
        first_gate(m)
        mid_sum[m].start()
        mid_sum[m].turn()

    norm1 = [None, None]

    def second_layer(m):
        norm1[m] = moments(mid_sum[m].total(), 0, counts[m])
        yield from mixer(1, m, *norm1[m])
        yield from gate_grad(1, m, lambda at, v: r.out_grads[m, at, :].astype(F32))
        yield from branch_grad(1, m)
        yield from mixer_grad(1, m)
        upper_sum[m].start()
        upper_sum[m].turn()

    for m in range(2):
        take(second_layer(m))

    gate_weights(1, r.mine_0)
    upper.to_core(gate_part)
    out_weights(1, r.mine_0, width)
    upper.to_core(out_part)
    in_weights(1, r.mine_0, width + states)
    upper.to_core(in_part)
    layer_rows(1)

    def second_grad(m, total):
        gain, first, second, inv = stream_grad(1, m, total, counts[m], norm1[m][1])

        def grad_of(at, v):
            grad_normed = r.grad_scaled[1, m, at, :] * gain
            normed = r.normed[1, m, at, :]
            grad_stream = inv * (grad_normed - v * (first + normed * second))
            out_grad = r.out_grads[m, at, :].astype(F32)
            grad = (out_grad + grad_stream.astype(BF16).astype(F32)).astype(BF16)
            r.grad_second[m, at, :] = grad
            return grad.astype(F32)

        return grad_of

    upper_total = [upper_sum[0].total()]
    take(gate_grad(0, 0, second_grad(0, upper_total[0])))
    upper.to_quad(gate_part)
    take(branch_grad(0, 0))
    upper.to_quad(out_part)
    upper.to_quad(in_part)
    take(mixer_grad(0, 0))
    upper_total.append(upper_sum[1].total())
    take(gate_grad(0, 1, second_grad(1, upper_total[1])))
    gate_weights(0, r.mine_1)
    lower.to_core(gate_part)
    take(branch_grad(0, 1))
    out_weights(0, r.mine_1, width)
    lower.to_core(out_part)
    upper.to_groups(gate_part)
    lower.to_quad(gate_part)
    last = mixer_grad(0, 1)
    next(last)
    upper.to_groups(out_part)
    next(last)
    upper.to_groups(in_part)
    take(last)
    lower.to_quad(out_part)
    in_weights(0, r.mine_1, width + states)
    lower.to_core(in_part)
    layer_rows(0)
    late_sum.start()
    upper.to_near(gate_part)
    lower.to_quad(in_part)
    late_sum.turn()
    mixed_rows(0)
    upper.to_near(out_part)
    lower.to_groups(gate_part)
    upper.to_near(in_part)
    mixed_rows(1)
    lower.to_groups(out_part)
    upper.to_sections(gate_part)
    upper.to_sections(out_part)
    lower.to_groups(in_part)
    lower.to_sections(gate_part)
    upper.to_sections(in_part)

    late = late_sum.total()
    r.late[section] = late
    block = r.late.at[section]
    for k in (1, 2, 3):
        remote(block, block, r.late_sem.at[0], r.late_sem.at[1], (beyond[k], dp))
    own_gain = r.gain[0:1, own_columns]
    for m in range(2):
        count = counts[m][:, 0:128]
        first = own_gain * late[2 * m : 2 * m + 1, :] / count
        second = own_gain * late[2 * m + 1 : 2 * m + 2, :] / count
        r.rows[m : m + 1, :] = norm0[m][1]
        inv = r.rows[m : m + 1, own_columns]

        def token_grad(t, carry, m=m, first=first, second=second, inv=inv):
            at = pl.ds(t * chunk, chunk)
            grad_normed = r.grad_scaled[0, m, at, own_columns] * own_gain
            normed = r.normed[0, m, at, own_columns]
            grad_stream = inv * (grad_normed - r.valid[m, at, :] * (first + normed * second))
            grad = r.grad_second[m, at, own_columns].astype(F32) + grad_stream
            high = grad.astype(BF16)
            r.narrow[at, :] = high
            r.narrow_rest[at, :] = (grad - high.astype(F32)).astype(BF16)
            return carry

        sweep(rows // chunk, token_grad, 0)
        r.token_grad[m] = matmul(r.gather[...], r.narrow[...]) + matmul(
            r.gather[...], r.narrow_rest[...]
        )
    r.upper_norm[...] = upper_total[0] + upper_total[1]
    lower.to_sections(out_part)
    lower.to_sections(in_part)
    for stage in (upper.to_sibling, lower.to_sibling):
        for part in range(3):
            stage(part)
    for k in range(2):
        landed(r.late.at[0 : cfg.sections - 1], r.late_sem.at[k])
    for batch in batches:
        batch.end()
    for each in small:
        each.end()


def lay_out_kernel(cfg, *refs):
    full = refs[1], refs[0]
    late, upper_norm, mixed, token_grad = refs[2:6]
    (
        mixed_out,
        token_grad_out,
        gain_out,
        bias_out,
        decay_out,
        freq_out,
        step_out,
        in_out,
        out_out,
        skip_out,
        gate_out,
        gbias_out,
    ) = refs[6:18]
    in_held, out_held, gate_held = refs[18:21]
    rows_held, sems = refs[21:28], refs[28]
    width, states, half = cfg.width, cfg.states, cfg.half
    tall = states // (2 * QUAD)
    copies = []

    def send(held, out, sem=None):
        copy = pltpu.make_async_copy(held, out, sems.at[3 + len(copies) if sem is None else sem])
        copy.start()
        if sem is None:
            copies.append(copy)

    send(mixed, mixed_out)
    send(token_grad, token_grad_out)
    def columns(at):
        return jnp.concatenate([late[s, at : at + 1, :] for s in range(cfg.sections)], axis=1)

    row_outs = (bias_out, gain_out, skip_out, gbias_out, decay_out, freq_out, step_out)
    values = [
        (columns(0) + columns(2), unfold(upper_norm, 0, 4)),
        (columns(1) + columns(3), unfold(upper_norm, 4, 4)),
        (columns(4), columns(6)),
        (columns(5), columns(7)),
    ]
    for k in range(3):
        places = [(6 * l + 2 * k + part) for l in range(2) for part in range(2)]
        row = [late[p // LATE_STATES, 8 + p % LATE_STATES, :][None] for p in places]
        values.append([jnp.concatenate(row[2 * l : 2 * l + 2], axis=1)[:, 0:half] for l in range(2)])
    for held, out, value in zip(rows_held, row_outs, values):
        for l in range(2):
            held[l : l + 1, :] = value[l]
        send(held, out)

    for l in (1, 0):
        parts = [(full[l], begin) for begin in (0, width, width + states)]
        for s in range(cfg.sections):
            mine = slice(s * 128, (s + 1) * 128)
            members = [(c, z) for c in range(2) for z in range(QUAD)]
            for (part, begin), held, out, wide, sem in (
                (parts[0], gate_held, gate_out, width, 0),
                (parts[2], in_held, in_out, states, 1),
            ):
                for c, z in members:
                    at = s * 128 + (c * QUAD + z) * 16
                    held[l, at : at + 16, :] = part[c, s, z, :, begin : begin + wide].astype(F32)
                send(held.at[l, mine], out.at[l, mine], sem)
            part, begin = parts[1]
            for c, z in members:
                for k in range(tall // 16):
                    first = (c * QUAD + z) * tall + 16 * k
                    out_held[l, first : first + 16, mine] = part[
                        c, s, z, :, begin + k * 128 : begin + (k + 1) * 128
                    ].astype(F32)
        send(out_held.at[l], out_out.at[l], 2)
    for copy in copies:
        copy.wait()
    for sem, out in enumerate((gate_out, in_out, out_out)):
        landed(out, sems.at[sem])


INPUTS = tuple(
    dict(
        tokens=0,
        lengths=0,
        out_grad=0,
        gain=0,
        bias=0,
        decay=0,
        freq=0,
        lstep=0,
        b_in=0,
        c_out=0,
        skip=0,
        gmat=0,
        gbias=0,
    )
)


def per_device(cfg, *args):
    rows, width, states, lanes = cfg.rows, cfg.width, cfg.states, cfg.lanes
    sections, dp, chips = cfg.sections, cfg.dp, cfg.dp // 2
    groups = chips // QUAD
    steps = rows // SUB
    vmem, dma = pltpu.VMEM, pltpu.SemaphoreType.DMA
    widths = (width + 2 * states,) * 2
    outs = {f"full_{k}": ((2, sections, QUAD, 16, w), BF16) for k, w in enumerate(widths)}
    outs.update(
        late=((sections, 16, 128), F32), upper_norm=((8, 128), F32), mixed=((2, rows, 128), BF16), token_grad=((2, rows, 128), F32)
    )
    scratch = dict(
        sum_own=vmem((len(SUM_ROWS), 24, 128), F32),
        sum_sibling=vmem((len(SUM_ROWS), 24, 128), F32),
        sum_slots=vmem((len(SUM_ROWS), min(dp, max(chips, 8)), 24, 128), F32),
        late_own=vmem((sections, 16, 128), F32),
        late_sem=dma((2,)),
        sum_sem=dma((first_sems(cfg)[-1],)),
        grad_send=dma((2, 5 + (groups > 1))),
        grad_recv=dma((2, 1 + 3 * (PART_SEMS + (groups > 1)))),
        fetch_sem=dma((9,)),
        lengths=pltpu.SMEM((2, 2), jnp.int32),
        tokens=vmem((2, rows, width), BF16),
        wide_par=vmem((4, 2, width), F32),
        state_par=vmem((3, 2, states // 2), F32),
        b_in=vmem((2, width, states), BF16),
        c_out=vmem((2, states, width), BF16),
        gmat=vmem((2, width, width), BF16),
        out_grad=vmem((2, rows, width), BF16),
        widen=vmem((states, 2 * lanes), BF16),
        q=vmem((2, rows, 2 * lanes), F32),
        spread=vmem((rows, rows), BF16),
        gather=vmem((rows, rows), BF16),
        first_in=vmem((2, rows, width), BF16),
        out_grads=vmem((2, rows, width), BF16),
        second_in=vmem((2, rows, width), F32),
        grad_second=vmem((2, rows, width), BF16),
        valid=vmem((2, rows, 128), F32),
        keep_start=vmem((2, rows, 128), F32),
        keep_end=vmem((2, rows, 128), F32),
        par=vmem((SUB, lanes), F32),
        b_pad=vmem((2, width, 2 * lanes), BF16),
        c_pad=vmem((2, 2 * lanes, width), BF16),
        normed=vmem((2, 2, rows, width), F32),
        scaled=vmem((2, 2 * rows, width), BF16),
        drive=vmem((2, 2, rows, 2 * lanes), F32),
        state=vmem((2, 2, (steps + 1) * SUB, 2 * lanes), F32),
        joined=vmem((2, 2 * rows, 2 * lanes), BF16),
        work=vmem((2, rows, width), F32),
        active=vmem((2, 2, rows, width), F32),
        active_low=vmem((2, 2 * rows, width), BF16),
        slope=vmem((2, 2, rows, width), F32),
        sig=vmem((2, 2, rows, width), F32),
        through=vmem((2, rows, width), F32),
        grad_logits=vmem((2, 2 * rows, width), BF16),
        branch=vmem((2, 2 * rows, width), BF16),
        grad_drive=vmem((2, 2 * rows, states), BF16),
        grad_scaled=vmem((2, 2, rows, width), F32),
        state_sums=vmem((2, 2, 4, SUB, lanes), F32),
        narrow=vmem((rows, 128), BF16),
        narrow_rest=vmem((rows, 128), BF16),
        rows=vmem((SUB, width), F32),
    )
    for k, w in enumerate(widths):
        blocks = (2, QUAD), (QUAD,), (QUAD,), (QUAD,), (groups,)
        for part, block in zip(STAGES, blocks):
            scratch[f"{part}_{k}"] = vmem((*block, 16, w), BF16)
    in_vmem = pl.BlockSpec(memory_space=pltpu.VMEM)
    in_hbm = pl.BlockSpec(memory_space=pltpu.HBM)
    names = tuple(f"{name}_far" for name in INPUTS) + tuple(outs) + tuple(scratch)
    made = pl.pallas_call(
        partial(main_kernel, cfg, names),
        name="layers",
        out_shape=[vmem(*spec) for spec in outs.values()],
        in_specs=[in_hbm for name in INPUTS],
        out_specs=[in_vmem for name in outs],
        scratch_shapes=list(scratch.values()),
        compiler_params=pltpu.CompilerParams(
            collective_id=0, has_side_effects=True, vmem_limit_bytes=56 * 2**20
        ),
    )(*args)
    shapes = [
        ((2, rows, 128), BF16),
        ((2, rows, 128), F32),
        ((2, width), F32),
        ((2, width), F32),
        ((2, states // 2), F32),
        ((2, states // 2), F32),
        ((2, states // 2), F32),
        ((2, width, states), F32),
        ((2, states, width), F32),
        ((2, width), F32),
        ((2, width, width), F32),
        ((2, width), F32),
    ]
    by_copy = (7, 8, 10)
    return pl.pallas_call(
        partial(lay_out_kernel, cfg),
        name="lay_out",
        out_shape=[jax.ShapeDtypeStruct(*spec) for spec in shapes],
        in_specs=[in_vmem] * 6,
        out_specs=[in_hbm] * 12,
        scratch_shapes=[vmem(*shapes[k]) for k in by_copy]
        + [vmem((2, width), F32)] * 4
        + [vmem((2, states // 2), F32)] * 3
        + [dma((12,))],
        compiler_params=pltpu.CompilerParams(vmem_limit_bytes=24 * 2**20),
    )(*made)


def solution(mesh):
    sections, dp = mesh.shape["section"], mesh.shape["dp"]

    def run(*args):
        _, rows, width = args[0].shape
        states = args[8].shape[2]
        cfg = SimpleNamespace(
            rows=rows // dp,
            width=width,
            states=states,
            half=states // 2,
            lanes=-(-states // 256) * 128,
            sections=sections,
            dp=dp,
        )
        split = P(None, "dp", None)
        shared = P()
        placed = P(None, "dp", "section")
        return jax.shard_map(
            partial(per_device, cfg),
            mesh=mesh,
            in_specs=(split, P(None, "dp"), split) + (shared,) * 10,
            out_specs=(placed, placed) + (shared,) * 10,
            check_vma=False,
        )(*args)

    return run
```

```python
from functools import partial
from types import SimpleNamespace

import jax
import jax.numpy as jnp
from jax import lax
from jax.experimental import pallas as pl
from jax.experimental.pallas import tpu as pltpu
from jax.sharding import PartitionSpec as P

epsilon = 1e-05
MESH = pl.DeviceIdType.MESH
F32 = jnp.float32
BF16 = jnp.bfloat16
SUB = 8
QUAD = 4
PART_SEMS = 9
LATE_STATES = 3
SUM_ROWS = (10, 8, 8, 8, 8, 8, 16)


STAGES = tuple(dict(mine=0, theirs=0, chip=0, quad=0, group=0, full=0))


def matmul(left, right):
    return jnp.dot(left, right, preferred_element_type=F32)


def matmul_nt(left, right):
    return lax.dot_general(left, right, (((1,), (1,)), ((), ())), preferred_element_type=F32)


def matmul_tn(left, right):
    return lax.dot_general(left, right, (((0,), (0,)), ((), ())), preferred_element_type=F32)


def cmul(ar, ai, br, bi):
    return ar * br - ai * bi, ar * bi + ai * br


def sweep(count, body, carry):
    for t in range(count):
        carry = body(t, carry)
    return carry


def repeat_lanes(x, times):
    return jnp.concatenate([x] * times, axis=1)


def fold_rows(x):
    return jnp.sum(x.reshape(x.shape[0] // SUB, SUB, x.shape[1]), axis=0)


def unfold(total, first, count):
    return jnp.concatenate([total[first + k : first + k + 1, :] for k in range(count)], axis=1)


def landed(block, sem):
    pltpu.make_async_copy(block, block, sem).wait()


def remote(src, dst, send_sem, recv_sem, device):
    pltpu.make_async_remote_copy(
        src_ref=src,
        dst_ref=dst,
        send_sem=send_sem,
        recv_sem=recv_sem,
        device_id=device,
        device_id_type=MESH,
    ).start()


def first_sems(cfg):
    begins = [0]
    for k in range(len(SUM_ROWS)):
        begins.append(begins[-1] + (2 if cfg.dp <= 8 and k < len(SUM_ROWS) - 1 else 4))
    return begins


class SmallSum:
    def __init__(self, place, direct, own, sibling, slots, sems):
        self.place, self.direct = place, direct
        self.own, self.sibling, self.slots, self.sems = own, sibling, slots, sems

    def to_all(self, slot, members, peer):
        self.members = members
        block = self.slots.at[slot]
        for step in range(1, members):
            to = (self.place.section, peer(step))
            remote(block, block, self.sems.at[0], self.sems.at[1], to)

    def start(self):
        at = self.place
        if self.direct:
            self.slots[at.dp] = self.own[...]
            self.to_all(at.dp, at.devices, at.dp_peer)
        else:
            to = (at.section, at.sibling)
            remote(self.own, self.sibling, self.sems.at[2], self.sems.at[3], to)

    def turn(self):
        at = self.place
        if not self.direct:
            landed(self.sibling, self.sems.at[3])
            self.slots[at.chip] = self.own[...] + self.sibling[...]
            self.to_all(at.chip, at.chips, at.chip_peer)

    def total(self):
        landed(self.slots.at[0 : self.members - 1], self.sems.at[1])
        result = self.slots[0]
        for member in range(1, self.members):
            result = result + self.slots[member]
        return result

    def end(self):
        if not self.direct:
            landed(self.own, self.sems.at[2])
        landed(self.slots.at[0 : self.members - 1], self.sems.at[0])


class GradSum:
    def __init__(self, place, parts, refs, send_sems, recv_sems):
        self.place, self.parts = place, parts
        self.mine, self.theirs, self.chip_part, self.quad_in, self.group_in, self.full = refs
        self.send_sems, self.recv_sems = send_sems, recv_sems

    def recv(self, part, k):
        if k == PART_SEMS:
            return self.recv_sems.at[1 + 3 * PART_SEMS + part]
        return self.recv_sems.at[1 + part * PART_SEMS + k]

    def send(self, part, src, dst, send, recv, device):
        columns = self.parts[part]
        sem = self.recv_sems.at[0] if recv is None else self.recv(part, recv)
        remote(src.at[..., columns], dst.at[..., columns], self.send_sems.at[send], sem, device)

    def landed(self, part, block, k):
        landed(block.at[..., self.parts[part]], self.recv(part, k))

    def to_core(self, part):
        at = self.place
        self.send(part, self.mine.at[1 - at.core], self.theirs, 0, 0, (at.section, at.sibling))

    def to_quad(self, part):
        at, columns = self.place, self.parts[part]
        self.landed(part, self.theirs, 0)
        for k in range(QUAD):
            both = self.mine[at.core, k, :, columns].astype(F32)
            both = both + self.theirs[k, :, columns].astype(F32)
            self.chip_part[k, :, columns] = both.astype(BF16)
        for step in range(1, QUAD):
            other = lax.rem(at.quad + step, QUAD)
            to = (at.section, at.quad_peer(step))
            self.send(part, self.chip_part.at[other], self.quad_in.at[at.quad], 1, 1, to)
        self.quad_in[at.quad, :, columns] = self.chip_part[at.quad, :, columns]

    def to_groups(self, part):
        at, columns = self.place, self.parts[part]
        self.landed(part, self.quad_in.at[0 : QUAD - 1], 1)
        total = self.quad_in[0, :, columns].astype(F32)
        for k in range(1, QUAD):
            total = total + self.quad_in[k, :, columns].astype(F32)
        if at.groups > 1:
            mine = self.group_in.at[at.group]
            mine[:, columns] = total.astype(BF16)
            for step in range(1, at.groups):
                self.send(part, mine, mine, 7, PART_SEMS, (at.section, at.chip_peer(step * QUAD)))
            self.landed(part, self.group_in.at[0 : at.groups - 1], PART_SEMS)
            total = self.group_in[0, :, columns].astype(F32)
            for other in range(1, at.groups):
                total = total + self.group_in[other, :, columns].astype(F32)
        piece = self.full.at[at.core, at.section, at.quad]
        piece[:, columns] = total.astype(BF16)
        self.to_members(part)
        self.over_sections(part, at.quad)

    def to_members(self, part):
        at = self.place
        piece = self.full.at[at.core, at.section, at.quad]
        for step in range(1, QUAD):
            self.send(part, piece, piece, 2, 1 + step, (at.section, at.quad_peer(step)))

    def over_sections(self, part, quad):
        at = self.place
        piece = self.full.at[at.core, at.section, quad]
        for k in (1, 2, 3):
            self.send(part, piece, piece, 3, 4 + k, (at.beyond(k), at.dp))

    def to_sections(self, part):
        at = self.place
        for step in range(1, QUAD):
            other = lax.rem(at.quad + QUAD - step, QUAD)
            self.landed(part, self.full.at[at.core, at.section, other], 1 + step)
            self.over_sections(part, other)
        self.to_other(part, at.section)

    def to_other(self, part, section):
        at = self.place
        block = self.full.at[at.core, section]
        self.send(part, block, block, 4, None, (at.section, at.sibling))

    def to_sibling(self, part):
        at = self.place
        for k in (1, 2, 3):
            self.landed(part, self.full.at[at.core, at.beyond(k)], 4 + k)
            self.to_other(part, at.beyond(k))

    def end(self):
        at = self.place
        landed(self.full.at[1 - at.core], self.recv_sems.at[0])
        landed(self.theirs, self.send_sems.at[0])
        landed(self.quad_in.at[0 : QUAD - 1], self.send_sems.at[1])
        landed(self.quad_in.at[0 : QUAD - 1], self.send_sems.at[2])
        self.end_sections()
        landed(self.full.at[at.core], self.send_sems.at[4])
        if at.groups > 1:
            landed(self.group_in.at[0 : at.groups - 1], self.send_sems.at[7])


    def end_sections(self):
        at = self.place
        landed(self.full.at[at.core, 0 : at.sections - 1], self.send_sems.at[3])


class CornerSum(GradSum):
    def to_groups(self, part):
        super().to_groups(part)
        at = self.place
        piece = self.full.at[at.core, at.section, at.quad]
        self.send(part, piece, piece, 5, 7, (at.beyond(3), at.dp))

    def over_sections(self, part, quad):
        at = self.place
        piece = self.full.at[at.core, at.section, quad]
        for k in (1, 2):
            self.send(part, piece, piece, 3, 4 + k, (at.beyond(k), at.dp))

    def to_corner(self, part):
        at = self.place
        piece = self.full.at[at.core, at.beyond(3), at.quad]
        self.landed(part, piece, 7)
        for step in range(1, QUAD):
            self.send(part, piece, piece, 6, 8, (at.section, at.quad_peer(step)))

    def to_sibling(self, part):
        at = self.place
        for k in (1, 2):
            self.landed(part, self.full.at[at.core, at.beyond(k)], 4 + k)
            self.to_other(part, at.beyond(k))
        self.landed(part, self.full.at[at.core, at.beyond(3), 0 : QUAD - 1], 8)
        self.to_other(part, at.beyond(3))

    def end_sections(self):
        at = self.place
        landed(self.full.at[at.core, 0:2], self.send_sems.at[3])
        landed(self.full.at[at.core, 0, 0], self.send_sems.at[5])
        landed(self.full.at[at.core, 0, 0 : QUAD - 1], self.send_sems.at[6])


class RelaySum(GradSum):
    def to_members(self, part):
        at = self.place
        piece = self.full.at[at.core, at.section, at.quad]
        self.send(part, piece, piece, 2, 2, (at.section, at.apart(2)))
        self.send(part, piece, piece, 2, 3, (at.section, at.apart(1)))

    def to_near(self, part):
        at = self.place
        far = 2 * (1 - at.high) + at.low
        piece = self.full.at[at.core, at.section, far]
        self.landed(part, piece, 2)
        self.send(part, piece, piece, 2, 4, (at.section, at.apart(1)))
        self.over_sections(part, far)
        near = 2 * at.high + 1 - at.low
        self.landed(part, self.full.at[at.core, at.section, near], 3)
        self.over_sections(part, near)

    def to_sections(self, part):
        at = self.place
        last = 2 * (1 - at.high) + 1 - at.low
        self.landed(part, self.full.at[at.core, at.section, last], 4)
        self.over_sections(part, last)
        self.to_other(part, at.section)


def main_kernel(cfg, names, *refs):
    r = SimpleNamespace(**dict(zip(names, refs)))
    rows, width, states, half, lanes = (
        cfg.rows,
        cfg.width,
        cfg.states,
        cfg.half,
        cfg.lanes,
    )
    steps = rows // SUB
    section = lax.axis_index("section")
    dp = lax.axis_index("dp")
    chips = cfg.dp // 2
    core, chip = lax.rem(dp, 2), lax.div(dp, 2)
    quad, group = lax.rem(chip, QUAD), lax.div(chip, QUAD)
    beyond = {
        1: section + 1 - 2 * lax.rem(section, 2),
        2: section + 2 - 4 * lax.div(section, 2),
        3: 3 - section,
    }
    place = SimpleNamespace(
        section=section,
        beyond=lambda k: beyond[k],
        sections=cfg.sections,
        dp=dp,
        core=core,
        chip=chip,
        chips=chips,
        quad=quad,
        group=group,
        groups=chips // QUAD,
        devices=cfg.dp,
        dp_peer=lambda step: lax.rem(dp + step, cfg.dp),
        sibling=dp + 1 - 2 * core,
        chip_peer=lambda step: lax.rem(chip + step, chips) * 2 + core,
        high=lax.div(quad, 2),
        low=lax.rem(quad, 2),
        apart=lambda by: (
            chip + by * (1 - 2 * (lax.rem(quad, 2) if by == 1 else lax.div(quad, 2)))
        )
        * 2
        + core,
        quad_peer=lambda step: (group * QUAD + lax.rem(quad + step, QUAD)) * 2 + core,
    )

    direct = cfg.dp <= 8
    if direct:
        peers = [(section, place.dp_peer(step)) for step in range(1, cfg.dp)]
    else:
        peers = [(section, place.sibling)]
        peers += [(section, place.chip_peer(step)) for step in range(1, chips)]
    peers += [(beyond[k], dp) for k in (1, 2, 3)]
    barrier = pltpu.get_barrier_semaphore()
    for peer in peers:
        pl.semaphore_signal(barrier, inc=1, device_id=peer, device_id_type=MESH)

    sum_sems = first_sems(cfg)
    small = [
        SmallSum(
            place,
            direct and k < len(SUM_ROWS) - 1,
            r.sum_own.at[k, 0:tall] if k < len(SUM_ROWS) - 1 else r.late_own.at[section],
            r.sum_sibling.at[k, 0:tall],
            r.sum_slots.at[k, :, 0:tall],
            r.sum_sem.at[sum_sems[k] : sum_sems[k + 1]],
        )
        for k, tall in enumerate(SUM_ROWS)
    ]
    first_sum, mid_sum, upper_sum = small[0:2], small[2:4], small[4:6]
    late_sum = small[6]
    gate_part, out_part, in_part = range(3)
    bounds = (0, width, width + states, width + 2 * states)
    batches = [
        (RelaySum if k == 0 else CornerSum)(
            place,
            [slice(*bounds[k : k + 2]) for k in range(3)],
            [getattr(r, f"{part}_{k}") for part in STAGES],
            r.grad_send.at[k],
            r.grad_recv.at[k],
        )
        for k in range(2)
    ]
    upper, lower = batches

    r.gain, r.bias, r.skip, r.gbias = [r.wide_par.at[k] for k in range(4)]
    r.decay, r.freq, r.lstep = [r.state_par.at[k] for k in range(3)]
    wide_far = (r.gain_far, r.bias_far, r.skip_far, r.gbias_far)
    state_far = (r.decay_far, r.freq_far, r.lstep_far)
    fetches = [[(r.lengths_far, r.lengths)]]
    fetches += [[(r.tokens_far.at[m], r.tokens.at[m])] for m in range(2)]
    fetches += [[(far, r.state_par.at[k]) for k, far in enumerate(state_far)]]
    fetches += [[(r.b_in_far, r.b_in)], [(r.out_grad_far, r.out_grad)], [(r.c_out_far, r.c_out)]]
    fetches += [[(far, r.wide_par.at[k]) for k, far in enumerate(wide_far)]]
    fetches += [[(r.gmat_far, r.gmat)]]
    for k, group_of in enumerate(fetches):
        for far, held in group_of:
            pltpu.make_async_copy(far, held, r.fetch_sem.at[k]).start()
    landed(r.lengths, r.fetch_sem.at[0])

    first_len = [r.lengths[m, 0] for m in range(2)]
    total_len = [r.lengths[m, 0] + r.lengths[m, 1] for m in range(2)]

    def put(index, at, row):
        for k in range(row.shape[1] // 128):
            r.sum_own[index, at + k : at + k + 1, :] = row[:, k * 128 : (k + 1) * 128]

    def put_late(at, row):
        for k in range(cfg.sections):
            r.late_own[k, at : at + 1, :] = row[:, k * 128 : (k + 1) * 128]

    chunk = 32
    for m in range(2):

        landed(r.tokens.at[m], r.fetch_sem.at[1 + m])

        def token_sums(t, carry, m=m):
            at = pl.ds(t * chunk, chunk)
            v = r.tokens[m, at, :].astype(F32)
            place_row = t * chunk + lax.broadcasted_iota(jnp.int32, (chunk, width), 0)
            kept = jnp.where(place_row < total_len[m], v, 0.0)
            return carry[0] + fold_rows(kept), carry[1] + fold_rows(kept * v)

        zero = jnp.zeros((SUB, width), F32)
        sums, squares = sweep(rows // chunk, token_sums, (zero, zero))
        put(m, 0, jnp.sum(sums, axis=0, keepdims=True))
        put(m, 4, jnp.sum(squares, axis=0, keepdims=True))
        if m == 0:
            for k in range(2):
                count = jnp.minimum(total_len[k], rows).astype(F32)
                r.sum_own[0, 8 + k : 9 + k, :] = jnp.full((1, 128), count, F32)
            pl.semaphore_wait(barrier, len(peers))
        first_sum[m].start()

    at_i = lax.broadcasted_iota(jnp.int32, (rows, rows), 0)
    at_r = lax.broadcasted_iota(jnp.int32, (rows, rows), 1)
    r.spread[...] = jnp.where(
        at_r == (at_i % SUB) * steps + at_i // SUB, 1.0, 0.0
    ).astype(BF16)
    r.gather[...] = jnp.where(
        at_i == (at_r % SUB) * steps + at_r // SUB, 1.0, 0.0
    ).astype(BF16)
    for m in range(2):
        r.first_in[m] = matmul(r.spread[...], r.tokens[m]).astype(BF16)
    for m in range(2):
        first_sum[m].turn()
    landed(r.out_grad, r.fetch_sem.at[5])
    for m in range(2):
        r.out_grads[m] = matmul(r.spread[...], r.out_grad[m]).astype(BF16)
    held = lax.broadcasted_iota(jnp.int32, (rows, 128), 0)
    held = (held % SUB) * steps + held // SUB
    all_start, all_end = [], []
    for m in range(2):
        one, zero = jnp.float32(1.0), jnp.float32(0.0)
        past = held >= total_len[m]
        starts = (held == 0) | (held == first_len[m]) | past
        ends = (held == first_len[m] - 1) | (held == total_len[m] - 1) | past | (held == rows - 1)
        r.valid[m] = jnp.where(past, zero, one)
        r.keep_start[m] = jnp.where(starts, zero, one)
        r.keep_end[m] = jnp.where(ends, zero, one)
        for kept, mask in ((all_start, r.keep_start), (all_end, r.keep_end)):
            kept.append(jnp.min(mask[m].reshape(steps, SUB, 128), axis=0))

    r.par[...] = jnp.zeros((SUB, lanes), F32)
    r.par[0:2, :] = jnp.ones((2, lanes), F32)
    landed(r.state_par, r.fetch_sem.at[3])
    r.par[0:2, 0:half] = r.decay[...]
    r.par[2:4, 0:half] = r.freq[...]
    r.par[4:6, 0:half] = r.lstep[...]
    decay, spin = r.par[0:2, :], r.par[2:4, :]
    step_size = jnp.exp(r.par[4:6, :])
    damping = jnp.exp(-decay * step_size)
    bar_re = damping * jnp.cos(spin * step_size)
    bar_im = damping * jnp.sin(spin * step_size)
    modulus = decay * decay + spin * spin
    fac_re = ((bar_re - 1.0) * -decay + bar_im * spin) / modulus
    fac_im = (bar_im * -decay - (bar_re - 1.0) * spin) / modulus
    pow_re, pow_im = bar_re, bar_im
    power = 1
    while power < steps:
        pow_re, pow_im = cmul(pow_re, pow_im, pow_re, pow_im)
        power *= 2

    lane = lax.broadcasted_iota(jnp.int32, (1, 128), 1)
    low_lanes = lane < half - 128
    turn_by = half - 128

    from_column = lax.broadcasted_iota(jnp.int32, (states, 2 * lanes), 0)
    to_column = lax.broadcasted_iota(jnp.int32, (states, 2 * lanes), 1)
    moved_to = jnp.where(from_column < half, from_column, from_column + (lanes - half))
    r.widen[...] = jnp.where(to_column == moved_to, 1.0, 0.0).astype(BF16)
    for held, k in ((r.b_in, 4), (r.c_out, 6), (r.wide_par, 7), (r.gmat, 8)):
        landed(held, r.fetch_sem.at[k])
    for l in range(2):
        r.b_pad[l] = matmul(r.b_in[l], r.widen[...]).astype(BF16)
        blank = jnp.zeros((lanes - half, width), BF16)
        r.c_pad[l, 0:half, :] = r.c_out[l, 0:half, :]
        r.c_pad[l, half:lanes, :] = blank
        r.c_pad[l, lanes : lanes + half, :] = r.c_out[l, half:states, :]
        r.c_pad[l, lanes + half : 2 * lanes, :] = blank

    def across(end, coef, reverse):
        end_re, end_im = end
        coef_re, coef_im = coef
        sub = lax.broadcasted_iota(jnp.int32, (SUB, lanes), 0)
        for by in (1, 2, 4):
            turn = SUB - by if reverse else by
            live = sub < SUB - by if reverse else sub >= by

            def moved(x):
                return jnp.where(live, pltpu.roll(x, turn, 0), 0.0)

            add_re, add_im = cmul(coef_re, coef_im, moved(end_re), moved(end_im))
            coef_re, coef_im = cmul(coef_re, coef_im, moved(coef_re), moved(coef_im))
            end_re, end_im = end_re + add_re, end_im + add_im
        turn = SUB - 1 if reverse else 1
        live = sub < SUB - 1 if reverse else sub >= 1
        return tuple(jnp.where(live, pltpu.roll(x, turn, 0), 0.0) for x in (end_re, end_im))

    def wide8(x, l):
        return jnp.broadcast_to(x[l : l + 1, :], (SUB, x.shape[1]))

    def group_rows(p):
        return pl.ds(p * SUB, SUB)

    def scan_coefs(l, m, reverse):
        keep = r.keep_end if reverse else r.keep_start
        all_kept = repeat_lanes((all_end if reverse else all_start)[m], lanes // 128)
        product = (all_kept * wide8(pow_re, l), all_kept * wide8(pow_im, l))
        return keep, wide8(bar_re, l), wide8(bar_im, l), product

    def advance(keep, m, at, br, bi, re, im, src_re, src_im):
        k = repeat_lanes(keep[m, at, :], lanes // 128)
        kr, ki = k * br, k * bi
        return kr * re - ki * im + src_re, kr * im + ki * re + src_im

    def scan_states(l, m):
        reverse = l == 1
        lead = 0 if reverse else 1
        keep, br, bi, product = scan_coefs(l, m, reverse)
        fr, fi = wide8(fac_re, l), wide8(fac_im, l)
        zero = jnp.zeros((SUB, lanes), F32)

        def ends(t, carry):
            p = steps - 1 - t if reverse else t
            at = group_rows(p)
            v = repeat_lanes(r.valid[m, at, :], lanes // 128)
            drive_re = r.drive[l, m, at, 0:lanes]
            drive_im = r.drive[l, m, at, lanes : 2 * lanes]
            src_re, src_im = cmul(fr, fi, v * drive_re, v * drive_im)
            r.state[l, m, group_rows(p + lead), 0:lanes] = src_re
            r.state[l, m, group_rows(p + lead), lanes : 2 * lanes] = src_im
            return advance(keep, m, at, br, bi, *carry, src_re, src_im)

        end = sweep(steps, ends, (zero, zero))
        enter = across(end, product, reverse)
        first = steps if reverse else 0
        r.state[l, m, first * SUB : (first + 1) * SUB, 0:lanes] = enter[0]
        r.state[l, m, first * SUB : (first + 1) * SUB, lanes : 2 * lanes] = enter[1]

        def fill(t, carry):
            done = []
            for k in range(2):
                p = steps - 1 - (2 * t + k) if reverse else 2 * t + k
                at, to = group_rows(p), group_rows(p + lead)
                src_re = r.state[l, m, to, 0:lanes]
                src_im = r.state[l, m, to, lanes : 2 * lanes]
                carry = advance(keep, m, at, br, bi, *carry, src_re, src_im)
                r.state[l, m, to, 0:lanes] = carry[0]
                r.state[l, m, to, lanes : 2 * lanes] = carry[1]
                done.append(jnp.concatenate([carry[0], -carry[1]], axis=1))
            pair = steps // 2 - 1 - t if reverse else t
            both = jnp.concatenate(done[::-1] if reverse else done, axis=0)
            to = pl.ds(m * rows + pair * 16, 16)
            r.joined[l, to, :] = both.astype(BF16)
            return carry

        sweep(steps // 2, fill, enter)

    def scan_grads(l, m):
        reverse = l == 0
        back = 1 if l == 1 else 0
        keep, br, bi, product = scan_coefs(l, m, reverse)
        keep_state = r.keep_start if l == 0 else r.keep_end
        fr, fi = 2.0 * wide8(fac_re, l), 2.0 * wide8(fac_im, l)
        zero = jnp.zeros((SUB, lanes), F32)

        def ends(t, carry):
            p = steps - 1 - t if reverse else t
            at = group_rows(p)
            q_re = r.q[m, at, 0:lanes]
            q_im = r.q[m, at, lanes : 2 * lanes]
            return advance(keep, m, at, br, bi, *carry, q_re, q_im)

        end = sweep(steps, ends, (zero, zero))
        enter = across(end, product, reverse)

        def fill(t, carry):
            w, bar_sum, fac_sum = carry
            done = []
            for k in range(2):
                p = steps - 1 - (2 * t + k) if reverse else 2 * t + k
                at, near = group_rows(p), group_rows(p + back)
                q_re = r.q[m, at, 0:lanes]
                q_im = r.q[m, at, lanes : 2 * lanes]
                w = advance(keep, m, at, br, bi, *w, q_re, q_im)
                kept = repeat_lanes(keep_state[m, at, :], lanes // 128)
                near_re = kept * r.state[l, m, near, 0:lanes]
                near_im = kept * r.state[l, m, near, lanes : 2 * lanes]
                term = cmul(*w, near_re, near_im)
                bar_sum = (bar_sum[0] + term[0], bar_sum[1] + term[1])
                v = repeat_lanes(r.valid[m, at, :], lanes // 128)
                vw = (v * w[0], v * w[1])
                drive_re = r.drive[l, m, at, 0:lanes]
                drive_im = r.drive[l, m, at, lanes : 2 * lanes]
                term = cmul(*vw, drive_re, drive_im)
                fac_sum = (fac_sum[0] + term[0], fac_sum[1] + term[1])
                gd_re, gd_im = cmul(fr, fi, *vw)
                im_low = pltpu.roll(-gd_im[:, 0:128], 64, 1)
                im_high = pltpu.roll(-gd_im[:, 128:256], 64, 1)
                done.append(
                    jnp.concatenate(
                        [
                            gd_re[:, 0:128],
                            jnp.where(low_lanes, gd_re[:, 128:256], im_low),
                            jnp.where(low_lanes, im_low, im_high),
                        ],
                        axis=1,
                    )
                )
            pair = steps // 2 - 1 - t if reverse else t
            both = jnp.concatenate(done[::-1] if reverse else done, axis=0)
            to = pl.ds(m * rows + pair * 16, 16)
            r.grad_drive[l, to, :] = both.astype(BF16)
            return w, bar_sum, fac_sum

        none = (zero, zero)
        _, bar_sum, fac_sum = sweep(steps // 2, fill, (enter, none, none))
        for k, part in enumerate((*bar_sum, *fac_sum)):
            r.state_sums[l, m, k] = part

    def row_of(ref, l):
        return ref[l : l + 1, :]

    def micro_rows(m):
        return slice(m * rows, (m + 1) * rows)

    gelu_chunk = 16

    def mixer(l, m, center, inv):
        gain, bias, skip = row_of(r.gain, l), row_of(r.bias, l), row_of(r.skip, l)

        def normalise(t, carry):
            at = pl.ds(t * chunk, chunk)
            if l == 0:
                v = r.first_in[m, at, :].astype(F32)
            else:
                v = r.second_in[m, at, :]
            normed = (v - center) * inv
            r.normed[l, m, at, :] = normed
            to = pl.ds(m * rows + t * chunk, chunk)
            r.scaled[l, to, :] = (normed * gain + bias).astype(BF16)
            return carry

        sweep(rows // chunk, normalise, 0)
        yield
        r.drive[l, m] = matmul(r.scaled[l, micro_rows(m), :], r.b_pad[l])
        yield
        scan_states(l, m)
        yield
        r.work[m] = matmul(r.joined[l, micro_rows(m), :], r.c_pad[l])

        yield

        def activate(t, carry):
            at = pl.ds(t * gelu_chunk, gelu_chunk)
            scaled = r.normed[l, m, at, :] * gain + bias
            y = (2.0 * r.work[m, at, :] + skip * scaled).astype(BF16).astype(F32)
            below = 0.5 + 0.5 * lax.erf(y * 0.7071067811865476)
            density = jnp.exp(-0.5 * y * y) * 0.3989422804014327
            active = y * below
            r.active[l, m, at, :] = active
            r.slope[l, m, at, :] = below + y * density
            to = pl.ds(m * rows + t * gelu_chunk, gelu_chunk)
            r.active_low[l, to, :] = active.astype(BF16)
            return carry

        sweep(rows // gelu_chunk, activate, 0)
        yield
        r.work[m] = matmul(r.active_low[l, micro_rows(m), :], r.gmat[l])

    def first_gate(m):
        gbias = row_of(r.gbias, 0)

        def gate(t, carry):
            at = pl.ds(t * gelu_chunk, gelu_chunk)
            opened = jax.nn.sigmoid(r.work[m, at, :] + gbias)
            r.sig[0, m, at, :] = opened
            v = repeat_lanes(r.valid[m, at, :], width // 128)
            gated = v * r.active[0, m, at, :] * opened
            second = r.first_in[m, at, :].astype(F32) + gated.astype(BF16).astype(F32)
            r.second_in[m, at, :] = second
            kept = v * second
            return carry[0] + fold_rows(kept), carry[1] + fold_rows(kept * second)

        zero = jnp.zeros((SUB, width), F32)
        sums, squares = sweep(rows // gelu_chunk, gate, (zero, zero))
        put(2 + m, 0, jnp.sum(sums, axis=0, keepdims=True))
        put(2 + m, 4, jnp.sum(squares, axis=0, keepdims=True))

    bias_sums = {}
    skip_sums = {}

    def gate_grad(l, m, grad_of):
        gbias = row_of(r.gbias, l)

        def gate(t, carry):
            at = pl.ds(t * gelu_chunk, gelu_chunk)
            if l == 1:
                opened = jax.nn.sigmoid(r.work[m, at, :] + gbias)
                r.sig[1, m, at, :] = opened
            else:
                opened = r.sig[0, m, at, :]
            v = repeat_lanes(r.valid[m, at, :], width // 128)
            masked = v * grad_of(at, v)
            through = masked * opened
            r.through[m, at, :] = through
            grad_logits = through * r.active[l, m, at, :] * (1.0 - opened)
            to = pl.ds(m * rows + t * gelu_chunk, gelu_chunk)
            r.grad_logits[l, to, :] = grad_logits.astype(BF16)
            return carry + fold_rows(grad_logits)

        zero = jnp.zeros((SUB, width), F32)
        bias_sums[l, m] = sweep(rows // gelu_chunk, gate, zero)
        yield

    def branch_grad(l, m):
        gain, bias = row_of(r.gain, l), row_of(r.bias, l)
        r.work[m] = matmul_nt(r.grad_logits[l, micro_rows(m), :], r.gmat[l])
        yield

        def branch(t, carry):
            at = pl.ds(t * chunk, chunk)
            grad_active = r.through[m, at, :] + r.work[m, at, :]
            g = (r.slope[l, m, at, :] * grad_active).astype(BF16)
            to = pl.ds(m * rows + t * chunk, chunk)
            r.branch[l, to, :] = g
            scaled = r.normed[l, m, at, :] * gain + bias
            return carry + fold_rows(g.astype(F32) * scaled)

        zero = jnp.zeros((SUB, width), F32)
        skip_sums[l, m] = sweep(rows // chunk, branch, zero)
        yield
        r.q[m] = matmul_nt(r.branch[l, micro_rows(m), :], r.c_pad[l])
        yield

    def mixer_grad(l, m):
        skip = row_of(r.skip, l)
        scan_grads(l, m)
        yield
        r.work[m] = matmul_nt(r.grad_drive[l, micro_rows(m), :], r.b_in[l])
        yield

        def scaled_grad(t, carry):
            at = pl.ds(t * chunk, chunk)
            to = pl.ds(m * rows + t * chunk, chunk)
            grad = r.work[m, at, :] + skip * r.branch[l, to, :].astype(F32)
            r.grad_scaled[l, m, at, :] = grad
            normed = r.normed[l, m, at, :]
            return carry[0] + fold_rows(grad), carry[1] + fold_rows(grad * normed)

        zero = jnp.zeros((SUB, width), F32)
        sums, products = sweep(rows // chunk, scaled_grad, (zero, zero))
        sums = jnp.sum(sums, axis=0, keepdims=True)
        products = jnp.sum(products, axis=0, keepdims=True)
        if l == 1:
            put(4 + m, 0, sums)
            put(4 + m, 4, products)
        else:
            put_late(2 * m, sums)
            put_late(2 * m + 1, products)

    def moments(total, at, count):
        center = unfold(total, at, 4) / count
        return center, lax.rsqrt(unfold(total, at + 4, 4) / count - center * center + epsilon)

    own_columns = pl.ds(pl.multiple_of(section * 128, 128), 128)

    def gate_weights(l, ref):
        grad = matmul_tn(r.active_low[l, :, own_columns], r.grad_logits[l])
        ref[:, :, :, 0:width] = grad.astype(BF16).reshape(2, QUAD, 16, width)

    def out_weights(l, ref, at):
        grad = 2.0 * matmul_tn(r.joined[l], r.branch[l, :, own_columns])
        grad = jnp.concatenate([grad[0:half, :], grad[lanes : lanes + half, :]], axis=0)
        tall = states // (2 * QUAD)
        for k in range(tall // 16):
            for c in range(2):
                for z in range(QUAD):
                    first = (c * QUAD + z) * tall + 16 * k
                    ref[c, z, :, at + 128 * k : at + 128 * (k + 1)] = grad[
                        first : first + 16, :
                    ].astype(BF16)

    def in_weights(l, ref, at):
        grad = matmul_tn(r.scaled[l, :, own_columns], r.grad_drive[l])
        ref[:, :, :, at : at + states] = grad.astype(BF16).reshape(2, QUAD, 16, states)

    def layer_rows(l):
        def both(sums):
            return jnp.sum(sums[l, 0] + sums[l, 1], axis=0, keepdims=True)

        put_late(4 + 2 * l, both(skip_sums))
        put_late(5 + 2 * l, both(bias_sums))
        part = [
            jnp.sum(r.state_sums[l, 0, k] + r.state_sums[l, 1, k], axis=0, keepdims=True)
            for k in range(4)
        ]
        gb_re, gb_im = 2.0 * part[0], -2.0 * part[1]
        gf_re, gf_im = 2.0 * part[2], -2.0 * part[3]
        one = slice(l, l + 1)
        lam_re, lam_im, size = -decay[one], spin[one], step_size[one]
        b_re, b_im, f_re, f_im = bar_re[one], bar_im[one], fac_re[one], fac_im[one]
        top_re, top_im = size * b_re - f_re, size * b_im - f_im
        square = modulus[one]
        d_re = (top_re * lam_re + top_im * lam_im) / square
        d_im = (top_im * lam_re - top_re * lam_im) / square
        gl_re = size * (b_re * gb_re + b_im * gb_im) + (d_re * gf_re + d_im * gf_im)
        gl_im = size * (b_re * gb_im - b_im * gb_re) + (d_re * gf_im - d_im * gf_re)
        e_re, e_im = cmul(lam_re, lam_im, b_re, b_im)
        g_step = size * ((e_re * gb_re + e_im * gb_im) + (b_re * gf_re + b_im * gf_im))
        parts = [
            row[:, k : k + 128] for row in (-gl_re, gl_im, g_step) for k in range(0, lanes, 128)
        ]
        for k, row in enumerate(parts):
            k += l * len(parts)
            at = 8 + k % LATE_STATES
            r.late_own[k // LATE_STATES, at : at + 1, :] = row

    def mixed_rows(m):
        def mix(t, carry):
            at = pl.ds(t * chunk, chunk)
            gated = (
                r.valid[m, at, :]
                * r.active[1, m, at, own_columns]
                * r.sig[1, m, at, own_columns]
            )
            stream = r.second_in[m, at, own_columns].astype(BF16).astype(F32)
            r.narrow[at, :] = (stream + gated).astype(BF16)
            return carry

        sweep(rows // chunk, mix, 0)
        r.mixed[m] = matmul(r.gather[...], r.narrow[...]).astype(BF16)

    def stream_grad(l, m, total, count, inv):
        gain = row_of(r.gain, l)
        first = gain * unfold(total, 0, 4) / count
        second = gain * unfold(total, 4, 4) / count
        return gain, first, second, inv

    def take(steps):
        for _ in steps:
            pass

    counts, norm0 = [None, None], [None, None]
    for m in range(2):
        total = first_sum[m].total()
        if m == 0:
            counts = [repeat_lanes(total[8 + k : 9 + k, :], width // 128) for k in range(2)]
        norm0[m] = moments(total, 0, counts[m])
        take(mixer(0, m, *norm0[m]))
        first_gate(m)
        mid_sum[m].start()
        mid_sum[m].turn()

    norm1 = [None, None]

    def second_layer(m):
        norm1[m] = moments(mid_sum[m].total(), 0, counts[m])
        yield from mixer(1, m, *norm1[m])
        yield from gate_grad(1, m, lambda at, v: r.out_grads[m, at, :].astype(F32))
        yield from branch_grad(1, m)
        yield from mixer_grad(1, m)
        upper_sum[m].start()
        upper_sum[m].turn()

    for m in range(2):
        take(second_layer(m))

    gate_weights(1, r.mine_0)
    upper.to_core(gate_part)
    out_weights(1, r.mine_0, width)
    upper.to_core(out_part)
    in_weights(1, r.mine_0, width + states)
    upper.to_core(in_part)
    layer_rows(1)

    def second_grad(m, total):
        gain, first, second, inv = stream_grad(1, m, total, counts[m], norm1[m][1])

        def grad_of(at, v):
            grad_normed = r.grad_scaled[1, m, at, :] * gain
            normed = r.normed[1, m, at, :]
            grad_stream = inv * (grad_normed - v * (first + normed * second))
            out_grad = r.out_grads[m, at, :].astype(F32)
            grad = (out_grad + grad_stream.astype(BF16).astype(F32)).astype(BF16)
            r.grad_second[m, at, :] = grad
            return grad.astype(F32)

        return grad_of

    upper_total = [upper_sum[0].total()]
    take(gate_grad(0, 0, second_grad(0, upper_total[0])))
    upper.to_quad(gate_part)
    take(branch_grad(0, 0))
    upper.to_quad(out_part)
    upper.to_quad(in_part)
    take(mixer_grad(0, 0))
    upper_total.append(upper_sum[1].total())
    take(gate_grad(0, 1, second_grad(1, upper_total[1])))
    gate_weights(0, r.mine_1)
    lower.to_core(gate_part)
    take(branch_grad(0, 1))
    out_weights(0, r.mine_1, width)
    lower.to_core(out_part)
    upper.to_groups(gate_part)
    lower.to_quad(gate_part)
    last = mixer_grad(0, 1)
    next(last)
    upper.to_groups(out_part)
    next(last)
    upper.to_groups(in_part)
    take(last)
    lower.to_quad(out_part)
    in_weights(0, r.mine_1, width + states)
    lower.to_core(in_part)
    layer_rows(0)
    late_sum.start()
    upper.to_near(gate_part)
    lower.to_quad(in_part)
    late_sum.turn()
    mixed_rows(0)
    lower.to_groups(gate_part)
    upper.to_near(out_part)
    upper.to_near(in_part)
    mixed_rows(1)
    lower.to_groups(out_part)
    upper.to_sections(gate_part)
    lower.to_groups(in_part)
    lower.to_corner(gate_part)
    upper.to_sections(out_part)
    upper.to_sections(in_part)
    lower.to_sections(gate_part)

    late = late_sum.total()
    r.late[section] = late
    block = r.late.at[section]
    for k in (1, 2, 3):
        remote(block, block, r.late_sem.at[0], r.late_sem.at[1], (beyond[k], dp))
    own_gain = r.gain[0:1, own_columns]
    for m in range(2):
        count = counts[m][:, 0:128]
        first = own_gain * late[2 * m : 2 * m + 1, :] / count
        second = own_gain * late[2 * m + 1 : 2 * m + 2, :] / count
        r.rows[m : m + 1, :] = norm0[m][1]
        inv = r.rows[m : m + 1, own_columns]

        def token_grad(t, carry, m=m, first=first, second=second, inv=inv):
            at = pl.ds(t * chunk, chunk)
            grad_normed = r.grad_scaled[0, m, at, own_columns] * own_gain
            normed = r.normed[0, m, at, own_columns]
            grad_stream = inv * (grad_normed - r.valid[m, at, :] * (first + normed * second))
            grad = r.grad_second[m, at, own_columns].astype(F32) + grad_stream
            high = grad.astype(BF16)
            r.narrow[at, :] = high
            r.narrow_rest[at, :] = (grad - high.astype(F32)).astype(BF16)
            return carry

        sweep(rows // chunk, token_grad, 0)
        r.token_grad[m] = matmul(r.gather[...], r.narrow[...]) + matmul(
            r.gather[...], r.narrow_rest[...]
        )
    r.upper_norm[...] = upper_total[0] + upper_total[1]
    lower.to_corner(out_part)
    lower.to_sections(out_part)
    lower.to_corner(in_part)
    lower.to_sections(in_part)
    upper.to_sibling(gate_part)
    upper.to_sibling(out_part)
    upper.to_sibling(in_part)
    lower.to_sibling(gate_part)
    lower.to_sibling(out_part)
    lower.to_sibling(in_part)
    for k in range(2):
        landed(r.late.at[0 : cfg.sections - 1], r.late_sem.at[k])
    for batch in batches:
        batch.end()
    for each in small:
        each.end()


def lay_out_kernel(cfg, *refs):
    full = refs[1], refs[0]
    late, upper_norm, mixed, token_grad = refs[2:6]
    (
        mixed_out,
        token_grad_out,
        gain_out,
        bias_out,
        decay_out,
        freq_out,
        step_out,
        in_out,
        out_out,
        skip_out,
        gate_out,
        gbias_out,
    ) = refs[6:18]
    in_held, out_held, gate_held = refs[18:21]
    rows_held, sems = refs[21:28], refs[28]
    width, states, half = cfg.width, cfg.states, cfg.half
    tall = states // (2 * QUAD)
    copies = []

    def send(held, out, sem=None):
        copy = pltpu.make_async_copy(held, out, sems.at[3 + len(copies) if sem is None else sem])
        copy.start()
        if sem is None:
            copies.append(copy)

    send(mixed, mixed_out)
    send(token_grad, token_grad_out)
    def columns(at):
        return jnp.concatenate([late[s, at : at + 1, :] for s in range(cfg.sections)], axis=1)

    row_outs = (bias_out, gain_out, skip_out, gbias_out, decay_out, freq_out, step_out)
    values = [
        (columns(0) + columns(2), unfold(upper_norm, 0, 4)),
        (columns(1) + columns(3), unfold(upper_norm, 4, 4)),
        (columns(4), columns(6)),
        (columns(5), columns(7)),
    ]
    for k in range(3):
        places = [(6 * l + 2 * k + part) for l in range(2) for part in range(2)]
        row = [late[p // LATE_STATES, 8 + p % LATE_STATES, :][None] for p in places]
        values.append([jnp.concatenate(row[2 * l : 2 * l + 2], axis=1)[:, 0:half] for l in range(2)])
    for held, out, value in zip(rows_held, row_outs, values):
        for l in range(2):
            held[l : l + 1, :] = value[l]
        send(held, out)

    for l in (1, 0):
        parts = [(full[l], begin) for begin in (0, width, width + states)]
        for s in range(cfg.sections):
            mine = slice(s * 128, (s + 1) * 128)
            members = [(c, z) for c in range(2) for z in range(QUAD)]
            for (part, begin), held, out, wide, sem in (
                (parts[0], gate_held, gate_out, width, 0),
                (parts[2], in_held, in_out, states, 1),
            ):
                for c, z in members:
                    at = s * 128 + (c * QUAD + z) * 16
                    held[l, at : at + 16, :] = part[c, s, z, :, begin : begin + wide].astype(F32)
                send(held.at[l, mine], out.at[l, mine], sem)
            part, begin = parts[1]
            for c, z in members:
                for k in range(tall // 16):
                    first = (c * QUAD + z) * tall + 16 * k
                    out_held[l, first : first + 16, mine] = part[
                        c, s, z, :, begin + k * 128 : begin + (k + 1) * 128
                    ].astype(F32)
        send(out_held.at[l], out_out.at[l], 2)
    for copy in copies:
        copy.wait()
    for sem, out in enumerate((gate_out, in_out, out_out)):
        landed(out, sems.at[sem])


INPUTS = tuple(
    dict(
        tokens=0,
        lengths=0,
        out_grad=0,
        gain=0,
        bias=0,
        decay=0,
        freq=0,
        lstep=0,
        b_in=0,
        c_out=0,
        skip=0,
        gmat=0,
        gbias=0,
    )
)


def per_device(cfg, *args):
    rows, width, states, lanes = cfg.rows, cfg.width, cfg.states, cfg.lanes
    sections, dp, chips = cfg.sections, cfg.dp, cfg.dp // 2
    groups = chips // QUAD
    steps = rows // SUB
    vmem, dma = pltpu.VMEM, pltpu.SemaphoreType.DMA
    widths = (width + 2 * states,) * 2
    outs = {f"full_{k}": ((2, sections, QUAD, 16, w), BF16) for k, w in enumerate(widths)}
    outs.update(
        late=((sections, 16, 128), F32), upper_norm=((8, 128), F32), mixed=((2, rows, 128), BF16), token_grad=((2, rows, 128), F32)
    )
    scratch = dict(
        sum_own=vmem((len(SUM_ROWS), 24, 128), F32),
        sum_sibling=vmem((len(SUM_ROWS), 24, 128), F32),
        sum_slots=vmem((len(SUM_ROWS), min(dp, max(chips, 8)), 24, 128), F32),
        late_own=vmem((sections, 16, 128), F32),
        late_sem=dma((2,)),
        sum_sem=dma((first_sems(cfg)[-1],)),
        grad_send=dma((2, 7 + (groups > 1))),
        grad_recv=dma((2, 1 + 3 * (PART_SEMS + (groups > 1)))),
        fetch_sem=dma((9,)),
        lengths=pltpu.SMEM((2, 2), jnp.int32),
        tokens=vmem((2, rows, width), BF16),
        wide_par=vmem((4, 2, width), F32),
        state_par=vmem((3, 2, states // 2), F32),
        b_in=vmem((2, width, states), BF16),
        c_out=vmem((2, states, width), BF16),
        gmat=vmem((2, width, width), BF16),
        out_grad=vmem((2, rows, width), BF16),
        widen=vmem((states, 2 * lanes), BF16),
        q=vmem((2, rows, 2 * lanes), F32),
        spread=vmem((rows, rows), BF16),
        gather=vmem((rows, rows), BF16),
        first_in=vmem((2, rows, width), BF16),
        out_grads=vmem((2, rows, width), BF16),
        second_in=vmem((2, rows, width), F32),
        grad_second=vmem((2, rows, width), BF16),
        valid=vmem((2, rows, 128), F32),
        keep_start=vmem((2, rows, 128), F32),
        keep_end=vmem((2, rows, 128), F32),
        par=vmem((SUB, lanes), F32),
        b_pad=vmem((2, width, 2 * lanes), BF16),
        c_pad=vmem((2, 2 * lanes, width), BF16),
        normed=vmem((2, 2, rows, width), F32),
        scaled=vmem((2, 2 * rows, width), BF16),
        drive=vmem((2, 2, rows, 2 * lanes), F32),
        state=vmem((2, 2, (steps + 1) * SUB, 2 * lanes), F32),
        joined=vmem((2, 2 * rows, 2 * lanes), BF16),
        work=vmem((2, rows, width), F32),
        active=vmem((2, 2, rows, width), F32),
        active_low=vmem((2, 2 * rows, width), BF16),
        slope=vmem((2, 2, rows, width), F32),
        sig=vmem((2, 2, rows, width), F32),
        through=vmem((2, rows, width), F32),
        grad_logits=vmem((2, 2 * rows, width), BF16),
        branch=vmem((2, 2 * rows, width), BF16),
        grad_drive=vmem((2, 2 * rows, states), BF16),
        grad_scaled=vmem((2, 2, rows, width), F32),
        state_sums=vmem((2, 2, 4, SUB, lanes), F32),
        narrow=vmem((rows, 128), BF16),
        narrow_rest=vmem((rows, 128), BF16),
        rows=vmem((SUB, width), F32),
    )
    for k, w in enumerate(widths):
        blocks = (2, QUAD), (QUAD,), (QUAD,), (QUAD,), (groups,)
        for part, block in zip(STAGES, blocks):
            scratch[f"{part}_{k}"] = vmem((*block, 16, w), BF16)
    in_vmem = pl.BlockSpec(memory_space=pltpu.VMEM)
    in_hbm = pl.BlockSpec(memory_space=pltpu.HBM)
    names = tuple(f"{name}_far" for name in INPUTS) + tuple(outs) + tuple(scratch)
    made = pl.pallas_call(
        partial(main_kernel, cfg, names),
        name="layers",
        out_shape=[vmem(*spec) for spec in outs.values()],
        in_specs=[in_hbm for name in INPUTS],
        out_specs=[in_vmem for name in outs],
        scratch_shapes=list(scratch.values()),
        compiler_params=pltpu.CompilerParams(
            collective_id=0, has_side_effects=True, vmem_limit_bytes=56 * 2**20
        ),
    )(*args)
    shapes = [
        ((2, rows, 128), BF16),
        ((2, rows, 128), F32),
        ((2, width), F32),
        ((2, width), F32),
        ((2, states // 2), F32),
        ((2, states // 2), F32),
        ((2, states // 2), F32),
        ((2, width, states), F32),
        ((2, states, width), F32),
        ((2, width), F32),
        ((2, width, width), F32),
        ((2, width), F32),
    ]
    by_copy = (7, 8, 10)
    return pl.pallas_call(
        partial(lay_out_kernel, cfg),
        name="lay_out",
        out_shape=[jax.ShapeDtypeStruct(*spec) for spec in shapes],
        in_specs=[in_vmem] * 6,
        out_specs=[in_hbm] * 12,
        scratch_shapes=[vmem(*shapes[k]) for k in by_copy]
        + [vmem((2, width), F32)] * 4
        + [vmem((2, states // 2), F32)] * 3
        + [dma((12,))],
        compiler_params=pltpu.CompilerParams(vmem_limit_bytes=24 * 2**20),
    )(*made)


def solution(mesh):
    sections, dp = mesh.shape["section"], mesh.shape["dp"]

    def run(*args):
        _, rows, width = args[0].shape
        states = args[8].shape[2]
        cfg = SimpleNamespace(
            rows=rows // dp,
            width=width,
            states=states,
            half=states // 2,
            lanes=-(-states // 256) * 128,
            sections=sections,
            dp=dp,
        )
        split = P(None, "dp", None)
        shared = P()
        placed = P(None, "dp", "section")
        return jax.shard_map(
            partial(per_device, cfg),
            mesh=mesh,
            in_specs=(split, P(None, "dp"), split) + (shared,) * 10,
            out_specs=(placed, placed) + (shared,) * 10,
            check_vma=False,
        )(*args)

    return run
```

```python
from functools import partial
from types import SimpleNamespace

import jax
import jax.numpy as jnp
from jax import lax
from jax.experimental import pallas as pl
from jax.experimental.pallas import tpu as pltpu
from jax.sharding import PartitionSpec as P

epsilon = 1e-05
MESH = pl.DeviceIdType.MESH
F32 = jnp.float32
BF16 = jnp.bfloat16
SUB = 8
QUAD = 4
PART_SEMS = 9
LATE_STATES = 3
SUM_ROWS = (10, 8, 8, 8, 8, 8, 16)


STAGES = tuple(dict(mine=0, theirs=0, chip=0, quad=0, group=0, full=0))


def matmul(left, right):
    return jnp.dot(left, right, preferred_element_type=F32)


def matmul_nt(left, right):
    return lax.dot_general(left, right, (((1,), (1,)), ((), ())), preferred_element_type=F32)


def matmul_tn(left, right):
    return lax.dot_general(left, right, (((0,), (0,)), ((), ())), preferred_element_type=F32)


def cmul(ar, ai, br, bi):
    return ar * br - ai * bi, ar * bi + ai * br


def sweep(count, body, carry):
    for t in range(count):
        carry = body(t, carry)
    return carry


def repeat_lanes(x, times):
    return jnp.concatenate([x] * times, axis=1)


def fold_rows(x):
    return jnp.sum(x.reshape(x.shape[0] // SUB, SUB, x.shape[1]), axis=0)


def unfold(total, first, count):
    return jnp.concatenate([total[first + k : first + k + 1, :] for k in range(count)], axis=1)


def landed(block, sem):
    pltpu.make_async_copy(block, block, sem).wait()


def remote(src, dst, send_sem, recv_sem, device):
    pltpu.make_async_remote_copy(
        src_ref=src,
        dst_ref=dst,
        send_sem=send_sem,
        recv_sem=recv_sem,
        device_id=device,
        device_id_type=MESH,
    ).start()


def first_sems(cfg):
    begins = [0]
    for k in range(len(SUM_ROWS)):
        begins.append(begins[-1] + (2 if cfg.dp <= 8 and k < len(SUM_ROWS) - 1 else 4))
    return begins


class SmallSum:
    def __init__(self, place, direct, own, sibling, slots, sems):
        self.place, self.direct = place, direct
        self.own, self.sibling, self.slots, self.sems = own, sibling, slots, sems

    def to_all(self, slot, members, peer):
        self.members = members
        block = self.slots.at[slot]
        for step in range(1, members):
            to = (self.place.section, peer(step))
            remote(block, block, self.sems.at[0], self.sems.at[1], to)

    def start(self):
        at = self.place
        if self.direct:
            self.slots[at.dp] = self.own[...]
            self.to_all(at.dp, at.devices, at.dp_peer)
        else:
            to = (at.section, at.sibling)
            remote(self.own, self.sibling, self.sems.at[2], self.sems.at[3], to)

    def turn(self):
        at = self.place
        if not self.direct:
            landed(self.sibling, self.sems.at[3])
            self.slots[at.chip] = self.own[...] + self.sibling[...]
            self.to_all(at.chip, at.chips, at.chip_peer)

    def total(self):
        landed(self.slots.at[0 : self.members - 1], self.sems.at[1])
        result = self.slots[0]
        for member in range(1, self.members):
            result = result + self.slots[member]
        return result

    def end(self):
        if not self.direct:
            landed(self.own, self.sems.at[2])
        landed(self.slots.at[0 : self.members - 1], self.sems.at[0])


class GradSum:
    def __init__(self, place, parts, refs, send_sems, recv_sems):
        self.place, self.parts = place, parts
        self.mine, self.theirs, self.chip_part, self.quad_in, self.group_in, self.full = refs
        self.send_sems, self.recv_sems = send_sems, recv_sems

    def recv(self, part, k):
        if k == PART_SEMS:
            return self.recv_sems.at[1 + 3 * PART_SEMS + part]
        return self.recv_sems.at[1 + part * PART_SEMS + k]

    def send(self, part, src, dst, send, recv, device):
        columns = self.parts[part]
        sem = self.recv_sems.at[0] if recv is None else self.recv(part, recv)
        remote(src.at[..., columns], dst.at[..., columns], self.send_sems.at[send], sem, device)

    def landed(self, part, block, k):
        landed(block.at[..., self.parts[part]], self.recv(part, k))

    def to_core(self, part):
        at = self.place
        self.send(part, self.mine.at[1 - at.core], self.theirs, 0, 0, (at.section, at.sibling))

    def to_quad(self, part):
        at, columns = self.place, self.parts[part]
        self.landed(part, self.theirs, 0)
        for k in range(QUAD):
            both = self.mine[at.core, k, :, columns].astype(F32)
            both = both + self.theirs[k, :, columns].astype(F32)
            self.chip_part[k, :, columns] = both.astype(BF16)
        for step in range(1, QUAD):
            other = lax.rem(at.quad + step, QUAD)
            to = (at.section, at.quad_peer(step))
            self.send(part, self.chip_part.at[other], self.quad_in.at[at.quad], 1, 1, to)
        self.quad_in[at.quad, :, columns] = self.chip_part[at.quad, :, columns]

    def to_groups(self, part):
        at, columns = self.place, self.parts[part]
        self.landed(part, self.quad_in.at[0 : QUAD - 1], 1)
        total = self.quad_in[0, :, columns].astype(F32)
        for k in range(1, QUAD):
            total = total + self.quad_in[k, :, columns].astype(F32)
        if at.groups > 1:
            mine = self.group_in.at[at.group]
            mine[:, columns] = total.astype(BF16)
            for step in range(1, at.groups):
                self.send(part, mine, mine, 7, PART_SEMS, (at.section, at.chip_peer(step * QUAD)))
            self.landed(part, self.group_in.at[0 : at.groups - 1], PART_SEMS)
            total = self.group_in[0, :, columns].astype(F32)
            for other in range(1, at.groups):
                total = total + self.group_in[other, :, columns].astype(F32)
        piece = self.full.at[at.core, at.section, at.quad]
        piece[:, columns] = total.astype(BF16)
        self.to_members(part)
        self.over_sections(part, at.quad)

    def to_members(self, part):
        at = self.place
        piece = self.full.at[at.core, at.section, at.quad]
        for step in range(1, QUAD):
            self.send(part, piece, piece, 2, 1 + step, (at.section, at.quad_peer(step)))

    def over_sections(self, part, quad):
        at = self.place
        piece = self.full.at[at.core, at.section, quad]
        for k in (1, 2, 3):
            self.send(part, piece, piece, 3, 4 + k, (at.beyond(k), at.dp))

    def to_sections(self, part):
        at = self.place
        for step in range(1, QUAD):
            other = lax.rem(at.quad + QUAD - step, QUAD)
            self.landed(part, self.full.at[at.core, at.section, other], 1 + step)
            self.over_sections(part, other)
        self.to_other(part, at.section)

    def to_other(self, part, section):
        at = self.place
        block = self.full.at[at.core, section]
        self.send(part, block, block, 4, None, (at.section, at.sibling))

    def to_sibling(self, part):
        at = self.place
        for k in (1, 2, 3):
            self.landed(part, self.full.at[at.core, at.beyond(k)], 4 + k)
            self.to_other(part, at.beyond(k))

    def end(self):
        at = self.place
        landed(self.full.at[1 - at.core], self.recv_sems.at[0])
        landed(self.theirs, self.send_sems.at[0])
        landed(self.quad_in.at[0 : QUAD - 1], self.send_sems.at[1])
        landed(self.quad_in.at[0 : QUAD - 1], self.send_sems.at[2])
        self.end_sections()
        landed(self.full.at[at.core], self.send_sems.at[4])
        if at.groups > 1:
            landed(self.group_in.at[0 : at.groups - 1], self.send_sems.at[7])


    def end_sections(self):
        at = self.place
        landed(self.full.at[at.core, 0 : at.sections - 1], self.send_sems.at[3])


class CornerSum(GradSum):
    def to_members(self, part):
        at = self.place
        piece = self.full.at[at.core, at.section, at.quad]
        self.send(part, piece, piece, 5, 7, (at.beyond(3), at.dp))
        super().to_members(part)

    def over_sections(self, part, quad):
        at = self.place
        piece = self.full.at[at.core, at.section, quad]
        for k in (1, 2):
            self.send(part, piece, piece, 3, 4 + k, (at.beyond(k), at.dp))

    def to_corner(self, part):
        at = self.place
        piece = self.full.at[at.core, at.beyond(3), at.quad]
        self.landed(part, piece, 7)
        for step in range(1, QUAD):
            self.send(part, piece, piece, 6, 8, (at.section, at.quad_peer(step)))

    def to_sibling(self, part):
        at = self.place
        for k in (1, 2):
            self.landed(part, self.full.at[at.core, at.beyond(k)], 4 + k)
            self.to_other(part, at.beyond(k))
        self.landed(part, self.full.at[at.core, at.beyond(3), 0 : QUAD - 1], 8)
        self.to_other(part, at.beyond(3))

    def end_sections(self):
        at = self.place
        landed(self.full.at[at.core, 0:2], self.send_sems.at[3])
        landed(self.full.at[at.core, 0, 0], self.send_sems.at[5])
        landed(self.full.at[at.core, 0, 0 : QUAD - 1], self.send_sems.at[6])


class RelaySum(GradSum):
    def to_members(self, part):
        at = self.place
        piece = self.full.at[at.core, at.section, at.quad]
        self.send(part, piece, piece, 2, 2, (at.section, at.apart(2)))
        self.send(part, piece, piece, 2, 3, (at.section, at.apart(1)))

    def to_near(self, part):
        at = self.place
        far = 2 * (1 - at.high) + at.low
        piece = self.full.at[at.core, at.section, far]
        self.landed(part, piece, 2)
        self.send(part, piece, piece, 2, 4, (at.section, at.apart(1)))
        self.over_sections(part, far)
        near = 2 * at.high + 1 - at.low
        self.landed(part, self.full.at[at.core, at.section, near], 3)
        self.over_sections(part, near)

    def to_sections(self, part):
        at = self.place
        last = 2 * (1 - at.high) + 1 - at.low
        self.landed(part, self.full.at[at.core, at.section, last], 4)
        self.over_sections(part, last)
        self.to_other(part, at.section)


def main_kernel(cfg, names, *refs):
    r = SimpleNamespace(**dict(zip(names, refs)))
    rows, width, states, half, lanes = (
        cfg.rows,
        cfg.width,
        cfg.states,
        cfg.half,
        cfg.lanes,
    )
    steps = rows // SUB
    section = lax.axis_index("section")
    dp = lax.axis_index("dp")
    chips = cfg.dp // 2
    core, chip = lax.rem(dp, 2), lax.div(dp, 2)
    quad, group = lax.rem(chip, QUAD), lax.div(chip, QUAD)
    beyond = {
        1: section + 1 - 2 * lax.rem(section, 2),
        2: section + 2 - 4 * lax.div(section, 2),
        3: 3 - section,
    }
    place = SimpleNamespace(
        section=section,
        beyond=lambda k: beyond[k],
        sections=cfg.sections,
        dp=dp,
        core=core,
        chip=chip,
        chips=chips,
        quad=quad,
        group=group,
        groups=chips // QUAD,
        devices=cfg.dp,
        dp_peer=lambda step: lax.rem(dp + step, cfg.dp),
        sibling=dp + 1 - 2 * core,
        chip_peer=lambda step: lax.rem(chip + step, chips) * 2 + core,
        high=lax.div(quad, 2),
        low=lax.rem(quad, 2),
        apart=lambda by: (
            chip + by * (1 - 2 * (lax.rem(quad, 2) if by == 1 else lax.div(quad, 2)))
        )
        * 2
        + core,
        quad_peer=lambda step: (group * QUAD + lax.rem(quad + step, QUAD)) * 2 + core,
    )

    direct = cfg.dp <= 8
    if direct:
        peers = [(section, place.dp_peer(step)) for step in range(1, cfg.dp)]
    else:
        peers = [(section, place.sibling)]
        peers += [(section, place.chip_peer(step)) for step in range(1, chips)]
    peers += [(beyond[k], dp) for k in (1, 2, 3)]
    barrier = pltpu.get_barrier_semaphore()
    for peer in peers:
        pl.semaphore_signal(barrier, inc=1, device_id=peer, device_id_type=MESH)

    sum_sems = first_sems(cfg)
    small = [
        SmallSum(
            place,
            direct and k < len(SUM_ROWS) - 1,
            r.sum_own.at[k, 0:tall] if k < len(SUM_ROWS) - 1 else r.late_own.at[section],
            r.sum_sibling.at[k, 0:tall],
            r.sum_slots.at[k, :, 0:tall],
            r.sum_sem.at[sum_sems[k] : sum_sems[k + 1]],
        )
        for k, tall in enumerate(SUM_ROWS)
    ]
    first_sum, mid_sum, upper_sum = small[0:2], small[2:4], small[4:6]
    late_sum = small[6]
    gate_part, out_part, in_part = range(3)
    bounds = (0, width, width + states, width + 2 * states)
    batches = [
        (RelaySum if k == 0 else CornerSum)(
            place,
            [slice(*bounds[k : k + 2]) for k in range(3)],
            [getattr(r, f"{part}_{k}") for part in STAGES],
            r.grad_send.at[k],
            r.grad_recv.at[k],
        )
        for k in range(2)
    ]
    upper, lower = batches

    r.gain, r.bias, r.skip, r.gbias = [r.wide_par.at[k] for k in range(4)]
    r.decay, r.freq, r.lstep = [r.state_par.at[k] for k in range(3)]
    wide_far = (r.gain_far, r.bias_far, r.skip_far, r.gbias_far)
    state_far = (r.decay_far, r.freq_far, r.lstep_far)
    fetches = [[(r.lengths_far, r.lengths)]]
    fetches += [[(r.tokens_far.at[m], r.tokens.at[m])] for m in range(2)]
    fetches += [[(far, r.state_par.at[k]) for k, far in enumerate(state_far)]]
    fetches += [[(r.b_in_far, r.b_in)], [(r.out_grad_far, r.out_grad)], [(r.c_out_far, r.c_out)]]
    fetches += [[(far, r.wide_par.at[k]) for k, far in enumerate(wide_far)]]
    fetches += [[(r.gmat_far, r.gmat)]]
    for k, group_of in enumerate(fetches):
        for far, held in group_of:
            pltpu.make_async_copy(far, held, r.fetch_sem.at[k]).start()
    landed(r.lengths, r.fetch_sem.at[0])

    first_len = [r.lengths[m, 0] for m in range(2)]
    total_len = [r.lengths[m, 0] + r.lengths[m, 1] for m in range(2)]

    def put(index, at, row):
        for k in range(row.shape[1] // 128):
            r.sum_own[index, at + k : at + k + 1, :] = row[:, k * 128 : (k + 1) * 128]

    def put_late(at, row):
        for k in range(cfg.sections):
            r.late_own[k, at : at + 1, :] = row[:, k * 128 : (k + 1) * 128]

    chunk = 32
    for m in range(2):

        landed(r.tokens.at[m], r.fetch_sem.at[1 + m])

        def token_sums(t, carry, m=m):
            at = pl.ds(t * chunk, chunk)
            v = r.tokens[m, at, :].astype(F32)
            place_row = t * chunk + lax.broadcasted_iota(jnp.int32, (chunk, width), 0)
            kept = jnp.where(place_row < total_len[m], v, 0.0)
            return carry[0] + fold_rows(kept), carry[1] + fold_rows(kept * v)

        zero = jnp.zeros((SUB, width), F32)
        sums, squares = sweep(rows // chunk, token_sums, (zero, zero))
        put(m, 0, jnp.sum(sums, axis=0, keepdims=True))
        put(m, 4, jnp.sum(squares, axis=0, keepdims=True))
        if m == 0:
            for k in range(2):
                count = jnp.minimum(total_len[k], rows).astype(F32)
                r.sum_own[0, 8 + k : 9 + k, :] = jnp.full((1, 128), count, F32)
            pl.semaphore_wait(barrier, len(peers))
        first_sum[m].start()

    at_i = lax.broadcasted_iota(jnp.int32, (rows, rows), 0)
    at_r = lax.broadcasted_iota(jnp.int32, (rows, rows), 1)
    r.spread[...] = jnp.where(
        at_r == (at_i % SUB) * steps + at_i // SUB, 1.0, 0.0
    ).astype(BF16)
    r.gather[...] = jnp.where(
        at_i == (at_r % SUB) * steps + at_r // SUB, 1.0, 0.0
    ).astype(BF16)
    for m in range(2):
        r.first_in[m] = matmul(r.spread[...], r.tokens[m]).astype(BF16)
    for m in range(2):
        first_sum[m].turn()
    landed(r.out_grad, r.fetch_sem.at[5])
    for m in range(2):
        r.out_grads[m] = matmul(r.spread[...], r.out_grad[m]).astype(BF16)
    held = lax.broadcasted_iota(jnp.int32, (rows, 128), 0)
    held = (held % SUB) * steps + held // SUB
    all_start, all_end = [], []
    for m in range(2):
        one, zero = jnp.float32(1.0), jnp.float32(0.0)
        past = held >= total_len[m]
        starts = (held == 0) | (held == first_len[m]) | past
        ends = (held == first_len[m] - 1) | (held == total_len[m] - 1) | past | (held == rows - 1)
        r.valid[m] = jnp.where(past, zero, one)
        r.keep_start[m] = jnp.where(starts, zero, one)
        r.keep_end[m] = jnp.where(ends, zero, one)
        for kept, mask in ((all_start, r.keep_start), (all_end, r.keep_end)):
            kept.append(jnp.min(mask[m].reshape(steps, SUB, 128), axis=0))

    r.par[...] = jnp.zeros((SUB, lanes), F32)
    r.par[0:2, :] = jnp.ones((2, lanes), F32)
    landed(r.state_par, r.fetch_sem.at[3])
    r.par[0:2, 0:half] = r.decay[...]
    r.par[2:4, 0:half] = r.freq[...]
    r.par[4:6, 0:half] = r.lstep[...]
    decay, spin = r.par[0:2, :], r.par[2:4, :]
    step_size = jnp.exp(r.par[4:6, :])
    damping = jnp.exp(-decay * step_size)
    bar_re = damping * jnp.cos(spin * step_size)
    bar_im = damping * jnp.sin(spin * step_size)
    modulus = decay * decay + spin * spin
    fac_re = ((bar_re - 1.0) * -decay + bar_im * spin) / modulus
    fac_im = (bar_im * -decay - (bar_re - 1.0) * spin) / modulus
    pow_re, pow_im = bar_re, bar_im
    power = 1
    while power < steps:
        pow_re, pow_im = cmul(pow_re, pow_im, pow_re, pow_im)
        power *= 2

    lane = lax.broadcasted_iota(jnp.int32, (1, 128), 1)
    low_lanes = lane < half - 128
    turn_by = half - 128

    from_column = lax.broadcasted_iota(jnp.int32, (states, 2 * lanes), 0)
    to_column = lax.broadcasted_iota(jnp.int32, (states, 2 * lanes), 1)
    moved_to = jnp.where(from_column < half, from_column, from_column + (lanes - half))
    r.widen[...] = jnp.where(to_column == moved_to, 1.0, 0.0).astype(BF16)
    for held, k in ((r.b_in, 4), (r.c_out, 6), (r.wide_par, 7), (r.gmat, 8)):
        landed(held, r.fetch_sem.at[k])
    for l in range(2):
        r.b_pad[l] = matmul(r.b_in[l], r.widen[...]).astype(BF16)
        blank = jnp.zeros((lanes - half, width), BF16)
        r.c_pad[l, 0:half, :] = r.c_out[l, 0:half, :]
        r.c_pad[l, half:lanes, :] = blank
        r.c_pad[l, lanes : lanes + half, :] = r.c_out[l, half:states, :]
        r.c_pad[l, lanes + half : 2 * lanes, :] = blank

    def across(end, coef, reverse):
        end_re, end_im = end
        coef_re, coef_im = coef
        sub = lax.broadcasted_iota(jnp.int32, (SUB, lanes), 0)
        for by in (1, 2, 4):
            turn = SUB - by if reverse else by
            live = sub < SUB - by if reverse else sub >= by

            def moved(x):
                return jnp.where(live, pltpu.roll(x, turn, 0), 0.0)

            add_re, add_im = cmul(coef_re, coef_im, moved(end_re), moved(end_im))
            coef_re, coef_im = cmul(coef_re, coef_im, moved(coef_re), moved(coef_im))
            end_re, end_im = end_re + add_re, end_im + add_im
        turn = SUB - 1 if reverse else 1
        live = sub < SUB - 1 if reverse else sub >= 1
        return tuple(jnp.where(live, pltpu.roll(x, turn, 0), 0.0) for x in (end_re, end_im))

    def wide8(x, l):
        return jnp.broadcast_to(x[l : l + 1, :], (SUB, x.shape[1]))

    def group_rows(p):
        return pl.ds(p * SUB, SUB)

    def scan_coefs(l, m, reverse):
        keep = r.keep_end if reverse else r.keep_start
        all_kept = repeat_lanes((all_end if reverse else all_start)[m], lanes // 128)
        product = (all_kept * wide8(pow_re, l), all_kept * wide8(pow_im, l))
        return keep, wide8(bar_re, l), wide8(bar_im, l), product

    def advance(keep, m, at, br, bi, re, im, src_re, src_im):
        k = repeat_lanes(keep[m, at, :], lanes // 128)
        kr, ki = k * br, k * bi
        return kr * re - ki * im + src_re, kr * im + ki * re + src_im

    def scan_states(l, m):
        reverse = l == 1
        lead = 0 if reverse else 1
        keep, br, bi, product = scan_coefs(l, m, reverse)
        fr, fi = wide8(fac_re, l), wide8(fac_im, l)
        zero = jnp.zeros((SUB, lanes), F32)

        def ends(t, carry):
            p = steps - 1 - t if reverse else t
            at = group_rows(p)
            v = repeat_lanes(r.valid[m, at, :], lanes // 128)
            drive_re = r.drive[l, m, at, 0:lanes]
            drive_im = r.drive[l, m, at, lanes : 2 * lanes]
            src_re, src_im = cmul(fr, fi, v * drive_re, v * drive_im)
            r.state[l, m, group_rows(p + lead), 0:lanes] = src_re
            r.state[l, m, group_rows(p + lead), lanes : 2 * lanes] = src_im
            return advance(keep, m, at, br, bi, *carry, src_re, src_im)

        end = sweep(steps, ends, (zero, zero))
        enter = across(end, product, reverse)
        first = steps if reverse else 0
        r.state[l, m, first * SUB : (first + 1) * SUB, 0:lanes] = enter[0]
        r.state[l, m, first * SUB : (first + 1) * SUB, lanes : 2 * lanes] = enter[1]

        def fill(t, carry):
            done = []
            for k in range(2):
                p = steps - 1 - (2 * t + k) if reverse else 2 * t + k
                at, to = group_rows(p), group_rows(p + lead)
                src_re = r.state[l, m, to, 0:lanes]
                src_im = r.state[l, m, to, lanes : 2 * lanes]
                carry = advance(keep, m, at, br, bi, *carry, src_re, src_im)
                r.state[l, m, to, 0:lanes] = carry[0]
                r.state[l, m, to, lanes : 2 * lanes] = carry[1]
                done.append(jnp.concatenate([carry[0], -carry[1]], axis=1))
            pair = steps // 2 - 1 - t if reverse else t
            both = jnp.concatenate(done[::-1] if reverse else done, axis=0)
            to = pl.ds(m * rows + pair * 16, 16)
            r.joined[l, to, :] = both.astype(BF16)
            return carry

        sweep(steps // 2, fill, enter)

    def scan_grads(l, m):
        reverse = l == 0
        back = 1 if l == 1 else 0
        keep, br, bi, product = scan_coefs(l, m, reverse)
        keep_state = r.keep_start if l == 0 else r.keep_end
        fr, fi = 2.0 * wide8(fac_re, l), 2.0 * wide8(fac_im, l)
        zero = jnp.zeros((SUB, lanes), F32)

        def ends(t, carry):
            p = steps - 1 - t if reverse else t
            at = group_rows(p)
            q_re = r.q[m, at, 0:lanes]
            q_im = r.q[m, at, lanes : 2 * lanes]
            return advance(keep, m, at, br, bi, *carry, q_re, q_im)

        end = sweep(steps, ends, (zero, zero))
        enter = across(end, product, reverse)

        def fill(t, carry):
            w, bar_sum, fac_sum = carry
            done = []
            for k in range(2):
                p = steps - 1 - (2 * t + k) if reverse else 2 * t + k
                at, near = group_rows(p), group_rows(p + back)
                q_re = r.q[m, at, 0:lanes]
                q_im = r.q[m, at, lanes : 2 * lanes]
                w = advance(keep, m, at, br, bi, *w, q_re, q_im)
                kept = repeat_lanes(keep_state[m, at, :], lanes // 128)
                near_re = kept * r.state[l, m, near, 0:lanes]
                near_im = kept * r.state[l, m, near, lanes : 2 * lanes]
                term = cmul(*w, near_re, near_im)
                bar_sum = (bar_sum[0] + term[0], bar_sum[1] + term[1])
                v = repeat_lanes(r.valid[m, at, :], lanes // 128)
                vw = (v * w[0], v * w[1])
                drive_re = r.drive[l, m, at, 0:lanes]
                drive_im = r.drive[l, m, at, lanes : 2 * lanes]
                term = cmul(*vw, drive_re, drive_im)
                fac_sum = (fac_sum[0] + term[0], fac_sum[1] + term[1])
                gd_re, gd_im = cmul(fr, fi, *vw)
                im_low = pltpu.roll(-gd_im[:, 0:128], 64, 1)
                im_high = pltpu.roll(-gd_im[:, 128:256], 64, 1)
                done.append(
                    jnp.concatenate(
                        [
                            gd_re[:, 0:128],
                            jnp.where(low_lanes, gd_re[:, 128:256], im_low),
                            jnp.where(low_lanes, im_low, im_high),
                        ],
                        axis=1,
                    )
                )
            pair = steps // 2 - 1 - t if reverse else t
            both = jnp.concatenate(done[::-1] if reverse else done, axis=0)
            to = pl.ds(m * rows + pair * 16, 16)
            r.grad_drive[l, to, :] = both.astype(BF16)
            return w, bar_sum, fac_sum

        none = (zero, zero)
        _, bar_sum, fac_sum = sweep(steps // 2, fill, (enter, none, none))
        for k, part in enumerate((*bar_sum, *fac_sum)):
            r.state_sums[l, m, k] = part

    def row_of(ref, l):
        return ref[l : l + 1, :]

    def micro_rows(m):
        return slice(m * rows, (m + 1) * rows)

    gelu_chunk = 16

    def mixer(l, m, center, inv):
        gain, bias, skip = row_of(r.gain, l), row_of(r.bias, l), row_of(r.skip, l)

        def normalise(t, carry):
            at = pl.ds(t * chunk, chunk)
            if l == 0:
                v = r.first_in[m, at, :].astype(F32)
            else:
                v = r.second_in[m, at, :]
            normed = (v - center) * inv
            r.normed[l, m, at, :] = normed
            to = pl.ds(m * rows + t * chunk, chunk)
            r.scaled[l, to, :] = (normed * gain + bias).astype(BF16)
            return carry

        sweep(rows // chunk, normalise, 0)
        yield
        r.drive[l, m] = matmul(r.scaled[l, micro_rows(m), :], r.b_pad[l])
        yield
        scan_states(l, m)
        yield
        r.work[m] = matmul(r.joined[l, micro_rows(m), :], r.c_pad[l])

        yield

        def activate(t, carry):
            at = pl.ds(t * gelu_chunk, gelu_chunk)
            scaled = r.normed[l, m, at, :] * gain + bias
            y = (2.0 * r.work[m, at, :] + skip * scaled).astype(BF16).astype(F32)
            below = 0.5 + 0.5 * lax.erf(y * 0.7071067811865476)
            density = jnp.exp(-0.5 * y * y) * 0.3989422804014327
            active = y * below
            r.active[l, m, at, :] = active
            r.slope[l, m, at, :] = below + y * density
            to = pl.ds(m * rows + t * gelu_chunk, gelu_chunk)
            r.active_low[l, to, :] = active.astype(BF16)
            return carry

        sweep(rows // gelu_chunk, activate, 0)
        yield
        r.work[m] = matmul(r.active_low[l, micro_rows(m), :], r.gmat[l])

    def first_gate(m):
        gbias = row_of(r.gbias, 0)

        def gate(t, carry):
            at = pl.ds(t * gelu_chunk, gelu_chunk)
            opened = jax.nn.sigmoid(r.work[m, at, :] + gbias)
            r.sig[0, m, at, :] = opened
            v = repeat_lanes(r.valid[m, at, :], width // 128)
            gated = v * r.active[0, m, at, :] * opened
            second = r.first_in[m, at, :].astype(F32) + gated.astype(BF16).astype(F32)
            r.second_in[m, at, :] = second
            kept = v * second
            return carry[0] + fold_rows(kept), carry[1] + fold_rows(kept * second)

        zero = jnp.zeros((SUB, width), F32)
        sums, squares = sweep(rows // gelu_chunk, gate, (zero, zero))
        put(2 + m, 0, jnp.sum(sums, axis=0, keepdims=True))
        put(2 + m, 4, jnp.sum(squares, axis=0, keepdims=True))

    bias_sums = {}
    skip_sums = {}

    def gate_grad(l, m, grad_of):
        gbias = row_of(r.gbias, l)

        def gate(t, carry):
            at = pl.ds(t * gelu_chunk, gelu_chunk)
            if l == 1:
                opened = jax.nn.sigmoid(r.work[m, at, :] + gbias)
                r.sig[1, m, at, :] = opened
            else:
                opened = r.sig[0, m, at, :]
            v = repeat_lanes(r.valid[m, at, :], width // 128)
            masked = v * grad_of(at, v)
            through = masked * opened
            r.through[m, at, :] = through
            grad_logits = through * r.active[l, m, at, :] * (1.0 - opened)
            to = pl.ds(m * rows + t * gelu_chunk, gelu_chunk)
            r.grad_logits[l, to, :] = grad_logits.astype(BF16)
            return carry + fold_rows(grad_logits)

        zero = jnp.zeros((SUB, width), F32)
        bias_sums[l, m] = sweep(rows // gelu_chunk, gate, zero)
        yield

    def branch_grad(l, m):
        gain, bias = row_of(r.gain, l), row_of(r.bias, l)
        r.work[m] = matmul_nt(r.grad_logits[l, micro_rows(m), :], r.gmat[l])
        yield

        def branch(t, carry):
            at = pl.ds(t * chunk, chunk)
            grad_active = r.through[m, at, :] + r.work[m, at, :]
            g = (r.slope[l, m, at, :] * grad_active).astype(BF16)
            to = pl.ds(m * rows + t * chunk, chunk)
            r.branch[l, to, :] = g
            scaled = r.normed[l, m, at, :] * gain + bias
            return carry + fold_rows(g.astype(F32) * scaled)

        zero = jnp.zeros((SUB, width), F32)
        skip_sums[l, m] = sweep(rows // chunk, branch, zero)
        yield
        r.q[m] = matmul_nt(r.branch[l, micro_rows(m), :], r.c_pad[l])
        yield

    def mixer_grad(l, m):
        skip = row_of(r.skip, l)
        scan_grads(l, m)
        yield
        r.work[m] = matmul_nt(r.grad_drive[l, micro_rows(m), :], r.b_in[l])
        yield

        def scaled_grad(t, carry):
            at = pl.ds(t * chunk, chunk)
            to = pl.ds(m * rows + t * chunk, chunk)
            grad = r.work[m, at, :] + skip * r.branch[l, to, :].astype(F32)
            r.grad_scaled[l, m, at, :] = grad
            normed = r.normed[l, m, at, :]
            return carry[0] + fold_rows(grad), carry[1] + fold_rows(grad * normed)

        zero = jnp.zeros((SUB, width), F32)
        sums, products = sweep(rows // chunk, scaled_grad, (zero, zero))
        sums = jnp.sum(sums, axis=0, keepdims=True)
        products = jnp.sum(products, axis=0, keepdims=True)
        if l == 1:
            put(4 + m, 0, sums)
            put(4 + m, 4, products)
        else:
            put_late(2 * m, sums)
            put_late(2 * m + 1, products)

    def moments(total, at, count):
        center = unfold(total, at, 4) / count
        return center, lax.rsqrt(unfold(total, at + 4, 4) / count - center * center + epsilon)

    own_columns = pl.ds(pl.multiple_of(section * 128, 128), 128)

    def gate_weights(l, ref):
        grad = matmul_tn(r.active_low[l, :, own_columns], r.grad_logits[l])
        ref[:, :, :, 0:width] = grad.astype(BF16).reshape(2, QUAD, 16, width)

    def out_weights(l, ref, at):
        grad = 2.0 * matmul_tn(r.joined[l], r.branch[l, :, own_columns])
        grad = jnp.concatenate([grad[0:half, :], grad[lanes : lanes + half, :]], axis=0)
        tall = states // (2 * QUAD)
        for k in range(tall // 16):
            for c in range(2):
                for z in range(QUAD):
                    first = (c * QUAD + z) * tall + 16 * k
                    ref[c, z, :, at + 128 * k : at + 128 * (k + 1)] = grad[
                        first : first + 16, :
                    ].astype(BF16)

    def in_weights(l, ref, at):
        grad = matmul_tn(r.scaled[l, :, own_columns], r.grad_drive[l])
        ref[:, :, :, at : at + states] = grad.astype(BF16).reshape(2, QUAD, 16, states)

    def layer_rows(l):
        def both(sums):
            return jnp.sum(sums[l, 0] + sums[l, 1], axis=0, keepdims=True)

        put_late(4 + 2 * l, both(skip_sums))
        put_late(5 + 2 * l, both(bias_sums))
        part = [
            jnp.sum(r.state_sums[l, 0, k] + r.state_sums[l, 1, k], axis=0, keepdims=True)
            for k in range(4)
        ]
        gb_re, gb_im = 2.0 * part[0], -2.0 * part[1]
        gf_re, gf_im = 2.0 * part[2], -2.0 * part[3]
        one = slice(l, l + 1)
        lam_re, lam_im, size = -decay[one], spin[one], step_size[one]
        b_re, b_im, f_re, f_im = bar_re[one], bar_im[one], fac_re[one], fac_im[one]
        top_re, top_im = size * b_re - f_re, size * b_im - f_im
        square = modulus[one]
        d_re = (top_re * lam_re + top_im * lam_im) / square
        d_im = (top_im * lam_re - top_re * lam_im) / square
        gl_re = size * (b_re * gb_re + b_im * gb_im) + (d_re * gf_re + d_im * gf_im)
        gl_im = size * (b_re * gb_im - b_im * gb_re) + (d_re * gf_im - d_im * gf_re)
        e_re, e_im = cmul(lam_re, lam_im, b_re, b_im)
        g_step = size * ((e_re * gb_re + e_im * gb_im) + (b_re * gf_re + b_im * gf_im))
        parts = [
            row[:, k : k + 128] for row in (-gl_re, gl_im, g_step) for k in range(0, lanes, 128)
        ]
        for k, row in enumerate(parts):
            k += l * len(parts)
            at = 8 + k % LATE_STATES
            r.late_own[k // LATE_STATES, at : at + 1, :] = row

    def mixed_rows(m):
        def mix(t, carry):
            at = pl.ds(t * chunk, chunk)
            gated = (
                r.valid[m, at, :]
                * r.active[1, m, at, own_columns]
                * r.sig[1, m, at, own_columns]
            )
            stream = r.second_in[m, at, own_columns].astype(BF16).astype(F32)
            r.narrow[at, :] = (stream + gated).astype(BF16)
            return carry

        sweep(rows // chunk, mix, 0)
        r.mixed[m] = matmul(r.gather[...], r.narrow[...]).astype(BF16)

    def stream_grad(l, m, total, count, inv):
        gain = row_of(r.gain, l)
        first = gain * unfold(total, 0, 4) / count
        second = gain * unfold(total, 4, 4) / count
        return gain, first, second, inv

    def take(steps):
        for _ in steps:
            pass

    counts, norm0 = [None, None], [None, None]
    for m in range(2):
        total = first_sum[m].total()
        if m == 0:
            counts = [repeat_lanes(total[8 + k : 9 + k, :], width // 128) for k in range(2)]
        norm0[m] = moments(total, 0, counts[m])
        take(mixer(0, m, *norm0[m]))
        first_gate(m)
        mid_sum[m].start()
        mid_sum[m].turn()

    norm1 = [None, None]

    def second_layer(m):
        norm1[m] = moments(mid_sum[m].total(), 0, counts[m])
        yield from mixer(1, m, *norm1[m])
        yield from gate_grad(1, m, lambda at, v: r.out_grads[m, at, :].astype(F32))
        yield from branch_grad(1, m)
        yield from mixer_grad(1, m)
        upper_sum[m].start()
        upper_sum[m].turn()

    for m in range(2):
        take(second_layer(m))

    gate_weights(1, r.mine_0)
    upper.to_core(gate_part)
    out_weights(1, r.mine_0, width)
    upper.to_core(out_part)
    in_weights(1, r.mine_0, width + states)
    upper.to_core(in_part)
    layer_rows(1)

    def second_grad(m, total):
        gain, first, second, inv = stream_grad(1, m, total, counts[m], norm1[m][1])

        def grad_of(at, v):
            grad_normed = r.grad_scaled[1, m, at, :] * gain
            normed = r.normed[1, m, at, :]
            grad_stream = inv * (grad_normed - v * (first + normed * second))
            out_grad = r.out_grads[m, at, :].astype(F32)
            grad = (out_grad + grad_stream.astype(BF16).astype(F32)).astype(BF16)
            r.grad_second[m, at, :] = grad
            return grad.astype(F32)

        return grad_of

    upper_total = [upper_sum[0].total()]
    take(gate_grad(0, 0, second_grad(0, upper_total[0])))
    upper.to_quad(gate_part)
    take(branch_grad(0, 0))
    upper.to_quad(out_part)
    upper.to_quad(in_part)
    take(mixer_grad(0, 0))
    upper_total.append(upper_sum[1].total())
    take(gate_grad(0, 1, second_grad(1, upper_total[1])))
    gate_weights(0, r.mine_1)
    lower.to_core(gate_part)
    take(branch_grad(0, 1))
    out_weights(0, r.mine_1, width)
    lower.to_core(out_part)
    upper.to_groups(gate_part)
    lower.to_quad(gate_part)
    last = mixer_grad(0, 1)
    next(last)
    upper.to_groups(out_part)
    next(last)
    upper.to_groups(in_part)
    take(last)
    lower.to_quad(out_part)
    in_weights(0, r.mine_1, width + states)
    lower.to_core(in_part)
    layer_rows(0)
    late_sum.start()
    upper.to_near(gate_part)
    lower.to_quad(in_part)
    late_sum.turn()
    mixed_rows(0)
    lower.to_groups(gate_part)
    upper.to_near(out_part)
    lower.to_groups(out_part)
    upper.to_near(in_part)
    mixed_rows(1)
    lower.to_groups(in_part)
    upper.to_sections(gate_part)
    lower.to_corner(gate_part)
    upper.to_sections(out_part)
    upper.to_sections(in_part)
    lower.to_sections(gate_part)

    late = late_sum.total()
    r.late[section] = late
    block = r.late.at[section]
    for k in (1, 2, 3):
        remote(block, block, r.late_sem.at[0], r.late_sem.at[1], (beyond[k], dp))
    own_gain = r.gain[0:1, own_columns]
    for m in range(2):
        count = counts[m][:, 0:128]
        first = own_gain * late[2 * m : 2 * m + 1, :] / count
        second = own_gain * late[2 * m + 1 : 2 * m + 2, :] / count
        r.rows[m : m + 1, :] = norm0[m][1]
        inv = r.rows[m : m + 1, own_columns]

        def token_grad(t, carry, m=m, first=first, second=second, inv=inv):
            at = pl.ds(t * chunk, chunk)
            grad_normed = r.grad_scaled[0, m, at, own_columns] * own_gain
            normed = r.normed[0, m, at, own_columns]
            grad_stream = inv * (grad_normed - r.valid[m, at, :] * (first + normed * second))
            grad = r.grad_second[m, at, own_columns].astype(F32) + grad_stream
            high = grad.astype(BF16)
            r.narrow[at, :] = high
            r.narrow_rest[at, :] = (grad - high.astype(F32)).astype(BF16)
            return carry

        sweep(rows // chunk, token_grad, 0)
        r.token_grad[m] = matmul(r.gather[...], r.narrow[...]) + matmul(
            r.gather[...], r.narrow_rest[...]
        )
    r.upper_norm[...] = upper_total[0] + upper_total[1]
    lower.to_corner(out_part)
    lower.to_sections(out_part)
    lower.to_corner(in_part)
    lower.to_sections(in_part)
    upper.to_sibling(gate_part)
    upper.to_sibling(out_part)
    upper.to_sibling(in_part)
    lower.to_sibling(gate_part)
    lower.to_sibling(out_part)
    lower.to_sibling(in_part)
    for k in range(2):
        landed(r.late.at[0 : cfg.sections - 1], r.late_sem.at[k])
    for batch in batches:
        batch.end()
    for each in small:
        each.end()


def lay_out_kernel(cfg, *refs):
    full = refs[1], refs[0]
    late, upper_norm, mixed, token_grad = refs[2:6]
    (
        mixed_out,
        token_grad_out,
        gain_out,
        bias_out,
        decay_out,
        freq_out,
        step_out,
        in_out,
        out_out,
        skip_out,
        gate_out,
        gbias_out,
    ) = refs[6:18]
    in_held, out_held, gate_held = refs[18:21]
    rows_held, sems = refs[21:28], refs[28]
    width, states, half = cfg.width, cfg.states, cfg.half
    tall = states // (2 * QUAD)
    copies = []

    def send(held, out, sem=None):
        copy = pltpu.make_async_copy(held, out, sems.at[3 + len(copies) if sem is None else sem])
        copy.start()
        if sem is None:
            copies.append(copy)

    send(mixed, mixed_out)
    send(token_grad, token_grad_out)
    def columns(at):
        return jnp.concatenate([late[s, at : at + 1, :] for s in range(cfg.sections)], axis=1)

    row_outs = (bias_out, gain_out, skip_out, gbias_out, decay_out, freq_out, step_out)
    values = [
        (columns(0) + columns(2), unfold(upper_norm, 0, 4)),
        (columns(1) + columns(3), unfold(upper_norm, 4, 4)),
        (columns(4), columns(6)),
        (columns(5), columns(7)),
    ]
    for k in range(3):
        places = [(6 * l + 2 * k + part) for l in range(2) for part in range(2)]
        row = [late[p // LATE_STATES, 8 + p % LATE_STATES, :][None] for p in places]
        values.append([jnp.concatenate(row[2 * l : 2 * l + 2], axis=1)[:, 0:half] for l in range(2)])
    for held, out, value in zip(rows_held, row_outs, values):
        for l in range(2):
            held[l : l + 1, :] = value[l]
        send(held, out)

    for l in (1, 0):
        parts = [(full[l], begin) for begin in (0, width, width + states)]
        for s in range(cfg.sections):
            mine = slice(s * 128, (s + 1) * 128)
            members = [(c, z) for c in range(2) for z in range(QUAD)]
            for (part, begin), held, out, wide, sem in (
                (parts[0], gate_held, gate_out, width, 0),
                (parts[2], in_held, in_out, states, 1),
            ):
                for c, z in members:
                    at = s * 128 + (c * QUAD + z) * 16
                    held[l, at : at + 16, :] = part[c, s, z, :, begin : begin + wide].astype(F32)
                send(held.at[l, mine], out.at[l, mine], sem)
            part, begin = parts[1]
            for c, z in members:
                for k in range(tall // 16):
                    first = (c * QUAD + z) * tall + 16 * k
                    out_held[l, first : first + 16, mine] = part[
                        c, s, z, :, begin + k * 128 : begin + (k + 1) * 128
                    ].astype(F32)
        send(out_held.at[l], out_out.at[l], 2)
    for copy in copies:
        copy.wait()
    for sem, out in enumerate((gate_out, in_out, out_out)):
        landed(out, sems.at[sem])


INPUTS = tuple(
    dict(
        tokens=0,
        lengths=0,
        out_grad=0,
        gain=0,
        bias=0,
        decay=0,
        freq=0,
        lstep=0,
        b_in=0,
        c_out=0,
        skip=0,
        gmat=0,
        gbias=0,
    )
)


def per_device(cfg, *args):
    rows, width, states, lanes = cfg.rows, cfg.width, cfg.states, cfg.lanes
    sections, dp, chips = cfg.sections, cfg.dp, cfg.dp // 2
    groups = chips // QUAD
    steps = rows // SUB
    vmem, dma = pltpu.VMEM, pltpu.SemaphoreType.DMA
    widths = (width + 2 * states,) * 2
    outs = {f"full_{k}": ((2, sections, QUAD, 16, w), BF16) for k, w in enumerate(widths)}
    outs.update(
        late=((sections, 16, 128), F32), upper_norm=((8, 128), F32), mixed=((2, rows, 128), BF16), token_grad=((2, rows, 128), F32)
    )
    scratch = dict(
        sum_own=vmem((len(SUM_ROWS), 24, 128), F32),
        sum_sibling=vmem((len(SUM_ROWS), 24, 128), F32),
        sum_slots=vmem((len(SUM_ROWS), min(dp, max(chips, 8)), 24, 128), F32),
        late_own=vmem((sections, 16, 128), F32),
        late_sem=dma((2,)),
        sum_sem=dma((first_sems(cfg)[-1],)),
        grad_send=dma((2, 7 + (groups > 1))),
        grad_recv=dma((2, 1 + 3 * (PART_SEMS + (groups > 1)))),
        fetch_sem=dma((9,)),
        lengths=pltpu.SMEM((2, 2), jnp.int32),
        tokens=vmem((2, rows, width), BF16),
        wide_par=vmem((4, 2, width), F32),
        state_par=vmem((3, 2, states // 2), F32),
        b_in=vmem((2, width, states), BF16),
        c_out=vmem((2, states, width), BF16),
        gmat=vmem((2, width, width), BF16),
        out_grad=vmem((2, rows, width), BF16),
        widen=vmem((states, 2 * lanes), BF16),
        q=vmem((2, rows, 2 * lanes), F32),
        spread=vmem((rows, rows), BF16),
        gather=vmem((rows, rows), BF16),
        first_in=vmem((2, rows, width), BF16),
        out_grads=vmem((2, rows, width), BF16),
        second_in=vmem((2, rows, width), F32),
        grad_second=vmem((2, rows, width), BF16),
        valid=vmem((2, rows, 128), F32),
        keep_start=vmem((2, rows, 128), F32),
        keep_end=vmem((2, rows, 128), F32),
        par=vmem((SUB, lanes), F32),
        b_pad=vmem((2, width, 2 * lanes), BF16),
        c_pad=vmem((2, 2 * lanes, width), BF16),
        normed=vmem((2, 2, rows, width), F32),
        scaled=vmem((2, 2 * rows, width), BF16),
        drive=vmem((2, 2, rows, 2 * lanes), F32),
        state=vmem((2, 2, (steps + 1) * SUB, 2 * lanes), F32),
        joined=vmem((2, 2 * rows, 2 * lanes), BF16),
        work=vmem((2, rows, width), F32),
        active=vmem((2, 2, rows, width), F32),
        active_low=vmem((2, 2 * rows, width), BF16),
        slope=vmem((2, 2, rows, width), F32),
        sig=vmem((2, 2, rows, width), F32),
        through=vmem((2, rows, width), F32),
        grad_logits=vmem((2, 2 * rows, width), BF16),
        branch=vmem((2, 2 * rows, width), BF16),
        grad_drive=vmem((2, 2 * rows, states), BF16),
        grad_scaled=vmem((2, 2, rows, width), F32),
        state_sums=vmem((2, 2, 4, SUB, lanes), F32),
        narrow=vmem((rows, 128), BF16),
        narrow_rest=vmem((rows, 128), BF16),
        rows=vmem((SUB, width), F32),
    )
    for k, w in enumerate(widths):
        blocks = (2, QUAD), (QUAD,), (QUAD,), (QUAD,), (groups,)
        for part, block in zip(STAGES, blocks):
            scratch[f"{part}_{k}"] = vmem((*block, 16, w), BF16)
    in_vmem = pl.BlockSpec(memory_space=pltpu.VMEM)
    in_hbm = pl.BlockSpec(memory_space=pltpu.HBM)
    names = tuple(f"{name}_far" for name in INPUTS) + tuple(outs) + tuple(scratch)
    made = pl.pallas_call(
        partial(main_kernel, cfg, names),
        name="layers",
        out_shape=[vmem(*spec) for spec in outs.values()],
        in_specs=[in_hbm for name in INPUTS],
        out_specs=[in_vmem for name in outs],
        scratch_shapes=list(scratch.values()),
        compiler_params=pltpu.CompilerParams(
            collective_id=0, has_side_effects=True, vmem_limit_bytes=56 * 2**20
        ),
    )(*args)
    shapes = [
        ((2, rows, 128), BF16),
        ((2, rows, 128), F32),
        ((2, width), F32),
        ((2, width), F32),
        ((2, states // 2), F32),
        ((2, states // 2), F32),
        ((2, states // 2), F32),
        ((2, width, states), F32),
        ((2, states, width), F32),
        ((2, width), F32),
        ((2, width, width), F32),
        ((2, width), F32),
    ]
    by_copy = (7, 8, 10)
    return pl.pallas_call(
        partial(lay_out_kernel, cfg),
        name="lay_out",
        out_shape=[jax.ShapeDtypeStruct(*spec) for spec in shapes],
        in_specs=[in_vmem] * 6,
        out_specs=[in_hbm] * 12,
        scratch_shapes=[vmem(*shapes[k]) for k in by_copy]
        + [vmem((2, width), F32)] * 4
        + [vmem((2, states // 2), F32)] * 3
        + [dma((12,))],
        compiler_params=pltpu.CompilerParams(vmem_limit_bytes=24 * 2**20),
    )(*made)


def solution(mesh):
    sections, dp = mesh.shape["section"], mesh.shape["dp"]

    def run(*args):
        _, rows, width = args[0].shape
        states = args[8].shape[2]
        cfg = SimpleNamespace(
            rows=rows // dp,
            width=width,
            states=states,
            half=states // 2,
            lanes=-(-states // 256) * 128,
            sections=sections,
            dp=dp,
        )
        split = P(None, "dp", None)
        shared = P()
        placed = P(None, "dp", "section")
        return jax.shard_map(
            partial(per_device, cfg),
            mesh=mesh,
            in_specs=(split, P(None, "dp"), split) + (shared,) * 10,
            out_specs=(placed, placed) + (shared,) * 10,
            check_vma=False,
        )(*args)

    return run
```

```python
from functools import partial
from types import SimpleNamespace

import jax
import jax.numpy as jnp
from jax import lax
from jax.experimental import pallas as pl
from jax.experimental.pallas import tpu as pltpu
from jax.sharding import PartitionSpec as P

epsilon = 1e-05
MESH = pl.DeviceIdType.MESH
F32 = jnp.float32
BF16 = jnp.bfloat16
SUB = 8
QUAD = 4
FAR_FIRST = (4, 6, 2, 3, 5, 7, 1)
PART_SEMS = 9
LATE_STATES = 3
SUM_ROWS = (10, 8, 8, 8, 8, 8, 16)


STAGES = tuple(dict(mine=0, theirs=0, chip=0, quad=0, group=0, full=0))


def matmul(left, right):
    return jnp.dot(left, right, preferred_element_type=F32)


def matmul_nt(left, right):
    return lax.dot_general(left, right, (((1,), (1,)), ((), ())), preferred_element_type=F32)


def matmul_tn(left, right):
    return lax.dot_general(left, right, (((0,), (0,)), ((), ())), preferred_element_type=F32)


def cmul(ar, ai, br, bi):
    return ar * br - ai * bi, ar * bi + ai * br


def sweep(count, body, carry):
    for t in range(count):
        carry = body(t, carry)
    return carry


def repeat_lanes(x, times):
    return jnp.concatenate([x] * times, axis=1)


def fold_rows(x):
    return jnp.sum(x.reshape(x.shape[0] // SUB, SUB, x.shape[1]), axis=0)


def unfold(total, first, count):
    return jnp.concatenate([total[first + k : first + k + 1, :] for k in range(count)], axis=1)


def landed(block, sem):
    pltpu.make_async_copy(block, block, sem).wait()


def remote(src, dst, send_sem, recv_sem, device):
    pltpu.make_async_remote_copy(
        src_ref=src,
        dst_ref=dst,
        send_sem=send_sem,
        recv_sem=recv_sem,
        device_id=device,
        device_id_type=MESH,
    ).start()


def first_sems(cfg):
    begins = [0]
    for k in range(len(SUM_ROWS)):
        begins.append(begins[-1] + (2 if cfg.dp <= 8 and k < len(SUM_ROWS) - 1 else 4))
    return begins


class SmallSum:
    def __init__(self, place, direct, own, sibling, slots, sems):
        self.place, self.direct = place, direct
        self.own, self.sibling, self.slots, self.sems = own, sibling, slots, sems

    def to_all(self, slot, members, peer):
        self.members = members
        block = self.slots.at[slot]
        for step in FAR_FIRST if members == 8 else range(1, members):
            to = (self.place.section, peer(step))
            remote(block, block, self.sems.at[0], self.sems.at[1], to)

    def start(self):
        at = self.place
        if self.direct:
            self.slots[at.dp] = self.own[...]
            self.to_all(at.dp, at.devices, at.dp_peer)
        else:
            to = (at.section, at.sibling)
            remote(self.own, self.sibling, self.sems.at[2], self.sems.at[3], to)

    def turn(self):
        at = self.place
        if not self.direct:
            landed(self.sibling, self.sems.at[3])
            self.slots[at.chip] = self.own[...] + self.sibling[...]
            self.to_all(at.chip, at.chips, at.chip_peer)

    def total(self):
        landed(self.slots.at[0 : self.members - 1], self.sems.at[1])
        result = self.slots[0]
        for member in range(1, self.members):
            result = result + self.slots[member]
        return result

    def end(self):
        if not self.direct:
            landed(self.own, self.sems.at[2])
        landed(self.slots.at[0 : self.members - 1], self.sems.at[0])


class GradSum:
    def __init__(self, place, parts, refs, send_sems, recv_sems):
        self.place, self.parts = place, parts
        self.mine, self.theirs, self.chip_part, self.quad_in, self.group_in, self.full = refs
        self.send_sems, self.recv_sems = send_sems, recv_sems

    def recv(self, part, k):
        if k == PART_SEMS:
            return self.recv_sems.at[1 + 3 * PART_SEMS + part]
        return self.recv_sems.at[1 + part * PART_SEMS + k]

    def send(self, part, src, dst, send, recv, device):
        columns = self.parts[part]
        sem = self.recv_sems.at[0] if recv is None else self.recv(part, recv)
        remote(src.at[..., columns], dst.at[..., columns], self.send_sems.at[send], sem, device)

    def landed(self, part, block, k):
        landed(block.at[..., self.parts[part]], self.recv(part, k))

    def to_core(self, part):
        at = self.place
        self.send(part, self.mine.at[1 - at.core], self.theirs, 0, 0, (at.section, at.sibling))

    def to_quad(self, part):
        at, columns = self.place, self.parts[part]
        self.landed(part, self.theirs, 0)
        for k in range(QUAD):
            both = self.mine[at.core, k, :, columns].astype(F32)
            both = both + self.theirs[k, :, columns].astype(F32)
            self.chip_part[k, :, columns] = both.astype(BF16)
        for step in range(1, QUAD):
            other = lax.rem(at.quad + step, QUAD)
            to = (at.section, at.quad_peer(step))
            self.send(part, self.chip_part.at[other], self.quad_in.at[at.quad], 1, 1, to)
        self.quad_in[at.quad, :, columns] = self.chip_part[at.quad, :, columns]

    def to_groups(self, part):
        at, columns = self.place, self.parts[part]
        self.landed(part, self.quad_in.at[0 : QUAD - 1], 1)
        total = self.quad_in[0, :, columns].astype(F32)
        for k in range(1, QUAD):
            total = total + self.quad_in[k, :, columns].astype(F32)
        if at.groups > 1:
            mine = self.group_in.at[at.group]
            mine[:, columns] = total.astype(BF16)
            for step in range(1, at.groups):
                self.send(part, mine, mine, 7, PART_SEMS, (at.section, at.chip_peer(step * QUAD)))
            self.landed(part, self.group_in.at[0 : at.groups - 1], PART_SEMS)
            total = self.group_in[0, :, columns].astype(F32)
            for other in range(1, at.groups):
                total = total + self.group_in[other, :, columns].astype(F32)
        piece = self.full.at[at.core, at.section, at.quad]
        piece[:, columns] = total.astype(BF16)
        self.to_members(part)
        self.over_sections(part, at.quad)

    def to_members(self, part):
        at = self.place
        piece = self.full.at[at.core, at.section, at.quad]
        for step in range(1, QUAD):
            self.send(part, piece, piece, 2, 1 + step, (at.section, at.quad_peer(step)))

    def over_sections(self, part, quad):
        at = self.place
        piece = self.full.at[at.core, at.section, quad]
        for k in (1, 2, 3):
            self.send(part, piece, piece, 3, 4 + k, (at.beyond(k), at.dp))

    def to_sections(self, part):
        at = self.place
        for step in range(1, QUAD):
            other = lax.rem(at.quad + QUAD - step, QUAD)
            self.landed(part, self.full.at[at.core, at.section, other], 1 + step)
            self.over_sections(part, other)
        self.to_other(part, at.section)

    def to_other(self, part, section):
        at = self.place
        block = self.full.at[at.core, section]
        self.send(part, block, block, 4, None, (at.section, at.sibling))

    def to_sibling(self, part):
        at = self.place
        for k in (1, 2, 3):
            self.landed(part, self.full.at[at.core, at.beyond(k)], 4 + k)
            self.to_other(part, at.beyond(k))

    def end(self):
        at = self.place
        landed(self.full.at[1 - at.core], self.recv_sems.at[0])
        landed(self.theirs, self.send_sems.at[0])
        landed(self.quad_in.at[0 : QUAD - 1], self.send_sems.at[1])
        landed(self.quad_in.at[0 : QUAD - 1], self.send_sems.at[2])
        self.end_sections()
        landed(self.full.at[at.core], self.send_sems.at[4])
        if at.groups > 1:
            landed(self.group_in.at[0 : at.groups - 1], self.send_sems.at[7])


    def end_sections(self):
        at = self.place
        landed(self.full.at[at.core, 0 : at.sections - 1], self.send_sems.at[3])


class CornerSum(GradSum):
    def to_members(self, part):
        at = self.place
        piece = self.full.at[at.core, at.section, at.quad]
        self.send(part, piece, piece, 5, 7, (at.beyond(3), at.dp))
        super().to_members(part)

    def over_sections(self, part, quad):
        at = self.place
        piece = self.full.at[at.core, at.section, quad]
        for k in (1, 2):
            self.send(part, piece, piece, 3, 4 + k, (at.beyond(k), at.dp))

    def to_corner(self, part):
        at = self.place
        piece = self.full.at[at.core, at.beyond(3), at.quad]
        self.landed(part, piece, 7)
        for step in range(1, QUAD):
            self.send(part, piece, piece, 6, 8, (at.section, at.quad_peer(step)))

    def to_sibling(self, part):
        at = self.place
        for k in (1, 2):
            self.landed(part, self.full.at[at.core, at.beyond(k)], 4 + k)
            self.to_other(part, at.beyond(k))
        self.landed(part, self.full.at[at.core, at.beyond(3), 0 : QUAD - 1], 8)
        self.to_other(part, at.beyond(3))

    def end_sections(self):
        at = self.place
        landed(self.full.at[at.core, 0:2], self.send_sems.at[3])
        landed(self.full.at[at.core, 0, 0], self.send_sems.at[5])
        landed(self.full.at[at.core, 0, 0 : QUAD - 1], self.send_sems.at[6])


class RelaySum(GradSum):
    def to_members(self, part):
        at = self.place
        piece = self.full.at[at.core, at.section, at.quad]
        self.send(part, piece, piece, 2, 2, (at.section, at.apart(2)))
        self.send(part, piece, piece, 2, 3, (at.section, at.apart(1)))

    def to_near(self, part):
        at = self.place
        far = 2 * (1 - at.high) + at.low
        piece = self.full.at[at.core, at.section, far]
        self.landed(part, piece, 2)
        self.send(part, piece, piece, 2, 4, (at.section, at.apart(1)))
        self.over_sections(part, far)
        near = 2 * at.high + 1 - at.low
        self.landed(part, self.full.at[at.core, at.section, near], 3)
        self.over_sections(part, near)

    def to_sections(self, part):
        at = self.place
        last = 2 * (1 - at.high) + 1 - at.low
        self.landed(part, self.full.at[at.core, at.section, last], 4)
        self.over_sections(part, last)
        self.to_other(part, at.section)


def main_kernel(cfg, names, *refs):
    r = SimpleNamespace(**dict(zip(names, refs)))
    rows, width, states, half, lanes = (
        cfg.rows,
        cfg.width,
        cfg.states,
        cfg.half,
        cfg.lanes,
    )
    steps = rows // SUB
    section = lax.axis_index("section")
    dp = lax.axis_index("dp")
    chips = cfg.dp // 2
    core, chip = lax.rem(dp, 2), lax.div(dp, 2)
    quad, group = lax.rem(chip, QUAD), lax.div(chip, QUAD)
    beyond = {
        1: section + 1 - 2 * lax.rem(section, 2),
        2: section + 2 - 4 * lax.div(section, 2),
        3: 3 - section,
    }
    place = SimpleNamespace(
        section=section,
        beyond=lambda k: beyond[k],
        sections=cfg.sections,
        dp=dp,
        core=core,
        chip=chip,
        chips=chips,
        quad=quad,
        group=group,
        groups=chips // QUAD,
        devices=cfg.dp,
        dp_peer=lambda step: lax.rem(dp + step, cfg.dp),
        sibling=dp + 1 - 2 * core,
        chip_peer=lambda step: lax.rem(chip + step, chips) * 2 + core,
        high=lax.div(quad, 2),
        low=lax.rem(quad, 2),
        apart=lambda by: (
            chip + by * (1 - 2 * (lax.rem(quad, 2) if by == 1 else lax.div(quad, 2)))
        )
        * 2
        + core,
        quad_peer=lambda step: (group * QUAD + lax.rem(quad + step, QUAD)) * 2 + core,
    )

    direct = cfg.dp <= 8
    if direct:
        peers = [(section, place.dp_peer(step)) for step in range(1, cfg.dp)]
    else:
        peers = [(section, place.sibling)]
        peers += [(section, place.chip_peer(step)) for step in range(1, chips)]
    peers += [(beyond[k], dp) for k in (1, 2, 3)]
    barrier = pltpu.get_barrier_semaphore()
    for peer in peers:
        pl.semaphore_signal(barrier, inc=1, device_id=peer, device_id_type=MESH)

    sum_sems = first_sems(cfg)
    small = [
        SmallSum(
            place,
            direct and k < len(SUM_ROWS) - 1,
            r.sum_own.at[k, 0:tall] if k < len(SUM_ROWS) - 1 else r.late_own.at[section],
            r.sum_sibling.at[k, 0:tall],
            r.sum_slots.at[k, :, 0:tall],
            r.sum_sem.at[sum_sems[k] : sum_sems[k + 1]],
        )
        for k, tall in enumerate(SUM_ROWS)
    ]
    first_sum, mid_sum, upper_sum = small[0:2], small[2:4], small[4:6]
    late_sum = small[6]
    gate_part, out_part, in_part = range(3)
    bounds = (0, width, width + states, width + 2 * states)
    batches = [
        (RelaySum if k == 0 else CornerSum)(
            place,
            [slice(*bounds[k : k + 2]) for k in range(3)],
            [getattr(r, f"{part}_{k}") for part in STAGES],
            r.grad_send.at[k],
            r.grad_recv.at[k],
        )
        for k in range(2)
    ]
    upper, lower = batches

    r.gain, r.bias, r.skip, r.gbias = [r.wide_par.at[k] for k in range(4)]
    r.decay, r.freq, r.lstep = [r.state_par.at[k] for k in range(3)]
    wide_far = (r.gain_far, r.bias_far, r.skip_far, r.gbias_far)
    state_far = (r.decay_far, r.freq_far, r.lstep_far)
    fetches = [[(r.lengths_far, r.lengths)]]
    fetches += [[(r.tokens_far.at[m], r.tokens.at[m])] for m in range(2)]
    fetches += [[(far, r.state_par.at[k]) for k, far in enumerate(state_far)]]
    fetches += [[(r.b_in_far, r.b_in)], [(r.out_grad_far, r.out_grad)], [(r.c_out_far, r.c_out)]]
    fetches += [[(far, r.wide_par.at[k]) for k, far in enumerate(wide_far)]]
    fetches += [[(r.gmat_far, r.gmat)]]
    for k, group_of in enumerate(fetches):
        for far, held in group_of:
            pltpu.make_async_copy(far, held, r.fetch_sem.at[k]).start()
    landed(r.lengths, r.fetch_sem.at[0])

    first_len = [r.lengths[m, 0] for m in range(2)]
    total_len = [r.lengths[m, 0] + r.lengths[m, 1] for m in range(2)]

    def put(index, at, row):
        for k in range(row.shape[1] // 128):
            r.sum_own[index, at + k : at + k + 1, :] = row[:, k * 128 : (k + 1) * 128]

    def put_late(at, row):
        for k in range(cfg.sections):
            r.late_own[k, at : at + 1, :] = row[:, k * 128 : (k + 1) * 128]

    chunk = 32
    for m in range(2):

        landed(r.tokens.at[m], r.fetch_sem.at[1 + m])

        def token_sums(t, carry, m=m):
            at = pl.ds(t * chunk, chunk)
            v = r.tokens[m, at, :].astype(F32)
            place_row = t * chunk + lax.broadcasted_iota(jnp.int32, (chunk, width), 0)
            kept = jnp.where(place_row < total_len[m], v, 0.0)
            return carry[0] + fold_rows(kept), carry[1] + fold_rows(kept * v)

        zero = jnp.zeros((SUB, width), F32)
        sums, squares = sweep(rows // chunk, token_sums, (zero, zero))
        put(m, 0, jnp.sum(sums, axis=0, keepdims=True))
        put(m, 4, jnp.sum(squares, axis=0, keepdims=True))
        if m == 0:
            for k in range(2):
                count = jnp.minimum(total_len[k], rows).astype(F32)
                r.sum_own[0, 8 + k : 9 + k, :] = jnp.full((1, 128), count, F32)
            pl.semaphore_wait(barrier, len(peers))
        first_sum[m].start()

    at_i = lax.broadcasted_iota(jnp.int32, (rows, rows), 0)
    at_r = lax.broadcasted_iota(jnp.int32, (rows, rows), 1)
    r.spread[...] = jnp.where(
        at_r == (at_i % SUB) * steps + at_i // SUB, 1.0, 0.0
    ).astype(BF16)
    r.gather[...] = jnp.where(
        at_i == (at_r % SUB) * steps + at_r // SUB, 1.0, 0.0
    ).astype(BF16)
    for m in range(2):
        r.first_in[m] = matmul(r.spread[...], r.tokens[m]).astype(BF16)
    for m in range(2):
        first_sum[m].turn()
    landed(r.out_grad, r.fetch_sem.at[5])
    for m in range(2):
        r.out_grads[m] = matmul(r.spread[...], r.out_grad[m]).astype(BF16)
    held = lax.broadcasted_iota(jnp.int32, (rows, 128), 0)
    held = (held % SUB) * steps + held // SUB
    all_start, all_end = [], []
    for m in range(2):
        one, zero = jnp.float32(1.0), jnp.float32(0.0)
        past = held >= total_len[m]
        starts = (held == 0) | (held == first_len[m]) | past
        ends = (held == first_len[m] - 1) | (held == total_len[m] - 1) | past | (held == rows - 1)
        r.valid[m] = jnp.where(past, zero, one)
        r.keep_start[m] = jnp.where(starts, zero, one)
        r.keep_end[m] = jnp.where(ends, zero, one)
        for kept, mask in ((all_start, r.keep_start), (all_end, r.keep_end)):
            kept.append(jnp.min(mask[m].reshape(steps, SUB, 128), axis=0))

    r.par[...] = jnp.zeros((SUB, lanes), F32)
    r.par[0:2, :] = jnp.ones((2, lanes), F32)
    landed(r.state_par, r.fetch_sem.at[3])
    r.par[0:2, 0:half] = r.decay[...]
    r.par[2:4, 0:half] = r.freq[...]
    r.par[4:6, 0:half] = r.lstep[...]
    decay, spin = r.par[0:2, :], r.par[2:4, :]
    step_size = jnp.exp(r.par[4:6, :])
    damping = jnp.exp(-decay * step_size)
    bar_re = damping * jnp.cos(spin * step_size)
    bar_im = damping * jnp.sin(spin * step_size)
    modulus = decay * decay + spin * spin
    fac_re = ((bar_re - 1.0) * -decay + bar_im * spin) / modulus
    fac_im = (bar_im * -decay - (bar_re - 1.0) * spin) / modulus
    pow_re, pow_im = bar_re, bar_im
    power = 1
    while power < steps:
        pow_re, pow_im = cmul(pow_re, pow_im, pow_re, pow_im)
        power *= 2

    lane = lax.broadcasted_iota(jnp.int32, (1, 128), 1)
    low_lanes = lane < half - 128
    turn_by = half - 128

    from_column = lax.broadcasted_iota(jnp.int32, (states, 2 * lanes), 0)
    to_column = lax.broadcasted_iota(jnp.int32, (states, 2 * lanes), 1)
    moved_to = jnp.where(from_column < half, from_column, from_column + (lanes - half))
    r.widen[...] = jnp.where(to_column == moved_to, 1.0, 0.0).astype(BF16)
    for held, k in ((r.b_in, 4), (r.c_out, 6), (r.wide_par, 7), (r.gmat, 8)):
        landed(held, r.fetch_sem.at[k])
    for l in range(2):
        r.b_pad[l] = matmul(r.b_in[l], r.widen[...]).astype(BF16)
        blank = jnp.zeros((lanes - half, width), BF16)
        r.c_pad[l, 0:half, :] = r.c_out[l, 0:half, :]
        r.c_pad[l, half:lanes, :] = blank
        r.c_pad[l, lanes : lanes + half, :] = r.c_out[l, half:states, :]
        r.c_pad[l, lanes + half : 2 * lanes, :] = blank

    def across(end, coef, reverse):
        end_re, end_im = end
        coef_re, coef_im = coef
        sub = lax.broadcasted_iota(jnp.int32, (SUB, lanes), 0)
        for by in (1, 2, 4):
            turn = SUB - by if reverse else by
            live = sub < SUB - by if reverse else sub >= by

            def moved(x):
                return jnp.where(live, pltpu.roll(x, turn, 0), 0.0)

            add_re, add_im = cmul(coef_re, coef_im, moved(end_re), moved(end_im))
            coef_re, coef_im = cmul(coef_re, coef_im, moved(coef_re), moved(coef_im))
            end_re, end_im = end_re + add_re, end_im + add_im
        turn = SUB - 1 if reverse else 1
        live = sub < SUB - 1 if reverse else sub >= 1
        return tuple(jnp.where(live, pltpu.roll(x, turn, 0), 0.0) for x in (end_re, end_im))

    def wide8(x, l):
        return jnp.broadcast_to(x[l : l + 1, :], (SUB, x.shape[1]))

    def group_rows(p):
        return pl.ds(p * SUB, SUB)

    def scan_coefs(l, m, reverse):
        keep = r.keep_end if reverse else r.keep_start
        all_kept = repeat_lanes((all_end if reverse else all_start)[m], lanes // 128)
        product = (all_kept * wide8(pow_re, l), all_kept * wide8(pow_im, l))
        return keep, wide8(bar_re, l), wide8(bar_im, l), product

    def advance(keep, m, at, br, bi, re, im, src_re, src_im):
        k = repeat_lanes(keep[m, at, :], lanes // 128)
        kr, ki = k * br, k * bi
        return kr * re - ki * im + src_re, kr * im + ki * re + src_im

    def scan_states(l, m):
        reverse = l == 1
        lead = 0 if reverse else 1
        keep, br, bi, product = scan_coefs(l, m, reverse)
        fr, fi = wide8(fac_re, l), wide8(fac_im, l)
        zero = jnp.zeros((SUB, lanes), F32)

        def ends(t, carry):
            p = steps - 1 - t if reverse else t
            at = group_rows(p)
            v = repeat_lanes(r.valid[m, at, :], lanes // 128)
            drive_re = r.drive[l, m, at, 0:lanes]
            drive_im = r.drive[l, m, at, lanes : 2 * lanes]
            src_re, src_im = cmul(fr, fi, v * drive_re, v * drive_im)
            r.state[l, m, group_rows(p + lead), 0:lanes] = src_re
            r.state[l, m, group_rows(p + lead), lanes : 2 * lanes] = src_im
            return advance(keep, m, at, br, bi, *carry, src_re, src_im)

        end = sweep(steps, ends, (zero, zero))
        enter = across(end, product, reverse)
        first = steps if reverse else 0
        r.state[l, m, first * SUB : (first + 1) * SUB, 0:lanes] = enter[0]
        r.state[l, m, first * SUB : (first + 1) * SUB, lanes : 2 * lanes] = enter[1]

        def fill(t, carry):
            done = []
            for k in range(2):
                p = steps - 1 - (2 * t + k) if reverse else 2 * t + k
                at, to = group_rows(p), group_rows(p + lead)
                src_re = r.state[l, m, to, 0:lanes]
                src_im = r.state[l, m, to, lanes : 2 * lanes]
                carry = advance(keep, m, at, br, bi, *carry, src_re, src_im)
                r.state[l, m, to, 0:lanes] = carry[0]
                r.state[l, m, to, lanes : 2 * lanes] = carry[1]
                done.append(jnp.concatenate([carry[0], -carry[1]], axis=1))
            pair = steps // 2 - 1 - t if reverse else t
            both = jnp.concatenate(done[::-1] if reverse else done, axis=0)
            to = pl.ds(m * rows + pair * 16, 16)
            r.joined[l, to, :] = both.astype(BF16)
            return carry

        sweep(steps // 2, fill, enter)

    def scan_grads(l, m):
        reverse = l == 0
        back = 1 if l == 1 else 0
        keep, br, bi, product = scan_coefs(l, m, reverse)
        keep_state = r.keep_start if l == 0 else r.keep_end
        fr, fi = 2.0 * wide8(fac_re, l), 2.0 * wide8(fac_im, l)
        zero = jnp.zeros((SUB, lanes), F32)

        def ends(t, carry):
            p = steps - 1 - t if reverse else t
            at = group_rows(p)
            q_re = r.q[m, at, 0:lanes]
            q_im = r.q[m, at, lanes : 2 * lanes]
            return advance(keep, m, at, br, bi, *carry, q_re, q_im)

        end = sweep(steps, ends, (zero, zero))
        enter = across(end, product, reverse)

        def fill(t, carry):
            w, bar_sum, fac_sum = carry
            done = []
            for k in range(2):
                p = steps - 1 - (2 * t + k) if reverse else 2 * t + k
                at, near = group_rows(p), group_rows(p + back)
                q_re = r.q[m, at, 0:lanes]
                q_im = r.q[m, at, lanes : 2 * lanes]
                w = advance(keep, m, at, br, bi, *w, q_re, q_im)
                kept = repeat_lanes(keep_state[m, at, :], lanes // 128)
                near_re = kept * r.state[l, m, near, 0:lanes]
                near_im = kept * r.state[l, m, near, lanes : 2 * lanes]
                term = cmul(*w, near_re, near_im)
                bar_sum = (bar_sum[0] + term[0], bar_sum[1] + term[1])
                v = repeat_lanes(r.valid[m, at, :], lanes // 128)
                vw = (v * w[0], v * w[1])
                drive_re = r.drive[l, m, at, 0:lanes]
                drive_im = r.drive[l, m, at, lanes : 2 * lanes]
                term = cmul(*vw, drive_re, drive_im)
                fac_sum = (fac_sum[0] + term[0], fac_sum[1] + term[1])
                gd_re, gd_im = cmul(fr, fi, *vw)
                im_low = pltpu.roll(-gd_im[:, 0:128], 64, 1)
                im_high = pltpu.roll(-gd_im[:, 128:256], 64, 1)
                done.append(
                    jnp.concatenate(
                        [
                            gd_re[:, 0:128],
                            jnp.where(low_lanes, gd_re[:, 128:256], im_low),
                            jnp.where(low_lanes, im_low, im_high),
                        ],
                        axis=1,
                    )
                )
            pair = steps // 2 - 1 - t if reverse else t
            both = jnp.concatenate(done[::-1] if reverse else done, axis=0)
            to = pl.ds(m * rows + pair * 16, 16)
            r.grad_drive[l, to, :] = both.astype(BF16)
            return w, bar_sum, fac_sum

        none = (zero, zero)
        _, bar_sum, fac_sum = sweep(steps // 2, fill, (enter, none, none))
        for k, part in enumerate((*bar_sum, *fac_sum)):
            r.state_sums[l, m, k] = part

    def row_of(ref, l):
        return ref[l : l + 1, :]

    def micro_rows(m):
        return slice(m * rows, (m + 1) * rows)

    gelu_chunk = 16
    halves = (slice(0, rows // 2), slice(rows // 2, rows))

    def moved(m, part):
        return slice(m * rows + part.start, m * rows + part.stop)


    def mixer(l, m, center, inv):
        gain, bias, skip = row_of(r.gain, l), row_of(r.bias, l), row_of(r.skip, l)

        def normalise(t, carry):
            at = pl.ds(t * chunk, chunk)
            if l == 0:
                v = r.first_in[m, at, :].astype(F32)
            else:
                v = r.second_in[m, at, :]
            normed = (v - center) * inv
            r.normed[l, m, at, :] = normed
            to = pl.ds(m * rows + t * chunk, chunk)
            r.scaled[l, to, :] = (normed * gain + bias).astype(BF16)
            return carry

        sweep(rows // chunk, normalise, 0)
        yield
        r.drive[l, m] = matmul(r.scaled[l, micro_rows(m), :], r.b_pad[l])
        yield
        scan_states(l, m)
        yield
        for part in halves:
            r.work[m, part, :] = matmul(r.joined[l, moved(m, part), :], r.c_pad[l])

        yield

        def activate(t, carry):
            at = pl.ds(t * gelu_chunk, gelu_chunk)
            scaled = r.normed[l, m, at, :] * gain + bias
            y = (2.0 * r.work[m, at, :] + skip * scaled).astype(BF16).astype(F32)
            below = 0.5 + 0.5 * lax.erf(y * 0.7071067811865476)
            density = jnp.exp(-0.5 * y * y) * 0.3989422804014327
            active = y * below
            r.active[l, m, at, :] = active
            r.slope[l, m, at, :] = below + y * density
            to = pl.ds(m * rows + t * gelu_chunk, gelu_chunk)
            r.active_low[l, to, :] = active.astype(BF16)
            return carry

        for k, part in enumerate(halves):
            for t in range(rows // gelu_chunk // 2):
                activate(k * (rows // gelu_chunk // 2) + t, 0)
            r.work[m, part, :] = matmul(r.active_low[l, moved(m, part), :], r.gmat[l])

    def first_gate(m):
        gbias = row_of(r.gbias, 0)

        def gate(t, carry):
            at = pl.ds(t * gelu_chunk, gelu_chunk)
            opened = jax.nn.sigmoid(r.work[m, at, :] + gbias)
            r.sig[0, m, at, :] = opened
            v = repeat_lanes(r.valid[m, at, :], width // 128)
            gated = v * r.active[0, m, at, :] * opened
            second = r.first_in[m, at, :].astype(F32) + gated.astype(BF16).astype(F32)
            r.second_in[m, at, :] = second
            kept = v * second
            return carry[0] + fold_rows(kept), carry[1] + fold_rows(kept * second)

        zero = jnp.zeros((SUB, width), F32)
        sums, squares = sweep(rows // gelu_chunk, gate, (zero, zero))
        put(2 + m, 0, jnp.sum(sums, axis=0, keepdims=True))
        put(2 + m, 4, jnp.sum(squares, axis=0, keepdims=True))

    bias_sums = {}
    skip_sums = {}

    def gate_grad(l, m, grad_of):
        gbias = row_of(r.gbias, l)

        def gate(t, carry):
            at = pl.ds(t * gelu_chunk, gelu_chunk)
            if l == 1:
                opened = jax.nn.sigmoid(r.work[m, at, :] + gbias)
                r.sig[1, m, at, :] = opened
            else:
                opened = r.sig[0, m, at, :]
            v = repeat_lanes(r.valid[m, at, :], width // 128)
            masked = v * grad_of(at, v)
            through = masked * opened
            r.through[m, at, :] = through
            grad_logits = through * r.active[l, m, at, :] * (1.0 - opened)
            to = pl.ds(m * rows + t * gelu_chunk, gelu_chunk)
            r.grad_logits[l, to, :] = grad_logits.astype(BF16)
            return carry + fold_rows(grad_logits)

        zero = jnp.zeros((SUB, width), F32)
        bias_sums[l, m] = sweep(rows // gelu_chunk, gate, zero)
        yield

    def branch_grad(l, m):
        gain, bias = row_of(r.gain, l), row_of(r.bias, l)
        r.work[m] = matmul_nt(r.grad_logits[l, micro_rows(m), :], r.gmat[l])
        yield

        def branch(t, carry):
            at = pl.ds(t * chunk, chunk)
            grad_active = r.through[m, at, :] + r.work[m, at, :]
            g = (r.slope[l, m, at, :] * grad_active).astype(BF16)
            to = pl.ds(m * rows + t * chunk, chunk)
            r.branch[l, to, :] = g
            scaled = r.normed[l, m, at, :] * gain + bias
            return carry + fold_rows(g.astype(F32) * scaled)

        zero = jnp.zeros((SUB, width), F32)
        skip_sums[l, m] = sweep(rows // chunk, branch, zero)
        yield
        r.q[m] = matmul_nt(r.branch[l, micro_rows(m), :], r.c_pad[l])
        yield

    def mixer_grad(l, m):
        skip = row_of(r.skip, l)
        scan_grads(l, m)
        yield
        r.work[m] = matmul_nt(r.grad_drive[l, micro_rows(m), :], r.b_in[l])
        yield

        def scaled_grad(t, carry):
            at = pl.ds(t * chunk, chunk)
            to = pl.ds(m * rows + t * chunk, chunk)
            grad = r.work[m, at, :] + skip * r.branch[l, to, :].astype(F32)
            r.grad_scaled[l, m, at, :] = grad
            normed = r.normed[l, m, at, :]
            return carry[0] + fold_rows(grad), carry[1] + fold_rows(grad * normed)

        zero = jnp.zeros((SUB, width), F32)
        sums, products = sweep(rows // chunk, scaled_grad, (zero, zero))
        sums = jnp.sum(sums, axis=0, keepdims=True)
        products = jnp.sum(products, axis=0, keepdims=True)
        if l == 1:
            put(4 + m, 0, sums)
            put(4 + m, 4, products)
        else:
            put_late(2 * m, sums)
            put_late(2 * m + 1, products)

    def moments(total, at, count):
        center = unfold(total, at, 4) / count
        return center, lax.rsqrt(unfold(total, at + 4, 4) / count - center * center + epsilon)

    own_columns = pl.ds(pl.multiple_of(section * 128, 128), 128)

    def gate_weights(l, ref):
        grad = matmul_tn(r.active_low[l, :, own_columns], r.grad_logits[l])
        ref[:, :, :, 0:width] = grad.astype(BF16).reshape(2, QUAD, 16, width)

    def out_weights(l, ref, at):
        grad = 2.0 * matmul_tn(r.joined[l], r.branch[l, :, own_columns])
        grad = jnp.concatenate([grad[0:half, :], grad[lanes : lanes + half, :]], axis=0)
        tall = states // (2 * QUAD)
        for k in range(tall // 16):
            for c in range(2):
                for z in range(QUAD):
                    first = (c * QUAD + z) * tall + 16 * k
                    ref[c, z, :, at + 128 * k : at + 128 * (k + 1)] = grad[
                        first : first + 16, :
                    ].astype(BF16)

    def in_weights(l, ref, at):
        grad = matmul_tn(r.scaled[l, :, own_columns], r.grad_drive[l])
        ref[:, :, :, at : at + states] = grad.astype(BF16).reshape(2, QUAD, 16, states)

    def layer_rows(l):
        def both(sums):
            return jnp.sum(sums[l, 0] + sums[l, 1], axis=0, keepdims=True)

        put_late(4 + 2 * l, both(skip_sums))
        put_late(5 + 2 * l, both(bias_sums))
        part = [
            jnp.sum(r.state_sums[l, 0, k] + r.state_sums[l, 1, k], axis=0, keepdims=True)
            for k in range(4)
        ]
        gb_re, gb_im = 2.0 * part[0], -2.0 * part[1]
        gf_re, gf_im = 2.0 * part[2], -2.0 * part[3]
        one = slice(l, l + 1)
        lam_re, lam_im, size = -decay[one], spin[one], step_size[one]
        b_re, b_im, f_re, f_im = bar_re[one], bar_im[one], fac_re[one], fac_im[one]
        top_re, top_im = size * b_re - f_re, size * b_im - f_im
        square = modulus[one]
        d_re = (top_re * lam_re + top_im * lam_im) / square
        d_im = (top_im * lam_re - top_re * lam_im) / square
        gl_re = size * (b_re * gb_re + b_im * gb_im) + (d_re * gf_re + d_im * gf_im)
        gl_im = size * (b_re * gb_im - b_im * gb_re) + (d_re * gf_im - d_im * gf_re)
        e_re, e_im = cmul(lam_re, lam_im, b_re, b_im)
        g_step = size * ((e_re * gb_re + e_im * gb_im) + (b_re * gf_re + b_im * gf_im))
        parts = [
            row[:, k : k + 128] for row in (-gl_re, gl_im, g_step) for k in range(0, lanes, 128)
        ]
        for k, row in enumerate(parts):
            k += l * len(parts)
            at = 8 + k % LATE_STATES
            r.late_own[k // LATE_STATES, at : at + 1, :] = row

    def mixed_rows(m):
        def mix(t, carry):
            at = pl.ds(t * chunk, chunk)
            gated = (
                r.valid[m, at, :]
                * r.active[1, m, at, own_columns]
                * r.sig[1, m, at, own_columns]
            )
            stream = r.second_in[m, at, own_columns].astype(BF16).astype(F32)
            r.narrow[at, :] = (stream + gated).astype(BF16)
            return carry

        sweep(rows // chunk, mix, 0)
        r.mixed[m] = matmul(r.gather[...], r.narrow[...]).astype(BF16)

    def stream_grad(l, m, total, count, inv):
        gain = row_of(r.gain, l)
        first = gain * unfold(total, 0, 4) / count
        second = gain * unfold(total, 4, 4) / count
        return gain, first, second, inv

    def take(steps):
        for _ in steps:
            pass

    counts, norm0 = [None, None], [None, None]
    for m in range(2):
        total = first_sum[m].total()
        if m == 0:
            counts = [repeat_lanes(total[8 + k : 9 + k, :], width // 128) for k in range(2)]
        norm0[m] = moments(total, 0, counts[m])
        take(mixer(0, m, *norm0[m]))
        first_gate(m)
        mid_sum[m].start()
        mid_sum[m].turn()

    norm1 = [None, None]

    def second_layer(m):
        norm1[m] = moments(mid_sum[m].total(), 0, counts[m])
        yield from mixer(1, m, *norm1[m])
        yield from gate_grad(1, m, lambda at, v: r.out_grads[m, at, :].astype(F32))
        yield from branch_grad(1, m)
        yield from mixer_grad(1, m)
        upper_sum[m].start()
        upper_sum[m].turn()

    for m in range(2):
        take(second_layer(m))

    gate_weights(1, r.mine_0)
    upper.to_core(gate_part)
    out_weights(1, r.mine_0, width)
    upper.to_core(out_part)
    in_weights(1, r.mine_0, width + states)
    upper.to_core(in_part)
    layer_rows(1)

    def second_grad(m, total):
        gain, first, second, inv = stream_grad(1, m, total, counts[m], norm1[m][1])

        def grad_of(at, v):
            grad_normed = r.grad_scaled[1, m, at, :] * gain
            normed = r.normed[1, m, at, :]
            grad_stream = inv * (grad_normed - v * (first + normed * second))
            out_grad = r.out_grads[m, at, :].astype(F32)
            grad = (out_grad + grad_stream.astype(BF16).astype(F32)).astype(BF16)
            r.grad_second[m, at, :] = grad
            return grad.astype(F32)

        return grad_of

    upper_total = [upper_sum[0].total()]
    take(gate_grad(0, 0, second_grad(0, upper_total[0])))
    upper.to_quad(gate_part)
    take(branch_grad(0, 0))
    upper.to_quad(out_part)
    upper.to_quad(in_part)
    take(mixer_grad(0, 0))
    upper_total.append(upper_sum[1].total())
    take(gate_grad(0, 1, second_grad(1, upper_total[1])))
    gate_weights(0, r.mine_1)
    lower.to_core(gate_part)
    take(branch_grad(0, 1))
    upper.to_groups(gate_part)
    lower.to_quad(gate_part)
    last = mixer_grad(0, 1)
    next(last)
    out_weights(0, r.mine_1, width)
    lower.to_core(out_part)
    upper.to_groups(out_part)
    next(last)
    upper.to_groups(in_part)
    take(last)
    lower.to_quad(out_part)
    in_weights(0, r.mine_1, width + states)
    lower.to_core(in_part)
    layer_rows(0)
    late_sum.start()
    upper.to_near(gate_part)
    lower.to_quad(in_part)
    late_sum.turn()
    mixed_rows(0)
    lower.to_groups(gate_part)
    upper.to_near(out_part)
    lower.to_groups(out_part)
    upper.to_near(in_part)
    mixed_rows(1)
    lower.to_groups(in_part)
    upper.to_sections(gate_part)
    lower.to_corner(gate_part)
    upper.to_sections(out_part)
    upper.to_sections(in_part)
    lower.to_sections(gate_part)

    late = late_sum.total()
    r.late[section] = late
    block = r.late.at[section]
    for k in (1, 2, 3):
        remote(block, block, r.late_sem.at[0], r.late_sem.at[1], (beyond[k], dp))
    own_gain = r.gain[0:1, own_columns]
    for m in range(2):
        count = counts[m][:, 0:128]
        first = own_gain * late[2 * m : 2 * m + 1, :] / count
        second = own_gain * late[2 * m + 1 : 2 * m + 2, :] / count
        r.rows[m : m + 1, :] = norm0[m][1]
        inv = r.rows[m : m + 1, own_columns]

        def token_grad(t, carry, m=m, first=first, second=second, inv=inv):
            at = pl.ds(t * chunk, chunk)
            grad_normed = r.grad_scaled[0, m, at, own_columns] * own_gain
            normed = r.normed[0, m, at, own_columns]
            grad_stream = inv * (grad_normed - r.valid[m, at, :] * (first + normed * second))
            grad = r.grad_second[m, at, own_columns].astype(F32) + grad_stream
            high = grad.astype(BF16)
            r.narrow[at, :] = high
            r.narrow_rest[at, :] = (grad - high.astype(F32)).astype(BF16)
            return carry

        sweep(rows // chunk, token_grad, 0)
        r.token_grad[m] = matmul(r.gather[...], r.narrow[...]) + matmul(
            r.gather[...], r.narrow_rest[...]
        )
    r.upper_norm[...] = upper_total[0] + upper_total[1]
    lower.to_corner(out_part)
    lower.to_sections(out_part)
    lower.to_corner(in_part)
    lower.to_sections(in_part)
    upper.to_sibling(gate_part)
    upper.to_sibling(out_part)
    upper.to_sibling(in_part)
    lower.to_sibling(gate_part)
    lower.to_sibling(out_part)
    lower.to_sibling(in_part)
    for k in range(2):
        landed(r.late.at[0 : cfg.sections - 1], r.late_sem.at[k])
    for batch in batches:
        batch.end()
    for each in small:
        each.end()


def lay_out_kernel(cfg, *refs):
    full = refs[1], refs[0]
    late, upper_norm, mixed, token_grad = refs[2:6]
    (
        mixed_out,
        token_grad_out,
        gain_out,
        bias_out,
        decay_out,
        freq_out,
        step_out,
        in_out,
        out_out,
        skip_out,
        gate_out,
        gbias_out,
    ) = refs[6:18]
    in_held, out_held, gate_held = refs[18:21]
    rows_held, sems = refs[21:28], refs[28]
    width, states, half = cfg.width, cfg.states, cfg.half
    tall = states // (2 * QUAD)
    copies = []

    def send(held, out, sem=None):
        copy = pltpu.make_async_copy(held, out, sems.at[3 + len(copies) if sem is None else sem])
        copy.start()
        if sem is None:
            copies.append(copy)

    send(mixed, mixed_out)
    send(token_grad, token_grad_out)
    def columns(at):
        return jnp.concatenate([late[s, at : at + 1, :] for s in range(cfg.sections)], axis=1)

    row_outs = (bias_out, gain_out, skip_out, gbias_out, decay_out, freq_out, step_out)
    values = [
        (columns(0) + columns(2), unfold(upper_norm, 0, 4)),
        (columns(1) + columns(3), unfold(upper_norm, 4, 4)),
        (columns(4), columns(6)),
        (columns(5), columns(7)),
    ]
    for k in range(3):
        places = [(6 * l + 2 * k + part) for l in range(2) for part in range(2)]
        row = [late[p // LATE_STATES, 8 + p % LATE_STATES, :][None] for p in places]
        values.append([jnp.concatenate(row[2 * l : 2 * l + 2], axis=1)[:, 0:half] for l in range(2)])
    for held, out, value in zip(rows_held, row_outs, values):
        for l in range(2):
            held[l : l + 1, :] = value[l]
        send(held, out)

    for l in (1, 0):
        parts = [(full[l], begin) for begin in (0, width, width + states)]
        for s in range(cfg.sections):
            mine = slice(s * 128, (s + 1) * 128)
            members = [(c, z) for c in range(2) for z in range(QUAD)]
            for (part, begin), held, out, wide, sem in (
                (parts[0], gate_held, gate_out, width, 0),
                (parts[2], in_held, in_out, states, 1),
            ):
                for c, z in members:
                    at = s * 128 + (c * QUAD + z) * 16
                    held[l, at : at + 16, :] = part[c, s, z, :, begin : begin + wide].astype(F32)
                send(held.at[l, mine], out.at[l, mine], sem)
            part, begin = parts[1]
            for c, z in members:
                for k in range(tall // 16):
                    first = (c * QUAD + z) * tall + 16 * k
                    out_held[l, first : first + 16, mine] = part[
                        c, s, z, :, begin + k * 128 : begin + (k + 1) * 128
                    ].astype(F32)
        send(out_held.at[l], out_out.at[l], 2)
    for copy in copies:
        copy.wait()
    for sem, out in enumerate((gate_out, in_out, out_out)):
        landed(out, sems.at[sem])


INPUTS = tuple(
    dict(
        tokens=0,
        lengths=0,
        out_grad=0,
        gain=0,
        bias=0,
        decay=0,
        freq=0,
        lstep=0,
        b_in=0,
        c_out=0,
        skip=0,
        gmat=0,
        gbias=0,
    )
)


def per_device(cfg, *args):
    rows, width, states, lanes = cfg.rows, cfg.width, cfg.states, cfg.lanes
    sections, dp, chips = cfg.sections, cfg.dp, cfg.dp // 2
    groups = chips // QUAD
    steps = rows // SUB
    vmem, dma = pltpu.VMEM, pltpu.SemaphoreType.DMA
    widths = (width + 2 * states,) * 2
    outs = {f"full_{k}": ((2, sections, QUAD, 16, w), BF16) for k, w in enumerate(widths)}
    outs.update(
        late=((sections, 16, 128), F32), upper_norm=((8, 128), F32), mixed=((2, rows, 128), BF16), token_grad=((2, rows, 128), F32)
    )
    scratch = dict(
        sum_own=vmem((len(SUM_ROWS), 24, 128), F32),
        sum_sibling=vmem((len(SUM_ROWS), 24, 128), F32),
        sum_slots=vmem((len(SUM_ROWS), min(dp, max(chips, 8)), 24, 128), F32),
        late_own=vmem((sections, 16, 128), F32),
        late_sem=dma((2,)),
        sum_sem=dma((first_sems(cfg)[-1],)),
        grad_send=dma((2, 7 + (groups > 1))),
        grad_recv=dma((2, 1 + 3 * (PART_SEMS + (groups > 1)))),
        fetch_sem=dma((9,)),
        lengths=pltpu.SMEM((2, 2), jnp.int32),
        tokens=vmem((2, rows, width), BF16),
        wide_par=vmem((4, 2, width), F32),
        state_par=vmem((3, 2, states // 2), F32),
        b_in=vmem((2, width, states), BF16),
        c_out=vmem((2, states, width), BF16),
        gmat=vmem((2, width, width), BF16),
        out_grad=vmem((2, rows, width), BF16),
        widen=vmem((states, 2 * lanes), BF16),
        q=vmem((2, rows, 2 * lanes), F32),
        spread=vmem((rows, rows), BF16),
        gather=vmem((rows, rows), BF16),
        first_in=vmem((2, rows, width), BF16),
        out_grads=vmem((2, rows, width), BF16),
        second_in=vmem((2, rows, width), F32),
        grad_second=vmem((2, rows, width), BF16),
        valid=vmem((2, rows, 128), F32),
        keep_start=vmem((2, rows, 128), F32),
        keep_end=vmem((2, rows, 128), F32),
        par=vmem((SUB, lanes), F32),
        b_pad=vmem((2, width, 2 * lanes), BF16),
        c_pad=vmem((2, 2 * lanes, width), BF16),
        normed=vmem((2, 2, rows, width), F32),
        scaled=vmem((2, 2 * rows, width), BF16),
        drive=vmem((2, 2, rows, 2 * lanes), F32),
        state=vmem((2, 2, (steps + 1) * SUB, 2 * lanes), F32),
        joined=vmem((2, 2 * rows, 2 * lanes), BF16),
        work=vmem((2, rows, width), F32),
        active=vmem((2, 2, rows, width), F32),
        active_low=vmem((2, 2 * rows, width), BF16),
        slope=vmem((2, 2, rows, width), F32),
        sig=vmem((2, 2, rows, width), F32),
        through=vmem((2, rows, width), F32),
        grad_logits=vmem((2, 2 * rows, width), BF16),
        branch=vmem((2, 2 * rows, width), BF16),
        grad_drive=vmem((2, 2 * rows, states), BF16),
        grad_scaled=vmem((2, 2, rows, width), F32),
        state_sums=vmem((2, 2, 4, SUB, lanes), F32),
        narrow=vmem((rows, 128), BF16),
        narrow_rest=vmem((rows, 128), BF16),
        rows=vmem((SUB, width), F32),
    )
    for k, w in enumerate(widths):
        blocks = (2, QUAD), (QUAD,), (QUAD,), (QUAD,), (groups,)
        for part, block in zip(STAGES, blocks):
            scratch[f"{part}_{k}"] = vmem((*block, 16, w), BF16)
    in_vmem = pl.BlockSpec(memory_space=pltpu.VMEM)
    in_hbm = pl.BlockSpec(memory_space=pltpu.HBM)
    names = tuple(f"{name}_far" for name in INPUTS) + tuple(outs) + tuple(scratch)
    made = pl.pallas_call(
        partial(main_kernel, cfg, names),
        name="layers",
        out_shape=[vmem(*spec) for spec in outs.values()],
        in_specs=[in_hbm for name in INPUTS],
        out_specs=[in_vmem for name in outs],
        scratch_shapes=list(scratch.values()),
        compiler_params=pltpu.CompilerParams(
            collective_id=0, has_side_effects=True, vmem_limit_bytes=56 * 2**20
        ),
    )(*args)
    shapes = [
        ((2, rows, 128), BF16),
        ((2, rows, 128), F32),
        ((2, width), F32),
        ((2, width), F32),
        ((2, states // 2), F32),
        ((2, states // 2), F32),
        ((2, states // 2), F32),
        ((2, width, states), F32),
        ((2, states, width), F32),
        ((2, width), F32),
        ((2, width, width), F32),
        ((2, width), F32),
    ]
    by_copy = (7, 8, 10)
    return pl.pallas_call(
        partial(lay_out_kernel, cfg),
        name="lay_out",
        out_shape=[jax.ShapeDtypeStruct(*spec) for spec in shapes],
        in_specs=[in_vmem] * 6,
        out_specs=[in_hbm] * 12,
        scratch_shapes=[vmem(*shapes[k]) for k in by_copy]
        + [vmem((2, width), F32)] * 4
        + [vmem((2, states // 2), F32)] * 3
        + [dma((12,))],
        compiler_params=pltpu.CompilerParams(vmem_limit_bytes=24 * 2**20),
    )(*made)


def solution(mesh):
    sections, dp = mesh.shape["section"], mesh.shape["dp"]

    def run(*args):
        _, rows, width = args[0].shape
        states = args[8].shape[2]
        cfg = SimpleNamespace(
            rows=rows // dp,
            width=width,
            states=states,
            half=states // 2,
            lanes=-(-states // 256) * 128,
            sections=sections,
            dp=dp,
        )
        split = P(None, "dp", None)
        shared = P()
        placed = P(None, "dp", "section")
        return jax.shard_map(
            partial(per_device, cfg),
            mesh=mesh,
            in_specs=(split, P(None, "dp"), split) + (shared,) * 10,
            out_specs=(placed, placed) + (shared,) * 10,
            check_vma=False,
        )(*args)

    return run
```

```python
from functools import partial
from types import SimpleNamespace

import jax
import jax.numpy as jnp
from jax import lax
from jax.experimental import pallas as pl
from jax.experimental.pallas import tpu as pltpu
from jax.sharding import PartitionSpec as P

epsilon = 1e-05
MESH = pl.DeviceIdType.MESH
F32 = jnp.float32
BF16 = jnp.bfloat16
SUB = 8
QUAD = 4
FAR_FIRST = (4, 6, 2, 3, 5, 7, 1)
LATE_STATES = 3
SUM_ROWS = (10, 8, 8, 8, 8, 8, 16)


STAGES = tuple(dict(mine=0, theirs=0, chip=0, quad=0, group=0, full=0))


def matmul(left, right):
    return jnp.dot(left, right, preferred_element_type=F32)


def matmul_nt(left, right):
    return lax.dot_general(left, right, (((1,), (1,)), ((), ())), preferred_element_type=F32)


def matmul_tn(left, right):
    return lax.dot_general(left, right, (((0,), (0,)), ((), ())), preferred_element_type=F32)


def cmul(ar, ai, br, bi):
    return ar * br - ai * bi, ar * bi + ai * br


def sweep(count, body, carry):
    for t in range(count):
        carry = body(t, carry)
    return carry


def repeat_lanes(x, times):
    return jnp.concatenate([x] * times, axis=1)


def fold_rows(x):
    return jnp.sum(x.reshape(x.shape[0] // SUB, SUB, x.shape[1]), axis=0)


def unfold(total, first, count):
    return jnp.concatenate([total[first + k : first + k + 1, :] for k in range(count)], axis=1)


def landed(block, sem):
    pltpu.make_async_copy(block, block, sem).wait()


def remote(src, dst, send_sem, recv_sem, device):
    pltpu.make_async_remote_copy(
        src_ref=src,
        dst_ref=dst,
        send_sem=send_sem,
        recv_sem=recv_sem,
        device_id=device,
        device_id_type=MESH,
    ).start()


def first_sems(cfg):
    begins = [0]
    for k in range(len(SUM_ROWS)):
        begins.append(begins[-1] + (2 if cfg.dp <= 8 and k < len(SUM_ROWS) - 1 else 4))
    return begins


class SmallSum:
    def __init__(self, place, direct, own, sibling, slots, sems):
        self.place, self.direct = place, direct
        self.own, self.sibling, self.slots, self.sems = own, sibling, slots, sems

    def to_all(self, slot, members, peer):
        self.members = members
        block = self.slots.at[slot]
        for step in FAR_FIRST if members == 8 else range(1, members):
            to = (self.place.section, peer(step))
            remote(block, block, self.sems.at[0], self.sems.at[1], to)

    def start(self):
        at = self.place
        if self.direct:
            self.slots[at.dp] = self.own[...]
            self.to_all(at.dp, at.devices, at.dp_peer)
        else:
            to = (at.section, at.sibling)
            remote(self.own, self.sibling, self.sems.at[2], self.sems.at[3], to)

    def turn(self):
        at = self.place
        if not self.direct:
            landed(self.sibling, self.sems.at[3])
            self.slots[at.chip] = self.own[...] + self.sibling[...]
            self.to_all(at.chip, at.chips, at.chip_peer)

    def total(self):
        landed(self.slots.at[0 : self.members - 1], self.sems.at[1])
        result = self.slots[0]
        for member in range(1, self.members):
            result = result + self.slots[member]
        return result

    def end(self):
        if not self.direct:
            landed(self.own, self.sems.at[2])
        landed(self.slots.at[0 : self.members - 1], self.sems.at[0])


class GradSum:
    part_sems, sends = 6, 5

    def __init__(self, place, parts, refs, send_sems, recv_sems):
        self.place, self.parts = place, parts
        self.mine, self.theirs, self.chip_part, self.quad_in, self.group_in, self.full = refs
        self.send_sems, self.recv_sems = send_sems, recv_sems

    def recv(self, part, k):
        if k == self.part_sems:
            return self.recv_sems.at[1 + 3 * self.part_sems + part]
        return self.recv_sems.at[1 + part * self.part_sems + k]

    def send(self, part, src, dst, send, recv, device):
        columns = self.parts[part]
        sem = self.recv_sems.at[0] if recv is None else self.recv(part, recv)
        remote(src.at[..., columns], dst.at[..., columns], self.send_sems.at[send], sem, device)

    def landed(self, part, block, k):
        landed(block.at[..., self.parts[part]], self.recv(part, k))

    def to_core(self, part):
        at = self.place
        self.send(part, self.mine.at[1 - at.core], self.theirs, 0, 0, (at.section, at.sibling))

    def to_quad(self, part):
        at, columns = self.place, self.parts[part]
        self.landed(part, self.theirs, 0)
        for k in range(QUAD):
            both = self.mine[at.core, k, :, columns].astype(F32)
            both = both + self.theirs[k, :, columns].astype(F32)
            self.chip_part[k, :, columns] = both.astype(BF16)
        for step in range(1, QUAD):
            other = lax.rem(at.quad + step, QUAD)
            to = (at.section, at.quad_peer(step))
            self.send(part, self.chip_part.at[other], self.quad_in.at[at.quad], 1, 1, to)
        self.quad_in[at.quad, :, columns] = self.chip_part[at.quad, :, columns]

    def to_groups(self, part):
        at, columns = self.place, self.parts[part]
        self.landed(part, self.quad_in.at[0 : QUAD - 1], 1)
        total = self.quad_in[0, :, columns].astype(F32)
        for k in range(1, QUAD):
            total = total + self.quad_in[k, :, columns].astype(F32)
        if at.groups > 1:
            mine = self.group_in.at[at.group]
            mine[:, columns] = total.astype(BF16)
            for step in range(1, at.groups):
                self.send(part, mine, mine, self.sends, self.part_sems, (at.section, at.chip_peer(step * QUAD)))
            self.landed(part, self.group_in.at[0 : at.groups - 1], self.part_sems)
            total = self.group_in[0, :, columns].astype(F32)
            for other in range(1, at.groups):
                total = total + self.group_in[other, :, columns].astype(F32)
        piece = self.full.at[at.core, at.section, at.quad]
        piece[:, columns] = total.astype(BF16)
        self.to_members(part)
        self.over_sections(part, at.quad)

    def to_members(self, part):
        at = self.place
        piece = self.full.at[at.core, at.section, at.quad]
        for step in range(1, QUAD):
            self.send(part, piece, piece, 2, 1 + step, (at.section, at.quad_peer(step)))

    def over_sections(self, part, quad):
        at = self.place
        piece = self.full.at[at.core, at.section, quad]
        for k in (1, 2, 3):
            self.send(part, piece, piece, 3, 5, (at.beyond(k), at.dp))

    def to_sections(self, part):
        at = self.place
        for step in range(1, QUAD):
            other = lax.rem(at.quad + QUAD - step, QUAD)
            self.landed(part, self.full.at[at.core, at.section, other], 1 + step)
            self.over_sections(part, other)
        self.to_other(part, at.section)

    def to_other(self, part, section):
        at = self.place
        block = self.full.at[at.core, section]
        self.send(part, block, block, 4, None, (at.section, at.sibling))

    def to_sibling(self, part):
        at = self.place
        self.landed(part, self.full.at[at.core, 0 : at.sections - 1], 5)
        for k in (1, 2, 3):
            self.to_other(part, at.beyond(k))

    def end(self):
        at = self.place
        landed(self.full.at[1 - at.core], self.recv_sems.at[0])
        landed(self.theirs, self.send_sems.at[0])
        landed(self.quad_in.at[0 : QUAD - 1], self.send_sems.at[1])
        landed(self.quad_in.at[0 : QUAD - 1], self.send_sems.at[2])
        self.end_sections()
        landed(self.full.at[at.core], self.send_sems.at[4])
        if at.groups > 1:
            landed(self.group_in.at[0 : at.groups - 1], self.send_sems.at[self.sends])


    def end_sections(self):
        at = self.place
        landed(self.full.at[at.core, 0 : at.sections - 1], self.send_sems.at[3])


class CornerSum(GradSum):
    part_sems, sends = 8, 7

    def to_members(self, part):
        at = self.place
        piece = self.full.at[at.core, at.section, at.quad]
        self.send(part, piece, piece, 5, 6, (at.beyond(3), at.dp))
        super().to_members(part)

    def over_sections(self, part, quad):
        at = self.place
        piece = self.full.at[at.core, at.section, quad]
        for k in (1, 2):
            self.send(part, piece, piece, 3, 5, (at.beyond(k), at.dp))

    def to_corner(self, part):
        at = self.place
        piece = self.full.at[at.core, at.beyond(3), at.quad]
        self.landed(part, piece, 6)
        for step in range(1, QUAD):
            self.send(part, piece, piece, 6, 7, (at.section, at.quad_peer(step)))

    def to_sibling(self, part):
        at = self.place
        self.landed(part, self.full.at[at.core, 0:2], 5)
        for k in (1, 2):
            self.to_other(part, at.beyond(k))
        self.landed(part, self.full.at[at.core, at.beyond(3), 0 : QUAD - 1], 7)
        self.to_other(part, at.beyond(3))

    def end_sections(self):
        at = self.place
        landed(self.full.at[at.core, 0:2], self.send_sems.at[3])
        landed(self.full.at[at.core, 0, 0], self.send_sems.at[5])
        landed(self.full.at[at.core, 0, 0 : QUAD - 1], self.send_sems.at[6])


class RelaySum(GradSum):
    def to_members(self, part):
        at = self.place
        piece = self.full.at[at.core, at.section, at.quad]
        self.send(part, piece, piece, 2, 2, (at.section, at.apart(2)))
        self.send(part, piece, piece, 2, 3, (at.section, at.apart(1)))

    def to_near(self, part):
        at = self.place
        far = 2 * (1 - at.high) + at.low
        piece = self.full.at[at.core, at.section, far]
        self.landed(part, piece, 2)
        self.send(part, piece, piece, 2, 4, (at.section, at.apart(1)))
        self.over_sections(part, far)
        near = 2 * at.high + 1 - at.low
        self.landed(part, self.full.at[at.core, at.section, near], 3)
        self.over_sections(part, near)

    def to_sections(self, part):
        at = self.place
        last = 2 * (1 - at.high) + 1 - at.low
        self.landed(part, self.full.at[at.core, at.section, last], 4)
        self.over_sections(part, last)
        self.to_other(part, at.section)


def grad_sems(groups):
    ends = [0]
    for kind in (RelaySum, CornerSum):
        ends.append(ends[-1] + kind.sends + (groups > 1))
        ends.append(ends[-1] + 1 + 3 * (kind.part_sems + (groups > 1)))
    return ends


def main_kernel(cfg, names, *refs):
    r = SimpleNamespace(**dict(zip(names, refs)))
    rows, width, states, half, lanes = (
        cfg.rows,
        cfg.width,
        cfg.states,
        cfg.half,
        cfg.lanes,
    )
    steps = rows // SUB
    section = lax.axis_index("section")
    dp = lax.axis_index("dp")
    chips = cfg.dp // 2
    core, chip = lax.rem(dp, 2), lax.div(dp, 2)
    quad, group = lax.rem(chip, QUAD), lax.div(chip, QUAD)
    beyond = {
        1: section + 1 - 2 * lax.rem(section, 2),
        2: section + 2 - 4 * lax.div(section, 2),
        3: 3 - section,
    }
    place = SimpleNamespace(
        section=section,
        beyond=lambda k: beyond[k],
        sections=cfg.sections,
        dp=dp,
        core=core,
        chip=chip,
        chips=chips,
        quad=quad,
        group=group,
        groups=chips // QUAD,
        devices=cfg.dp,
        dp_peer=lambda step: lax.rem(dp + step, cfg.dp),
        sibling=dp + 1 - 2 * core,
        chip_peer=lambda step: lax.rem(chip + step, chips) * 2 + core,
        high=lax.div(quad, 2),
        low=lax.rem(quad, 2),
        apart=lambda by: (
            chip + by * (1 - 2 * (lax.rem(quad, 2) if by == 1 else lax.div(quad, 2)))
        )
        * 2
        + core,
        quad_peer=lambda step: (group * QUAD + lax.rem(quad + step, QUAD)) * 2 + core,
    )

    direct = cfg.dp <= 8
    if direct:
        peers = [(section, place.dp_peer(step)) for step in range(1, cfg.dp)]
    else:
        peers = [(section, place.sibling)]
        peers += [(section, place.chip_peer(step)) for step in range(1, chips)]
    peers += [(beyond[k], dp) for k in (1, 2, 3)]
    barrier = pltpu.get_barrier_semaphore()
    for peer in peers:
        pl.semaphore_signal(barrier, inc=1, device_id=peer, device_id_type=MESH)

    sum_sems = first_sems(cfg)
    small = [
        SmallSum(
            place,
            direct and k < len(SUM_ROWS) - 1,
            r.sum_own.at[k, 0:tall] if k < len(SUM_ROWS) - 1 else r.late_own.at[section],
            r.sum_sibling.at[k, 0:tall],
            r.sum_slots.at[k, :, 0:tall],
            r.sum_sem.at[sum_sems[k] : sum_sems[k + 1]],
        )
        for k, tall in enumerate(SUM_ROWS)
    ]
    first_sum, mid_sum, upper_sum = small[0:2], small[2:4], small[4:6]
    late_sum = small[6]
    gate_part, out_part, in_part = range(3)
    bounds = (0, width, width + states, width + 2 * states)
    ends = grad_sems(place.groups)
    batches = [
        (RelaySum if k == 0 else CornerSum)(
            place,
            [slice(*bounds[k : k + 2]) for k in range(3)],
            [getattr(r, f"{part}_{k}") for part in STAGES],
            r.grad_sem.at[ends[2 * k] : ends[2 * k + 1]],
            r.grad_sem.at[ends[2 * k + 1] : ends[2 * k + 2]],
        )
        for k in range(2)
    ]
    upper, lower = batches

    r.gain, r.bias, r.skip, r.gbias = [r.wide_par.at[k] for k in range(4)]
    r.decay, r.freq, r.lstep = [r.state_par.at[k] for k in range(3)]
    wide_far = (r.gain_far, r.bias_far, r.skip_far, r.gbias_far)
    state_far = (r.decay_far, r.freq_far, r.lstep_far)
    fetches = [[(r.lengths_far, r.lengths)]]
    fetches += [[(r.tokens_far.at[m], r.tokens.at[m])] for m in range(2)]
    fetches += [[(far, r.state_par.at[k]) for k, far in enumerate(state_far)]]
    fetches += [[(r.b_in_far, r.b_in)], [(r.out_grad_far, r.out_grad)], [(r.c_out_far, r.c_out)]]
    fetches += [[(far, r.wide_par.at[k]) for k, far in enumerate(wide_far)]]
    fetches += [[(r.gmat_far, r.gmat)]]
    for k, group_of in enumerate(fetches):
        for far, held in group_of:
            pltpu.make_async_copy(far, held, r.fetch_sem.at[k]).start()
    landed(r.lengths, r.fetch_sem.at[0])

    first_len = [r.lengths[m, 0] for m in range(2)]
    total_len = [r.lengths[m, 0] + r.lengths[m, 1] for m in range(2)]

    def put(index, at, row):
        for k in range(row.shape[1] // 128):
            r.sum_own[index, at + k : at + k + 1, :] = row[:, k * 128 : (k + 1) * 128]

    def put_late(at, row):
        for k in range(cfg.sections):
            r.late_own[k, at : at + 1, :] = row[:, k * 128 : (k + 1) * 128]

    chunk = 32
    for m in range(2):

        landed(r.tokens.at[m], r.fetch_sem.at[1 + m])

        def token_sums(t, carry, m=m):
            at = pl.ds(t * chunk, chunk)
            v = r.tokens[m, at, :].astype(F32)
            place_row = t * chunk + lax.broadcasted_iota(jnp.int32, (chunk, width), 0)
            kept = jnp.where(place_row < total_len[m], v, 0.0)
            return carry[0] + fold_rows(kept), carry[1] + fold_rows(kept * v)

        zero = jnp.zeros((SUB, width), F32)
        sums, squares = sweep(rows // chunk, token_sums, (zero, zero))
        put(m, 0, jnp.sum(sums, axis=0, keepdims=True))
        put(m, 4, jnp.sum(squares, axis=0, keepdims=True))
        if m == 0:
            for k in range(2):
                count = jnp.minimum(total_len[k], rows).astype(F32)
                r.sum_own[0, 8 + k : 9 + k, :] = jnp.full((1, 128), count, F32)
            pl.semaphore_wait(barrier, len(peers))
        first_sum[m].start()

    at_i = lax.broadcasted_iota(jnp.int32, (rows, rows), 0)
    at_r = lax.broadcasted_iota(jnp.int32, (rows, rows), 1)
    r.spread[...] = jnp.where(
        at_r == (at_i % SUB) * steps + at_i // SUB, 1.0, 0.0
    ).astype(BF16)
    r.gather[...] = jnp.where(
        at_i == (at_r % SUB) * steps + at_r // SUB, 1.0, 0.0
    ).astype(BF16)
    for m in range(2):
        r.first_in[m] = matmul(r.spread[...], r.tokens[m]).astype(BF16)
    for m in range(2):
        first_sum[m].turn()
    landed(r.out_grad, r.fetch_sem.at[5])
    for m in range(2):
        r.out_grads[m] = matmul(r.spread[...], r.out_grad[m]).astype(BF16)
    held = lax.broadcasted_iota(jnp.int32, (rows, 128), 0)
    held = (held % SUB) * steps + held // SUB
    all_start, all_end = [], []
    for m in range(2):
        one, zero = jnp.float32(1.0), jnp.float32(0.0)
        past = held >= total_len[m]
        starts = (held == 0) | (held == first_len[m]) | past
        ends = (held == first_len[m] - 1) | (held == total_len[m] - 1) | past | (held == rows - 1)
        r.valid[m] = jnp.where(past, zero, one)
        r.keep_start[m] = jnp.where(starts, zero, one)
        r.keep_end[m] = jnp.where(ends, zero, one)
        for kept, mask in ((all_start, r.keep_start), (all_end, r.keep_end)):
            kept.append(jnp.min(mask[m].reshape(steps, SUB, 128), axis=0))

    r.par[...] = jnp.zeros((SUB, lanes), F32)
    r.par[0:2, :] = jnp.ones((2, lanes), F32)
    landed(r.state_par, r.fetch_sem.at[3])
    r.par[0:2, 0:half] = r.decay[...]
    r.par[2:4, 0:half] = r.freq[...]
    r.par[4:6, 0:half] = r.lstep[...]
    decay, spin = r.par[0:2, :], r.par[2:4, :]
    step_size = jnp.exp(r.par[4:6, :])
    damping = jnp.exp(-decay * step_size)
    bar_re = damping * jnp.cos(spin * step_size)
    bar_im = damping * jnp.sin(spin * step_size)
    modulus = decay * decay + spin * spin
    fac_re = ((bar_re - 1.0) * -decay + bar_im * spin) / modulus
    fac_im = (bar_im * -decay - (bar_re - 1.0) * spin) / modulus
    pow_re, pow_im = bar_re, bar_im
    power = 1
    while power < steps:
        pow_re, pow_im = cmul(pow_re, pow_im, pow_re, pow_im)
        power *= 2

    lane = lax.broadcasted_iota(jnp.int32, (1, 128), 1)
    low_lanes = lane < half - 128
    turn_by = half - 128

    from_column = lax.broadcasted_iota(jnp.int32, (states, 2 * lanes), 0)
    to_column = lax.broadcasted_iota(jnp.int32, (states, 2 * lanes), 1)
    moved_to = jnp.where(from_column < half, from_column, from_column + (lanes - half))
    r.widen[...] = jnp.where(to_column == moved_to, 1.0, 0.0).astype(BF16)
    for held, k in ((r.b_in, 4), (r.c_out, 6), (r.wide_par, 7), (r.gmat, 8)):
        landed(held, r.fetch_sem.at[k])
    for l in range(2):
        r.b_pad[l] = matmul(r.b_in[l], r.widen[...]).astype(BF16)
        blank = jnp.zeros((lanes - half, width), BF16)
        r.c_pad[l, 0:half, :] = r.c_out[l, 0:half, :]
        r.c_pad[l, half:lanes, :] = blank
        r.c_pad[l, lanes : lanes + half, :] = r.c_out[l, half:states, :]
        r.c_pad[l, lanes + half : 2 * lanes, :] = blank

    def across(end, coef, reverse):
        end_re, end_im = end
        coef_re, coef_im = coef
        sub = lax.broadcasted_iota(jnp.int32, (SUB, lanes), 0)
        for by in (1, 2, 4):
            turn = SUB - by if reverse else by
            live = sub < SUB - by if reverse else sub >= by

            def moved(x):
                return jnp.where(live, pltpu.roll(x, turn, 0), 0.0)

            add_re, add_im = cmul(coef_re, coef_im, moved(end_re), moved(end_im))
            coef_re, coef_im = cmul(coef_re, coef_im, moved(coef_re), moved(coef_im))
            end_re, end_im = end_re + add_re, end_im + add_im
        turn = SUB - 1 if reverse else 1
        live = sub < SUB - 1 if reverse else sub >= 1
        return tuple(jnp.where(live, pltpu.roll(x, turn, 0), 0.0) for x in (end_re, end_im))

    def wide8(x, l):
        return jnp.broadcast_to(x[l : l + 1, :], (SUB, x.shape[1]))

    def group_rows(p):
        return pl.ds(p * SUB, SUB)

    def scan_coefs(l, m, reverse):
        keep = r.keep_end if reverse else r.keep_start
        all_kept = repeat_lanes((all_end if reverse else all_start)[m], lanes // 128)
        product = (all_kept * wide8(pow_re, l), all_kept * wide8(pow_im, l))
        return keep, wide8(bar_re, l), wide8(bar_im, l), product

    def advance(keep, m, at, br, bi, re, im, src_re, src_im):
        k = repeat_lanes(keep[m, at, :], lanes // 128)
        kr, ki = k * br, k * bi
        return kr * re - ki * im + src_re, kr * im + ki * re + src_im

    def scan_states(l, m):
        reverse = l == 1
        lead = 0 if reverse else 1
        keep, br, bi, product = scan_coefs(l, m, reverse)
        fr, fi = wide8(fac_re, l), wide8(fac_im, l)
        zero = jnp.zeros((SUB, lanes), F32)

        def ends(t, carry):
            p = steps - 1 - t if reverse else t
            at = group_rows(p)
            v = repeat_lanes(r.valid[m, at, :], lanes // 128)
            drive_re = r.drive[l, m, at, 0:lanes]
            drive_im = r.drive[l, m, at, lanes : 2 * lanes]
            src_re, src_im = cmul(fr, fi, v * drive_re, v * drive_im)
            r.state[l, m, group_rows(p + lead), 0:lanes] = src_re
            r.state[l, m, group_rows(p + lead), lanes : 2 * lanes] = src_im
            return advance(keep, m, at, br, bi, *carry, src_re, src_im)

        end = sweep(steps, ends, (zero, zero))
        enter = across(end, product, reverse)
        first = steps if reverse else 0
        r.state[l, m, first * SUB : (first + 1) * SUB, 0:lanes] = enter[0]
        r.state[l, m, first * SUB : (first + 1) * SUB, lanes : 2 * lanes] = enter[1]

        def fill(t, carry):
            done = []
            for k in range(2):
                p = steps - 1 - (2 * t + k) if reverse else 2 * t + k
                at, to = group_rows(p), group_rows(p + lead)
                src_re = r.state[l, m, to, 0:lanes]
                src_im = r.state[l, m, to, lanes : 2 * lanes]
                carry = advance(keep, m, at, br, bi, *carry, src_re, src_im)
                r.state[l, m, to, 0:lanes] = carry[0]
                r.state[l, m, to, lanes : 2 * lanes] = carry[1]
                done.append(jnp.concatenate([carry[0], -carry[1]], axis=1))
            pair = steps // 2 - 1 - t if reverse else t
            both = jnp.concatenate(done[::-1] if reverse else done, axis=0)
            to = pl.ds(m * rows + pair * 16, 16)
            r.joined[l, to, :] = both.astype(BF16)
            return carry

        sweep(steps // 2, fill, enter)

    def scan_grads(l, m):
        reverse = l == 0
        back = 1 if l == 1 else 0
        keep, br, bi, product = scan_coefs(l, m, reverse)
        keep_state = r.keep_start if l == 0 else r.keep_end
        fr, fi = 2.0 * wide8(fac_re, l), 2.0 * wide8(fac_im, l)
        zero = jnp.zeros((SUB, lanes), F32)

        def ends(t, carry):
            p = steps - 1 - t if reverse else t
            at = group_rows(p)
            q_re = r.q[m, at, 0:lanes]
            q_im = r.q[m, at, lanes : 2 * lanes]
            return advance(keep, m, at, br, bi, *carry, q_re, q_im)

        end = sweep(steps, ends, (zero, zero))
        enter = across(end, product, reverse)

        def fill(t, carry):
            w, bar_sum, fac_sum = carry
            done = []
            for k in range(2):
                p = steps - 1 - (2 * t + k) if reverse else 2 * t + k
                at, near = group_rows(p), group_rows(p + back)
                q_re = r.q[m, at, 0:lanes]
                q_im = r.q[m, at, lanes : 2 * lanes]
                w = advance(keep, m, at, br, bi, *w, q_re, q_im)
                kept = repeat_lanes(keep_state[m, at, :], lanes // 128)
                near_re = kept * r.state[l, m, near, 0:lanes]
                near_im = kept * r.state[l, m, near, lanes : 2 * lanes]
                term = cmul(*w, near_re, near_im)
                bar_sum = (bar_sum[0] + term[0], bar_sum[1] + term[1])
                v = repeat_lanes(r.valid[m, at, :], lanes // 128)
                vw = (v * w[0], v * w[1])
                drive_re = r.drive[l, m, at, 0:lanes]
                drive_im = r.drive[l, m, at, lanes : 2 * lanes]
                term = cmul(*vw, drive_re, drive_im)
                fac_sum = (fac_sum[0] + term[0], fac_sum[1] + term[1])
                gd_re, gd_im = cmul(fr, fi, *vw)
                im_low = pltpu.roll(-gd_im[:, 0:128], 64, 1)
                im_high = pltpu.roll(-gd_im[:, 128:256], 64, 1)
                done.append(
                    jnp.concatenate(
                        [
                            gd_re[:, 0:128],
                            jnp.where(low_lanes, gd_re[:, 128:256], im_low),
                            jnp.where(low_lanes, im_low, im_high),
                        ],
                        axis=1,
                    )
                )
            pair = steps // 2 - 1 - t if reverse else t
            both = jnp.concatenate(done[::-1] if reverse else done, axis=0)
            to = pl.ds(m * rows + pair * 16, 16)
            r.grad_drive[l, to, :] = both.astype(BF16)
            return w, bar_sum, fac_sum

        none = (zero, zero)
        _, bar_sum, fac_sum = sweep(steps // 2, fill, (enter, none, none))
        for k, part in enumerate((*bar_sum, *fac_sum)):
            r.state_sums[l, m, k] = part

    def row_of(ref, l):
        return ref[l : l + 1, :]

    def micro_rows(m):
        return slice(m * rows, (m + 1) * rows)

    gelu_chunk = 16
    halves = (slice(0, rows // 2), slice(rows // 2, rows))

    def moved(m, part):
        return slice(m * rows + part.start, m * rows + part.stop)


    def mixer(l, m, center, inv):
        gain, bias, skip = row_of(r.gain, l), row_of(r.bias, l), row_of(r.skip, l)

        def normalise(t, carry):
            at = pl.ds(t * chunk, chunk)
            if l == 0:
                v = r.first_in[m, at, :].astype(F32)
            else:
                v = r.second_in[m, at, :]
            normed = (v - center) * inv
            r.normed[l, m, at, :] = normed
            to = pl.ds(m * rows + t * chunk, chunk)
            r.scaled[l, to, :] = (normed * gain + bias).astype(BF16)
            return carry

        sweep(rows // chunk, normalise, 0)
        yield
        r.drive[l, m] = matmul(r.scaled[l, micro_rows(m), :], r.b_pad[l])
        yield
        scan_states(l, m)
        yield
        for part in halves:
            r.work[m, part, :] = matmul(r.joined[l, moved(m, part), :], r.c_pad[l])

        yield

        def activate(t, carry):
            at = pl.ds(t * gelu_chunk, gelu_chunk)
            scaled = r.normed[l, m, at, :] * gain + bias
            y = (2.0 * r.work[m, at, :] + skip * scaled).astype(BF16).astype(F32)
            below = 0.5 + 0.5 * lax.erf(y * 0.7071067811865476)
            density = jnp.exp(-0.5 * y * y) * 0.3989422804014327
            active = y * below
            r.active[l, m, at, :] = active
            r.slope[l, m, at, :] = below + y * density
            to = pl.ds(m * rows + t * gelu_chunk, gelu_chunk)
            r.active_low[l, to, :] = active.astype(BF16)
            return carry

        for k, part in enumerate(halves):
            for t in range(rows // gelu_chunk // 2):
                activate(k * (rows // gelu_chunk // 2) + t, 0)
            r.work[m, part, :] = matmul(r.active_low[l, moved(m, part), :], r.gmat[l])

    def first_gate(m):
        gbias = row_of(r.gbias, 0)

        def gate(t, carry):
            at = pl.ds(t * gelu_chunk, gelu_chunk)
            opened = jax.nn.sigmoid(r.work[m, at, :] + gbias)
            r.sig[0, m, at, :] = opened
            v = repeat_lanes(r.valid[m, at, :], width // 128)
            gated = v * r.active[0, m, at, :] * opened
            second = r.first_in[m, at, :].astype(F32) + gated.astype(BF16).astype(F32)
            r.second_in[m, at, :] = second
            kept = v * second
            return carry[0] + fold_rows(kept), carry[1] + fold_rows(kept * second)

        zero = jnp.zeros((SUB, width), F32)
        sums, squares = sweep(rows // gelu_chunk, gate, (zero, zero))
        put(2 + m, 0, jnp.sum(sums, axis=0, keepdims=True))
        put(2 + m, 4, jnp.sum(squares, axis=0, keepdims=True))

    bias_sums = {}
    skip_sums = {}

    def gate_grad(l, m, grad_of):
        gbias = row_of(r.gbias, l)

        def gate(t, carry):
            at = pl.ds(t * gelu_chunk, gelu_chunk)
            if l == 1:
                opened = jax.nn.sigmoid(r.work[m, at, :] + gbias)
                r.sig[1, m, at, :] = opened
            else:
                opened = r.sig[0, m, at, :]
            v = repeat_lanes(r.valid[m, at, :], width // 128)
            masked = v * grad_of(at, v)
            through = masked * opened
            r.through[m, at, :] = through
            grad_logits = through * r.active[l, m, at, :] * (1.0 - opened)
            to = pl.ds(m * rows + t * gelu_chunk, gelu_chunk)
            r.grad_logits[l, to, :] = grad_logits.astype(BF16)
            return carry + fold_rows(grad_logits)

        zero = jnp.zeros((SUB, width), F32)
        bias_sums[l, m] = sweep(rows // gelu_chunk, gate, zero)
        yield

    def branch_grad(l, m):
        gain, bias = row_of(r.gain, l), row_of(r.bias, l)
        r.work[m] = matmul_nt(r.grad_logits[l, micro_rows(m), :], r.gmat[l])
        yield

        def branch(t, carry):
            at = pl.ds(t * chunk, chunk)
            grad_active = r.through[m, at, :] + r.work[m, at, :]
            g = (r.slope[l, m, at, :] * grad_active).astype(BF16)
            to = pl.ds(m * rows + t * chunk, chunk)
            r.branch[l, to, :] = g
            scaled = r.normed[l, m, at, :] * gain + bias
            return carry + fold_rows(g.astype(F32) * scaled)

        zero = jnp.zeros((SUB, width), F32)
        skip_sums[l, m] = sweep(rows // chunk, branch, zero)
        yield
        r.q[m] = matmul_nt(r.branch[l, micro_rows(m), :], r.c_pad[l])
        yield

    def mixer_grad(l, m):
        skip = row_of(r.skip, l)
        scan_grads(l, m)
        yield
        r.work[m] = matmul_nt(r.grad_drive[l, micro_rows(m), :], r.b_in[l])
        yield

        def scaled_grad(t, carry):
            at = pl.ds(t * chunk, chunk)
            to = pl.ds(m * rows + t * chunk, chunk)
            grad = r.work[m, at, :] + skip * r.branch[l, to, :].astype(F32)
            r.grad_scaled[l, m, at, :] = grad
            normed = r.normed[l, m, at, :]
            return carry[0] + fold_rows(grad), carry[1] + fold_rows(grad * normed)

        zero = jnp.zeros((SUB, width), F32)
        sums, products = sweep(rows // chunk, scaled_grad, (zero, zero))
        sums = jnp.sum(sums, axis=0, keepdims=True)
        products = jnp.sum(products, axis=0, keepdims=True)
        if l == 1:
            put(4 + m, 0, sums)
            put(4 + m, 4, products)
        else:
            put_late(2 * m, sums)
            put_late(2 * m + 1, products)

    def moments(total, at, count):
        center = unfold(total, at, 4) / count
        return center, lax.rsqrt(unfold(total, at + 4, 4) / count - center * center + epsilon)

    own_columns = pl.ds(pl.multiple_of(section * 128, 128), 128)

    def gate_weights(l, ref):
        grad = matmul_tn(r.active_low[l, :, own_columns], r.grad_logits[l])
        ref[:, :, :, 0:width] = grad.astype(BF16).reshape(2, QUAD, 16, width)

    def out_weights(l, ref, at):
        grad = 2.0 * matmul_tn(r.joined[l], r.branch[l, :, own_columns])
        grad = jnp.concatenate([grad[0:half, :], grad[lanes : lanes + half, :]], axis=0)
        tall = states // (2 * QUAD)
        for k in range(tall // 16):
            for c in range(2):
                for z in range(QUAD):
                    first = (c * QUAD + z) * tall + 16 * k
                    ref[c, z, :, at + 128 * k : at + 128 * (k + 1)] = grad[
                        first : first + 16, :
                    ].astype(BF16)

    def in_weights(l, ref, at):
        grad = matmul_tn(r.scaled[l, :, own_columns], r.grad_drive[l])
        ref[:, :, :, at : at + states] = grad.astype(BF16).reshape(2, QUAD, 16, states)

    def layer_rows(l):
        def both(sums):
            return jnp.sum(sums[l, 0] + sums[l, 1], axis=0, keepdims=True)

        put_late(4 + 2 * l, both(skip_sums))
        put_late(5 + 2 * l, both(bias_sums))
        part = [
            jnp.sum(r.state_sums[l, 0, k] + r.state_sums[l, 1, k], axis=0, keepdims=True)
            for k in range(4)
        ]
        gb_re, gb_im = 2.0 * part[0], -2.0 * part[1]
        gf_re, gf_im = 2.0 * part[2], -2.0 * part[3]
        one = slice(l, l + 1)
        lam_re, lam_im, size = -decay[one], spin[one], step_size[one]
        b_re, b_im, f_re, f_im = bar_re[one], bar_im[one], fac_re[one], fac_im[one]
        top_re, top_im = size * b_re - f_re, size * b_im - f_im
        square = modulus[one]
        d_re = (top_re * lam_re + top_im * lam_im) / square
        d_im = (top_im * lam_re - top_re * lam_im) / square
        gl_re = size * (b_re * gb_re + b_im * gb_im) + (d_re * gf_re + d_im * gf_im)
        gl_im = size * (b_re * gb_im - b_im * gb_re) + (d_re * gf_im - d_im * gf_re)
        e_re, e_im = cmul(lam_re, lam_im, b_re, b_im)
        g_step = size * ((e_re * gb_re + e_im * gb_im) + (b_re * gf_re + b_im * gf_im))
        parts = [
            row[:, k : k + 128] for row in (-gl_re, gl_im, g_step) for k in range(0, lanes, 128)
        ]
        for k, row in enumerate(parts):
            k += l * len(parts)
            at = 8 + k % LATE_STATES
            r.late_own[k // LATE_STATES, at : at + 1, :] = row

    def mixed_rows(m):
        def mix(t, carry):
            at = pl.ds(t * chunk, chunk)
            gated = (
                r.valid[m, at, :]
                * r.active[1, m, at, own_columns]
                * r.sig[1, m, at, own_columns]
            )
            stream = r.second_in[m, at, own_columns].astype(BF16).astype(F32)
            r.narrow[at, :] = (stream + gated).astype(BF16)
            return carry

        sweep(rows // chunk, mix, 0)
        r.mixed[m] = matmul(r.gather[...], r.narrow[...]).astype(BF16)

    def stream_grad(l, m, total, count, inv):
        gain = row_of(r.gain, l)
        first = gain * unfold(total, 0, 4) / count
        second = gain * unfold(total, 4, 4) / count
        return gain, first, second, inv

    def take(steps):
        for _ in steps:
            pass

    counts, norm0 = [None, None], [None, None]
    for m in range(2):
        total = first_sum[m].total()
        if m == 0:
            counts = [repeat_lanes(total[8 + k : 9 + k, :], width // 128) for k in range(2)]
        norm0[m] = moments(total, 0, counts[m])
        take(mixer(0, m, *norm0[m]))
        first_gate(m)
        mid_sum[m].start()
        mid_sum[m].turn()

    norm1 = [None, None]

    def second_layer(m):
        norm1[m] = moments(mid_sum[m].total(), 0, counts[m])
        yield from mixer(1, m, *norm1[m])
        yield from gate_grad(1, m, lambda at, v: r.out_grads[m, at, :].astype(F32))
        yield from branch_grad(1, m)
        yield from mixer_grad(1, m)
        upper_sum[m].start()
        upper_sum[m].turn()

    for m in range(2):
        take(second_layer(m))

    gate_weights(1, r.mine_0)
    upper.to_core(gate_part)
    out_weights(1, r.mine_0, width)
    upper.to_core(out_part)
    in_weights(1, r.mine_0, width + states)
    upper.to_core(in_part)
    layer_rows(1)

    def second_grad(m, total):
        gain, first, second, inv = stream_grad(1, m, total, counts[m], norm1[m][1])

        def grad_of(at, v):
            grad_normed = r.grad_scaled[1, m, at, :] * gain
            normed = r.normed[1, m, at, :]
            grad_stream = inv * (grad_normed - v * (first + normed * second))
            out_grad = r.out_grads[m, at, :].astype(F32)
            grad = (out_grad + grad_stream.astype(BF16).astype(F32)).astype(BF16)
            r.grad_second[m, at, :] = grad
            return grad.astype(F32)

        return grad_of

    upper_total = [upper_sum[0].total()]
    take(gate_grad(0, 0, second_grad(0, upper_total[0])))
    upper.to_quad(gate_part)
    take(branch_grad(0, 0))
    upper.to_quad(out_part)
    upper.to_quad(in_part)
    take(mixer_grad(0, 0))
    upper_total.append(upper_sum[1].total())
    take(gate_grad(0, 1, second_grad(1, upper_total[1])))
    gate_weights(0, r.mine_1)
    lower.to_core(gate_part)
    take(branch_grad(0, 1))
    upper.to_groups(gate_part)
    lower.to_quad(gate_part)
    last = mixer_grad(0, 1)
    next(last)
    out_weights(0, r.mine_1, width)
    lower.to_core(out_part)
    upper.to_groups(out_part)
    next(last)
    upper.to_groups(in_part)
    take(last)
    lower.to_quad(out_part)
    in_weights(0, r.mine_1, width + states)
    lower.to_core(in_part)
    layer_rows(0)
    late_sum.start()
    upper.to_near(gate_part)
    lower.to_quad(in_part)
    late_sum.turn()
    mixed_rows(0)
    lower.to_groups(gate_part)
    upper.to_near(out_part)
    lower.to_groups(out_part)
    upper.to_near(in_part)
    mixed_rows(1)
    lower.to_groups(in_part)
    upper.to_sections(gate_part)
    lower.to_corner(gate_part)
    upper.to_sections(out_part)
    upper.to_sections(in_part)
    lower.to_sections(gate_part)

    late = late_sum.total()
    r.late[section] = late
    block = r.late.at[section]
    for k in (1, 2, 3):
        remote(block, block, r.late_sem.at[0], r.late_sem.at[1], (beyond[k], dp))
    own_gain = r.gain[0:1, own_columns]
    for m in range(2):
        count = counts[m][:, 0:128]
        first = own_gain * late[2 * m : 2 * m + 1, :] / count
        second = own_gain * late[2 * m + 1 : 2 * m + 2, :] / count
        r.rows[m : m + 1, :] = norm0[m][1]
        inv = r.rows[m : m + 1, own_columns]

        def token_grad(t, carry, m=m, first=first, second=second, inv=inv):
            at = pl.ds(t * chunk, chunk)
            grad_normed = r.grad_scaled[0, m, at, own_columns] * own_gain
            normed = r.normed[0, m, at, own_columns]
            grad_stream = inv * (grad_normed - r.valid[m, at, :] * (first + normed * second))
            grad = r.grad_second[m, at, own_columns].astype(F32) + grad_stream
            high = grad.astype(BF16)
            r.narrow[at, :] = high
            r.narrow_rest[at, :] = (grad - high.astype(F32)).astype(BF16)
            return carry

        sweep(rows // chunk, token_grad, 0)
        r.token_grad[m] = matmul(r.gather[...], r.narrow[...]) + matmul(
            r.gather[...], r.narrow_rest[...]
        )
    r.upper_norm[...] = upper_total[0] + upper_total[1]
    lower.to_corner(out_part)
    lower.to_sections(out_part)
    lower.to_corner(in_part)
    lower.to_sections(in_part)
    upper.to_sibling(gate_part)
    upper.to_sibling(out_part)
    upper.to_sibling(in_part)
    lower.to_sibling(gate_part)
    lower.to_sibling(out_part)
    lower.to_sibling(in_part)
    for k in range(2):
        landed(r.late.at[0 : cfg.sections - 1], r.late_sem.at[k])
    for batch in batches:
        batch.end()
    for each in small:
        each.end()


def lay_out_kernel(cfg, *refs):
    full = refs[1], refs[0]
    late, upper_norm, mixed, token_grad = refs[2:6]
    (
        mixed_out,
        token_grad_out,
        gain_out,
        bias_out,
        decay_out,
        freq_out,
        step_out,
        in_out,
        out_out,
        skip_out,
        gate_out,
        gbias_out,
    ) = refs[6:18]
    in_held, out_held, gate_held = refs[18:21]
    rows_held, sems = refs[21:28], refs[28]
    width, states, half = cfg.width, cfg.states, cfg.half
    tall = states // (2 * QUAD)
    copies = []

    def send(held, out, sem=None):
        copy = pltpu.make_async_copy(held, out, sems.at[3 + len(copies) if sem is None else sem])
        copy.start()
        if sem is None:
            copies.append(copy)

    send(mixed, mixed_out)
    send(token_grad, token_grad_out)
    def columns(at):
        return jnp.concatenate([late[s, at : at + 1, :] for s in range(cfg.sections)], axis=1)

    row_outs = (bias_out, gain_out, skip_out, gbias_out, decay_out, freq_out, step_out)
    values = [
        (columns(0) + columns(2), unfold(upper_norm, 0, 4)),
        (columns(1) + columns(3), unfold(upper_norm, 4, 4)),
        (columns(4), columns(6)),
        (columns(5), columns(7)),
    ]
    for k in range(3):
        places = [(6 * l + 2 * k + part) for l in range(2) for part in range(2)]
        row = [late[p // LATE_STATES, 8 + p % LATE_STATES, :][None] for p in places]
        values.append([jnp.concatenate(row[2 * l : 2 * l + 2], axis=1)[:, 0:half] for l in range(2)])
    for held, out, value in zip(rows_held, row_outs, values):
        for l in range(2):
            held[l : l + 1, :] = value[l]
        send(held, out)

    for l in (1, 0):
        parts = [(full[l], begin) for begin in (0, width, width + states)]
        for s in range(cfg.sections):
            mine = slice(s * 128, (s + 1) * 128)
            members = [(c, z) for c in range(2) for z in range(QUAD)]
            for (part, begin), held, out, wide, sem in (
                (parts[0], gate_held, gate_out, width, 0),
                (parts[2], in_held, in_out, states, 1),
            ):
                for c, z in members:
                    at = s * 128 + (c * QUAD + z) * 16
                    held[l, at : at + 16, :] = part[c, s, z, :, begin : begin + wide].astype(F32)
                send(held.at[l, mine], out.at[l, mine], sem)
            part, begin = parts[1]
            for c, z in members:
                for k in range(tall // 16):
                    first = (c * QUAD + z) * tall + 16 * k
                    out_held[l, first : first + 16, mine] = part[
                        c, s, z, :, begin + k * 128 : begin + (k + 1) * 128
                    ].astype(F32)
        send(out_held.at[l], out_out.at[l], 2)
    for copy in copies:
        copy.wait()
    for sem, out in enumerate((gate_out, in_out, out_out)):
        landed(out, sems.at[sem])


INPUTS = tuple(
    dict(
        tokens=0,
        lengths=0,
        out_grad=0,
        gain=0,
        bias=0,
        decay=0,
        freq=0,
        lstep=0,
        b_in=0,
        c_out=0,
        skip=0,
        gmat=0,
        gbias=0,
    )
)


def per_device(cfg, *args):
    rows, width, states, lanes = cfg.rows, cfg.width, cfg.states, cfg.lanes
    sections, dp, chips = cfg.sections, cfg.dp, cfg.dp // 2
    groups = chips // QUAD
    steps = rows // SUB
    vmem, dma = pltpu.VMEM, pltpu.SemaphoreType.DMA
    widths = (width + 2 * states,) * 2
    outs = {f"full_{k}": ((2, sections, QUAD, 16, w), BF16) for k, w in enumerate(widths)}
    outs.update(
        late=((sections, 16, 128), F32), upper_norm=((8, 128), F32), mixed=((2, rows, 128), BF16), token_grad=((2, rows, 128), F32)
    )
    scratch = dict(
        sum_own=vmem((len(SUM_ROWS), 24, 128), F32),
        sum_sibling=vmem((len(SUM_ROWS), 24, 128), F32),
        sum_slots=vmem((len(SUM_ROWS), min(dp, max(chips, 8)), 24, 128), F32),
        late_own=vmem((sections, 16, 128), F32),
        late_sem=dma((2,)),
        sum_sem=dma((first_sems(cfg)[-1],)),
        grad_sem=dma((grad_sems(groups)[-1],)),
        fetch_sem=dma((9,)),
        lengths=pltpu.SMEM((2, 2), jnp.int32),
        tokens=vmem((2, rows, width), BF16),
        wide_par=vmem((4, 2, width), F32),
        state_par=vmem((3, 2, states // 2), F32),
        b_in=vmem((2, width, states), BF16),
        c_out=vmem((2, states, width), BF16),
        gmat=vmem((2, width, width), BF16),
        out_grad=vmem((2, rows, width), BF16),
        widen=vmem((states, 2 * lanes), BF16),
        q=vmem((2, rows, 2 * lanes), F32),
        spread=vmem((rows, rows), BF16),
        gather=vmem((rows, rows), BF16),
        first_in=vmem((2, rows, width), BF16),
        out_grads=vmem((2, rows, width), BF16),
        second_in=vmem((2, rows, width), F32),
        grad_second=vmem((2, rows, width), BF16),
        valid=vmem((2, rows, 128), F32),
        keep_start=vmem((2, rows, 128), F32),
        keep_end=vmem((2, rows, 128), F32),
        par=vmem((SUB, lanes), F32),
        b_pad=vmem((2, width, 2 * lanes), BF16),
        c_pad=vmem((2, 2 * lanes, width), BF16),
        normed=vmem((2, 2, rows, width), F32),
        scaled=vmem((2, 2 * rows, width), BF16),
        drive=vmem((2, 2, rows, 2 * lanes), F32),
        state=vmem((2, 2, (steps + 1) * SUB, 2 * lanes), F32),
        joined=vmem((2, 2 * rows, 2 * lanes), BF16),
        work=vmem((2, rows, width), F32),
        active=vmem((2, 2, rows, width), F32),
        active_low=vmem((2, 2 * rows, width), BF16),
        slope=vmem((2, 2, rows, width), F32),
        sig=vmem((2, 2, rows, width), F32),
        through=vmem((2, rows, width), F32),
        grad_logits=vmem((2, 2 * rows, width), BF16),
        branch=vmem((2, 2 * rows, width), BF16),
        grad_drive=vmem((2, 2 * rows, states), BF16),
        grad_scaled=vmem((2, 2, rows, width), F32),
        state_sums=vmem((2, 2, 4, SUB, lanes), F32),
        narrow=vmem((rows, 128), BF16),
        narrow_rest=vmem((rows, 128), BF16),
        rows=vmem((SUB, width), F32),
    )
    for k, w in enumerate(widths):
        blocks = (2, QUAD), (QUAD,), (QUAD,), (QUAD,), (groups,)
        for part, block in zip(STAGES, blocks):
            scratch[f"{part}_{k}"] = vmem((*block, 16, w), BF16)
    in_vmem = pl.BlockSpec(memory_space=pltpu.VMEM)
    in_hbm = pl.BlockSpec(memory_space=pltpu.HBM)
    names = tuple(f"{name}_far" for name in INPUTS) + tuple(outs) + tuple(scratch)
    made = pl.pallas_call(
        partial(main_kernel, cfg, names),
        name="layers",
        out_shape=[vmem(*spec) for spec in outs.values()],
        in_specs=[in_hbm for name in INPUTS],
        out_specs=[in_vmem for name in outs],
        scratch_shapes=list(scratch.values()),
        compiler_params=pltpu.CompilerParams(
            collective_id=0, has_side_effects=True, vmem_limit_bytes=56 * 2**20
        ),
    )(*args)
    shapes = [
        ((2, rows, 128), BF16),
        ((2, rows, 128), F32),
        ((2, width), F32),
        ((2, width), F32),
        ((2, states // 2), F32),
        ((2, states // 2), F32),
        ((2, states // 2), F32),
        ((2, width, states), F32),
        ((2, states, width), F32),
        ((2, width), F32),
        ((2, width, width), F32),
        ((2, width), F32),
    ]
    by_copy = (7, 8, 10)
    return pl.pallas_call(
        partial(lay_out_kernel, cfg),
        name="lay_out",
        out_shape=[jax.ShapeDtypeStruct(*spec) for spec in shapes],
        in_specs=[in_vmem] * 6,
        out_specs=[in_hbm] * 12,
        scratch_shapes=[vmem(*shapes[k]) for k in by_copy]
        + [vmem((2, width), F32)] * 4
        + [vmem((2, states // 2), F32)] * 3
        + [dma((12,))],
        compiler_params=pltpu.CompilerParams(vmem_limit_bytes=24 * 2**20),
    )(*made)


def solution(mesh):
    sections, dp = mesh.shape["section"], mesh.shape["dp"]

    def run(*args):
        _, rows, width = args[0].shape
        states = args[8].shape[2]
        cfg = SimpleNamespace(
            rows=rows // dp,
            width=width,
            states=states,
            half=states // 2,
            lanes=-(-states // 256) * 128,
            sections=sections,
            dp=dp,
        )
        split = P(None, "dp", None)
        shared = P()
        placed = P(None, "dp", "section")
        return jax.shard_map(
            partial(per_device, cfg),
            mesh=mesh,
            in_specs=(split, P(None, "dp"), split) + (shared,) * 10,
            out_specs=(placed, placed) + (shared,) * 10,
            check_vma=False,
        )(*args)

    return run
```
